32 devices in a mesh: panel: 8 (over z, y), rhs: 4 (over x, core).
Axes of the slice: x: 2, y: 2, z: 4, core: 2. Of those that a mesh axis runs over, the one named last changes fastest.
Arguments:
- tiles: bfloat16 [192, 5, 256, 256], P(('panel', 'rhs')), as said below
- pattern: int32 [192, 5], replicated, may hold values from 0 to 191, as said below
- counts: int32 [192], replicated, may hold values from 2 to 5
- inputs: bfloat16 [16, 49152], P('rhs', 'panel'), may hold values from -6 to 6
Outputs:
- applied: bfloat16 [16, 49152], P('rhs', 'panel')
The draws below stay inside these ranges and needn't reach their ends.
Inputs may be any that keep to these rules, and one draw needn't show every extreme that they name: pattern[b, 0] = b; pattern[b, 1] is the mate of b: mates are mutual (the mate of the mate of b is b), lie in another panel shard of 24 blocks, in the same index of rhs (block b belongs to device b // 6, that is panel index b // 24 and rhs index (b // 6) % 4); of one device's 6 block columns exactly 1 or zero have their mates in any one panel shard; for k >= 2, pattern[b, k] = (b // 6) * 6 + (b % 6 + k - 1) % 6; entries at or after counts[b] are ignored, as are the tiles there. `tiles`: every tile at slot 0 has all its singular values between 0.1 and 8.
All inputs are finite; a program needn't handle non-finite values.
Results may differ from the reference program's by a relative error of at most 0.0049.
Values may be sent and summed in bfloat16 or wider, within the bound.
No kernel may reach another device: no remote copies, remote signals or barrier semaphores. Data moves between devices by JAX's collectives and lax.ppermute only.
A program may use at most 128 MiB of HBM per device.

```python
import math
import jax
import jax.numpy as jnp
from jax import lax

BLOCK = 256
NEAR = 5
BLK_DEV = 6
STRIDES = 3
CAP = 1
SHARDS = 8
LANES = 4
NB = 192
NP = 49152
NRHS = 16


def mate_table(key):
    key_order, key_steps, key_slots = jax.random.split(key, 3)
    order = jax.vmap(lambda k: jax.random.permutation(k, SHARDS))(jax.random.split(key_order, LANES))
    choices_all = jnp.arange(1, SHARDS // 2).astype(jnp.int32)
    steps = jax.vmap(lambda k: jax.random.permutation(k, choices_all)[:STRIDES])(jax.random.split(key_steps, LANES))
    slots = jax.vmap(lambda k: jax.random.permutation(k, BLK_DEV))(jax.random.split(key_slots, LANES * SHARDS))
    slots = slots.reshape(LANES, SHARDS, BLK_DEV).astype(jnp.int32)
    place = jnp.argsort(order, axis=1).astype(jnp.int32)
    where = jnp.argsort(slots, axis=2).astype(jnp.int32)
    blocks = jnp.arange(NB).astype(jnp.int32)
    column = blocks % BLK_DEV
    device = blocks // BLK_DEV
    panel_of = device // LANES
    lane = device % LANES
    slot = where[lane, panel_of, column]
    group = slot // (2 * CAP)
    within = slot % (2 * CAP)
    spot = place[lane, panel_of]
    stride = steps[lane, group]
    forward = within < CAP
    spot_two = jnp.where(forward, (spot + stride) % SHARDS, (spot - stride) % SHARDS)
    slot_two = jnp.where(forward, slot + CAP, slot - CAP)
    panel_two = order[lane, spot_two]
    column_two = slots[lane, panel_two, slot_two]
    return ((panel_two * LANES + lane) * BLK_DEV + column_two).astype(jnp.int32)


def draw_pattern(key, part):
    mates = mate_table(key)
    blocks = jnp.arange(NB).astype(jnp.int32)
    base = blocks // BLK_DEV * BLK_DEV
    column = blocks % BLK_DEV
    steps = jnp.arange(1, NEAR - 1).astype(jnp.int32)
    locals_part = base[:, None] + (column[:, None] + steps[None, :]) % BLK_DEV
    return jnp.concatenate([blocks[:, None], mates[:, None], locals_part], axis=1).astype(jnp.int32)


def draw_counts(key, part):
    key = jax.random.fold_in(key, 7)
    key_level, key_each, key_spot = jax.random.split(key, 3)
    level = jax.random.randint(key_level, (NB // BLK_DEV,), 2, NEAR + 1)
    level_each = jnp.repeat(level, BLK_DEV)
    each = jax.random.randint(key_each, (NB,), 2, level_each + 1)
    spot = jax.random.randint(key_spot, (), 0, NB)
    each = jnp.where(jnp.arange(NB) == spot, NEAR, each)
    return each.astype(jnp.int32)


def draw_tiles(key, part):
    key = jax.random.fold_in(key, 11)
    key_noise = jax.random.fold_in(key, 0)
    key_column = jax.random.fold_in(key, 2)
    key_turn = jax.random.fold_in(key, 3)
    shape = (NB, NEAR, BLOCK, BLOCK)
    noise = jax.random.normal(key_noise, shape, jnp.float32)
    first = (jnp.arange(NEAR) == 0)[None, :, None, None]
    spread = jnp.where(first, 1.0, 0.8) / math.sqrt(BLOCK)
    ident = 4.0 * jnp.eye(BLOCK, dtype=jnp.float32)[None, None] * first
    column_scale = jnp.exp(jax.random.uniform(key_column, (NB, 1, 1, BLOCK), jnp.float32, math.log(0.1), 0.0))
    mixed = (noise * spread + ident) * column_scale
    levels = BLOCK.bit_length() - 1
    turn_keys = jax.random.split(key_turn, levels)
    for level in range(levels):
        distance = 2 ** level
        groups = BLOCK // (2 * distance)
        angle = jax.random.uniform(turn_keys[level], (NB, 1, 1, groups, 1, distance), jnp.float32, -math.pi, math.pi)
        cosine_term = jnp.cos(angle)
        sine_term = jnp.sin(angle)
        folded = mixed.reshape(NB, NEAR, BLOCK, groups, 2, distance)
        lower = folded[:, :, :, :, 0:1]
        upper = folded[:, :, :, :, 1:2]
        turned = jnp.concatenate([cosine_term * lower - sine_term * upper, sine_term * lower + cosine_term * upper], axis=4)
        mixed = turned.reshape(shape)
    return mixed.astype(jnp.bfloat16)


def level_of(rng, dims, shards, smallest, top_value):
    gain, own = 1.0, jax.random.fold_in(rng, 6)
    for dim, parts in shards:
        steps = jnp.exp(jax.random.uniform(jax.random.fold_in(own, dim), (parts,), jnp.float32, smallest / len(shards), top_value / len(shards)))
        gain = gain * jnp.repeat(steps, dims[dim] // parts).reshape([-1 if axis == dim else 1 for axis in range(len(dims))])
    return gain


def normal_values(key, extent, scale, bound, shards=(), kind=jnp.bfloat16):
    drawn = jax.random.normal(key, extent, jnp.float32) * scale
    if len(shards) > 0:
        drawn = level_of(key, extent, shards, -0.22, 0.18) * drawn
    return jnp.clip(drawn, min=-bound, max=bound).astype(kind)


def setup_inputs(seed: int = 0) -> dict:
    key_list = jax.random.split(jax.random.key(seed), 5)
    return {
        "tiles": draw_tiles(jax.random.fold_in(key_list[4], 71), 0),
        "pattern": draw_pattern(jax.random.fold_in(key_list[4], 71), 0),
        "counts": draw_counts(jax.random.fold_in(key_list[4], 71), 0),
        "inputs": normal_values(key_list[3], (NRHS, NP), 1.0, 6.0, ((0, 4), (1, 8))),
    }


def solve_batch(tiles, pattern, counts, index):
    hi = lax.Precision.HIGHEST
    own = tiles[index]
    mates = pattern[index, 1]
    other = tiles[mates]
    valid = (jnp.arange(NEAR) < counts[index][:, None]).astype(jnp.bfloat16)
    masked = (own * valid[:, :, None, None]).astype(jnp.float32)
    gjj = jnp.einsum('ckab,ckad->cbd', masked, masked, precision=hi)
    ajj = own[:, 0].astype(jnp.float32)
    aqj = own[:, 1].astype(jnp.float32)
    aqq = other[:, 0].astype(jnp.float32)
    ajq = other[:, 1].astype(jnp.float32)
    gjq = jnp.einsum('cab,cad->cbd', ajj, ajq, precision=hi) + jnp.einsum('cab,cad->cbd', aqj, aqq, precision=hi)
    gqq = jnp.einsum('cab,cad->cbd', ajq, ajq, precision=hi) + jnp.einsum('cab,cad->cbd', aqq, aqq, precision=hi)
    upper = jnp.concatenate([gjj, gjq], axis=2)
    lower = jnp.concatenate([jnp.swapaxes(gjq, 1, 2), gqq], axis=2)
    gram = jnp.concatenate([upper, lower], axis=1)
    right = jnp.concatenate([jnp.swapaxes(ajj, 1, 2), jnp.swapaxes(ajq, 1, 2)], axis=1)
    factor = jnp.linalg.cholesky(gram)
    solution = jax.scipy.linalg.cho_solve((factor, True), right)
    return solution.astype(jnp.bfloat16)

def reference(tiles, pattern, counts, inputs):
    batches = jnp.arange(NB).astype(jnp.int32).reshape(-1, BLK_DEV)
    solved = lax.map(lambda index: solve_batch(tiles, pattern, counts, index), batches)
    solved = solved.reshape(NB, 2 * BLOCK, BLOCK)
    diag_part = solved[:, :BLOCK].astype(jnp.float32)
    off_part = solved[:, BLOCK:]
    mates = pattern[:, 1]
    row_off = off_part[mates].astype(jnp.float32)
    blocks = inputs.reshape(NRHS, NB, BLOCK).astype(jnp.float32)
    mate_blocks = blocks[:, mates]
    hi = lax.Precision.HIGHEST
    result = jnp.einsum('rib,iab->ria', blocks, diag_part, precision=hi) + jnp.einsum('rib,iab->ria', mate_blocks, row_off, precision=hi)
    return result.astype(jnp.bfloat16).reshape(NRHS, NP)
```

```python
import functools
import jax
import jax.numpy as jnp
from jax import lax
from jax.experimental import pallas as pl
from jax.experimental.pallas import tpu as pltpu
from jax.sharding import PartitionSpec as P

STEP = 32
NT = (((1,), (1,)), ((), ()))
NN = (((1,), (0,)), ((), ()))
TN = (((0,), (0,)), ((), ()))


def dot(a, b, dims):
    return lax.dot_general(a, b, dims, preferred_element_type=jnp.float32)


def split3(a):
    one = a.astype(jnp.bfloat16)
    rest = a - one.astype(jnp.float32)
    two = rest.astype(jnp.bfloat16)
    three = (rest - two.astype(jnp.float32)).astype(jnp.bfloat16)
    return one, two, three


def dot6(a, b, dims):
    a1, a2, a3 = split3(a)
    b1, b2, b3 = split3(b)
    small = dot(a1, b3, dims) + dot(a3, b1, dims) + dot(a2, b2, dims)
    return dot(a1, b1, dims) + ((dot(a1, b2, dims) + dot(a2, b1, dims)) + small)


def factor(ref):
    systems, width, _ = ref.shape
    halves = width // 128
    groups = STEP // 8
    lane = lax.broadcasted_iota(jnp.int32, (8, 128), 1)
    sub = lax.broadcasted_iota(jnp.int32, (8, 128), 0)
    row_in = lax.broadcasted_iota(jnp.int32, (STEP, width), 0)
    col_in = lax.broadcasted_iota(jnp.int32, (STEP, width), 1)
    col_all = lax.broadcasted_iota(jnp.int32, (width, width), 1)

    def block(kb, carry):
        base = pl.multiple_of(kb * STEP, STEP)
        slabs = []
        for s in range(systems):
            slab = pltpu.roll(ref[s, pl.ds(base, STEP), :], width - base, 1)
            slabs.append([[slab[8 * g:8 * g + 8, 128 * h:128 * h + 128] for h in range(halves)] for g in range(groups)])
        for t in range(STEP):
            top, at = t // 8, t % 8
            for s in range(systems):
                x = slabs[s]
                columns = [jnp.broadcast_to(x[g][0][:, t:t + 1], (8, 128)) for g in range(top, groups)]
                scale = jnp.broadcast_to(lax.rsqrt(columns[0][at:at + 1, :]), (8, 128))
                rows = [jnp.broadcast_to(x[top][h][at:at + 1, :], (8, 128)) * scale for h in range(halves)]
                rows[0] = jnp.where(lane == t, scale, rows[0])
                for g in range(top, groups):
                    c = columns[g - top] * scale
                    if g == top:
                        c = jnp.where(sub > at, c, 0.0)
                    for h in range(halves):
                        old = x[g][h]
                        if h == 0:
                            old = jnp.where(lane == t, 0.0, old)
                        new = old - c * rows[h]
                        if g == top:
                            new = jnp.where(sub == at, rows[h], new)
                        x[g][h] = new
        for s in range(systems):
            slab = jnp.concatenate([jnp.concatenate(line, axis=1) for line in slabs[s]], axis=0)
            slab = jnp.where((col_in > row_in) & (col_in < STEP), 0.0, slab)
            slab = pltpu.roll(slab, base, 1)
            ahead = col_in >= base + STEP
            p1, p2, p3 = split3(slab)
            zero = jnp.zeros_like(p1)
            m1, m2, m3 = (jnp.where(ahead, p, zero) for p in (p1, p2, p3))
            left = jnp.concatenate([m1, m1, m2, m2, m1, m3], axis=0)
            right = jnp.concatenate([p1, p2, p1, p2, p3, p1], axis=0)
            update = dot(left, right, TN)
            pivot_columns = (col_all >= base) & (col_all < base + STEP)
            ref[s] = jnp.where(pivot_columns, 0.0, ref[s]) - update
            ref[s, pl.ds(base, STEP), :] = jnp.where(ahead, 0.0, slab)
        return carry

    lax.fori_loop(0, width // STEP, block, 0)


def own_kernel(counts_ref, tiles_ref, w_ref, z_ref):
    systems, kslots, width, _ = tiles_ref.shape
    for s in range(systems):
        near = tiles_ref[s, 0:2].reshape(2 * width, width)
        w_ref[s] = dot(near, near, TN)
        for k in range(2, kslots):
            @pl.when(k < counts_ref[s])
            def _():
                tile = tiles_ref[s, k]
                w_ref[s] += dot(tile, tile, TN)
    factor(w_ref)
    for s in range(systems):
        w1, w2, w3 = split3(w_ref[s])
        near = jnp.concatenate([tiles_ref[s, 1], tiles_ref[s, 0]], axis=0)
        z = dot(w1, near, NT) + (dot(w2, near, NT) + dot(w3, near, NT))
        z1, z2, z3 = split3(z)
        z_ref[s, 0] = z1
        z_ref[s, 1] = z2
        z_ref[s, 2] = z3


def pair_kernel(panel_ref, w_ref, z_ref, got_ref, x_ref, up_ref, low_ref, t_ref, v_ref, r_ref):
    systems, _, width, _ = z_ref.shape
    for s in range(systems):
        near = got_ref[panel_ref[s]].reshape(2 * width, width)
        x = x_ref[:, s * width:(s + 1) * width]
        z1, z2, z3 = z_ref[s, 0], z_ref[s, 1], z_ref[s, 2]
        v = dot(z1, near, NN) + (dot(z2, near, NN) + dot(z3, near, NN))
        first = dot(x, z1[:, width:], NT) + (dot(x, z2[:, width:], NT) + dot(x, z3[:, width:], NT))
        v_ref[s] = v
        up_ref[s] = first
        r_ref[s] = dot(x, near[width:], NN) - dot6(first, v, NN)
        t_ref[s] = dot(near, near, TN) - dot6(v, v, TN)
    factor(t_ref)
    for s in range(systems):
        y_low = dot6(dot6(r_ref[s], t_ref[s], NT), t_ref[s], NN)
        low_ref[s] = y_low
        up_ref[s] = dot6(up_ref[s] - dot6(y_low, v_ref[s], NT), w_ref[s], NN)


def on_device(tiles, pattern, counts, inputs):
    shards = lax.axis_size("panel")
    lanes = lax.axis_size("rhs")
    systems, kslots, width, _ = tiles.shape
    nrhs_dev = inputs.shape[0]
    nrhs = nrhs_dev * lanes
    per_panel = systems * lanes
    device = lax.axis_index("panel") * lanes + lax.axis_index("rhs")
    first = device * systems
    own_cnt = lax.dynamic_slice_in_dim(counts, first, systems, 0)
    mate_panel = lax.dynamic_slice(pattern, (first, 1), (systems, 1))[:, 0] // per_panel
    hit = mate_panel[None, :] == jnp.arange(shards, dtype=jnp.int32)[:, None]
    slot_of = jnp.sum(hit * jnp.arange(systems, dtype=jnp.int32)[None, :], axis=1)

    sendbuf = tiles[:, :2][slot_of]
    received = lax.all_to_all(sendbuf, "panel", split_axis=0, concat_axis=0, tiled=True)
    x = lax.all_to_all(inputs, "rhs", split_axis=1, concat_axis=0, tiled=True)

    vmem = pl.BlockSpec(memory_space=pltpu.VMEM)
    smem = pl.BlockSpec(memory_space=pltpu.SMEM)
    params = pltpu.CompilerParams(vmem_limit_bytes=56 * 1024 * 1024)
    w, z = pl.pallas_call(
        own_kernel,
        out_shape=(
            jax.ShapeDtypeStruct((systems, width, width), jnp.float32),
            jax.ShapeDtypeStruct((systems, 3, width, 2 * width), jnp.bfloat16),
        ),
        in_specs=[smem, vmem],
        out_specs=(vmem, vmem),
        compiler_params=params,
        cost_estimate=pl.CostEstimate(flops=40 * 10**9, bytes_accessed=8 * 10**6, transcendentals=0),
    )(own_cnt, tiles)
    up, low = pl.pallas_call(
        pair_kernel,
        out_shape=(
            jax.ShapeDtypeStruct((systems, nrhs, width), jnp.float32),
            jax.ShapeDtypeStruct((systems, nrhs, width), jnp.float32),
        ),
        in_specs=[smem, vmem, vmem, vmem, vmem],
        out_specs=(vmem, vmem),
        scratch_shapes=[
            pltpu.VMEM((systems, width, width), jnp.float32),
            pltpu.VMEM((systems, width, width), jnp.float32),
            pltpu.VMEM((systems, nrhs, width), jnp.float32),
        ],
        compiler_params=params,
    )(mate_panel, w, z, received, x)
    returned = lax.all_to_all(low[slot_of], "panel", split_axis=0, concat_axis=0, tiled=True)
    result = (up + returned[mate_panel]).astype(jnp.bfloat16)
    result = jnp.swapaxes(result, 0, 1).reshape(nrhs, systems * width)
    return lax.all_to_all(result, "rhs", split_axis=0, concat_axis=1, tiled=True)


def solution(mesh):
    return jax.shard_map(
        on_device,
        mesh=mesh,
        in_specs=(P(("panel", "rhs"), None, None, None), P(), P(), P("rhs", "panel")),
        out_specs=P("rhs", "panel"),
        check_vma=False,
    )
```

```python
import functools
import jax
import jax.numpy as jnp
from jax import lax
from jax.experimental import pallas as pl
from jax.experimental.pallas import tpu as pltpu
from jax.sharding import PartitionSpec as P

STEP = 32
PIVOTS = 8
NT = (((1,), (1,)), ((), ()))
NN = (((1,), (0,)), ((), ()))
TN = (((0,), (0,)), ((), ()))


def dot(a, b, dims):
    return lax.dot_general(a, b, dims, preferred_element_type=jnp.float32)


def split3(a):
    one = a.astype(jnp.bfloat16)
    rest = a - one.astype(jnp.float32)
    two = rest.astype(jnp.bfloat16)
    three = (rest - two.astype(jnp.float32)).astype(jnp.bfloat16)
    return one, two, three


def dot6(a, b, dims):
    a1, a2, a3 = split3(a)
    b1, b2, b3 = split3(b)
    small = dot(a1, b3, dims) + dot(a3, b1, dims) + dot(a2, b2, dims)
    return dot(a1, b1, dims) + ((dot(a1, b2, dims) + dot(a2, b1, dims)) + small)


def factor(ref, slab_ref, left_ref, right_ref):
    systems, width, _ = ref.shape
    halves = width // 128
    groups = STEP // 8
    lane = lax.broadcasted_iota(jnp.int32, (8, 128), 1)
    sub = lax.broadcasted_iota(jnp.int32, (8, 128), 0)
    row_in = lax.broadcasted_iota(jnp.int32, (STEP, width), 0)
    col_in = lax.broadcasted_iota(jnp.int32, (STEP, width), 1)
    row_all = lax.broadcasted_iota(jnp.int32, (width, width), 0)
    col_all = lax.broadcasted_iota(jnp.int32, (width, width), 1)

    def spread(row):
        return jnp.broadcast_to(row, (8, 128))

    def pivots(slabs):
        for first in range(0, STEP, PIVOTS):
            top = first // 8
            tall = range(top, groups)
            own = (lane >= first) & (lane < first + PIVOTS)
            one = jnp.where(lane - 8 * top == sub, 1.0, 0.0)
            columns = []
            for x in slabs:
                columns.append([{g: spread(x[g][0][:, first + q:first + q + 1]) for g in tall} for q in range(PIVOTS)])
                for g in tall:
                    x[g][0] = jnp.where(own, one if g == top else 0.0, x[g][0])
            if first % 8 == 0:
                scales = [jnp.ones((8, 128), jnp.float32) for _ in slabs]
            for q in range(PIVOTS):
                at = first % 8 + q
                for s, x in enumerate(slabs):
                    cols = columns[s]
                    scale = lax.rsqrt(spread(cols[q][top][at:at + 1, :]))
                    scales[s] = jnp.where(sub == at, scale, scales[s])
                    c = {g: cols[q][g] * scale for g in tall}
                    c[top] = jnp.where(sub > at, c[top], 0.0)
                    for later in range(q + 1, PIVOTS):
                        m = spread(c[top][first % 8 + later:first % 8 + later + 1, :])
                        for g in tall:
                            cols[later][g] = cols[later][g] - c[g] * m
                    for h in range(halves):
                        r = spread(x[top][h][at:at + 1, :]) * scale
                        for g in tall:
                            x[g][h] = x[g][h] - c[g] * r
            if (first + PIVOTS) % 8 == 0:
                for s, x in enumerate(slabs):
                    for h in range(halves):
                        x[top][h] = x[top][h] * scales[s]

    for s in range(systems):
        slab_ref[s] = ref[s, 0:STEP]
        left_ref[s] = jnp.zeros(left_ref.shape[1:], left_ref.dtype)
        right_ref[s] = jnp.zeros(right_ref.shape[1:], right_ref.dtype)

    def block(kb, carry):
        base = pl.multiple_of(kb * STEP, STEP)
        after = pl.multiple_of(jnp.minimum(base + STEP, width - STEP), STEP)
        done = (col_all >= base - STEP) & (col_all < base) & (row_all >= base + STEP)
        for s in range(systems):
            ref[s] = jnp.where(done, 0.0, ref[s]) - dot(left_ref[s], right_ref[s], TN)
        slabs = []
        for s in range(systems):
            slabs.append([[slab_ref[s, 8 * g:8 * g + 8, 128 * h:128 * h + 128] for h in range(halves)] for g in range(groups)])
        pivots(slabs)
        for s in range(systems):
            slab = jnp.concatenate([jnp.concatenate(line, axis=1) for line in slabs[s]], axis=0)
            slab = jnp.where((col_in > row_in) & (col_in < STEP), 0.0, slab)
            n1, n2, n3 = split3(slab[:, STEP:2 * STEP])
            q1, q2, q3 = split3(pltpu.roll(slab, width - STEP, 1))
            update = dot(
                jnp.concatenate([n1, n1, n2, n2, n1, n3], axis=0),
                jnp.concatenate([q1, q2, q1, q2, q3, q1], axis=0),
                TN,
            )
            coming = pltpu.roll(ref[s, pl.ds(after, STEP), :], width - after, 1)
            slab_ref[s] = jnp.where(col_in >= width - STEP, 0.0, coming) - update
            slab = pltpu.roll(slab, base, 1)
            ref[s, pl.ds(base, STEP), :] = jnp.where(col_in >= base + STEP, 0.0, slab)
            p1, p2, p3 = split3(slab)
            zero = jnp.zeros_like(p1)
            m1, m2, m3 = (jnp.where(col_in >= base + 2 * STEP, p, zero) for p in (p1, p2, p3))
            left_ref[s] = jnp.concatenate([m1, m1, m2, m2, m1, m3], axis=0)
            right_ref[s] = jnp.concatenate([p1, p2, p1, p2, p3, p1], axis=0)
        return carry

    lax.fori_loop(0, width // STEP, block, 0)


def factor_scratch(systems, width):
    return [
        pltpu.VMEM((systems, STEP, width), jnp.float32),
        pltpu.VMEM((systems, 6 * STEP, width), jnp.bfloat16),
        pltpu.VMEM((systems, 6 * STEP, width), jnp.bfloat16),
    ]


def own_kernel(counts_ref, tiles_ref, w_ref, z_ref, *scratch):
    systems, kslots, width, _ = tiles_ref.shape
    for s in range(systems):
        near = tiles_ref[s, 0:2].reshape(2 * width, width)
        w_ref[s] = dot(near, near, TN)
        for k in range(2, kslots):
            @pl.when(k < counts_ref[s])
            def _():
                tile = tiles_ref[s, k]
                w_ref[s] += dot(tile, tile, TN)
    factor(w_ref, *scratch)
    for s in range(systems):
        w1, w2, w3 = split3(w_ref[s])
        near = jnp.concatenate([tiles_ref[s, 1], tiles_ref[s, 0]], axis=0)
        z = dot(w1, near, NT) + (dot(w2, near, NT) + dot(w3, near, NT))
        z1, z2, z3 = split3(z)
        z_ref[s, 0] = z1
        z_ref[s, 1] = z2
        z_ref[s, 2] = z3


def pair_kernel(panel_ref, w_ref, z_ref, got_ref, x_ref, up_ref, low_ref, t_ref, vt_ref, r_ref, *scratch):
    systems, _, width, _ = z_ref.shape
    for s in range(systems):
        near = got_ref[panel_ref[s]].reshape(2 * width, width)
        near_t = near.T
        x = x_ref[:, s * width:(s + 1) * width]
        z1, z2, z3 = z_ref[s, 0], z_ref[s, 1], z_ref[s, 2]
        vt = dot(near_t, z1, NT) + (dot(near_t, z2, NT) + dot(near_t, z3, NT))
        first = dot(x, z1[:, width:], NT) + (dot(x, z2[:, width:], NT) + dot(x, z3[:, width:], NT))
        vt_ref[s] = vt
        up_ref[s] = first
        r_ref[s] = dot(x, near[width:], NN) - dot6(first, vt, NT)
        t_ref[s] = dot(near_t, near, NN) - dot6(vt, vt, NT)
    factor(t_ref, *scratch)
    for s in range(systems):
        y_low = dot6(dot6(r_ref[s], t_ref[s], NT), t_ref[s], NN)
        low_ref[s] = y_low
        up_ref[s] = dot6(up_ref[s] - dot6(y_low, vt_ref[s], NN), w_ref[s], NN)


def on_device(tiles, pattern, counts, inputs):
    shards = lax.axis_size("panel")
    lanes = lax.axis_size("rhs")
    systems, kslots, width, _ = tiles.shape
    nrhs_dev = inputs.shape[0]
    nrhs = nrhs_dev * lanes
    per_panel = systems * lanes
    device = lax.axis_index("panel") * lanes + lax.axis_index("rhs")
    first = device * systems
    own_cnt = lax.dynamic_slice_in_dim(counts, first, systems, 0)
    mate_panel = lax.dynamic_slice(pattern, (first, 1), (systems, 1))[:, 0] // per_panel
    hit = mate_panel[None, :] == jnp.arange(shards, dtype=jnp.int32)[:, None]
    slot_of = jnp.sum(hit * jnp.arange(systems, dtype=jnp.int32)[None, :], axis=1)

    sendbuf = tiles[:, :2][slot_of]
    received = lax.all_to_all(sendbuf, "panel", split_axis=0, concat_axis=0, tiled=True)
    x = lax.all_to_all(inputs, "rhs", split_axis=1, concat_axis=0, tiled=True)

    vmem = pl.BlockSpec(memory_space=pltpu.VMEM)
    smem = pl.BlockSpec(memory_space=pltpu.SMEM)
    params = pltpu.CompilerParams(vmem_limit_bytes=56 * 1024 * 1024)
    w, z = pl.pallas_call(
        own_kernel,
        out_shape=(
            jax.ShapeDtypeStruct((systems, width, width), jnp.float32),
            jax.ShapeDtypeStruct((systems, 3, width, 2 * width), jnp.bfloat16),
        ),
        in_specs=[smem, vmem],
        out_specs=(vmem, vmem),
        scratch_shapes=factor_scratch(systems, width),
        compiler_params=params,
        cost_estimate=pl.CostEstimate(flops=40 * 10**9, bytes_accessed=8 * 10**6, transcendentals=0),
    )(own_cnt, tiles)
    up, low = pl.pallas_call(
        pair_kernel,
        out_shape=(
            jax.ShapeDtypeStruct((systems, nrhs, width), jnp.float32),
            jax.ShapeDtypeStruct((systems, nrhs, width), jnp.float32),
        ),
        in_specs=[smem, vmem, vmem, vmem, vmem],
        out_specs=(vmem, vmem),
        scratch_shapes=[
            pltpu.VMEM((systems, width, width), jnp.float32),
            pltpu.VMEM((systems, width, width), jnp.float32),
            pltpu.VMEM((systems, nrhs, width), jnp.float32),
        ] + factor_scratch(systems, width),
        compiler_params=params,
    )(mate_panel, w, z, received, x)
    returned = lax.all_to_all(low[slot_of], "panel", split_axis=0, concat_axis=0, tiled=True)
    result = (up + returned[mate_panel]).astype(jnp.bfloat16)
    result = jnp.swapaxes(result, 0, 1).reshape(nrhs, systems * width)
    return lax.all_to_all(result, "rhs", split_axis=0, concat_axis=1, tiled=True)


def solution(mesh):
    return jax.shard_map(
        on_device,
        mesh=mesh,
        in_specs=(P(("panel", "rhs"), None, None, None), P(), P(), P("rhs", "panel")),
        out_specs=P("rhs", "panel"),
        check_vma=False,
    )
```

```python
import functools
import jax
import jax.numpy as jnp
from jax import lax
from jax.experimental import pallas as pl
from jax.experimental.pallas import tpu as pltpu
from jax.sharding import PartitionSpec as P

STEP = 32
PIVOTS = 4
NT = (((1,), (1,)), ((), ()))
NN = (((1,), (0,)), ((), ()))
TN = (((0,), (0,)), ((), ()))


def dot(a, b, dims):
    return lax.dot_general(a, b, dims, preferred_element_type=jnp.float32)


def split3(a):
    one = a.astype(jnp.bfloat16)
    rest = a - one.astype(jnp.float32)
    two = rest.astype(jnp.bfloat16)
    three = (rest - two.astype(jnp.float32)).astype(jnp.bfloat16)
    return one, two, three


def dot6(a, b, dims):
    a1, a2, a3 = split3(a)
    b1, b2, b3 = split3(b)
    small = dot(a1, b3, dims) + dot(a3, b1, dims) + dot(a2, b2, dims)
    return dot(a1, b1, dims) + ((dot(a1, b2, dims) + dot(a2, b1, dims)) + small)


def factor(ref, slab_ref, left_ref, right_ref):
    systems, width, _ = ref.shape
    halves = width // 128
    groups = STEP // 8
    lane = lax.broadcasted_iota(jnp.int32, (8, 128), 1)
    sub = lax.broadcasted_iota(jnp.int32, (8, 128), 0)
    row_in = lax.broadcasted_iota(jnp.int32, (STEP, width), 0)
    col_in = lax.broadcasted_iota(jnp.int32, (STEP, width), 1)
    row_all = lax.broadcasted_iota(jnp.int32, (width, width), 0)
    col_all = lax.broadcasted_iota(jnp.int32, (width, width), 1)

    def spread(row):
        return jnp.broadcast_to(row, (8, 128))

    def pivots(slabs):
        for first in range(0, STEP, PIVOTS):
            top = first // 8
            tall = range(top, groups)
            own = (lane >= first) & (lane < first + PIVOTS)
            one = jnp.where(lane - 8 * top == sub, 1.0, 0.0)
            columns = []
            for x in slabs:
                columns.append([{g: spread(x[g][0][:, first + q:first + q + 1]) for g in tall} for q in range(PIVOTS)])
                for g in tall:
                    x[g][0] = jnp.where(own, one if g == top else 0.0, x[g][0])
            if first % 8 == 0:
                scales = [jnp.ones((8, 128), jnp.float32) for _ in slabs]
            for q in range(PIVOTS):
                at = first % 8 + q
                for s, x in enumerate(slabs):
                    cols = columns[s]
                    scale = lax.rsqrt(spread(cols[q][top][at:at + 1, :]))
                    scales[s] = jnp.where(sub == at, scale, scales[s])
                    c = {g: cols[q][g] * scale for g in tall}
                    c[top] = jnp.where(sub > at, c[top], 0.0)
                    for later in range(q + 1, PIVOTS):
                        m = spread(c[top][first % 8 + later:first % 8 + later + 1, :])
                        for g in tall:
                            cols[later][g] = cols[later][g] - c[g] * m
                    for h in range(halves):
                        r = spread(x[top][h][at:at + 1, :]) * scale
                        for g in tall:
                            x[g][h] = x[g][h] - c[g] * r
            if (first + PIVOTS) % 8 == 0:
                for s, x in enumerate(slabs):
                    for h in range(halves):
                        x[top][h] = x[top][h] * scales[s]

    for s in range(systems):
        slab_ref[s] = ref[s, 0:STEP]
        left_ref[s] = jnp.zeros(left_ref.shape[1:], left_ref.dtype)
        right_ref[s] = jnp.zeros(right_ref.shape[1:], right_ref.dtype)

    def block(kb, carry):
        base = pl.multiple_of(kb * STEP, STEP)
        after = pl.multiple_of(jnp.minimum(base + STEP, width - STEP), STEP)
        done = (col_all >= base - STEP) & (col_all < base) & (row_all >= base + STEP)
        for s in range(systems):
            ref[s] = jnp.where(done, 0.0, ref[s]) - dot(left_ref[s], right_ref[s], TN)
        slabs = []
        for s in range(systems):
            slabs.append([[slab_ref[s, 8 * g:8 * g + 8, 128 * h:128 * h + 128] for h in range(halves)] for g in range(groups)])
        pivots(slabs)
        for s in range(systems):
            slab = jnp.concatenate([jnp.concatenate(line, axis=1) for line in slabs[s]], axis=0)
            slab = jnp.where((col_in > row_in) & (col_in < STEP), 0.0, slab)
            n1, n2, n3 = split3(slab[:, STEP:2 * STEP])
            q1, q2, q3 = split3(pltpu.roll(slab, width - STEP, 1))
            update = dot(
                jnp.concatenate([n1, n1, n2, n2, n1, n3], axis=0),
                jnp.concatenate([q1, q2, q1, q2, q3, q1], axis=0),
                TN,
            )
            coming = pltpu.roll(ref[s, pl.ds(after, STEP), :], width - after, 1)
            slab_ref[s] = jnp.where(col_in >= width - STEP, 0.0, coming) - update
            slab = pltpu.roll(slab, base, 1)
            ref[s, pl.ds(base, STEP), :] = jnp.where(col_in >= base + STEP, 0.0, slab)
            p1, p2, p3 = split3(slab)
            zero = jnp.zeros_like(p1)
            m1, m2, m3 = (jnp.where(col_in >= base + 2 * STEP, p, zero) for p in (p1, p2, p3))
            left_ref[s] = jnp.concatenate([m1, m1, m2, m2, m1, m3], axis=0)
            right_ref[s] = jnp.concatenate([p1, p2, p1, p2, p3, p1], axis=0)
        return carry

    lax.fori_loop(0, width // STEP, block, 0)


def factor_scratch(systems, width):
    return [
        pltpu.VMEM((systems, STEP, width), jnp.float32),
        pltpu.VMEM((systems, 6 * STEP, width), jnp.bfloat16),
        pltpu.VMEM((systems, 6 * STEP, width), jnp.bfloat16),
    ]


def own_kernel(counts_ref, tiles_ref, w_ref, z_ref, *scratch):
    systems, kslots, width, _ = tiles_ref.shape
    for s in range(systems):
        near = tiles_ref[s, 0:2].reshape(2 * width, width)
        w_ref[s] = dot(near, near, TN)
        for k in range(2, kslots):
            @pl.when(k < counts_ref[s])
            def _():
                tile = tiles_ref[s, k]
                w_ref[s] += dot(tile, tile, TN)
    factor(w_ref, *scratch)
    for s in range(systems):
        w1, w2, w3 = split3(w_ref[s])
        near = jnp.concatenate([tiles_ref[s, 1], tiles_ref[s, 0]], axis=0)
        z = dot(w1, near, NT) + (dot(w2, near, NT) + dot(w3, near, NT))
        z1, z2, z3 = split3(z)
        z_ref[s, 0] = z1
        z_ref[s, 1] = z2
        z_ref[s, 2] = z3


def pair_kernel(shifts, slot_ref, w_ref, z_ref, x_ref, *refs):
    got_refs, refs = refs[:shifts], refs[shifts:]
    up_ref, low_refs, refs = refs[0], refs[1:1 + shifts], refs[1 + shifts:]
    near_ref, low_ref, t_ref, vt_ref, r_ref, *scratch = refs
    systems, _, width, _ = z_ref.shape
    for e in range(shifts):
        @pl.when(slot_ref[e] >= 0)
        def _():
            near_ref[slot_ref[e]] = got_refs[e][0].reshape(2 * width, width)
    for s in range(systems):
        near = near_ref[s]
        near_t = near.T
        x = x_ref[:, s * width:(s + 1) * width]
        z1, z2, z3 = z_ref[s, 0], z_ref[s, 1], z_ref[s, 2]
        vt = dot(near_t, z1, NT) + (dot(near_t, z2, NT) + dot(near_t, z3, NT))
        first = dot(x, z1[:, width:], NT) + (dot(x, z2[:, width:], NT) + dot(x, z3[:, width:], NT))
        vt_ref[s] = vt
        up_ref[s] = first
        r_ref[s] = dot(x, near[width:], NN) - dot6(first, vt, NT)
        t_ref[s] = dot(near_t, near, NN) - dot6(vt, vt, NT)
    factor(t_ref, *scratch)
    for s in range(systems):
        y_low = dot6(dot6(r_ref[s], t_ref[s], NT), t_ref[s], NN)
        low_ref[s] = y_low
        up_ref[s] = dot6(up_ref[s] - dot6(y_low, vt_ref[s], NN), w_ref[s], NN)
    for e in range(shifts):
        low_refs[e][...] = low_ref[jnp.maximum(slot_ref[e], 0)]


def on_device(tiles, pattern, counts, inputs):
    shards = lax.axis_size("panel")
    lanes = lax.axis_size("rhs")
    systems, kslots, width, _ = tiles.shape
    nrhs_dev = inputs.shape[0]
    nrhs = nrhs_dev * lanes
    own_width = systems * width
    my_panel = lax.axis_index("panel")
    my_lane = lax.axis_index("rhs")
    first = (my_panel * lanes + my_lane) * systems
    own_cnt = lax.dynamic_slice_in_dim(counts, first, systems, 0)
    mate_panel = lax.dynamic_slice(pattern, (first, 1), (systems, 1))[:, 0] // (systems * lanes)
    hops = jnp.arange(1, shards, dtype=jnp.int32)

    def slots(panels):
        hit = mate_panel[None, :] == panels[:, None]
        return jnp.max(jnp.where(hit, jnp.arange(systems, dtype=jnp.int32)[None, :], -1), axis=1)

    def shift(value, axis, by):
        size = lax.axis_size(axis)
        return lax.ppermute(value, axis, [(i, (i + by) % size) for i in range(size)])

    to_slot = slots((my_panel + hops) % shards)
    from_slot = slots((my_panel - hops) % shards)
    received = []
    for e in range(1, shards):
        at = jnp.maximum(to_slot[e - 1], 0)
        received.append(shift(lax.dynamic_slice(tiles, (at, 0, 0, 0), (1, 2, width, width)), "panel", e))
    parts = [lax.dynamic_slice_in_dim(inputs, my_lane * own_width, own_width, 1)]
    for e in range(1, lanes):
        part = lax.dynamic_slice_in_dim(inputs, (my_lane + e) % lanes * own_width, own_width, 1)
        parts.append(shift(part, "rhs", e))
    x = jnp.concatenate(parts, axis=0)

    vmem = pl.BlockSpec(memory_space=pltpu.VMEM)
    smem = pl.BlockSpec(memory_space=pltpu.SMEM)
    params = pltpu.CompilerParams(vmem_limit_bytes=56 * 1024 * 1024)
    w, z = pl.pallas_call(
        own_kernel,
        out_shape=(
            jax.ShapeDtypeStruct((systems, width, width), jnp.float32),
            jax.ShapeDtypeStruct((systems, 3, width, 2 * width), jnp.bfloat16),
        ),
        in_specs=[smem, vmem],
        out_specs=(vmem, vmem),
        scratch_shapes=factor_scratch(systems, width),
        compiler_params=params,
        cost_estimate=pl.CostEstimate(flops=40 * 10**9, bytes_accessed=8 * 10**6, transcendentals=0),
    )(own_cnt, tiles)
    piece = jax.ShapeDtypeStruct((nrhs, width), jnp.float32)
    up, *low = pl.pallas_call(
        functools.partial(pair_kernel, shards - 1),
        out_shape=[jax.ShapeDtypeStruct((systems, nrhs, width), jnp.float32)] + [piece] * (shards - 1),
        in_specs=[smem] + [vmem] * (shards + 2),
        out_specs=[vmem] * shards,
        scratch_shapes=[
            pltpu.VMEM((systems, 2 * width, width), jnp.bfloat16),
            pltpu.VMEM((systems, nrhs, width), jnp.float32),
            pltpu.VMEM((systems, width, width), jnp.float32),
            pltpu.VMEM((systems, width, width), jnp.float32),
            pltpu.VMEM((systems, nrhs, width), jnp.float32),
        ] + factor_scratch(systems, width),
        compiler_params=params,
    )(from_slot, w, z, x, *received)
    returned = [shift(low[e - 1], "panel", -e) for e in range(1, shards)]
    result = up
    for e in range(1, shards):
        mine = to_slot[e - 1] == jnp.arange(systems, dtype=jnp.int32)
        result = result + jnp.where(mine[:, None, None], returned[e - 1][None], 0.0)
    result = jnp.swapaxes(result.astype(jnp.bfloat16), 0, 1).reshape(lanes, nrhs_dev, own_width)
    parts = [result[0]] + [shift(result[e], "rhs", -e) for e in range(1, lanes)]
    placed = jnp.stack(parts)[(jnp.arange(lanes, dtype=jnp.int32) - my_lane) % lanes]
    return jnp.swapaxes(placed, 0, 1).reshape(nrhs_dev, lanes * own_width)


def solution(mesh):
    return jax.shard_map(
        on_device,
        mesh=mesh,
        in_specs=(P(("panel", "rhs"), None, None, None), P(), P(), P("rhs", "panel")),
        out_specs=P("rhs", "panel"),
        check_vma=False,
    )
```

```python
import functools
import jax
import jax.numpy as jnp
from jax import lax
from jax.experimental import pallas as pl
from jax.experimental.pallas import tpu as pltpu
from jax.sharding import PartitionSpec as P

STEP = 32
NT = (((1,), (1,)), ((), ()))
NN = (((1,), (0,)), ((), ()))
TN = (((0,), (0,)), ((), ()))


def dot(a, b, dims):
    return lax.dot_general(a, b, dims, preferred_element_type=jnp.float32)


def split3(a):
    one = a.astype(jnp.bfloat16)
    rest = a - one.astype(jnp.float32)
    two = rest.astype(jnp.bfloat16)
    three = (rest - two.astype(jnp.float32)).astype(jnp.bfloat16)
    return one, two, three


def dot6(a, b, dims):
    a1, a2, a3 = a
    b1, b2, b3 = b
    small = dot(a1, b3, dims) + dot(a3, b1, dims) + dot(a2, b2, dims)
    return dot(a1, b1, dims) + ((dot(a1, b2, dims) + dot(a2, b1, dims)) + small)


def apply(rows, parts, dims):
    count = rows.shape[0]
    stack = jnp.concatenate(split3(rows), axis=0)
    high = dot(stack, parts[0], dims)
    low = dot(stack[:2 * count], parts[1], dims)
    return high[:count] + ((high[count:2 * count] + low[:count]) + (high[2 * count:] + low[count:]))


def factor(ref, slab_ref, left_ref, right_ref):
    systems, width, _ = ref.shape
    halves = width // 128
    groups = STEP // 8
    lane = lax.broadcasted_iota(jnp.int32, (8, 128), 1)
    sub = lax.broadcasted_iota(jnp.int32, (8, 128), 0)
    row_in = lax.broadcasted_iota(jnp.int32, (STEP, width), 0)
    col_in = lax.broadcasted_iota(jnp.int32, (STEP, width), 1)
    row_all = lax.broadcasted_iota(jnp.int32, (width, width), 0)
    col_all = lax.broadcasted_iota(jnp.int32, (width, width), 1)

    def spread(row):
        return jnp.broadcast_to(row, (8, 128))

    def pivots(slabs):
        for first in range(0, STEP, 4):
            top, at = first // 8, first % 8
            tall = range(top, groups)
            own = (lane >= first) & (lane < first + 4)
            one = jnp.where(lane - 8 * top == sub, 1.0, 0.0)
            if at == 0:
                inverses = [None] * len(slabs)
            columns, rows = [], []
            for x in slabs:
                columns.append([{g: spread(x[g][0][:, first + q:first + q + 1]) for g in tall} for q in range(4)])
                for g in tall:
                    x[g][0] = jnp.where(own, one if g == top else 0.0, x[g][0])
                rows.append([[spread(x[top][h][at + q:at + q + 1, :]) for h in range(halves)] for q in range(4)])
            for s, x in enumerate(slabs):
                u = columns[s]
                a = {(i, j): spread(u[j][top][at + i:at + i + 1, :]) for j in range(4) for i in range(j + 1)}
                low, inv = {}, []
                for i in range(4):
                    for j in range(i, 4):
                        for k in range(i):
                            a[i, j] = a[i, j] - low[i, k] * a[k, j]
                    inv.append(pl.reciprocal(a[i, i], approx=True))
                    for j in range(i + 1, 4):
                        low[j, i] = a[i, j] * inv[i]
                for i in range(4):
                    for k in range(i):
                        for g in tall:
                            u[i][g] = u[i][g] - u[k][g] * low[i, k]
                        for h in range(halves):
                            rows[s][i][h] = rows[s][i][h] - rows[s][k][h] * low[i, k]
                for i in range(4):
                    for g in tall:
                        m = u[i][g] * inv[i]
                        if g == top:
                            m = jnp.where(sub > at + i, m, 0.0)
                        for h in range(halves):
                            x[g][h] = x[g][h] - m * rows[s][i][h]
                    inverses[s] = inv[i] if at + i == 0 else jnp.where(sub >= at + i, inv[i], inverses[s])
            if at == 4:
                for s, x in enumerate(slabs):
                    scale = inverses[s] * lax.rsqrt(inverses[s])
                    for h in range(halves):
                        x[top][h] = x[top][h] * scale

    for s in range(systems):
        slab_ref[s] = ref[s, 0:STEP]
        left_ref[s] = jnp.zeros(left_ref.shape[1:], left_ref.dtype)
        right_ref[s] = jnp.zeros(right_ref.shape[1:], right_ref.dtype)

    def block(kb, carry):
        base = pl.multiple_of(kb * STEP, STEP)
        after = pl.multiple_of(jnp.minimum(base + STEP, width - STEP), STEP)
        done = (col_all >= base - STEP) & (col_all < base) & (row_all >= base + STEP)
        for s in range(systems):
            ref[s] = jnp.where(done, 0.0, ref[s]) - dot(left_ref[s], right_ref[s], TN)
        slabs = []
        for s in range(systems):
            slabs.append([[slab_ref[s, 8 * g:8 * g + 8, 128 * h:128 * h + 128] for h in range(halves)] for g in range(groups)])
        pivots(slabs)
        for s in range(systems):
            slab = jnp.concatenate([jnp.concatenate(line, axis=1) for line in slabs[s]], axis=0)
            slab = jnp.where((col_in > row_in) & (col_in < STEP), 0.0, slab)
            n1, n2, n3 = split3(slab[:, STEP:2 * STEP])
            q1, q2, q3 = split3(pltpu.roll(slab, width - STEP, 1))
            update = dot(
                jnp.concatenate([n1, n1, n2, n2, n1, n3], axis=0),
                jnp.concatenate([q1, q2, q1, q2, q3, q1], axis=0),
                TN,
            )
            coming = pltpu.roll(ref[s, pl.ds(after, STEP), :], width - after, 1)
            slab_ref[s] = jnp.where(col_in >= width - STEP, 0.0, coming) - update
            slab = pltpu.roll(slab, base, 1)
            ref[s, pl.ds(base, STEP), :] = jnp.where(col_in >= base + STEP, 0.0, slab)
            p1, p2, p3 = split3(slab)
            zero = jnp.zeros_like(p1)
            m1, m2, m3 = (jnp.where(col_in >= base + 2 * STEP, p, zero) for p in (p1, p2, p3))
            left_ref[s] = jnp.concatenate([m1, m1, m2, m2, m1, m3], axis=0)
            right_ref[s] = jnp.concatenate([p1, p2, p1, p2, p3, p1], axis=0)
        return carry

    lax.fori_loop(0, width // STEP, block, 0)


def factor_scratch(systems, width):
    return [
        pltpu.VMEM((systems, STEP, width), jnp.float32),
        pltpu.VMEM((systems, 6 * STEP, width), jnp.bfloat16),
        pltpu.VMEM((systems, 6 * STEP, width), jnp.bfloat16),
    ]


def own_kernel(counts_ref, tiles_ref, w_ref, z_ref, g_ref, *scratch):
    systems, kslots, width, _ = tiles_ref.shape
    for s in range(systems):
        near = tiles_ref[s, 0:2].reshape(2 * width, width)
        g_ref[s] = dot(near, near, TN)
        for k in range(2, kslots):
            @pl.when(k < counts_ref[s])
            def _():
                tile = tiles_ref[s, k]
                g_ref[s] += dot(tile, tile, TN)
    factor(g_ref, *scratch)
    for s in range(systems):
        w1, w2, w3 = split3(g_ref[s])
        w_ref[s, 0] = w1
        w_ref[s, 1] = w2
        near = jnp.concatenate([tiles_ref[s, 1], tiles_ref[s, 0]], axis=0)
        z = dot(w1, near, NT) + (dot(w2, near, NT) + dot(w3, near, NT))
        z1, z2, z3 = split3(z)
        z_ref[s, 0] = z1
        z_ref[s, 1] = z2
        z_ref[s, 2] = z3


def pair_kernel(lanes, place_ref, w_ref, z_ref, x_ref, got_ref, *refs):
    up_refs, refs = refs[:lanes], refs[lanes:]
    low_ref, near_ref, t_ref, v_ref, r_ref, first_ref, sems, *scratch = refs
    systems, _, width, _ = z_ref.shape
    count = x_ref.shape[0] // lanes
    copies = [pltpu.make_async_copy(got_ref.at[place_ref[s]], near_ref.at[s], sems.at[s]) for s in range(systems)]
    for copy in copies:
        copy.start()
    low_ref[...] = jnp.zeros(low_ref.shape, low_ref.dtype)
    for s in range(systems):
        copies[s].wait()
        near = near_ref[s].reshape(2 * width, width)
        near_t = near.T
        z1, z2, z3 = z_ref[s, 0], z_ref[s, 1], z_ref[s, 2]
        v = split3(dot(near_t, z1, NT) + (dot(near_t, z2, NT) + dot(near_t, z3, NT)))
        v_ref[s, 0] = v[0]
        v_ref[s, 1] = v[1]
        t_ref[s] = dot(near_t, near, NN) - dot6(v, v, NT)
    for s in range(systems):
        x = x_ref[:, s * width:(s + 1) * width]
        first_ref[s] = dot(x, z_ref[s, 0, :, width:], NT) + dot(x, z_ref[s, 1, :, width:], NT)
        r_ref[s] = dot(x, near_ref[s, 1], NN)
    for s in range(systems):
        r_ref[s] = r_ref[s] - apply(first_ref[s], (v_ref[s, 0], v_ref[s, 1]), NT)
    factor(t_ref, *scratch)
    parts = [split3(t_ref[s])[:2] for s in range(systems)]
    half = [apply(r_ref[s], parts[s], NT) for s in range(systems)]
    last = [apply(half[s], parts[s], NN) for s in range(systems)]
    mid = [first_ref[s] - apply(last[s], (v_ref[s, 0], v_ref[s, 1]), NN) for s in range(systems)]
    for s in range(systems):
        up = apply(mid[s], (w_ref[s, 0], w_ref[s, 1]), NN)
        for e in range(lanes):
            up_refs[e][s] = up[e * count:(e + 1) * count]
            owner = lax.rem(place_ref[systems] + e, lanes)
            low_ref[place_ref[s] * lanes + owner] = last[s][e * count:(e + 1) * count]


def place_kernel(lanes, place_ref, low_ref, *refs):
    up_refs, out_ref = refs[:lanes], refs[lanes]
    systems, _, width = up_refs[0].shape
    for e in range(lanes):
        owner = lax.rem(place_ref[systems * lanes] + lanes - e, lanes)
        for s in range(systems):
            at = owner * systems + s
            total = up_refs[e][s] + low_ref[place_ref[at] * lanes + owner]
            out_ref[:, pl.ds(pl.multiple_of(at * width, width), width)] = total.astype(out_ref.dtype)


def on_device(tiles, pattern, counts, inputs):
    shards = lax.axis_size("panel")
    lanes = lax.axis_size("rhs")
    systems, kslots, width, _ = tiles.shape
    nrhs_dev = inputs.shape[0]
    own_width = systems * width
    my_panel = lax.axis_index("panel")
    my_lane = lax.axis_index("rhs")
    per_panel = systems * lanes
    own_cnt = lax.dynamic_slice_in_dim(counts, my_panel * per_panel + my_lane * systems, systems, 0)
    panel_mates = lax.dynamic_slice(pattern, (my_panel * per_panel, 1), (per_panel, 1))[:, 0] // per_panel
    mate_panel = lax.dynamic_slice_in_dim(panel_mates, my_lane * systems, systems, 0)
    hit = mate_panel[None, :] == jnp.arange(shards, dtype=jnp.int32)[:, None]
    slot_of = jnp.sum(hit * jnp.arange(systems, dtype=jnp.int32)[None, :], axis=1)
    lane_word = my_lane[None].astype(jnp.int32)

    def shift(value, by):
        return lax.ppermute(value, "rhs", [(i, (i + by) % lanes) for i in range(lanes)])

    received = lax.all_to_all(tiles[:, :2][slot_of], "panel", split_axis=0, concat_axis=0, tiled=True)

    vmem = pl.BlockSpec(memory_space=pltpu.VMEM)
    smem = pl.BlockSpec(memory_space=pltpu.SMEM)
    params = pltpu.CompilerParams(vmem_limit_bytes=56 * 1024 * 1024)
    w, z = pl.pallas_call(
        own_kernel,
        out_shape=(
            jax.ShapeDtypeStruct((systems, 2, width, width), jnp.bfloat16),
            jax.ShapeDtypeStruct((systems, 3, width, 2 * width), jnp.bfloat16),
        ),
        in_specs=[smem, vmem],
        out_specs=(vmem, vmem),
        scratch_shapes=[pltpu.VMEM((systems, width, width), jnp.float32)] + factor_scratch(systems, width),
        compiler_params=params,
        cost_estimate=pl.CostEstimate(flops=40 * 10**9, bytes_accessed=8 * 10**6, transcendentals=0),
    )(own_cnt, tiles)

    inputs, w = lax.optimization_barrier((inputs, w))
    parts = [lax.dynamic_slice_in_dim(inputs, my_lane * own_width, own_width, 1)]
    for e in range(1, lanes):
        part = lax.dynamic_slice_in_dim(inputs, (my_lane + lanes - e) % lanes * own_width, own_width, 1)
        parts.append(shift(part, -e))
    x = jnp.concatenate(parts, axis=0)

    piece = jax.ShapeDtypeStruct((systems, nrhs_dev, width), jnp.float32)
    *up, low = pl.pallas_call(
        functools.partial(pair_kernel, lanes),
        out_shape=[piece] * lanes + [jax.ShapeDtypeStruct((shards * lanes, nrhs_dev, width), jnp.float32)],
        in_specs=[smem, vmem, vmem, vmem, pl.BlockSpec(memory_space=pl.ANY)],
        out_specs=[vmem] * (lanes + 1),
        scratch_shapes=[
            pltpu.VMEM((systems, 2, width, width), jnp.bfloat16),
            pltpu.VMEM((systems, width, width), jnp.float32),
            pltpu.VMEM((systems, 2, width, width), jnp.bfloat16),
            pltpu.VMEM((systems, lanes * nrhs_dev, width), jnp.float32),
            pltpu.VMEM((systems, lanes * nrhs_dev, width), jnp.float32),
            pltpu.SemaphoreType.DMA((systems,)),
        ] + factor_scratch(systems, width),
        compiler_params=params,
    )(jnp.concatenate([mate_panel, lane_word]), w, z, x, received)
    low = lax.all_to_all(low, ("panel", "rhs"), split_axis=0, concat_axis=0, tiled=True)
    up = [up[0]] + [shift(up[e], e) for e in range(1, lanes)]
    return pl.pallas_call(
        functools.partial(place_kernel, lanes),
        out_shape=jax.ShapeDtypeStruct((nrhs_dev, per_panel * width), jnp.bfloat16),
        in_specs=[smem] + [vmem] * (lanes + 1),
        out_specs=vmem,
    )(jnp.concatenate([panel_mates, lane_word]), low, *up)


def solution(mesh):
    return jax.shard_map(
        on_device,
        mesh=mesh,
        in_specs=(P(("panel", "rhs"), None, None, None), P(), P(), P("rhs", "panel")),
        out_specs=P("rhs", "panel"),
        check_vma=False,
    )
```

```python
import functools
import jax
import jax.numpy as jnp
from jax import lax
from jax.experimental import pallas as pl
from jax.experimental.pallas import tpu as pltpu
from jax.sharding import PartitionSpec as P

STEP = 32
PIVOTS = 4
NT = (((1,), (1,)), ((), ()))
NN = (((1,), (0,)), ((), ()))
TN = (((0,), (0,)), ((), ()))


def dot(a, b, dims):
    return lax.dot_general(a, b, dims, preferred_element_type=jnp.float32)


def split3(a):
    one = a.astype(jnp.bfloat16)
    rest = a - one.astype(jnp.float32)
    two = rest.astype(jnp.bfloat16)
    three = (rest - two.astype(jnp.float32)).astype(jnp.bfloat16)
    return one, two, three


def dot6(a, b, dims):
    a1, a2, a3 = a
    b1, b2, b3 = b
    small = dot(a1, b3, dims) + dot(a3, b1, dims) + dot(a2, b2, dims)
    return dot(a1, b1, dims) + ((dot(a1, b2, dims) + dot(a2, b1, dims)) + small)


def dot3(a, b, dims):
    return dot(a[0], b[0], dims) + (dot(a[0], b[1], dims) + dot(a[1], b[0], dims))


def apply(rows, parts, dims):
    count = rows.shape[0]
    stack = jnp.concatenate(split3(rows), axis=0)
    high = dot(stack, parts[0], dims)
    low = dot(stack[:2 * count], parts[1], dims)
    return high[:count] + ((high[count:2 * count] + low[:count]) + (high[2 * count:] + low[count:]))


def factor(ref, slab_ref, left_ref, right_ref):
    systems, width, _ = ref.shape
    halves = width // 128
    groups = STEP // 8
    lane = lax.broadcasted_iota(jnp.int32, (8, 128), 1)
    sub = lax.broadcasted_iota(jnp.int32, (8, 128), 0)
    row_in = lax.broadcasted_iota(jnp.int32, (STEP, width), 0)
    col_in = lax.broadcasted_iota(jnp.int32, (STEP, width), 1)
    row_all = lax.broadcasted_iota(jnp.int32, (width, width), 0)
    col_all = lax.broadcasted_iota(jnp.int32, (width, width), 1)

    def spread(row):
        return jnp.broadcast_to(row, (8, 128))

    def pivots(slabs):
        for first in range(0, STEP, PIVOTS):
            top, start = first // 8, first % 8
            tall = range(top, groups)
            own = (lane >= first) & (lane < first + PIVOTS)
            one = jnp.where(lane - 8 * top == sub, 1.0, 0.0)
            if start == 0:
                inverses = [None] * len(slabs)
            columns = []
            for x in slabs:
                columns.append([{g: spread(x[g][0][:, first + q:first + q + 1]) for g in tall} for q in range(PIVOTS)])
                for g in tall:
                    x[g][0] = jnp.where(own, one if g == top else 0.0, x[g][0])
            for q in range(PIVOTS):
                at = start + q
                for s, x in enumerate(slabs):
                    cols = columns[s]
                    inverse = pl.reciprocal(spread(cols[q][top][at:at + 1, :]), approx=True)
                    inverses[s] = inverse if at == 0 else jnp.where(sub >= at, inverse, inverses[s])
                    c = {g: cols[q][g] * inverse for g in tall}
                    for later in range(q + 1, PIVOTS):
                        m = spread(cols[q][top][start + later:start + later + 1, :])
                        for g in tall:
                            cols[later][g] = cols[later][g] - c[g] * m
                    c[top] = jnp.where(sub > at, c[top], 0.0)
                    for h in range(halves):
                        r = spread(x[top][h][at:at + 1, :])
                        for g in tall:
                            x[g][h] = x[g][h] - c[g] * r
            if start + PIVOTS == 8:
                for s, x in enumerate(slabs):
                    scale = inverses[s] * lax.rsqrt(inverses[s])
                    for h in range(halves):
                        x[top][h] = x[top][h] * scale

    for s in range(systems):
        slab_ref[s] = ref[s, 0:STEP]
        left_ref[s] = jnp.zeros(left_ref.shape[1:], left_ref.dtype)
        right_ref[s] = jnp.zeros(right_ref.shape[1:], right_ref.dtype)

    def block(kb, carry):
        base = pl.multiple_of(kb * STEP, STEP)
        after = pl.multiple_of(jnp.minimum(base + STEP, width - STEP), STEP)
        done = (col_all >= base - STEP) & (col_all < base) & (row_all >= base + STEP)
        for s in range(systems):
            ref[s] = jnp.where(done, 0.0, ref[s]) - dot(left_ref[s], right_ref[s], TN)
        slabs = []
        for s in range(systems):
            slabs.append([[slab_ref[s, 8 * g:8 * g + 8, 128 * h:128 * h + 128] for h in range(halves)] for g in range(groups)])
        pivots(slabs)
        for s in range(systems):
            slab = jnp.concatenate([jnp.concatenate(line, axis=1) for line in slabs[s]], axis=0)
            slab = jnp.where((col_in > row_in) & (col_in < STEP), 0.0, slab)
            n1, n2, n3 = split3(slab[:, STEP:2 * STEP])
            q1, q2, q3 = split3(pltpu.roll(slab, width - STEP, 1))
            update = dot(
                jnp.concatenate([n1, n1, n2, n2, n1, n3], axis=0),
                jnp.concatenate([q1, q2, q1, q2, q3, q1], axis=0),
                TN,
            )
            coming = pltpu.roll(ref[s, pl.ds(after, STEP), :], width - after, 1)
            slab_ref[s] = jnp.where(col_in >= width - STEP, 0.0, coming) - update
            slab = pltpu.roll(slab, base, 1)
            ref[s, pl.ds(base, STEP), :] = jnp.where(col_in >= base + STEP, 0.0, slab)
            p1, p2, p3 = split3(slab)
            zero = jnp.zeros_like(p1)
            m1, m2, m3 = (jnp.where(col_in >= base + 2 * STEP, p, zero) for p in (p1, p2, p3))
            left_ref[s] = jnp.concatenate([m1, m1, m2, m2, m1, m3], axis=0)
            right_ref[s] = jnp.concatenate([p1, p2, p1, p2, p3, p1], axis=0)
        return carry

    lax.fori_loop(0, width // STEP, block, 0)


def factor_scratch(systems, width):
    return [
        pltpu.VMEM((systems, STEP, width), jnp.float32),
        pltpu.VMEM((systems, 6 * STEP, width), jnp.bfloat16),
        pltpu.VMEM((systems, 6 * STEP, width), jnp.bfloat16),
    ]


def own_kernel(counts_ref, tiles_ref, w_ref, z_ref, g_ref, *scratch):
    systems, kslots, width, _ = tiles_ref.shape
    for s in range(systems):
        near = tiles_ref[s, 0:2].reshape(2 * width, width)
        g_ref[s] = dot(near, near, TN)
        for k in range(2, kslots):
            @pl.when(k < counts_ref[s])
            def _():
                tile = tiles_ref[s, k]
                g_ref[s] += dot(tile, tile, TN)
    factor(g_ref, *scratch)
    for s in range(systems):
        w1, w2, w3 = split3(g_ref[s])
        w_ref[s, 0] = w1
        w_ref[s, 1] = w2
        near = jnp.concatenate([tiles_ref[s, 1], tiles_ref[s, 0]], axis=0)
        z = dot(w1, near, NT) + (dot(w2, near, NT) + dot(w3, near, NT))
        z1, z2, z3 = split3(z)
        z_ref[s, 0] = z1
        z_ref[s, 1] = z2
        z_ref[s, 2] = z3


def mid_kernel(place_ref, w_ref, z_ref, x_ref, got_ref, q_ref, back_ref, first_ref, near_ref, t_ref, v_ref, r_ref, sems, *scratch):
    systems, _, width, _ = z_ref.shape
    part = near_ref.shape[3]
    copies = [pltpu.make_async_copy(got_ref.at[place_ref[s]], near_ref.at[s], sems.at[s]) for s in range(systems)]
    for copy in copies:
        copy.start()
    for s in range(systems):
        copies[s].wait()
        near = near_ref[s].reshape(2 * width, part)
        v = split3(dot(z_ref[s, 0], near, NN) + (dot(z_ref[s, 1], near, NN) + dot(z_ref[s, 2], near, NN)))
        vt = [one.T for one in v]
        for i in range(3):
            v_ref[s, i] = vt[i]
        t_ref[s] = dot(near.T, near, NN) - dot6(vt, v, NN)
        x = x_ref[:, s * width:(s + 1) * width]
        first = dot(x, z_ref[s, 0, :, width:], NT) + dot(x, z_ref[s, 1, :, width:], NT)
        first_ref[s, :, :width] = first
        r_ref[s] = dot(x, near[width:], NN) - apply(first, v, NN)
    factor(t_ref, *scratch)
    for s in range(systems):
        near_t = near_ref[s].reshape(2 * width, part).T
        own = split3(t_ref[s])
        vt = [v_ref[s, i] for i in range(3)]
        first_ref[s, :, width:] = apply(r_ref[s], own, NT)
        rest = near_t.astype(jnp.float32) - dot6(vt, [z_ref[s, i] for i in range(3)], NN)
        q = split3(dot6(own, split3(rest), NN))
        for i in range(3):
            q_ref[s, i] = q[i]
        left = split3(-dot3(own, split3(dot3(vt, (w_ref[s, 0], w_ref[s, 1]), NN)), NN))
        for i in range(2):
            back_ref[s, i, :, :width] = left[i]
            back_ref[s, i, :, width:] = own[i]


def last_kernel(lanes, place_ref, w_ref, back_ref, first_ref, x_ref, got_ref, z_any, q_any, *refs):
    up_refs, refs = refs[:lanes], refs[lanes:]
    low_ref, near_ref, z_ref, q_ref, t_ref, v_ref, r_ref, sems, *scratch = refs
    systems, _, width, _ = z_ref.shape
    part = near_ref.shape[3]
    count = x_ref.shape[0] // lanes
    copies = []
    for s in range(systems):
        pairs = ((got_ref.at[place_ref[s]], near_ref.at[s]), (z_any.at[s], z_ref.at[s]), (q_any.at[s], q_ref.at[s]))
        copies.append([pltpu.make_async_copy(a, b, sems.at[s, i]) for i, (a, b) in enumerate(pairs)])
        for copy in copies[s]:
            copy.start()
    low_ref[...] = jnp.zeros(low_ref.shape, low_ref.dtype)
    for s in range(systems):
        for copy in copies[s]:
            copy.wait()
        near = near_ref[s].reshape(2 * width, part)
        upper = dot(z_ref[s, 0], near, NN) + (dot(z_ref[s, 1], near, NN) + dot(z_ref[s, 2], near, NN))
        lower = dot(q_ref[s, 0], near, NN) + (dot(q_ref[s, 1], near, NN) + dot(q_ref[s, 2], near, NN))
        v = split3(jnp.concatenate([upper, lower], axis=0))
        vt = [one.T for one in v]
        v_ref[s, 0] = v[0]
        v_ref[s, 1] = v[1]
        t_ref[s] = dot(near.T, near, NN) - dot6(vt, v, NN)
    for s in range(systems):
        x = x_ref[:, s * width:(s + 1) * width]
        r_ref[s] = dot(x, near_ref[s, 1], NN) - apply(first_ref[s], (v_ref[s, 0], v_ref[s, 1]), NN)
    factor(t_ref, *scratch)
    parts = [split3(t_ref[s])[:2] for s in range(systems)]
    half = [apply(r_ref[s], parts[s], NT) for s in range(systems)]
    last = [apply(half[s], parts[s], NN) for s in range(systems)]
    mid = [first_ref[s] - apply(last[s], (v_ref[s, 0], v_ref[s, 1]), NT) for s in range(systems)]
    for s in range(systems):
        both = apply(mid[s][:, width:], (back_ref[s, 0], back_ref[s, 1]), NN)
        up = apply(mid[s][:, :width], (w_ref[s, 0], w_ref[s, 1]), NN) + both[:, :width]
        low = jnp.concatenate([both[:, width:], last[s]], axis=1)
        for e in range(lanes):
            up_refs[e][s] = up[e * count:(e + 1) * count]
            owner = lax.rem(place_ref[systems] + e, lanes)
            low_ref[place_ref[s] * lanes + owner] = low[e * count:(e + 1) * count]


def place_kernel(lanes, place_ref, low_ref, *refs):
    up_refs, out_ref = refs[:lanes], refs[lanes]
    systems, _, width = up_refs[0].shape
    for e in range(lanes):
        owner = lax.rem(place_ref[systems * lanes] + lanes - e, lanes)
        for s in range(systems):
            at = owner * systems + s
            total = up_refs[e][s] + low_ref[place_ref[at] * lanes + owner]
            out_ref[:, pl.ds(pl.multiple_of(at * width, width), width)] = total.astype(out_ref.dtype)


def on_device(tiles, pattern, counts, inputs):
    shards = lax.axis_size("panel")
    lanes = lax.axis_size("rhs")
    systems, kslots, width, _ = tiles.shape
    nrhs_dev = inputs.shape[0]
    own_width = systems * width
    my_panel = lax.axis_index("panel")
    my_lane = lax.axis_index("rhs")
    per_panel = systems * lanes
    own_cnt = lax.dynamic_slice_in_dim(counts, my_panel * per_panel + my_lane * systems, systems, 0)
    panel_mates = lax.dynamic_slice(pattern, (my_panel * per_panel, 1), (per_panel, 1))[:, 0] // per_panel
    mate_panel = lax.dynamic_slice_in_dim(panel_mates, my_lane * systems, systems, 0)
    hit = mate_panel[None, :] == jnp.arange(shards, dtype=jnp.int32)[:, None]
    slot_of = jnp.sum(hit * jnp.arange(systems, dtype=jnp.int32)[None, :], axis=1)
    lane_word = my_lane[None].astype(jnp.int32)

    def shift(value, by):
        return lax.ppermute(value, "rhs", [(i, (i + by) % lanes) for i in range(lanes)])

    def exchange(source, at, size):
        block = source[:, :2, :, at:at + size][slot_of]
        return lax.all_to_all(block, "panel", split_axis=0, concat_axis=0, tiled=True)

    part = width // 2
    got_one = exchange(tiles, 0, part)

    vmem = pl.BlockSpec(memory_space=pltpu.VMEM)
    smem = pl.BlockSpec(memory_space=pltpu.SMEM)
    anywhere = pl.BlockSpec(memory_space=pl.ANY)
    params = pltpu.CompilerParams(vmem_limit_bytes=28 * 1024 * 1024)
    w, z = pl.pallas_call(
        own_kernel,
        out_shape=(
            jax.ShapeDtypeStruct((systems, 2, width, width), jnp.bfloat16),
            jax.ShapeDtypeStruct((systems, 3, width, 2 * width), jnp.bfloat16),
        ),
        in_specs=[smem, vmem],
        out_specs=(vmem, vmem),
        scratch_shapes=[pltpu.VMEM((systems, width, width), jnp.float32)] + factor_scratch(systems, width),
        compiler_params=params,
        cost_estimate=pl.CostEstimate(flops=20 * 10**9, bytes_accessed=8 * 10**6, transcendentals=0),
    )(own_cnt, tiles)

    later, inputs, w = lax.optimization_barrier((tiles, inputs, w))
    got_two = exchange(later, part, width - part)
    parts = [lax.dynamic_slice_in_dim(inputs, my_lane * own_width, own_width, 1)]
    for e in range(1, lanes):
        part_e = lax.dynamic_slice_in_dim(inputs, (my_lane + lanes - e) % lanes * own_width, own_width, 1)
        parts.append(shift(part_e, -e))
    x = jnp.concatenate(parts, axis=0)
    nrhs = lanes * nrhs_dev
    place = jnp.concatenate([mate_panel, lane_word])

    q, back, first = pl.pallas_call(
        mid_kernel,
        out_shape=(
            jax.ShapeDtypeStruct((systems, 3, part, 2 * width), jnp.bfloat16),
            jax.ShapeDtypeStruct((systems, 2, part, width + part), jnp.bfloat16),
            jax.ShapeDtypeStruct((systems, nrhs, width + part), jnp.float32),
        ),
        in_specs=[smem, vmem, vmem, vmem, anywhere],
        out_specs=(vmem, vmem, vmem),
        scratch_shapes=[
            pltpu.VMEM((systems, 2, width, part), jnp.bfloat16),
            pltpu.VMEM((systems, part, part), jnp.float32),
            pltpu.VMEM((systems, 3, part, width), jnp.bfloat16),
            pltpu.VMEM((systems, nrhs, part), jnp.float32),
            pltpu.SemaphoreType.DMA((systems,)),
        ] + factor_scratch(systems, part),
        compiler_params=params,
        cost_estimate=pl.CostEstimate(flops=15 * 10**9, bytes_accessed=8 * 10**6, transcendentals=0),
    )(place, w, z, x, got_one)

    rest = width - part
    piece = jax.ShapeDtypeStruct((systems, nrhs_dev, width), jnp.float32)
    *up, low = pl.pallas_call(
        functools.partial(last_kernel, lanes),
        out_shape=[piece] * lanes + [jax.ShapeDtypeStruct((shards * lanes, nrhs_dev, width), jnp.float32)],
        in_specs=[smem, vmem, vmem, vmem, vmem, anywhere, anywhere, anywhere],
        out_specs=[vmem] * (lanes + 1),
        scratch_shapes=[
            pltpu.VMEM((systems, 2, width, rest), jnp.bfloat16),
            pltpu.VMEM((systems, 3, width, 2 * width), jnp.bfloat16),
            pltpu.VMEM((systems, 3, part, 2 * width), jnp.bfloat16),
            pltpu.VMEM((systems, rest, rest), jnp.float32),
            pltpu.VMEM((systems, 2, width + part, rest), jnp.bfloat16),
            pltpu.VMEM((systems, nrhs, rest), jnp.float32),
            pltpu.SemaphoreType.DMA((systems, 3)),
        ] + factor_scratch(systems, rest),
        compiler_params=params,
    )(place, w, back, first, x, got_two, z, q)
    low = lax.all_to_all(low, ("panel", "rhs"), split_axis=0, concat_axis=0, tiled=True)
    up = [up[0]] + [shift(up[e], e) for e in range(1, lanes)]
    return pl.pallas_call(
        functools.partial(place_kernel, lanes),
        out_shape=jax.ShapeDtypeStruct((nrhs_dev, per_panel * width), jnp.bfloat16),
        in_specs=[smem] + [vmem] * (lanes + 1),
        out_specs=vmem,
    )(jnp.concatenate([panel_mates, lane_word]), low, *up)


def solution(mesh):
    return jax.shard_map(
        on_device,
        mesh=mesh,
        in_specs=(P(("panel", "rhs"), None, None, None), P(), P(), P("rhs", "panel")),
        out_specs=P("rhs", "panel"),
        check_vma=False,
    )
```

```python
import functools
import jax
import jax.numpy as jnp
from jax import lax
from jax.experimental import pallas as pl
from jax.experimental.pallas import tpu as pltpu
from jax.sharding import PartitionSpec as P

STEP = 32
PIVOTS = 4
NT = (((1,), (1,)), ((), ()))
NN = (((1,), (0,)), ((), ()))
TN = (((0,), (0,)), ((), ()))


def dot(a, b, dims):
    return lax.dot_general(a, b, dims, preferred_element_type=jnp.float32)


def split3(a):
    one = a.astype(jnp.bfloat16)
    rest = a - one.astype(jnp.float32)
    two = rest.astype(jnp.bfloat16)
    three = (rest - two.astype(jnp.float32)).astype(jnp.bfloat16)
    return one, two, three


def dot6(a, b, dims):
    a1, a2, a3 = a
    b1, b2, b3 = b
    small = dot(a1, b3, dims) + dot(a3, b1, dims) + dot(a2, b2, dims)
    return dot(a1, b1, dims) + ((dot(a1, b2, dims) + dot(a2, b1, dims)) + small)


def apply(rows, parts, dims):
    count = rows.shape[0]
    stack = jnp.concatenate(split3(rows), axis=0)
    high = dot(stack, parts[0], dims)
    low = dot(stack[:2 * count], parts[1], dims)
    return high[:count] + ((high[count:2 * count] + low[:count]) + (high[2 * count:] + low[count:]))


def factor(ref, slab_ref, left_ref, right_ref):
    systems, width, _ = ref.shape
    halves = width // 128
    groups = STEP // 8
    lane = lax.broadcasted_iota(jnp.int32, (8, 128), 1)
    sub = lax.broadcasted_iota(jnp.int32, (8, 128), 0)
    row_in = lax.broadcasted_iota(jnp.int32, (STEP, width), 0)
    col_in = lax.broadcasted_iota(jnp.int32, (STEP, width), 1)
    row_all = lax.broadcasted_iota(jnp.int32, (width, width), 0)
    col_all = lax.broadcasted_iota(jnp.int32, (width, width), 1)

    def spread(row):
        return jnp.broadcast_to(row, (8, 128))

    def pivots(slabs):
        for first in range(0, STEP, PIVOTS):
            top, start = first // 8, first % 8
            tall = range(top, groups)
            own = (lane >= first) & (lane < first + PIVOTS)
            one = jnp.where(lane - 8 * top == sub, 1.0, 0.0)
            if start == 0:
                inverses = [None] * len(slabs)
            columns = []
            for x in slabs:
                columns.append([{g: spread(x[g][0][:, first + q:first + q + 1]) for g in tall} for q in range(PIVOTS)])
                for g in tall:
                    x[g][0] = jnp.where(own, one if g == top else 0.0, x[g][0])
            for q in range(PIVOTS):
                at = start + q
                for s, x in enumerate(slabs):
                    cols = columns[s]
                    inverse = pl.reciprocal(spread(cols[q][top][at:at + 1, :]), approx=True)
                    inverses[s] = inverse if at == 0 else jnp.where(sub >= at, inverse, inverses[s])
                    c = {g: cols[q][g] * inverse for g in tall}
                    for later in range(q + 1, PIVOTS):
                        m = spread(cols[q][top][start + later:start + later + 1, :])
                        for g in tall:
                            cols[later][g] = cols[later][g] - c[g] * m
                    c[top] = jnp.where(sub > at, c[top], 0.0)
                    for h in range(halves):
                        r = spread(x[top][h][at:at + 1, :])
                        for g in tall:
                            x[g][h] = x[g][h] - c[g] * r
            if start + PIVOTS == 8:
                for s, x in enumerate(slabs):
                    scale = inverses[s] * lax.rsqrt(inverses[s])
                    for h in range(halves):
                        x[top][h] = x[top][h] * scale

    for s in range(systems):
        slab_ref[s] = ref[s, 0:STEP]
        left_ref[s] = jnp.zeros(left_ref.shape[1:], left_ref.dtype)
        right_ref[s] = jnp.zeros(right_ref.shape[1:], right_ref.dtype)

    def block(kb, carry):
        base = pl.multiple_of(kb * STEP, STEP)
        after = pl.multiple_of(jnp.minimum(base + STEP, width - STEP), STEP)
        done = (col_all >= base - STEP) & (col_all < base) & (row_all >= base + STEP)
        for s in range(systems):
            ref[s] = jnp.where(done, 0.0, ref[s]) - dot(left_ref[s], right_ref[s], TN)
        slabs = []
        for s in range(systems):
            slabs.append([[slab_ref[s, 8 * g:8 * g + 8, 128 * h:128 * h + 128] for h in range(halves)] for g in range(groups)])
        pivots(slabs)
        for s in range(systems):
            slab = jnp.concatenate([jnp.concatenate(line, axis=1) for line in slabs[s]], axis=0)
            slab = jnp.where((col_in > row_in) & (col_in < STEP), 0.0, slab)
            n1, n2, n3 = split3(slab[:, STEP:2 * STEP])
            q1, q2, q3 = split3(pltpu.roll(slab, width - STEP, 1))
            update = dot(
                jnp.concatenate([n1, n1, n2, n2, n1, n3], axis=0),
                jnp.concatenate([q1, q2, q1, q2, q3, q1], axis=0),
                TN,
            )
            coming = pltpu.roll(ref[s, pl.ds(after, STEP), :], width - after, 1)
            slab_ref[s] = jnp.where(col_in >= width - STEP, 0.0, coming) - update
            slab = pltpu.roll(slab, base, 1)
            ref[s, pl.ds(base, STEP), :] = jnp.where(col_in >= base + STEP, 0.0, slab)
            p1, p2, p3 = split3(slab)
            zero = jnp.zeros_like(p1)
            m1, m2, m3 = (jnp.where(col_in >= base + 2 * STEP, p, zero) for p in (p1, p2, p3))
            left_ref[s] = jnp.concatenate([m1, m1, m2, m2, m1, m3], axis=0)
            right_ref[s] = jnp.concatenate([p1, p2, p1, p2, p3, p1], axis=0)
        return carry

    lax.fori_loop(0, width // STEP, block, 0)


def factor_pair(ref, tile_ref, *scratch):
    systems, width, _ = ref.shape
    half = width // 2
    for s in range(systems):
        tile_ref[s] = ref[s, :half, :half]
    factor(tile_ref, *scratch)
    for s in range(systems):
        ref[s, :half, :half] = tile_ref[s]
        u = split3(dot6(split3(tile_ref[s]), split3(ref[s, :half, half:]), NN))
        ref[s, :half, half:] = jnp.zeros((half, half), jnp.float32)
        ut = [one.T for one in u]
        tile_ref[s] = ref[s, half:, half:] - dot6(ut, u, NN)
        ref[s, half:, :half] = dot6(ut, split3(ref[s, :half, :half]), NN)
    factor(tile_ref, *scratch)
    for s in range(systems):
        ref[s, half:, half:] = tile_ref[s]
        ref[s, half:, :half] = -dot6(split3(tile_ref[s]), split3(ref[s, half:, :half]), NN)


def factor_scratch(systems, width):
    half = width // 2
    return [
        pltpu.VMEM((systems, half, half), jnp.float32),
        pltpu.VMEM((systems, STEP, half), jnp.float32),
        pltpu.VMEM((systems, 6 * STEP, half), jnp.bfloat16),
        pltpu.VMEM((systems, 6 * STEP, half), jnp.bfloat16),
    ]


def own_kernel(counts_ref, tiles_ref, w_ref, z_ref, g_ref, *scratch):
    systems, kslots, width, _ = tiles_ref.shape
    for s in range(systems):
        near = tiles_ref[s, 0:2].reshape(2 * width, width)
        g_ref[s] = dot(near, near, TN)
        for k in range(2, kslots):
            @pl.when(k < counts_ref[s])
            def _():
                tile = tiles_ref[s, k]
                g_ref[s] += dot(tile, tile, TN)
    factor_pair(g_ref, *scratch)
    for s in range(systems):
        w1, w2, w3 = split3(g_ref[s])
        w_ref[s, 0] = w1
        w_ref[s, 1] = w2
        near = jnp.concatenate([tiles_ref[s, 1], tiles_ref[s, 0]], axis=0)
        z = dot(w1, near, NT) + (dot(w2, near, NT) + dot(w3, near, NT))
        z1, z2, z3 = split3(z)
        z_ref[s, 0] = z1
        z_ref[s, 1] = z2
        z_ref[s, 2] = z3


def pair_kernel(lanes, place_ref, x_ref, w_any, z_any, got_ref, *refs):
    up_refs, refs = refs[:lanes], refs[lanes:]
    low_ref, near_ref, w_ref, z_ref, t_ref, v_ref, r_ref, first_ref, sems, *scratch = refs
    systems, _, width, _ = z_ref.shape
    count = x_ref.shape[0] // lanes
    copies = []
    for s in range(systems):
        pairs = ((got_ref.at[place_ref[s]], near_ref.at[s]), (z_any.at[s], z_ref.at[s]))
        copies.append([pltpu.make_async_copy(a, b, sems.at[s, i]) for i, (a, b) in enumerate(pairs)])
        for copy in copies[s]:
            copy.start()
    w_copy = pltpu.make_async_copy(w_any, w_ref, sems.at[systems, 0])
    w_copy.start()
    low_ref[...] = jnp.zeros(low_ref.shape, low_ref.dtype)
    for s in range(systems):
        for copy in copies[s]:
            copy.wait()
        near = near_ref[s].reshape(2 * width, width)
        near_t = near.T
        z1, z2, z3 = z_ref[s, 0], z_ref[s, 1], z_ref[s, 2]
        v = split3(dot(near_t, z1, NT) + (dot(near_t, z2, NT) + dot(near_t, z3, NT)))
        v_ref[s, 0] = v[0]
        v_ref[s, 1] = v[1]
        t_ref[s] = dot(near_t, near, NN) - dot6(v, v, NT)
    for s in range(systems):
        x = x_ref[:, s * width:(s + 1) * width]
        first_ref[s] = dot(x, z_ref[s, 0, :, width:], NT) + dot(x, z_ref[s, 1, :, width:], NT)
        r_ref[s] = dot(x, near_ref[s, 1], NN)
    for s in range(systems):
        r_ref[s] = r_ref[s] - apply(first_ref[s], (v_ref[s, 0], v_ref[s, 1]), NT)
    factor_pair(t_ref, *scratch)
    parts = [split3(t_ref[s])[:2] for s in range(systems)]
    half = [apply(r_ref[s], parts[s], NT) for s in range(systems)]
    last = [apply(half[s], parts[s], NN) for s in range(systems)]
    mid = [first_ref[s] - apply(last[s], (v_ref[s, 0], v_ref[s, 1]), NN) for s in range(systems)]
    w_copy.wait()
    for s in range(systems):
        up = apply(mid[s], (w_ref[s, 0], w_ref[s, 1]), NN)
        for e in range(lanes):
            up_refs[e][s] = up[e * count:(e + 1) * count]
            owner = lax.rem(place_ref[systems] + e, lanes)
            low_ref[place_ref[s] * lanes + owner] = last[s][e * count:(e + 1) * count]


def place_kernel(lanes, place_ref, low_ref, *refs):
    up_refs, out_ref = refs[:lanes], refs[lanes]
    systems, _, width = up_refs[0].shape
    for e in range(lanes):
        owner = lax.rem(place_ref[systems * lanes] + lanes - e, lanes)
        for s in range(systems):
            at = owner * systems + s
            total = up_refs[e][s] + low_ref[place_ref[at] * lanes + owner]
            out_ref[:, pl.ds(pl.multiple_of(at * width, width), width)] = total.astype(out_ref.dtype)


def on_device(tiles, pattern, counts, inputs):
    shards = lax.axis_size("panel")
    lanes = lax.axis_size("rhs")
    systems, kslots, width, _ = tiles.shape
    nrhs_dev = inputs.shape[0]
    own_width = systems * width
    my_panel = lax.axis_index("panel")
    my_lane = lax.axis_index("rhs")
    per_panel = systems * lanes
    own_cnt = lax.dynamic_slice_in_dim(counts, my_panel * per_panel + my_lane * systems, systems, 0)
    panel_mates = lax.dynamic_slice(pattern, (my_panel * per_panel, 1), (per_panel, 1))[:, 0] // per_panel
    mate_panel = lax.dynamic_slice_in_dim(panel_mates, my_lane * systems, systems, 0)
    hit = mate_panel[None, :] == jnp.arange(shards, dtype=jnp.int32)[:, None]
    slot_of = jnp.sum(hit * jnp.arange(systems, dtype=jnp.int32)[None, :], axis=1)
    lane_word = my_lane[None].astype(jnp.int32)

    def shift(value, by):
        return lax.ppermute(value, "rhs", [(i, (i + by) % lanes) for i in range(lanes)])

    received = lax.all_to_all(tiles[:, :2][slot_of], "panel", split_axis=0, concat_axis=0, tiled=True)

    vmem = pl.BlockSpec(memory_space=pltpu.VMEM)
    smem = pl.BlockSpec(memory_space=pltpu.SMEM)
    anywhere = pl.BlockSpec(memory_space=pl.ANY)
    params = pltpu.CompilerParams(vmem_limit_bytes=56 * 1024 * 1024)
    w, z = pl.pallas_call(
        own_kernel,
        out_shape=(
            jax.ShapeDtypeStruct((systems, 2, width, width), jnp.bfloat16),
            jax.ShapeDtypeStruct((systems, 3, width, 2 * width), jnp.bfloat16),
        ),
        in_specs=[smem, vmem],
        out_specs=(vmem, vmem),
        scratch_shapes=[pltpu.VMEM((systems, width, width), jnp.float32)] + factor_scratch(systems, width),
        compiler_params=params,
        cost_estimate=pl.CostEstimate(flops=40 * 10**9, bytes_accessed=8 * 10**6, transcendentals=0),
    )(own_cnt, tiles)

    inputs, w = lax.optimization_barrier((inputs, w))
    parts = [lax.dynamic_slice_in_dim(inputs, my_lane * own_width, own_width, 1)]
    for e in range(1, lanes):
        part = lax.dynamic_slice_in_dim(inputs, (my_lane + lanes - e) % lanes * own_width, own_width, 1)
        parts.append(shift(part, -e))
    x = jnp.concatenate(parts, axis=0)

    piece = jax.ShapeDtypeStruct((systems, nrhs_dev, width), jnp.float32)
    *up, low = pl.pallas_call(
        functools.partial(pair_kernel, lanes),
        out_shape=[piece] * lanes + [jax.ShapeDtypeStruct((shards * lanes, nrhs_dev, width), jnp.float32)],
        in_specs=[smem, vmem, anywhere, anywhere, anywhere],
        out_specs=[vmem] * (lanes + 1),
        scratch_shapes=[
            pltpu.VMEM((systems, 2, width, width), jnp.bfloat16),
            pltpu.VMEM((systems, 2, width, width), jnp.bfloat16),
            pltpu.VMEM((systems, 3, width, 2 * width), jnp.bfloat16),
            pltpu.VMEM((systems, width, width), jnp.float32),
            pltpu.VMEM((systems, 2, width, width), jnp.bfloat16),
            pltpu.VMEM((systems, lanes * nrhs_dev, width), jnp.float32),
            pltpu.VMEM((systems, lanes * nrhs_dev, width), jnp.float32),
            pltpu.SemaphoreType.DMA((systems + 1, 2)),
        ] + factor_scratch(systems, width),
        compiler_params=params,
    )(jnp.concatenate([mate_panel, lane_word]), x, w, z, received)
    low = lax.all_to_all(low, ("panel", "rhs"), split_axis=0, concat_axis=0, tiled=True)
    up = [up[0]] + [shift(up[e], e) for e in range(1, lanes)]
    return pl.pallas_call(
        functools.partial(place_kernel, lanes),
        out_shape=jax.ShapeDtypeStruct((nrhs_dev, per_panel * width), jnp.bfloat16),
        in_specs=[smem] + [vmem] * (lanes + 1),
        out_specs=vmem,
    )(jnp.concatenate([panel_mates, lane_word]), low, *up)


def solution(mesh):
    return jax.shard_map(
        on_device,
        mesh=mesh,
        in_specs=(P(("panel", "rhs"), None, None, None), P(), P(), P("rhs", "panel")),
        out_specs=P("rhs", "panel"),
        check_vma=False,
    )
```

```python
import functools
import jax
import jax.numpy as jnp
from jax import lax
from jax.experimental import pallas as pl
from jax.experimental.pallas import tpu as pltpu
from jax.sharding import PartitionSpec as P

STEP = 32
NT = (((1,), (1,)), ((), ()))
NN = (((1,), (0,)), ((), ()))
TN = (((0,), (0,)), ((), ()))


def dot(a, b, dims):
    return lax.dot_general(a, b, dims, preferred_element_type=jnp.float32)


def split3(a):
    one = a.astype(jnp.bfloat16)
    rest = a - one.astype(jnp.float32)
    two = rest.astype(jnp.bfloat16)
    three = (rest - two.astype(jnp.float32)).astype(jnp.bfloat16)
    return one, two, three


def dot6(a, b, dims):
    a1, a2, a3 = a
    b1, b2, b3 = b
    small = dot(a1, b3, dims) + dot(a3, b1, dims) + dot(a2, b2, dims)
    return dot(a1, b1, dims) + ((dot(a1, b2, dims) + dot(a2, b1, dims)) + small)


def apply(rows, parts, dims):
    count = rows.shape[0]
    stack = jnp.concatenate(split3(rows), axis=0)
    high = dot(stack, parts[0], dims)
    low = dot(stack[:2 * count], parts[1], dims)
    return high[:count] + ((high[count:2 * count] + low[:count]) + (high[2 * count:] + low[count:]))


def factor(ref, slab_ref, left_ref, right_ref):
    systems, width, _ = ref.shape
    halves = width // 128
    groups = STEP // 8
    lane = lax.broadcasted_iota(jnp.int32, (8, 128), 1)
    sub = lax.broadcasted_iota(jnp.int32, (8, 128), 0)
    row_in = lax.broadcasted_iota(jnp.int32, (STEP, width), 0)
    col_in = lax.broadcasted_iota(jnp.int32, (STEP, width), 1)
    row_all = lax.broadcasted_iota(jnp.int32, (width, width), 0)
    col_all = lax.broadcasted_iota(jnp.int32, (width, width), 1)

    def spread(row):
        return jnp.broadcast_to(row, (8, 128))

    def pivots(slabs):
        each = range(len(slabs))
        for first in range(0, STEP, 4):
            top, at = first // 8, first % 8
            tall = range(top, groups)
            own = (lane >= first) & (lane < first + 4)
            one = jnp.where(lane - 8 * top == sub, 1.0, 0.0)
            if at == 0:
                inverses = [None for _ in each]
            u = [[{g: spread(x[g][0][:, first + q:first + q + 1]) for g in tall} for q in range(4)] for x in slabs]
            a = [{(i, j): spread(u[s][j][top][at + i:at + i + 1, :]) for j in range(4) for i in range(j + 1)} for s in each]
            for x in slabs:
                for g in tall:
                    x[g][0] = jnp.where(own, one if g == top else 0.0, x[g][0])
            y = [[[spread(x[top][h][at + q:at + q + 1, :]) for h in range(halves)] for q in range(4)] for x in slabs]
            low = [{} for _ in each]
            inv = [[None] * 4 for _ in each]
            for p in (0, 2):
                n = p + 1
                delta = [a[s][p, p] * a[s][n, n] - a[s][p, n] * a[s][p, n] for s in each]
                for s in each:
                    inv[s][p] = pl.reciprocal(a[s][p, p], approx=True)
                    inv[s][n] = pl.reciprocal(delta[s], approx=True) * a[s][p, p]
                for j in range(n, 4):
                    for s in each:
                        low[s][j, p] = a[s][p, j] * inv[s][p]
                for j in range(n + 1, 4):
                    for s in each:
                        a[s][n, j] = a[s][n, j] - low[s][n, p] * a[s][p, j]
                for j in range(n + 1, 4):
                    for s in each:
                        low[s][j, n] = a[s][n, j] * inv[s][n]
                for i in range(n + 1, 4):
                    for j in range(i, 4):
                        for s in each:
                            a[s][i, j] = (a[s][i, j] - low[s][i, p] * a[s][p, j]) - low[s][i, n] * a[s][n, j]
            for i in range(4):
                for k in range(i):
                    for s in each:
                        for g in tall:
                            u[s][i][g] = u[s][i][g] - u[s][k][g] * low[s][i, k]
                        for h in range(halves):
                            y[s][i][h] = y[s][i][h] - y[s][k][h] * low[s][i, k]
                for s in each:
                    inverses[s] = inv[s][i] if at + i == 0 else jnp.where(sub >= at + i, inv[s][i], inverses[s])
                    for g in tall:
                        m = u[s][i][g] * inv[s][i]
                        if g == top:
                            m = jnp.where(sub > at + i, m, 0.0)
                        for h in range(halves):
                            slabs[s][g][h] = slabs[s][g][h] - m * y[s][i][h]
            if at == 4:
                for s in each:
                    scale = inverses[s] * lax.rsqrt(inverses[s])
                    for h in range(halves):
                        slabs[s][top][h] = slabs[s][top][h] * scale

    for s in range(systems):
        slab_ref[s] = ref[s, 0:STEP]
        left_ref[s] = jnp.zeros(left_ref.shape[1:], left_ref.dtype)
        right_ref[s] = jnp.zeros(right_ref.shape[1:], right_ref.dtype)

    def block(kb, carry):
        base = pl.multiple_of(kb * STEP, STEP)
        after = pl.multiple_of(jnp.minimum(base + STEP, width - STEP), STEP)
        done = (col_all >= base - STEP) & (col_all < base) & (row_all >= base + STEP)
        for s in range(systems):
            ref[s] = jnp.where(done, 0.0, ref[s]) - dot(left_ref[s], right_ref[s], TN)
        slabs = []
        for s in range(systems):
            slabs.append([[slab_ref[s, 8 * g:8 * g + 8, 128 * h:128 * h + 128] for h in range(halves)] for g in range(groups)])
        pivots(slabs)
        for s in range(systems):
            slab = jnp.concatenate([jnp.concatenate(line, axis=1) for line in slabs[s]], axis=0)
            slab = jnp.where((col_in > row_in) & (col_in < STEP), 0.0, slab)
            n1, n2, n3 = split3(slab[:, STEP:2 * STEP])
            q1, q2, q3 = split3(pltpu.roll(slab, width - STEP, 1))
            update = dot(
                jnp.concatenate([n1, n1, n2, n2, n1, n3], axis=0),
                jnp.concatenate([q1, q2, q1, q2, q3, q1], axis=0),
                TN,
            )
            coming = pltpu.roll(ref[s, pl.ds(after, STEP), :], width - after, 1)
            slab_ref[s] = jnp.where(col_in >= width - STEP, 0.0, coming) - update
            slab = pltpu.roll(slab, base, 1)
            ref[s, pl.ds(base, STEP), :] = jnp.where(col_in >= base + STEP, 0.0, slab)
            p1, p2, p3 = split3(slab)
            zero = jnp.zeros_like(p1)
            m1, m2, m3 = (jnp.where(col_in >= base + 2 * STEP, p, zero) for p in (p1, p2, p3))
            left_ref[s] = jnp.concatenate([m1, m1, m2, m2, m1, m3], axis=0)
            right_ref[s] = jnp.concatenate([p1, p2, p1, p2, p3, p1], axis=0)
        return carry

    lax.fori_loop(0, width // STEP, block, 0)


def factor_scratch(systems, width):
    return [
        pltpu.VMEM((systems, STEP, width), jnp.float32),
        pltpu.VMEM((systems, 6 * STEP, width), jnp.bfloat16),
        pltpu.VMEM((systems, 6 * STEP, width), jnp.bfloat16),
    ]


def scaled(matrix):
    factor_of = 1.0 / jnp.max(jnp.max(matrix, axis=1, keepdims=True), axis=0, keepdims=True)
    return matrix * factor_of, jnp.sqrt(factor_of)


def own_kernel(counts_ref, tiles_ref, w_ref, z_ref, g_ref, *scratch):
    systems, kslots, width, _ = tiles_ref.shape
    for s in range(systems):
        near = tiles_ref[s, 0:2].reshape(2 * width, width)
        g_ref[s] = dot(near, near, TN)
        for k in range(2, kslots):
            @pl.when(k < counts_ref[s])
            def _():
                tile = tiles_ref[s, k]
                g_ref[s] += dot(tile, tile, TN)
    roots = []
    for s in range(systems):
        g_ref[s], root = scaled(g_ref[s])
        roots.append(root)
    factor(g_ref, *scratch)
    for s in range(systems):
        w1, w2, w3 = split3(g_ref[s] * roots[s])
        w_ref[s, 0] = w1
        w_ref[s, 1] = w2
        near = jnp.concatenate([tiles_ref[s, 1], tiles_ref[s, 0]], axis=0)
        z = dot(w1, near, NT) + (dot(w2, near, NT) + dot(w3, near, NT))
        z1, z2, z3 = split3(z)
        z_ref[s, 0] = z1
        z_ref[s, 1] = z2
        z_ref[s, 2] = z3


def pair_kernel(lanes, place_ref, x_ref, w_any, z_any, got_ref, *refs):
    up_refs, refs = refs[:lanes], refs[lanes:]
    low_ref, near_ref, w_ref, z_ref, t_ref, v_ref, r_ref, first_ref, sems, *scratch = refs
    systems, _, width, _ = z_ref.shape
    count = x_ref.shape[0] // lanes
    copies = []
    for s in range(systems):
        pairs = ((got_ref.at[place_ref[s]], near_ref.at[s]), (z_any.at[s], z_ref.at[s]))
        copies.append([pltpu.make_async_copy(a, b, sems.at[s, i]) for i, (a, b) in enumerate(pairs)])
        for copy in copies[s]:
            copy.start()
    w_copy = pltpu.make_async_copy(w_any, w_ref, sems.at[systems, 0])
    w_copy.start()
    low_ref[...] = jnp.zeros(low_ref.shape, low_ref.dtype)
    roots = []
    for s in range(systems):
        for copy in copies[s]:
            copy.wait()
        near = near_ref[s].reshape(2 * width, width)
        near_t = near.T
        z1, z2, z3 = z_ref[s, 0], z_ref[s, 1], z_ref[s, 2]
        v = split3(dot(near_t, z1, NT) + (dot(near_t, z2, NT) + dot(near_t, z3, NT)))
        v_ref[s, 0] = v[0]
        v_ref[s, 1] = v[1]
        t_ref[s], root = scaled(dot(near_t, near, NN) - dot6(v, v, NT))
        roots.append(root)
    for s in range(systems):
        x = x_ref[:, s * width:(s + 1) * width]
        first_ref[s] = dot(x, z_ref[s, 0, :, width:], NT) + dot(x, z_ref[s, 1, :, width:], NT)
        r_ref[s] = dot(x, near_ref[s, 1], NN)
    for s in range(systems):
        r_ref[s] = r_ref[s] - apply(first_ref[s], (v_ref[s, 0], v_ref[s, 1]), NT)
    factor(t_ref, *scratch)
    parts = [split3(t_ref[s] * roots[s])[:2] for s in range(systems)]
    half = [apply(r_ref[s], parts[s], NT) for s in range(systems)]
    last = [apply(half[s], parts[s], NN) for s in range(systems)]
    mid = [first_ref[s] - apply(last[s], (v_ref[s, 0], v_ref[s, 1]), NN) for s in range(systems)]
    w_copy.wait()
    for s in range(systems):
        up = apply(mid[s], (w_ref[s, 0], w_ref[s, 1]), NN)
        for e in range(lanes):
            up_refs[e][s] = up[e * count:(e + 1) * count]
            owner = lax.rem(place_ref[systems] + e, lanes)
            low_ref[place_ref[s] * lanes + owner] = last[s][e * count:(e + 1) * count]


def place_kernel(lanes, place_ref, low_ref, *refs):
    up_refs, out_ref = refs[:lanes], refs[lanes]
    systems, _, width = up_refs[0].shape
    for e in range(lanes):
        owner = lax.rem(place_ref[systems * lanes] + lanes - e, lanes)
        for s in range(systems):
            at = owner * systems + s
            total = up_refs[e][s] + low_ref[place_ref[at] * lanes + owner]
            out_ref[:, pl.ds(pl.multiple_of(at * width, width), width)] = total.astype(out_ref.dtype)


def on_device(tiles, pattern, counts, inputs):
    shards = lax.axis_size("panel")
    lanes = lax.axis_size("rhs")
    systems, kslots, width, _ = tiles.shape
    nrhs_dev = inputs.shape[0]
    own_width = systems * width
    my_panel = lax.axis_index("panel")
    my_lane = lax.axis_index("rhs")
    per_panel = systems * lanes
    own_cnt = lax.dynamic_slice_in_dim(counts, my_panel * per_panel + my_lane * systems, systems, 0)
    panel_mates = lax.dynamic_slice(pattern, (my_panel * per_panel, 1), (per_panel, 1))[:, 0] // per_panel
    mate_panel = lax.dynamic_slice_in_dim(panel_mates, my_lane * systems, systems, 0)
    hit = mate_panel[None, :] == jnp.arange(shards, dtype=jnp.int32)[:, None]
    slot_of = jnp.sum(hit * jnp.arange(systems, dtype=jnp.int32)[None, :], axis=1)
    lane_word = my_lane[None].astype(jnp.int32)

    def shift(value, by):
        return lax.ppermute(value, "rhs", [(i, (i + by) % lanes) for i in range(lanes)])

    received = lax.all_to_all(tiles[:, :2][slot_of], "panel", split_axis=0, concat_axis=0, tiled=True)

    vmem = pl.BlockSpec(memory_space=pltpu.VMEM)
    smem = pl.BlockSpec(memory_space=pltpu.SMEM)
    anywhere = pl.BlockSpec(memory_space=pl.ANY)
    params = pltpu.CompilerParams(vmem_limit_bytes=56 * 1024 * 1024)
    w, z = pl.pallas_call(
        own_kernel,
        out_shape=(
            jax.ShapeDtypeStruct((systems, 2, width, width), jnp.bfloat16),
            jax.ShapeDtypeStruct((systems, 3, width, 2 * width), jnp.bfloat16),
        ),
        in_specs=[smem, vmem],
        out_specs=(vmem, vmem),
        scratch_shapes=[pltpu.VMEM((systems, width, width), jnp.float32)] + factor_scratch(systems, width),
        compiler_params=params,
        cost_estimate=pl.CostEstimate(flops=40 * 10**9, bytes_accessed=8 * 10**6, transcendentals=0),
    )(own_cnt, tiles)

    inputs, w = lax.optimization_barrier((inputs, w))
    parts = [lax.dynamic_slice_in_dim(inputs, my_lane * own_width, own_width, 1)]
    for e in range(1, lanes):
        part = lax.dynamic_slice_in_dim(inputs, (my_lane + lanes - e) % lanes * own_width, own_width, 1)
        parts.append(shift(part, -e))
    x = jnp.concatenate(parts, axis=0)

    piece = jax.ShapeDtypeStruct((systems, nrhs_dev, width), jnp.float32)
    *up, low = pl.pallas_call(
        functools.partial(pair_kernel, lanes),
        out_shape=[piece] * lanes + [jax.ShapeDtypeStruct((shards * lanes, nrhs_dev, width), jnp.float32)],
        in_specs=[smem, vmem, anywhere, anywhere, anywhere],
        out_specs=[vmem] * (lanes + 1),
        scratch_shapes=[
            pltpu.VMEM((systems, 2, width, width), jnp.bfloat16),
            pltpu.VMEM((systems, 2, width, width), jnp.bfloat16),
            pltpu.VMEM((systems, 3, width, 2 * width), jnp.bfloat16),
            pltpu.VMEM((systems, width, width), jnp.float32),
            pltpu.VMEM((systems, 2, width, width), jnp.bfloat16),
            pltpu.VMEM((systems, lanes * nrhs_dev, width), jnp.float32),
            pltpu.VMEM((systems, lanes * nrhs_dev, width), jnp.float32),
            pltpu.SemaphoreType.DMA((systems + 1, 2)),
        ] + factor_scratch(systems, width),
        compiler_params=params,
    )(jnp.concatenate([mate_panel, lane_word]), x, w, z, received)
    low = lax.all_to_all(low, ("panel", "rhs"), split_axis=0, concat_axis=0, tiled=True)
    up = [up[0]] + [shift(up[e], e) for e in range(1, lanes)]
    return pl.pallas_call(
        functools.partial(place_kernel, lanes),
        out_shape=jax.ShapeDtypeStruct((nrhs_dev, per_panel * width), jnp.bfloat16),
        in_specs=[smem] + [vmem] * (lanes + 1),
        out_specs=vmem,
    )(jnp.concatenate([panel_mates, lane_word]), low, *up)


def solution(mesh):
    return jax.shard_map(
        on_device,
        mesh=mesh,
        in_specs=(P(("panel", "rhs"), None, None, None), P(), P(), P("rhs", "panel")),
        out_specs=P("rhs", "panel"),
        check_vma=False,
    )
```

```python
import functools
import jax
import jax.numpy as jnp
from jax import lax
from jax.experimental import pallas as pl
from jax.experimental.pallas import tpu as pltpu
from jax.sharding import PartitionSpec as P

STEP = 32
PIVOTS = 4
TEAM = 3
NT = (((1,), (1,)), ((), ()))
NN = (((1,), (0,)), ((), ()))
TN = (((0,), (0,)), ((), ()))


def dot(a, b, dims):
    return lax.dot_general(a, b, dims, preferred_element_type=jnp.float32)


def split3(a):
    one = a.astype(jnp.bfloat16)
    rest = a - one.astype(jnp.float32)
    two = rest.astype(jnp.bfloat16)
    three = (rest - two.astype(jnp.float32)).astype(jnp.bfloat16)
    return one, two, three


def dot6(a, b, dims):
    a1, a2, a3 = a
    b1, b2, b3 = b
    small = dot(a1, b3, dims) + dot(a3, b1, dims) + dot(a2, b2, dims)
    return dot(a1, b1, dims) + ((dot(a1, b2, dims) + dot(a2, b1, dims)) + small)


def apply(rows, parts, dims):
    count = rows.shape[0]
    stack = jnp.concatenate(split3(rows), axis=0)
    high = dot(stack, parts[0], dims)
    low = dot(stack[:2 * count], parts[1], dims)
    return high[:count] + ((high[count:2 * count] + low[:count]) + (high[2 * count:] + low[count:]))


def factor(ref, slab_ref, left_ref, right_ref):
    systems, width, _ = ref.shape
    halves = width // 128
    groups = STEP // 8
    lane = lax.broadcasted_iota(jnp.int32, (8, 128), 1)
    sub = lax.broadcasted_iota(jnp.int32, (8, 128), 0)
    row_in = lax.broadcasted_iota(jnp.int32, (STEP, width), 0)
    col_in = lax.broadcasted_iota(jnp.int32, (STEP, width), 1)
    row_all = lax.broadcasted_iota(jnp.int32, (width, width), 0)
    col_all = lax.broadcasted_iota(jnp.int32, (width, width), 1)

    def spread(row):
        return jnp.broadcast_to(row, (8, 128))

    def pivots(slabs):
        for first in range(0, STEP, PIVOTS):
            top, start = first // 8, first % 8
            tall = range(top, groups)
            own = (lane >= first) & (lane < first + PIVOTS)
            one = jnp.where(lane - 8 * top == sub, 1.0, 0.0)
            if start == 0:
                inverses = [None] * len(slabs)
            columns = []
            for x in slabs:
                columns.append([{g: spread(x[g][0][:, first + q:first + q + 1]) for g in tall} for q in range(PIVOTS)])
                for g in tall:
                    x[g][0] = jnp.where(own, one if g == top else 0.0, x[g][0])
            for q in range(PIVOTS):
                at = start + q
                for s, x in enumerate(slabs):
                    cols = columns[s]
                    inverse = pl.reciprocal(spread(cols[q][top][at:at + 1, :]), approx=True)
                    inverses[s] = inverse if at == 0 else jnp.where(sub >= at, inverse, inverses[s])
                    c = {g: cols[q][g] * inverse for g in tall}
                    for later in range(q + 1, PIVOTS):
                        m = spread(cols[q][top][start + later:start + later + 1, :])
                        for g in tall:
                            cols[later][g] = cols[later][g] - c[g] * m
                    c[top] = jnp.where(sub > at, c[top], 0.0)
                    for h in range(halves):
                        r = spread(x[top][h][at:at + 1, :])
                        for g in tall:
                            x[g][h] = x[g][h] - c[g] * r
            if start + PIVOTS == 8:
                for s, x in enumerate(slabs):
                    scale = inverses[s] * lax.rsqrt(inverses[s])
                    for h in range(halves):
                        x[top][h] = x[top][h] * scale

    for s in range(systems):
        slab_ref[s] = ref[s, 0:STEP]
        left_ref[s] = jnp.zeros(left_ref.shape[1:], left_ref.dtype)
        right_ref[s] = jnp.zeros(right_ref.shape[1:], right_ref.dtype)

    def block(kb, carry):
        base = pl.multiple_of(kb * STEP, STEP)
        after = pl.multiple_of(jnp.minimum(base + STEP, width - STEP), STEP)
        done = (col_all >= base - STEP) & (col_all < base) & (row_all >= base + STEP)
        for s in range(systems):
            ref[s] = jnp.where(done, 0.0, ref[s]) - dot(left_ref[s], right_ref[s], TN)
        slabs = []
        for s in range(systems):
            slabs.append([[slab_ref[s, 8 * g:8 * g + 8, 128 * h:128 * h + 128] for h in range(halves)] for g in range(groups)])
        for s in range(0, systems, TEAM):
            pivots(slabs[s:s + TEAM])
        for s in range(systems):
            slab = jnp.concatenate([jnp.concatenate(line, axis=1) for line in slabs[s]], axis=0)
            slab = jnp.where((col_in > row_in) & (col_in < STEP), 0.0, slab)
            n1, n2, n3 = split3(slab[:, STEP:2 * STEP])
            q1, q2, q3 = split3(pltpu.roll(slab, width - STEP, 1))
            update = dot(
                jnp.concatenate([n1, n1, n2, n2, n1, n3], axis=0),
                jnp.concatenate([q1, q2, q1, q2, q3, q1], axis=0),
                TN,
            )
            coming = pltpu.roll(ref[s, pl.ds(after, STEP), :], width - after, 1)
            slab_ref[s] = jnp.where(col_in >= width - STEP, 0.0, coming) - update
            slab = pltpu.roll(slab, base, 1)
            ref[s, pl.ds(base, STEP), :] = jnp.where(col_in >= base + STEP, 0.0, slab)
            p1, p2, p3 = split3(slab)
            zero = jnp.zeros_like(p1)
            m1, m2, m3 = (jnp.where(col_in >= base + 2 * STEP, p, zero) for p in (p1, p2, p3))
            left_ref[s] = jnp.concatenate([m1, m1, m2, m2, m1, m3], axis=0)
            right_ref[s] = jnp.concatenate([p1, p2, p1, p2, p3, p1], axis=0)
        return carry

    lax.fori_loop(0, width // STEP, block, 0)


def factor_scratch(systems, width):
    return [
        pltpu.VMEM((systems, STEP, width), jnp.float32),
        pltpu.VMEM((systems, 6 * STEP, width), jnp.bfloat16),
        pltpu.VMEM((systems, 6 * STEP, width), jnp.bfloat16),
    ]


def own_kernel(counts_ref, tiles_ref, w_ref, z_ref, g_ref, *scratch):
    systems, kslots, width, _ = tiles_ref.shape
    for s in range(systems):
        near = tiles_ref[s, 0:2].reshape(2 * width, width)
        g_ref[s] = dot(near, near, TN)
        for k in range(2, kslots):
            @pl.when(k < counts_ref[s])
            def _():
                tile = tiles_ref[s, k]
                g_ref[s] += dot(tile, tile, TN)
    factor(g_ref, *scratch)
    for s in range(systems):
        w1, w2, w3 = split3(g_ref[s])
        w_ref[s, 0] = w1
        w_ref[s, 1] = w2
        near = jnp.concatenate([tiles_ref[s, 1], tiles_ref[s, 0]], axis=0)
        z = dot(w1, near, NT) + (dot(w2, near, NT) + dot(w3, near, NT))
        z1, z2, z3 = split3(z)
        z_ref[s, 0] = z1
        z_ref[s, 1] = z2
        z_ref[s, 2] = z3


def pair_kernel(lanes, place_ref, x_ref, w_any, z_any, got_ref, *refs):
    up_refs, refs = refs[:lanes], refs[lanes:]
    low_ref, near_ref, w_ref, z_ref, t_ref, v_ref, r_ref, first_ref, sems, *scratch = refs
    systems, _, width, _ = z_ref.shape
    count = x_ref.shape[0] // lanes
    copies = []
    for s in range(systems):
        pairs = ((got_ref.at[place_ref[s]], near_ref.at[s]), (z_any.at[s], z_ref.at[s]))
        copies.append([pltpu.make_async_copy(a, b, sems.at[s, i]) for i, (a, b) in enumerate(pairs)])
        for copy in copies[s]:
            copy.start()
    w_copy = pltpu.make_async_copy(w_any, w_ref, sems.at[systems, 0])
    w_copy.start()
    low_ref[...] = jnp.zeros(low_ref.shape, low_ref.dtype)
    for s in range(systems):
        for copy in copies[s]:
            copy.wait()
        near = near_ref[s].reshape(2 * width, width)
        near_t = near.T
        z1, z2, z3 = z_ref[s, 0], z_ref[s, 1], z_ref[s, 2]
        v = split3(dot(near_t, z1, NT) + (dot(near_t, z2, NT) + dot(near_t, z3, NT)))
        v_ref[s, 0] = v[0]
        v_ref[s, 1] = v[1]
        t_ref[s] = dot(near_t, near, NN) - dot6(v, v, NT)
    for s in range(systems):
        x = x_ref[:, s * width:(s + 1) * width]
        first_ref[s] = dot(x, z_ref[s, 0, :, width:], NT) + dot(x, z_ref[s, 1, :, width:], NT)
        r_ref[s] = dot(x, near_ref[s, 1], NN)
    for s in range(systems):
        r_ref[s] = r_ref[s] - apply(first_ref[s], (v_ref[s, 0], v_ref[s, 1]), NT)
    factor(t_ref, *scratch)
    parts = [split3(t_ref[s])[:2] for s in range(systems)]
    half = [apply(r_ref[s], parts[s], NT) for s in range(systems)]
    last = [apply(half[s], parts[s], NN) for s in range(systems)]
    mid = [first_ref[s] - apply(last[s], (v_ref[s, 0], v_ref[s, 1]), NN) for s in range(systems)]
    w_copy.wait()
    for s in range(systems):
        up = apply(mid[s], (w_ref[s, 0], w_ref[s, 1]), NN)
        for e in range(lanes):
            up_refs[e][s] = up[e * count:(e + 1) * count].astype(up_refs[e].dtype)
            owner = lax.rem(place_ref[systems] + e, lanes)
            low_ref[place_ref[s] * lanes + owner] = last[s][e * count:(e + 1) * count].astype(low_ref.dtype)


def place_kernel(lanes, place_ref, low_ref, *refs):
    up_refs, out_ref = refs[:lanes], refs[lanes]
    systems, _, width = up_refs[0].shape
    for e in range(lanes):
        owner = lax.rem(place_ref[systems * lanes] + lanes - e, lanes)
        for s in range(systems):
            at = owner * systems + s
            total = up_refs[e][s].astype(jnp.float32) + low_ref[place_ref[at] * lanes + owner].astype(jnp.float32)
            out_ref[:, pl.ds(pl.multiple_of(at * width, width), width)] = total.astype(out_ref.dtype)


def on_device(tiles, pattern, counts, inputs):
    shards = lax.axis_size("panel")
    lanes = lax.axis_size("rhs")
    systems, kslots, width, _ = tiles.shape
    nrhs_dev = inputs.shape[0]
    own_width = systems * width
    my_panel = lax.axis_index("panel")
    my_lane = lax.axis_index("rhs")
    per_panel = systems * lanes
    own_cnt = lax.dynamic_slice_in_dim(counts, my_panel * per_panel + my_lane * systems, systems, 0)
    panel_mates = lax.dynamic_slice(pattern, (my_panel * per_panel, 1), (per_panel, 1))[:, 0] // per_panel
    mate_panel = lax.dynamic_slice_in_dim(panel_mates, my_lane * systems, systems, 0)
    hit = mate_panel[None, :] == jnp.arange(shards, dtype=jnp.int32)[:, None]
    slot_of = jnp.sum(hit * jnp.arange(systems, dtype=jnp.int32)[None, :], axis=1)
    lane_word = my_lane[None].astype(jnp.int32)

    def shift(value, by):
        return lax.ppermute(value, "rhs", [(i, (i + by) % lanes) for i in range(lanes)])

    received = lax.all_to_all(tiles[:, :2][slot_of], "panel", split_axis=0, concat_axis=0, tiled=True)

    vmem = pl.BlockSpec(memory_space=pltpu.VMEM)
    smem = pl.BlockSpec(memory_space=pltpu.SMEM)
    anywhere = pl.BlockSpec(memory_space=pl.ANY)
    params = pltpu.CompilerParams(vmem_limit_bytes=56 * 1024 * 1024)
    w, z = pl.pallas_call(
        own_kernel,
        out_shape=(
            jax.ShapeDtypeStruct((systems, 2, width, width), jnp.bfloat16),
            jax.ShapeDtypeStruct((systems, 3, width, 2 * width), jnp.bfloat16),
        ),
        in_specs=[smem, vmem],
        out_specs=(vmem, vmem),
        scratch_shapes=[pltpu.VMEM((systems, width, width), jnp.float32)] + factor_scratch(systems, width),
        compiler_params=params,
        cost_estimate=pl.CostEstimate(flops=40 * 10**9, bytes_accessed=8 * 10**6, transcendentals=0),
    )(own_cnt, tiles)

    inputs, w = lax.optimization_barrier((inputs, w))
    parts = [lax.dynamic_slice_in_dim(inputs, my_lane * own_width, own_width, 1)]
    for e in range(1, lanes):
        part = lax.dynamic_slice_in_dim(inputs, (my_lane + lanes - e) % lanes * own_width, own_width, 1)
        parts.append(shift(part, -e))
    x = jnp.concatenate(parts, axis=0)

    piece = jax.ShapeDtypeStruct((systems, nrhs_dev, width), jnp.bfloat16)
    *up, low = pl.pallas_call(
        functools.partial(pair_kernel, lanes),
        out_shape=[piece] * lanes + [jax.ShapeDtypeStruct((shards * lanes, nrhs_dev, width), jnp.bfloat16)],
        in_specs=[smem, vmem, anywhere, anywhere, anywhere],
        out_specs=[vmem] * (lanes + 1),
        scratch_shapes=[
            pltpu.VMEM((systems, 2, width, width), jnp.bfloat16),
            pltpu.VMEM((systems, 2, width, width), jnp.bfloat16),
            pltpu.VMEM((systems, 3, width, 2 * width), jnp.bfloat16),
            pltpu.VMEM((systems, width, width), jnp.float32),
            pltpu.VMEM((systems, 2, width, width), jnp.bfloat16),
            pltpu.VMEM((systems, lanes * nrhs_dev, width), jnp.float32),
            pltpu.VMEM((systems, lanes * nrhs_dev, width), jnp.float32),
            pltpu.SemaphoreType.DMA((systems + 1, 2)),
        ] + factor_scratch(systems, width),
        compiler_params=params,
    )(jnp.concatenate([mate_panel, lane_word]), x, w, z, received)
    low = lax.all_to_all(low, ("panel", "rhs"), split_axis=0, concat_axis=0, tiled=True)
    up = [up[0]] + [shift(up[e], e) for e in range(1, lanes)]
    return pl.pallas_call(
        functools.partial(place_kernel, lanes),
        out_shape=jax.ShapeDtypeStruct((nrhs_dev, per_panel * width), jnp.bfloat16),
        in_specs=[smem] + [vmem] * (lanes + 1),
        out_specs=vmem,
    )(jnp.concatenate([panel_mates, lane_word]), low, *up)


def solution(mesh):
    return jax.shard_map(
        on_device,
        mesh=mesh,
        in_specs=(P(("panel", "rhs"), None, None, None), P(), P(), P("rhs", "panel")),
        out_specs=P("rhs", "panel"),
        check_vma=False,
    )
```

```python
import functools
import jax
import jax.numpy as jnp
from jax import lax
from jax.experimental import pallas as pl
from jax.experimental.pallas import tpu as pltpu
from jax.sharding import PartitionSpec as P

STEP = 32
PIVOTS = 4
NT = (((1,), (1,)), ((), ()))
NN = (((1,), (0,)), ((), ()))
TN = (((0,), (0,)), ((), ()))


def dot(a, b, dims):
    return lax.dot_general(a, b, dims, preferred_element_type=jnp.float32)


def split3(a):
    one = a.astype(jnp.bfloat16)
    rest = a - one.astype(jnp.float32)
    two = rest.astype(jnp.bfloat16)
    three = (rest - two.astype(jnp.float32)).astype(jnp.bfloat16)
    return one, two, three


def dot6(a, b, dims):
    a1, a2, a3 = a
    b1, b2, b3 = b
    small = dot(a1, b3, dims) + dot(a3, b1, dims) + dot(a2, b2, dims)
    return dot(a1, b1, dims) + ((dot(a1, b2, dims) + dot(a2, b1, dims)) + small)


def apply(rows, parts, dims):
    count = rows.shape[0]
    stack = jnp.concatenate(split3(rows), axis=0)
    high = dot(stack, parts[0], dims)
    low = dot(stack[:2 * count], parts[1], dims)
    return high[:count] + ((high[count:2 * count] + low[:count]) + (high[2 * count:] + low[count:]))


def factor(ref, slab_ref, past_ref):
    systems, width, _ = ref.shape
    halves = width // 128
    groups = STEP // 8
    lane = lax.broadcasted_iota(jnp.int32, (8, 128), 1)
    sub = lax.broadcasted_iota(jnp.int32, (8, 128), 0)
    row_in = lax.broadcasted_iota(jnp.int32, (STEP, width), 0)
    col_in = lax.broadcasted_iota(jnp.int32, (STEP, width), 1)
    row_all = lax.broadcasted_iota(jnp.int32, (width, width), 0)
    col_all = lax.broadcasted_iota(jnp.int32, (width, width), 1)

    def spread(row):
        return jnp.broadcast_to(row, (8, 128))

    def pivots(slabs, pieces):
        placed = 0
        for first in range(0, STEP, PIVOTS):
            top, start = first // 8, first % 8
            tall = range(top, groups)
            own = (lane >= first) & (lane < first + PIVOTS)
            one = jnp.where(lane - 8 * top == sub, 1.0, 0.0)
            if start == 0:
                inverses = [None] * len(slabs)
            columns = []
            for x in slabs:
                columns.append([{g: spread(x[g][0][:, first + q:first + q + 1]) for g in tall} for q in range(PIVOTS)])
                for g in tall:
                    x[g][0] = jnp.where(own, one if g == top else 0.0, x[g][0])
            for q in range(PIVOTS):
                at = start + q
                for s, x in enumerate(slabs):
                    cols = columns[s]
                    inverse = pl.reciprocal(spread(cols[q][top][at:at + 1, :]), approx=True)
                    inverses[s] = inverse if at == 0 else jnp.where(sub >= at, inverse, inverses[s])
                    c = {g: cols[q][g] * inverse for g in tall}
                    for later in range(q + 1, PIVOTS):
                        m = spread(cols[q][top][start + later:start + later + 1, :])
                        for g in tall:
                            cols[later][g] = cols[later][g] - c[g] * m
                    c[top] = jnp.where(sub > at, c[top], 0.0)
                    for h in range(halves):
                        r = spread(x[top][h][at:at + 1, :])
                        for g in tall:
                            x[g][h] = x[g][h] - c[g] * r
                while placed * STEP < (first + q + 1) * len(pieces):
                    pieces[placed]()
                    placed += 1
            if start + PIVOTS == 8:
                for s, x in enumerate(slabs):
                    scale = inverses[s] * lax.rsqrt(inverses[s])
                    for h in range(halves):
                        x[top][h] = x[top][h] * scale

    for s in range(systems):
        slab_ref[s] = ref[s, 0:STEP]
        past_ref[s] = jnp.zeros(past_ref.shape[1:], past_ref.dtype)

    def block(kb, carry):
        base = pl.multiple_of(kb * STEP, STEP)
        after = pl.multiple_of(jnp.minimum(base + STEP, width - STEP), STEP)
        done = (col_all >= base - STEP) & (col_all < base) & (row_all >= base + STEP)
        pieces = []
        for s in range(systems):
            held = {}

            def prepare(s=s, held=held):
                p1, p2, p3 = split3(past_ref[s])
                zero = jnp.zeros_like(p1)
                m1, m2, m3 = (jnp.where(col_in >= base + STEP, p, zero) for p in (p1, p2, p3))
                held["left"] = jnp.concatenate([m1, m1, m2, m2, m1, m3], axis=0)
                held["right"] = jnp.concatenate([p1, p2, p1, p2, p3, p1], axis=0)

            def trail(at, s=s, held=held):
                rows = slice(at, at + 128)
                update = dot(held["left"][:, rows], held["right"], TN)
                ref[s, rows] = jnp.where(done[rows], 0.0, ref[s, rows]) - update

            pieces.append(prepare)
            pieces.extend(functools.partial(trail, at) for at in range(0, width, 128))
        slabs = []
        for s in range(systems):
            slabs.append([[slab_ref[s, 8 * g:8 * g + 8, 128 * h:128 * h + 128] for h in range(halves)] for g in range(groups)])
        pivots(slabs, pieces)
        for s in range(systems):
            slab = jnp.concatenate([jnp.concatenate(line, axis=1) for line in slabs[s]], axis=0)
            slab = jnp.where((col_in > row_in) & (col_in < STEP), 0.0, slab)
            n1, n2, n3 = split3(slab[:, STEP:2 * STEP])
            q1, q2, q3 = split3(pltpu.roll(slab, width - STEP, 1))
            update = dot(
                jnp.concatenate([n1, n1, n2, n2, n1, n3], axis=0),
                jnp.concatenate([q1, q2, q1, q2, q3, q1], axis=0),
                TN,
            )
            coming = pltpu.roll(ref[s, pl.ds(after, STEP), :], width - after, 1)
            slab_ref[s] = jnp.where(col_in >= width - STEP, 0.0, coming) - update
            slab = pltpu.roll(slab, base, 1)
            ref[s, pl.ds(base, STEP), :] = jnp.where(col_in >= base + STEP, 0.0, slab)
            past_ref[s] = slab
        return carry

    lax.fori_loop(0, width // STEP, block, 0)


def factor_scratch(systems, width):
    return [pltpu.VMEM((systems, STEP, width), jnp.float32)] * 2


def own_kernel(counts_ref, tiles_ref, w_ref, z_ref, g_ref, *scratch):
    systems, kslots, width, _ = tiles_ref.shape
    for s in range(systems):
        near = tiles_ref[s, 0:2].reshape(2 * width, width)
        g_ref[s] = dot(near, near, TN)
        for k in range(2, kslots):
            @pl.when(k < counts_ref[s])
            def _():
                tile = tiles_ref[s, k]
                g_ref[s] += dot(tile, tile, TN)
    factor(g_ref, *scratch)
    for s in range(systems):
        w1, w2, w3 = split3(g_ref[s])
        w_ref[s, 0] = w1
        w_ref[s, 1] = w2
        near = jnp.concatenate([tiles_ref[s, 1], tiles_ref[s, 0]], axis=0)
        z = dot(w1, near, NT) + (dot(w2, near, NT) + dot(w3, near, NT))
        z1, z2, z3 = split3(z)
        z_ref[s, 0] = z1
        z_ref[s, 1] = z2
        z_ref[s, 2] = z3


def pair_kernel(lanes, place_ref, x_ref, w_any, z_any, got_ref, *refs):
    up_refs, refs = refs[:lanes], refs[lanes:]
    low_ref, near_ref, w_ref, z_ref, t_ref, v_ref, r_ref, first_ref, sems, *scratch = refs
    systems, _, width, _ = z_ref.shape
    count = x_ref.shape[0] // lanes
    copies = []
    for s in range(systems):
        pairs = ((got_ref.at[place_ref[s]], near_ref.at[s]), (z_any.at[s], z_ref.at[s]))
        copies.append([pltpu.make_async_copy(a, b, sems.at[s, i]) for i, (a, b) in enumerate(pairs)])
        for copy in copies[s]:
            copy.start()
    w_copy = pltpu.make_async_copy(w_any, w_ref, sems.at[systems, 0])
    w_copy.start()
    low_ref[...] = jnp.zeros(low_ref.shape, low_ref.dtype)
    for s in range(systems):
        for copy in copies[s]:
            copy.wait()
        near = near_ref[s].reshape(2 * width, width)
        near_t = near.T
        z1, z2, z3 = z_ref[s, 0], z_ref[s, 1], z_ref[s, 2]
        v = split3(dot(near_t, z1, NT) + (dot(near_t, z2, NT) + dot(near_t, z3, NT)))
        v_ref[s, 0] = v[0]
        v_ref[s, 1] = v[1]
        t_ref[s] = dot(near_t, near, NN) - dot6(v, v, NT)
    for s in range(systems):
        x = x_ref[:, s * width:(s + 1) * width]
        first_ref[s] = dot(x, z_ref[s, 0, :, width:], NT) + dot(x, z_ref[s, 1, :, width:], NT)
        r_ref[s] = dot(x, near_ref[s, 1], NN)
    for s in range(systems):
        r_ref[s] = r_ref[s] - apply(first_ref[s], (v_ref[s, 0], v_ref[s, 1]), NT)
    factor(t_ref, *scratch)
    parts = [split3(t_ref[s])[:2] for s in range(systems)]
    half = [apply(r_ref[s], parts[s], NT) for s in range(systems)]
    last = [apply(half[s], parts[s], NN) for s in range(systems)]
    mid = [first_ref[s] - apply(last[s], (v_ref[s, 0], v_ref[s, 1]), NN) for s in range(systems)]
    w_copy.wait()
    for s in range(systems):
        up = apply(mid[s], (w_ref[s, 0], w_ref[s, 1]), NN)
        for e in range(lanes):
            up_refs[e][s] = up[e * count:(e + 1) * count]
            owner = lax.rem(place_ref[systems] + e, lanes)
            low_ref[place_ref[s] * lanes + owner] = last[s][e * count:(e + 1) * count].astype(low_ref.dtype)


def place_kernel(lanes, place_ref, low_ref, *refs):
    up_refs, out_ref = refs[:lanes], refs[lanes]
    systems, _, width = up_refs[0].shape
    for e in range(lanes):
        owner = lax.rem(place_ref[systems * lanes] + lanes - e, lanes)
        for s in range(systems):
            at = owner * systems + s
            total = up_refs[e][s] + low_ref[place_ref[at] * lanes + owner].astype(jnp.float32)
            out_ref[:, pl.ds(pl.multiple_of(at * width, width), width)] = total.astype(out_ref.dtype)


def on_device(tiles, pattern, counts, inputs):
    shards = lax.axis_size("panel")
    lanes = lax.axis_size("rhs")
    systems, kslots, width, _ = tiles.shape
    nrhs_dev = inputs.shape[0]
    own_width = systems * width
    my_panel = lax.axis_index("panel")
    my_lane = lax.axis_index("rhs")
    per_panel = systems * lanes
    own_cnt = lax.dynamic_slice_in_dim(counts, my_panel * per_panel + my_lane * systems, systems, 0)
    panel_mates = lax.dynamic_slice(pattern, (my_panel * per_panel, 1), (per_panel, 1))[:, 0] // per_panel
    mate_panel = lax.dynamic_slice_in_dim(panel_mates, my_lane * systems, systems, 0)
    hit = mate_panel[None, :] == jnp.arange(shards, dtype=jnp.int32)[:, None]
    slot_of = jnp.sum(hit * jnp.arange(systems, dtype=jnp.int32)[None, :], axis=1)
    lane_word = my_lane[None].astype(jnp.int32)

    def shift(value, by):
        return lax.ppermute(value, "rhs", [(i, (i + by) % lanes) for i in range(lanes)])

    received = lax.all_to_all(tiles[:, :2][slot_of], "panel", split_axis=0, concat_axis=0, tiled=True)

    vmem = pl.BlockSpec(memory_space=pltpu.VMEM)
    smem = pl.BlockSpec(memory_space=pltpu.SMEM)
    anywhere = pl.BlockSpec(memory_space=pl.ANY)
    params = pltpu.CompilerParams(vmem_limit_bytes=56 * 1024 * 1024)
    w, z = pl.pallas_call(
        own_kernel,
        out_shape=(
            jax.ShapeDtypeStruct((systems, 2, width, width), jnp.bfloat16),
            jax.ShapeDtypeStruct((systems, 3, width, 2 * width), jnp.bfloat16),
        ),
        in_specs=[smem, vmem],
        out_specs=(vmem, vmem),
        scratch_shapes=[pltpu.VMEM((systems, width, width), jnp.float32)] + factor_scratch(systems, width),
        compiler_params=params,
        cost_estimate=pl.CostEstimate(flops=40 * 10**9, bytes_accessed=8 * 10**6, transcendentals=0),
    )(own_cnt, tiles)

    inputs, w = lax.optimization_barrier((inputs, w))
    parts = [lax.dynamic_slice_in_dim(inputs, my_lane * own_width, own_width, 1)]
    for e in range(1, lanes):
        part = lax.dynamic_slice_in_dim(inputs, (my_lane + lanes - e) % lanes * own_width, own_width, 1)
        parts.append(shift(part, -e))
    x = jnp.concatenate(parts, axis=0)

    piece = jax.ShapeDtypeStruct((systems, nrhs_dev, width), jnp.float32)
    *up, low = pl.pallas_call(
        functools.partial(pair_kernel, lanes),
        out_shape=[piece] * lanes + [jax.ShapeDtypeStruct((shards * lanes, nrhs_dev, width), jnp.bfloat16)],
        in_specs=[smem, vmem, anywhere, anywhere, anywhere],
        out_specs=[vmem] * (lanes + 1),
        scratch_shapes=[
            pltpu.VMEM((systems, 2, width, width), jnp.bfloat16),
            pltpu.VMEM((systems, 2, width, width), jnp.bfloat16),
            pltpu.VMEM((systems, 3, width, 2 * width), jnp.bfloat16),
            pltpu.VMEM((systems, width, width), jnp.float32),
            pltpu.VMEM((systems, 2, width, width), jnp.bfloat16),
            pltpu.VMEM((systems, lanes * nrhs_dev, width), jnp.float32),
            pltpu.VMEM((systems, lanes * nrhs_dev, width), jnp.float32),
            pltpu.SemaphoreType.DMA((systems + 1, 2)),
        ] + factor_scratch(systems, width),
        compiler_params=params,
    )(jnp.concatenate([mate_panel, lane_word]), x, w, z, received)
    low = lax.all_to_all(low, ("panel", "rhs"), split_axis=0, concat_axis=0, tiled=True)
    up = [up[0]] + [shift(up[e], e) for e in range(1, lanes)]
    return pl.pallas_call(
        functools.partial(place_kernel, lanes),
        out_shape=jax.ShapeDtypeStruct((nrhs_dev, per_panel * width), jnp.bfloat16),
        in_specs=[smem] + [vmem] * (lanes + 1),
        out_specs=vmem,
    )(jnp.concatenate([panel_mates, lane_word]), low, *up)


def solution(mesh):
    return jax.shard_map(
        on_device,
        mesh=mesh,
        in_specs=(P(("panel", "rhs"), None, None, None), P(), P(), P("rhs", "panel")),
        out_specs=P("rhs", "panel"),
        check_vma=False,
    )
```

```python
import functools
import jax
import jax.numpy as jnp
from jax import lax
from jax.experimental import pallas as pl
from jax.experimental.pallas import tpu as pltpu
from jax.sharding import PartitionSpec as P

STEP = 32
PIVOTS = 4
NT = (((1,), (1,)), ((), ()))
NN = (((1,), (0,)), ((), ()))
TN = (((0,), (0,)), ((), ()))


def dot(a, b, dims):
    return lax.dot_general(a, b, dims, preferred_element_type=jnp.float32)


def split3(a):
    one = a.astype(jnp.bfloat16)
    rest = a - one.astype(jnp.float32)
    two = rest.astype(jnp.bfloat16)
    three = (rest - two.astype(jnp.float32)).astype(jnp.bfloat16)
    return one, two, three


def dot6(a, b, dims):
    a1, a2, a3 = a
    b1, b2, b3 = b
    small = dot(a1, b3, dims) + dot(a3, b1, dims) + dot(a2, b2, dims)
    return dot(a1, b1, dims) + ((dot(a1, b2, dims) + dot(a2, b1, dims)) + small)


def apply(rows, parts, dims):
    count = rows.shape[0]
    stack = jnp.concatenate(split3(rows), axis=0)
    high = dot(stack, parts[0], dims)
    low = dot(stack[:2 * count], parts[1], dims)
    return high[:count] + ((high[count:2 * count] + low[:count]) + (high[2 * count:] + low[count:]))


def factor(ref, slab_ref, past_ref):
    systems, width, _ = ref.shape
    teams, height, _ = slab_ref.shape
    team = height // STEP
    groups = STEP // 8
    lane = lax.broadcasted_iota(jnp.int32, (8, 128), 1)
    sub = lax.broadcasted_iota(jnp.int32, (8, 128), 0)
    member = lane // STEP
    place = lane % STEP
    col_in = lax.broadcasted_iota(jnp.int32, (STEP, width), 1)
    row_all = lax.broadcasted_iota(jnp.int32, (width, width), 0)
    col_all = lax.broadcasted_iota(jnp.int32, (width, width), 1)
    row_team = lax.broadcasted_iota(jnp.int32, (height, width), 0)
    col_team = lax.broadcasted_iota(jnp.int32, (height, width), 1)
    row_diag = lax.broadcasted_iota(jnp.int32, (height, 128), 0)
    col_diag = lax.broadcasted_iota(jnp.int32, (height, 128), 1)
    same = row_diag // STEP == col_diag // STEP
    lower = same & (col_diag <= row_diag)

    def spread(row):
        return jnp.broadcast_to(row, (8, 128))

    def wide(parts):
        one, two, three = parts
        return jnp.concatenate([one, one, two, two, one, three], axis=1)

    def deep(parts):
        if height < 128:
            filler = jnp.zeros((128 - height, width), jnp.bfloat16)
            parts = [jnp.concatenate([part, filler], axis=0) for part in parts]
        one, two, three = parts
        return jnp.concatenate([one, two, one, two, three, one], axis=0)

    def pivots(packs, pieces):
        placed = 0
        for first in range(0, STEP, PIVOTS):
            top, start = first // 8, first % 8
            tall = range(top, groups)
            own = (place >= first) & (place < first + PIVOTS)
            one = jnp.where(place - 8 * top == sub, 1.0, 0.0)
            if start == 0:
                inverses = [None] * len(packs)
            columns = []
            for x in packs:
                columns.append([
                    {g: jnp.take_along_axis(x[g], lane - place + (first + q), axis=1) for g in tall} for q in range(PIVOTS)
                ])
                for g in tall:
                    x[g] = jnp.where(own, one if g == top else 0.0, x[g])
            for q in range(PIVOTS):
                at = start + q
                for s, x in enumerate(packs):
                    cols = columns[s]
                    inverse = pl.reciprocal(spread(cols[q][top][at:at + 1, :]), approx=True)
                    inverses[s] = inverse if at == 0 else jnp.where(sub >= at, inverse, inverses[s])
                    c = {g: cols[q][g] * inverse for g in tall}
                    for later in range(q + 1, PIVOTS):
                        m = spread(cols[q][top][start + later:start + later + 1, :])
                        for g in tall:
                            cols[later][g] = cols[later][g] - c[g] * m
                    c[top] = jnp.where(sub > at, c[top], 0.0)
                    r = spread(x[top][at:at + 1, :])
                    for g in tall:
                        x[g] = x[g] - c[g] * r
                while placed * STEP < (first + q + 1) * len(pieces):
                    pieces[placed]()
                    placed += 1
            if start + PIVOTS == 8:
                for s, x in enumerate(packs):
                    x[top] = x[top] * (inverses[s] * lax.rsqrt(inverses[s]))

    for t in range(teams):
        for i in range(team):
            slab_ref[t, i * STEP:(i + 1) * STEP] = ref[t * team + i, 0:STEP]
        past_ref[t] = jnp.zeros(past_ref.shape[1:], past_ref.dtype)

    def block(kb, carry):
        base = pl.multiple_of(kb * STEP, STEP)
        after = pl.multiple_of(jnp.minimum(base + STEP, width - STEP), STEP)
        done = (col_all >= base - STEP) & (col_all < base) & (row_all >= base + STEP)
        pieces = []
        for s in range(systems):
            held = {}

            def prepare(s=s, held=held):
                i = s % team
                p1, p2, p3 = split3(past_ref[s // team, i * STEP:(i + 1) * STEP])
                zero = jnp.zeros_like(p1)
                m1, m2, m3 = (jnp.where(col_in >= base + STEP, p, zero) for p in (p1, p2, p3))
                held["left"] = jnp.concatenate([m1, m1, m2, m2, m1, m3], axis=0)
                held["right"] = jnp.concatenate([p1, p2, p1, p2, p3, p1], axis=0)

            def trail(at, s=s, held=held):
                rows = slice(at, at + 128)
                update = dot(held["left"][:, rows], held["right"], TN)
                ref[s, rows] = jnp.where(done[rows], 0.0, ref[s, rows]) - update

            pieces.append(prepare)
            pieces.extend(functools.partial(trail, at) for at in range(0, width, 128))
        packs = []
        for t in range(teams):
            pack = []
            for g in range(groups):
                x = jnp.where(place - 8 * g == sub, 1.0, 0.0)
                for i in range(team):
                    piece = slab_ref[t, i * STEP + 8 * g:i * STEP + 8 * g + 8, 0:128]
                    if i > 0:
                        piece = pltpu.roll(piece, i * STEP, 1)
                    x = jnp.where(member == i, piece, x)
                pack.append(x)
            packs.append(pack)
        sides = []
        for t in range(teams):
            ident = jnp.where(col_team == row_team % STEP, 1.0, 0.0)
            sides.append(deep(split3(jnp.where(col_team < STEP, ident, slab_ref[t]))))
        pivots(packs, pieces)
        for t in range(teams):
            inner = jnp.concatenate(packs[t], axis=0)
            inner = jnp.where(lower, jnp.concatenate([inner] * team, axis=0), 0.0)
            slab = dot(wide(split3(inner)), sides[t], NN)
            ahead = []
            for i in range(team):
                piece = slab[i * STEP:(i + 1) * STEP, 0:128]
                if i != 1:
                    piece = pltpu.roll(piece, (i - 1) * STEP % 128, 1)
                ahead.append(piece)
            ahead = jnp.where(same, jnp.concatenate(ahead, axis=0), 0.0)
            if height < 128:
                ahead = jnp.concatenate([ahead, jnp.zeros((128 - height, 128), jnp.float32)], axis=0)
            ahead = wide(split3(ahead.T[:height]))
            update = dot(ahead, deep(split3(pltpu.roll(slab, width - STEP, 1))), NN)
            coming = [pltpu.roll(ref[t * team + i, pl.ds(after, STEP), :], width - after, 1) for i in range(team)]
            slab_ref[t] = jnp.where(col_team >= width - STEP, 0.0, jnp.concatenate(coming, axis=0)) - update
            slab = pltpu.roll(slab, base, 1)
            past_ref[t] = slab
            for i in range(team):
                own_rows = slab[i * STEP:(i + 1) * STEP]
                ref[t * team + i, pl.ds(base, STEP), :] = jnp.where(col_in >= base + STEP, 0.0, own_rows)
        return carry

    lax.fori_loop(0, width // STEP, block, 0)


def factor_scratch(systems, width):
    team = max(n for n in range(1, 128 // STEP + 1) if systems % n == 0)
    return [pltpu.VMEM((systems // team, team * STEP, width), jnp.float32)] * 2


def own_kernel(counts_ref, tiles_ref, w_ref, z_ref, g_ref, *scratch):
    systems, kslots, width, _ = tiles_ref.shape
    for s in range(systems):
        near = tiles_ref[s, 0:2].reshape(2 * width, width)
        g_ref[s] = dot(near, near, TN)
        for k in range(2, kslots):
            @pl.when(k < counts_ref[s])
            def _():
                tile = tiles_ref[s, k]
                g_ref[s] += dot(tile, tile, TN)
    factor(g_ref, *scratch)
    for s in range(systems):
        w1, w2, w3 = split3(g_ref[s])
        w_ref[s, 0] = w1
        w_ref[s, 1] = w2
        near = jnp.concatenate([tiles_ref[s, 1], tiles_ref[s, 0]], axis=0)
        z = dot(w1, near, NT) + (dot(w2, near, NT) + dot(w3, near, NT))
        z1, z2, z3 = split3(z)
        z_ref[s, 0] = z1
        z_ref[s, 1] = z2
        z_ref[s, 2] = z3


def pair_kernel(lanes, place_ref, x_ref, w_any, z_any, got_ref, *refs):
    up_refs, refs = refs[:lanes], refs[lanes:]
    low_ref, near_ref, w_ref, z_ref, t_ref, v_ref, r_ref, first_ref, sems, *scratch = refs
    systems, _, width, _ = z_ref.shape
    count = x_ref.shape[0] // lanes
    copies = []
    for s in range(systems):
        pairs = ((got_ref.at[place_ref[s]], near_ref.at[s]), (z_any.at[s], z_ref.at[s]))
        copies.append([pltpu.make_async_copy(a, b, sems.at[s, i]) for i, (a, b) in enumerate(pairs)])
        for copy in copies[s]:
            copy.start()
    w_copy = pltpu.make_async_copy(w_any, w_ref, sems.at[systems, 0])
    w_copy.start()
    low_ref[...] = jnp.zeros(low_ref.shape, low_ref.dtype)
    for s in range(systems):
        for copy in copies[s]:
            copy.wait()
        near = near_ref[s].reshape(2 * width, width)
        near_t = near.T
        z1, z2, z3 = z_ref[s, 0], z_ref[s, 1], z_ref[s, 2]
        v = split3(dot(near_t, z1, NT) + (dot(near_t, z2, NT) + dot(near_t, z3, NT)))
        v_ref[s, 0] = v[0]
        v_ref[s, 1] = v[1]
        t_ref[s] = dot(near_t, near, NN) - dot6(v, v, NT)
    for s in range(systems):
        x = x_ref[:, s * width:(s + 1) * width]
        first_ref[s] = dot(x, z_ref[s, 0, :, width:], NT) + dot(x, z_ref[s, 1, :, width:], NT)
        r_ref[s] = dot(x, near_ref[s, 1], NN)
    for s in range(systems):
        r_ref[s] = r_ref[s] - apply(first_ref[s], (v_ref[s, 0], v_ref[s, 1]), NT)
    factor(t_ref, *scratch)
    parts = [split3(t_ref[s])[:2] for s in range(systems)]
    half = [apply(r_ref[s], parts[s], NT) for s in range(systems)]
    last = [apply(half[s], parts[s], NN) for s in range(systems)]
    mid = [first_ref[s] - apply(last[s], (v_ref[s, 0], v_ref[s, 1]), NN) for s in range(systems)]
    w_copy.wait()
    for s in range(systems):
        up = apply(mid[s], (w_ref[s, 0], w_ref[s, 1]), NN)
        for e in range(lanes):
            up_refs[e][s] = up[e * count:(e + 1) * count]
            owner = lax.rem(place_ref[systems] + e, lanes)
            low_ref[place_ref[s] * lanes + owner] = last[s][e * count:(e + 1) * count].astype(low_ref.dtype)


def place_kernel(lanes, place_ref, low_ref, *refs):
    up_refs, out_ref = refs[:lanes], refs[lanes]
    systems, _, width = up_refs[0].shape
    for e in range(lanes):
        owner = lax.rem(place_ref[systems * lanes] + lanes - e, lanes)
        for s in range(systems):
            at = owner * systems + s
            total = up_refs[e][s] + low_ref[place_ref[at] * lanes + owner].astype(jnp.float32)
            out_ref[:, pl.ds(pl.multiple_of(at * width, width), width)] = total.astype(out_ref.dtype)


def on_device(tiles, pattern, counts, inputs):
    shards = lax.axis_size("panel")
    lanes = lax.axis_size("rhs")
    systems, kslots, width, _ = tiles.shape
    nrhs_dev = inputs.shape[0]
    own_width = systems * width
    my_panel = lax.axis_index("panel")
    my_lane = lax.axis_index("rhs")
    per_panel = systems * lanes
    own_cnt = lax.dynamic_slice_in_dim(counts, my_panel * per_panel + my_lane * systems, systems, 0)
    panel_mates = lax.dynamic_slice(pattern, (my_panel * per_panel, 1), (per_panel, 1))[:, 0] // per_panel
    mate_panel = lax.dynamic_slice_in_dim(panel_mates, my_lane * systems, systems, 0)
    hit = mate_panel[None, :] == jnp.arange(shards, dtype=jnp.int32)[:, None]
    slot_of = jnp.sum(hit * jnp.arange(systems, dtype=jnp.int32)[None, :], axis=1)
    lane_word = my_lane[None].astype(jnp.int32)

    def shift(value, by):
        return lax.ppermute(value, "rhs", [(i, (i + by) % lanes) for i in range(lanes)])

    received = lax.all_to_all(tiles[:, :2][slot_of], "panel", split_axis=0, concat_axis=0, tiled=True)

    vmem = pl.BlockSpec(memory_space=pltpu.VMEM)
    smem = pl.BlockSpec(memory_space=pltpu.SMEM)
    anywhere = pl.BlockSpec(memory_space=pl.ANY)
    params = pltpu.CompilerParams(vmem_limit_bytes=56 * 1024 * 1024)
    w, z = pl.pallas_call(
        own_kernel,
        out_shape=(
            jax.ShapeDtypeStruct((systems, 2, width, width), jnp.bfloat16),
            jax.ShapeDtypeStruct((systems, 3, width, 2 * width), jnp.bfloat16),
        ),
        in_specs=[smem, vmem],
        out_specs=(vmem, vmem),
        scratch_shapes=[pltpu.VMEM((systems, width, width), jnp.float32)] + factor_scratch(systems, width),
        compiler_params=params,
        cost_estimate=pl.CostEstimate(flops=40 * 10**9, bytes_accessed=8 * 10**6, transcendentals=0),
    )(own_cnt, tiles)

    inputs, w = lax.optimization_barrier((inputs, w))
    parts = [lax.dynamic_slice_in_dim(inputs, my_lane * own_width, own_width, 1)]
    for e in range(1, lanes):
        part = lax.dynamic_slice_in_dim(inputs, (my_lane + lanes - e) % lanes * own_width, own_width, 1)
        parts.append(shift(part, -e))
    x = jnp.concatenate(parts, axis=0)

    piece = jax.ShapeDtypeStruct((systems, nrhs_dev, width), jnp.float32)
    *up, low = pl.pallas_call(
        functools.partial(pair_kernel, lanes),
        out_shape=[piece] * lanes + [jax.ShapeDtypeStruct((shards * lanes, nrhs_dev, width), jnp.bfloat16)],
        in_specs=[smem, vmem, anywhere, anywhere, anywhere],
        out_specs=[vmem] * (lanes + 1),
        scratch_shapes=[
            pltpu.VMEM((systems, 2, width, width), jnp.bfloat16),
            pltpu.VMEM((systems, 2, width, width), jnp.bfloat16),
            pltpu.VMEM((systems, 3, width, 2 * width), jnp.bfloat16),
            pltpu.VMEM((systems, width, width), jnp.float32),
            pltpu.VMEM((systems, 2, width, width), jnp.bfloat16),
            pltpu.VMEM((systems, lanes * nrhs_dev, width), jnp.float32),
            pltpu.VMEM((systems, lanes * nrhs_dev, width), jnp.float32),
            pltpu.SemaphoreType.DMA((systems + 1, 2)),
        ] + factor_scratch(systems, width),
        compiler_params=params,
    )(jnp.concatenate([mate_panel, lane_word]), x, w, z, received)
    low = lax.all_to_all(low, ("panel", "rhs"), split_axis=0, concat_axis=0, tiled=True)
    up = [up[0]] + [shift(up[e], e) for e in range(1, lanes)]
    return pl.pallas_call(
        functools.partial(place_kernel, lanes),
        out_shape=jax.ShapeDtypeStruct((nrhs_dev, per_panel * width), jnp.bfloat16),
        in_specs=[smem] + [vmem] * (lanes + 1),
        out_specs=vmem,
    )(jnp.concatenate([panel_mates, lane_word]), low, *up)


def solution(mesh):
    return jax.shard_map(
        on_device,
        mesh=mesh,
        in_specs=(P(("panel", "rhs"), None, None, None), P(), P(), P("rhs", "panel")),
        out_specs=P("rhs", "panel"),
        check_vma=False,
    )
```

```python
import functools
import jax
import jax.numpy as jnp
from jax import lax
from jax.experimental import pallas as pl
from jax.experimental.pallas import tpu as pltpu
from jax.sharding import PartitionSpec as P

STEP = 32
NT = (((1,), (1,)), ((), ()))
NN = (((1,), (0,)), ((), ()))
TN = (((0,), (0,)), ((), ()))


def dot(a, b, dims):
    return lax.dot_general(a, b, dims, preferred_element_type=jnp.float32)


def split3(a):
    one = a.astype(jnp.bfloat16)
    rest = a - one.astype(jnp.float32)
    two = rest.astype(jnp.bfloat16)
    three = (rest - two.astype(jnp.float32)).astype(jnp.bfloat16)
    return one, two, three


def dot6(a, b, dims):
    a1, a2, a3 = a
    b1, b2, b3 = b
    small = dot(a1, b3, dims) + dot(a3, b1, dims) + dot(a2, b2, dims)
    return dot(a1, b1, dims) + ((dot(a1, b2, dims) + dot(a2, b1, dims)) + small)


def dot3(a, b, dims):
    return dot(a[0], b[0], dims) + (dot(a[0], b[1], dims) + dot(a[1], b[0], dims))


def wide(parts):
    one, two, three = parts
    return jnp.concatenate([one, one, two, two, one, three], axis=1)


def deep(parts):
    one, two, three = parts
    return jnp.concatenate([one, two, one, two, three, one], axis=0)


def thirds(array):
    count = array.shape[0] // 3
    return array[:count] + (array[count:2 * count] + array[2 * count:])


def apply(rows, parts, dims):
    count = rows.shape[0]
    stack = jnp.concatenate(split3(rows), axis=0)
    high = dot(stack, parts[0], dims)
    low = dot(stack[:2 * count], parts[1], dims)
    return high[:count] + ((high[count:2 * count] + low[:count]) + (high[2 * count:] + low[count:]))


def factor(ref, slab_ref, past_ref):
    systems, width, _ = ref.shape
    teams, height, _ = slab_ref.shape
    team = height // STEP
    groups = STEP // 8
    lane = lax.broadcasted_iota(jnp.int32, (8, 128), 1)
    sub = lax.broadcasted_iota(jnp.int32, (8, 128), 0)
    member = lane // STEP
    place = lane % STEP
    col_in = lax.broadcasted_iota(jnp.int32, (STEP, width), 1)
    row_all = lax.broadcasted_iota(jnp.int32, (width, width), 0)
    col_all = lax.broadcasted_iota(jnp.int32, (width, width), 1)
    row_team = lax.broadcasted_iota(jnp.int32, (height, width), 0)
    col_team = lax.broadcasted_iota(jnp.int32, (height, width), 1)
    row_diag = lax.broadcasted_iota(jnp.int32, (height, 128), 0)
    col_diag = lax.broadcasted_iota(jnp.int32, (height, 128), 1)
    same = row_diag // STEP == col_diag // STEP
    lower = same & (col_diag <= row_diag)

    def spread(row):
        return jnp.broadcast_to(row, (8, 128))

    def padded(parts):
        if height == 128:
            return parts
        filler = jnp.zeros((128 - height, width), jnp.bfloat16)
        return [jnp.concatenate([part, filler], axis=0) for part in parts]

    def pivots(packs, pieces):
        placed = 0
        for first in range(0, STEP, 4):
            top, start = first // 8, first % 8
            tall = range(top, groups)
            own = (place >= first) & (place < first + 4)
            one = jnp.where(place - 8 * top == sub, 1.0, 0.0)
            each = range(len(packs))
            if start == 0:
                inverses = [None for _ in each]
            u = [
                [{g: jnp.take_along_axis(x[g], lane - place + (first + q), axis=1) for g in tall} for q in range(4)]
                for x in packs
            ]
            a = [{(i, j): spread(u[s][j][top][start + i:start + i + 1, :]) for j in range(4) for i in range(j + 1)} for s in each]
            for x in packs:
                for g in tall:
                    x[g] = jnp.where(own, one if g == top else 0.0, x[g])
            y = [[spread(x[top][start + q:start + q + 1, :]) for q in range(4)] for x in packs]
            low = [{} for _ in each]
            inv = [[None] * 4 for _ in each]
            for p in (0, 2):
                n = p + 1
                delta = [a[s][p, p] * a[s][n, n] - a[s][p, n] * a[s][p, n] for s in each]
                for s in each:
                    inv[s][p] = pl.reciprocal(a[s][p, p], approx=True)
                    inv[s][n] = pl.reciprocal(delta[s], approx=True) * a[s][p, p]
                for j in range(n, 4):
                    for s in each:
                        low[s][j, p] = a[s][p, j] * inv[s][p]
                for j in range(n + 1, 4):
                    for s in each:
                        a[s][n, j] = a[s][n, j] - low[s][n, p] * a[s][p, j]
                for j in range(n + 1, 4):
                    for s in each:
                        low[s][j, n] = a[s][n, j] * inv[s][n]
                for i in range(n + 1, 4):
                    for j in range(i, 4):
                        for s in each:
                            a[s][i, j] = (a[s][i, j] - low[s][i, p] * a[s][p, j]) - low[s][i, n] * a[s][n, j]
            for q in range(4):
                at = start + q
                for s in each:
                    for k in range(q):
                        for g in tall:
                            u[s][q][g] = u[s][q][g] - u[s][k][g] * low[s][q, k]
                        y[s][q] = y[s][q] - y[s][k] * low[s][q, k]
                    inverses[s] = inv[s][q] if at == 0 else jnp.where(sub >= at, inv[s][q], inverses[s])
                    for g in tall:
                        m = u[s][q][g] * inv[s][q]
                        if g == top:
                            m = jnp.where(sub > at, m, 0.0)
                        packs[s][g] = packs[s][g] - m * y[s][q]
                while placed * STEP < (first + q + 1) * len(pieces):
                    pieces[placed]()
                    placed += 1
            if start + 4 == 8:
                for s, x in enumerate(packs):
                    x[top] = x[top] * (inverses[s] * lax.rsqrt(inverses[s]))

    for t in range(teams):
        for i in range(team):
            slab_ref[t, i * STEP:(i + 1) * STEP] = ref[t * team + i, 0:STEP]
        past_ref[t] = jnp.zeros(past_ref.shape[1:], past_ref.dtype)

    def block(kb, carry):
        base = pl.multiple_of(kb * STEP, STEP)
        after = pl.multiple_of(jnp.minimum(base + STEP, width - STEP), STEP)
        done = (col_all >= base - STEP) & (col_all < base) & (row_all >= base + STEP)
        pieces = []
        for s in range(systems):
            held = {}

            def prepare(s=s, held=held):
                i = s % team
                p1, p2, p3 = split3(past_ref[s // team, i * STEP:(i + 1) * STEP])
                zero = jnp.zeros_like(p1)
                m1, m2, m3 = (jnp.where(col_in >= base + STEP, p, zero) for p in (p1, p2, p3))
                held["left"] = jnp.concatenate([m1, m1, m2, m2, m1, m3], axis=0)
                held["right"] = jnp.concatenate([p1, p2, p1, p2, p3, p1], axis=0)

            def trail(at, s=s, held=held):
                rows = slice(at, at + 128)
                update = dot(held["left"][:, rows], held["right"], TN)
                ref[s, rows] = jnp.where(done[rows], 0.0, ref[s, rows]) - update

            pieces.append(prepare)
            pieces.extend(functools.partial(trail, at) for at in range(0, width, 128))
        packs = []
        for t in range(teams):
            pack = []
            for g in range(groups):
                x = jnp.where(place - 8 * g == sub, 1.0, 0.0)
                for i in range(team):
                    piece = slab_ref[t, i * STEP + 8 * g:i * STEP + 8 * g + 8, 0:128]
                    if i > 0:
                        piece = pltpu.roll(piece, i * STEP, 1)
                    x = jnp.where(member == i, piece, x)
                pack.append(x)
            packs.append(pack)
        sides = []
        for t in range(teams):
            ident = jnp.where(col_team == row_team % STEP, 1.0, 0.0)
            sides.append(deep(padded(split3(jnp.where(col_team < STEP, ident, slab_ref[t])))))
        pivots(packs, pieces)
        for t in range(teams):
            inner = jnp.concatenate(packs[t], axis=0)
            inner = jnp.where(lower, jnp.concatenate([inner] * team, axis=0), 0.0)
            slab = dot(wide(split3(inner)), sides[t], NN)
            ahead = []
            for i in range(team):
                piece = slab[i * STEP:(i + 1) * STEP, 0:128]
                if i != 1:
                    piece = pltpu.roll(piece, (i - 1) * STEP % 128, 1)
                ahead.append(piece)
            ahead = jnp.where(same, jnp.concatenate(ahead, axis=0), 0.0)
            if height < 128:
                ahead = jnp.concatenate([ahead, jnp.zeros((128 - height, 128), jnp.float32)], axis=0)
            ahead = wide(split3(ahead.T[:height]))
            update = dot(ahead, deep(padded(split3(pltpu.roll(slab, width - STEP, 1)))), NN)
            coming = [pltpu.roll(ref[t * team + i, pl.ds(after, STEP), :], width - after, 1) for i in range(team)]
            slab_ref[t] = jnp.where(col_team >= width - STEP, 0.0, jnp.concatenate(coming, axis=0)) - update
            slab = pltpu.roll(slab, base, 1)
            past_ref[t] = slab
            for i in range(team):
                own_rows = slab[i * STEP:(i + 1) * STEP]
                ref[t * team + i, pl.ds(base, STEP), :] = jnp.where(col_in >= base + STEP, 0.0, own_rows)
        return carry

    lax.fori_loop(0, width // STEP, block, 0)


def factor_scratch(systems, width):
    team = max(n for n in range(1, 128 // STEP + 1) if systems % n == 0)
    return [pltpu.VMEM((systems // team, team * STEP, width), jnp.float32)] * 2


def scaled(matrix):
    factor_of = 1.0 / jnp.max(jnp.max(matrix, axis=1, keepdims=True), axis=0, keepdims=True)
    return matrix * factor_of, jnp.sqrt(factor_of)


def gram_kernel(counts_ref, tiles_ref, g_ref):
    systems, kslots, width, _ = tiles_ref.shape
    for s in range(systems):
        near = tiles_ref[s, 0:2].reshape(2 * width, width)
        g_ref[s] = dot(near, near, TN)
    for s in range(systems):
        for k in range(2, kslots):
            @pl.when(k < counts_ref[s])
            def _():
                tile = tiles_ref[s, k]
                g_ref[s] += dot(tile, tile, TN)


def own_kernel(g_ref, tiles_any, w_ref, z_ref, near_ref, t_ref, sem, *scratch):
    systems, _, width, _ = near_ref.shape
    copy = pltpu.make_async_copy(tiles_any.at[:, 0:2], near_ref, sem)
    copy.start()
    roots = []
    for s in range(systems):
        t_ref[s], root = scaled(g_ref[s])
        roots.append(root)
    factor(t_ref, *scratch)
    copy.wait()
    for s in range(systems):
        w1, w2, w3 = split3(t_ref[s] * roots[s])
        w_ref[s, 0] = w1
        w_ref[s, 1] = w2
        near = jnp.concatenate([near_ref[s, 1], near_ref[s, 0]], axis=0)
        z = dot(w1, near, NT) + (dot(w2, near, NT) + dot(w3, near, NT))
        z1, z2, z3 = split3(z)
        z_ref[s, 0] = z1
        z_ref[s, 1] = z2
        z_ref[s, 2] = z3


def mid_kernel(place_ref, x_ref, got_ref, w_any, z_any, q_ref, back_ref, first_ref, rhs_ref,
               near_ref, w_ref, z_ref, t_ref, v_ref, r_ref, sems, *scratch):
    systems, _, width, _ = z_ref.shape
    part = near_ref.shape[3]
    copies = []
    for s in range(systems):
        pairs = ((got_ref.at[place_ref[s]], near_ref.at[s]), (z_any.at[s], z_ref.at[s]))
        copies.append([pltpu.make_async_copy(a, b, sems.at[s, i]) for i, (a, b) in enumerate(pairs)])
        for copy in copies[s]:
            copy.start()
    w_copy = pltpu.make_async_copy(w_any, w_ref, sems.at[systems, 0])
    w_copy.start()
    roots = []
    for s in range(systems):
        for copy in copies[s]:
            copy.wait()
        near = near_ref[s].reshape(2 * width, part)
        v = split3(thirds(dot(z_ref[s].reshape(3 * width, 2 * width), near, NN)))
        vt = [one.T for one in v]
        for i in range(3):
            v_ref[s, i] = vt[i]
        t_ref[s], root = scaled(dot(near.T, near, NN) - dot(wide(vt), deep(v), NN))
        roots.append(root)
        x = x_ref[:, s * width:(s + 1) * width]
        first = dot(x, z_ref[s, 0, :, width:], NT) + dot(x, z_ref[s, 1, :, width:], NT)
        first_ref[s, :, :width] = first
        r_ref[s] = dot(x, near[width:], NN) - apply(first, v, NN)
    factor(t_ref, *scratch)
    w_copy.wait()
    for s in range(systems):
        near_t = near_ref[s].reshape(2 * width, part).T
        own = split3(t_ref[s] * roots[s])
        vt = [v_ref[s, i] for i in range(3)]
        more = apply(r_ref[s], own, NT)
        first_ref[s, :, width:] = more
        rest = near_t.astype(jnp.float32) - dot6(vt, [z_ref[s, i] for i in range(3)], NN)
        q = split3(dot(wide(own), deep(split3(rest)), NN))
        for i in range(3):
            q_ref[s, i] = q[i]
        x = x_ref[:, s * width:(s + 1) * width].astype(jnp.float32)
        first = first_ref[s, :, :width]
        rhs = jnp.concatenate([jnp.zeros_like(x), x], axis=1) - apply(first, (z_ref[s, 0], z_ref[s, 1]), NN)
        rhs_ref[s] = rhs - apply(more, q, NN)
        left = split3(-dot3(own, split3(dot3(vt, (w_ref[s, 0], w_ref[s, 1]), NN)), NN))
        for i in range(2):
            back_ref[s, i, :, :width] = left[i]
            back_ref[s, i, :, width:] = own[i]


def last_kernel(lanes, place_ref, first_ref, rhs_ref, got_ref, z_any, q_any, w_any, back_any, *refs):
    up_refs, refs = refs[:lanes], refs[lanes:]
    low_ref, near_ref, z_ref, q_ref, w_ref, back_ref, t_ref, v_ref, r_ref, sems, *scratch = refs
    systems, _, width, _ = z_ref.shape
    part = near_ref.shape[3]
    count = first_ref.shape[1] // lanes
    copies = []
    for s in range(systems):
        pairs = ((got_ref.at[place_ref[s]], near_ref.at[s]), (z_any.at[s], z_ref.at[s]), (q_any.at[s], q_ref.at[s]))
        copies.append([pltpu.make_async_copy(a, b, sems.at[s, i]) for i, (a, b) in enumerate(pairs)])
        for copy in copies[s]:
            copy.start()
    ends = [
        pltpu.make_async_copy(w_any, w_ref, sems.at[systems, 0]),
        pltpu.make_async_copy(back_any, back_ref, sems.at[systems, 1]),
    ]
    for copy in ends:
        copy.start()
    low_ref[...] = jnp.zeros(low_ref.shape, low_ref.dtype)
    roots = []
    for s in range(systems):
        for copy in copies[s]:
            copy.wait()
        near = near_ref[s].reshape(2 * width, part)
        upper = thirds(dot(z_ref[s].reshape(3 * width, 2 * width), near, NN))
        lower = thirds(dot(q_ref[s].reshape(-1, 2 * width), near, NN))
        v = split3(jnp.concatenate([upper, lower], axis=0))
        v_ref[s, 0] = v[0]
        v_ref[s, 1] = v[1]
        vt = [one.T for one in v]
        t_ref[s], root = scaled(dot(near.T, near, NN) - dot(wide(vt), deep(v), NN))
        roots.append(root)
        r_ref[s] = thirds(dot(jnp.concatenate(split3(rhs_ref[s]), axis=0), near, NN))
    factor(t_ref, *scratch)
    parts = [split3(t_ref[s] * roots[s])[:2] for s in range(systems)]
    half = [apply(r_ref[s], parts[s], NT) for s in range(systems)]
    last = [apply(half[s], parts[s], NN) for s in range(systems)]
    mid = [first_ref[s] - apply(last[s], (v_ref[s, 0], v_ref[s, 1]), NT) for s in range(systems)]
    for copy in ends:
        copy.wait()
    for s in range(systems):
        both = apply(mid[s][:, width:], (back_ref[s, 0], back_ref[s, 1]), NN)
        up = apply(mid[s][:, :width], (w_ref[s, 0], w_ref[s, 1]), NN) + both[:, :width]
        low = jnp.concatenate([both[:, width:], last[s]], axis=1)
        for e in range(lanes):
            up_refs[e][s] = up[e * count:(e + 1) * count]
            owner = lax.rem(place_ref[systems] + e, lanes)
            low_ref[place_ref[s] * lanes + owner] = low[e * count:(e + 1) * count].astype(low_ref.dtype)


def place_kernel(lanes, place_ref, low_ref, *refs):
    up_refs, out_ref = refs[:lanes], refs[lanes]
    systems, _, width = up_refs[0].shape
    for e in range(lanes):
        owner = lax.rem(place_ref[systems * lanes] + lanes - e, lanes)
        for s in range(systems):
            at = owner * systems + s
            total = up_refs[e][s] + low_ref[place_ref[at] * lanes + owner].astype(jnp.float32)
            out_ref[:, pl.ds(pl.multiple_of(at * width, width), width)] = total.astype(out_ref.dtype)


def on_device(tiles, pattern, counts, inputs):
    shards = lax.axis_size("panel")
    lanes = lax.axis_size("rhs")
    systems, kslots, width, _ = tiles.shape
    nrhs_dev = inputs.shape[0]
    own_width = systems * width
    my_panel = lax.axis_index("panel")
    my_lane = lax.axis_index("rhs")
    per_panel = systems * lanes
    own_cnt = lax.dynamic_slice_in_dim(counts, my_panel * per_panel + my_lane * systems, systems, 0)
    panel_mates = lax.dynamic_slice(pattern, (my_panel * per_panel, 1), (per_panel, 1))[:, 0] // per_panel
    mate_panel = lax.dynamic_slice_in_dim(panel_mates, my_lane * systems, systems, 0)
    hit = mate_panel[None, :] == jnp.arange(shards, dtype=jnp.int32)[:, None]
    slot_of = jnp.sum(hit * jnp.arange(systems, dtype=jnp.int32)[None, :], axis=1)
    lane_word = my_lane[None].astype(jnp.int32)

    def shift(value, by):
        return lax.ppermute(value, "rhs", [(i, (i + by) % lanes) for i in range(lanes)])

    part = width // 2
    rest = width - part
    ordered = tiles[:, :2][slot_of]
    half_one, half_two = ordered[..., :part], ordered[..., part:]
    got_one = lax.all_to_all(half_one, "panel", split_axis=0, concat_axis=0, tiled=True)

    vmem = pl.BlockSpec(memory_space=pltpu.VMEM)
    smem = pl.BlockSpec(memory_space=pltpu.SMEM)
    anywhere = pl.BlockSpec(memory_space=pl.ANY)
    params = pltpu.CompilerParams(vmem_limit_bytes=56 * 1024 * 1024)
    g = pl.pallas_call(
        gram_kernel,
        out_shape=jax.ShapeDtypeStruct((systems, width, width), jnp.float32),
        in_specs=[smem, vmem],
        out_specs=vmem,
        compiler_params=params,
        cost_estimate=pl.CostEstimate(flops=5 * 10**9, bytes_accessed=6 * 10**6, transcendentals=0),
    )(own_cnt, tiles)
    half_two, g = lax.optimization_barrier((half_two, g))
    got_two = lax.all_to_all(half_two, "panel", split_axis=0, concat_axis=0, tiled=True)
    w, z = pl.pallas_call(
        own_kernel,
        out_shape=(
            jax.ShapeDtypeStruct((systems, 2, width, width), jnp.bfloat16),
            jax.ShapeDtypeStruct((systems, 3, width, 2 * width), jnp.bfloat16),
        ),
        in_specs=[vmem, anywhere],
        out_specs=(vmem, vmem),
        scratch_shapes=[
            pltpu.VMEM((systems, 2, width, width), jnp.bfloat16),
            pltpu.VMEM((systems, width, width), jnp.float32),
            pltpu.SemaphoreType.DMA,
        ] + factor_scratch(systems, width),
        compiler_params=params,
        cost_estimate=pl.CostEstimate(flops=30 * 10**9, bytes_accessed=8 * 10**6, transcendentals=0),
    )(g, tiles)

    inputs, w = lax.optimization_barrier((inputs, w))
    parts = [lax.dynamic_slice_in_dim(inputs, my_lane * own_width, own_width, 1)]
    for e in range(1, lanes):
        block = lax.dynamic_slice_in_dim(inputs, (my_lane + lanes - e) % lanes * own_width, own_width, 1)
        parts.append(shift(block, -e))
    x = jnp.concatenate(parts, axis=0)

    nrhs = lanes * nrhs_dev
    where = jnp.concatenate([mate_panel, lane_word])
    q, back, first, rhs = pl.pallas_call(
        mid_kernel,
        out_shape=(
            jax.ShapeDtypeStruct((systems, 3, part, 2 * width), jnp.bfloat16),
            jax.ShapeDtypeStruct((systems, 2, part, width + part), jnp.bfloat16),
            jax.ShapeDtypeStruct((systems, nrhs, width + part), jnp.float32),
            jax.ShapeDtypeStruct((systems, nrhs, 2 * width), jnp.float32),
        ),
        in_specs=[smem, vmem, anywhere, anywhere, anywhere],
        out_specs=(vmem, vmem, vmem, vmem),
        scratch_shapes=[
            pltpu.VMEM((systems, 2, width, part), jnp.bfloat16),
            pltpu.VMEM((systems, 2, width, width), jnp.bfloat16),
            pltpu.VMEM((systems, 3, width, 2 * width), jnp.bfloat16),
            pltpu.VMEM((systems, part, part), jnp.float32),
            pltpu.VMEM((systems, 3, part, width), jnp.bfloat16),
            pltpu.VMEM((systems, nrhs, part), jnp.float32),
            pltpu.SemaphoreType.DMA((systems + 1, 2)),
        ] + factor_scratch(systems, part),
        compiler_params=params,
        cost_estimate=pl.CostEstimate(flops=20 * 10**9, bytes_accessed=8 * 10**6, transcendentals=0),
    )(where, x, got_one, w, z)

    piece = jax.ShapeDtypeStruct((systems, nrhs_dev, width), jnp.float32)
    *up, low = pl.pallas_call(
        functools.partial(last_kernel, lanes),
        out_shape=[piece] * lanes + [jax.ShapeDtypeStruct((shards * lanes, nrhs_dev, width), jnp.bfloat16)],
        in_specs=[smem, vmem, vmem] + [anywhere] * 5,
        out_specs=[vmem] * (lanes + 1),
        scratch_shapes=[
            pltpu.VMEM((systems, 2, width, rest), jnp.bfloat16),
            pltpu.VMEM((systems, 3, width, 2 * width), jnp.bfloat16),
            pltpu.VMEM((systems, 3, part, 2 * width), jnp.bfloat16),
            pltpu.VMEM((systems, 2, width, width), jnp.bfloat16),
            pltpu.VMEM((systems, 2, part, width + part), jnp.bfloat16),
            pltpu.VMEM((systems, rest, rest), jnp.float32),
            pltpu.VMEM((systems, 2, width + part, rest), jnp.bfloat16),
            pltpu.VMEM((systems, nrhs, rest), jnp.float32),
            pltpu.SemaphoreType.DMA((systems + 1, 3)),
        ] + factor_scratch(systems, rest),
        compiler_params=params,
    )(where, first, rhs, got_two, z, q, w, back)
    low = lax.all_to_all(low, ("panel", "rhs"), split_axis=0, concat_axis=0, tiled=True)
    up = [up[0]] + [shift(up[e], e) for e in range(1, lanes)]
    return pl.pallas_call(
        functools.partial(place_kernel, lanes),
        out_shape=jax.ShapeDtypeStruct((nrhs_dev, per_panel * width), jnp.bfloat16),
        in_specs=[smem] + [vmem] * (lanes + 1),
        out_specs=vmem,
    )(jnp.concatenate([panel_mates, lane_word]), low, *up)


def solution(mesh):
    return jax.shard_map(
        on_device,
        mesh=mesh,
        in_specs=(P(("panel", "rhs"), None, None, None), P(), P(), P("rhs", "panel")),
        out_specs=P("rhs", "panel"),
        check_vma=False,
    )
```

```python
import functools
import jax
import jax.numpy as jnp
from jax import lax
from jax.experimental import pallas as pl
from jax.experimental.pallas import tpu as pltpu
from jax.sharding import PartitionSpec as P

STEP = 32
NT = (((1,), (1,)), ((), ()))
NN = (((1,), (0,)), ((), ()))
TN = (((0,), (0,)), ((), ()))


def dot(a, b, dims):
    return lax.dot_general(a, b, dims, preferred_element_type=jnp.float32)


def split3(a):
    one = a.astype(jnp.bfloat16)
    rest = a - one.astype(jnp.float32)
    two = rest.astype(jnp.bfloat16)
    three = (rest - two.astype(jnp.float32)).astype(jnp.bfloat16)
    return one, two, three


def dot6(a, b, dims):
    a1, a2, a3 = a
    b1, b2, b3 = b
    small = dot(a1, b3, dims) + dot(a3, b1, dims) + dot(a2, b2, dims)
    return dot(a1, b1, dims) + ((dot(a1, b2, dims) + dot(a2, b1, dims)) + small)


def wide(parts):
    one, two, three = parts
    return jnp.concatenate([one, one, two, two, one, three], axis=1)


def deep(parts):
    one, two, three = parts
    return jnp.concatenate([one, two, one, two, three, one], axis=0)


def thirds(array):
    count = array.shape[0] // 3
    return array[:count] + (array[count:2 * count] + array[2 * count:])


def apply(rows, parts, dims):
    count = rows.shape[0]
    stack = jnp.concatenate(split3(rows), axis=0)
    high = dot(stack, parts[0], dims)
    low = dot(stack[:2 * count], parts[1], dims)
    return high[:count] + ((high[count:2 * count] + low[:count]) + (high[2 * count:] + low[count:]))


def factor(ref, slab_ref, past_ref):
    systems, width, _ = ref.shape
    teams, height, _ = slab_ref.shape
    team = height // STEP
    groups = STEP // 8
    lane = lax.broadcasted_iota(jnp.int32, (8, 128), 1)
    sub = lax.broadcasted_iota(jnp.int32, (8, 128), 0)
    member = lane // STEP
    place = lane % STEP
    col_in = lax.broadcasted_iota(jnp.int32, (STEP, width), 1)
    row_all = lax.broadcasted_iota(jnp.int32, (width, width), 0)
    col_all = lax.broadcasted_iota(jnp.int32, (width, width), 1)
    row_team = lax.broadcasted_iota(jnp.int32, (height, width), 0)
    col_team = lax.broadcasted_iota(jnp.int32, (height, width), 1)
    row_diag = lax.broadcasted_iota(jnp.int32, (height, 128), 0)
    col_diag = lax.broadcasted_iota(jnp.int32, (height, 128), 1)
    same = row_diag // STEP == col_diag // STEP
    lower = same & (col_diag <= row_diag)

    def spread(row):
        return jnp.broadcast_to(row, (8, 128))

    def padded(parts):
        if height == 128:
            return parts
        filler = jnp.zeros((128 - height, width), jnp.bfloat16)
        return [jnp.concatenate([part, filler], axis=0) for part in parts]

    def pivots(packs, pieces):
        placed = 0
        for first in range(0, STEP, 4):
            top, start = first // 8, first % 8
            tall = range(top, groups)
            own = (place >= first) & (place < first + 4)
            one = jnp.where(place - 8 * top == sub, 1.0, 0.0)
            each = range(len(packs))
            if start == 0:
                inverses = [None for _ in each]
            u = [
                [{g: jnp.take_along_axis(x[g], lane - place + (first + q), axis=1) for g in tall} for q in range(4)]
                for x in packs
            ]
            a = [{(i, j): spread(u[s][j][top][start + i:start + i + 1, :]) for j in range(4) for i in range(j + 1)} for s in each]
            for x in packs:
                for g in tall:
                    x[g] = jnp.where(own, one if g == top else 0.0, x[g])
            y = [[spread(x[top][start + q:start + q + 1, :]) for q in range(4)] for x in packs]
            low = [{} for _ in each]
            inv = [[None] * 4 for _ in each]
            for p in (0, 2):
                n = p + 1
                delta = [a[s][p, p] * a[s][n, n] - a[s][p, n] * a[s][p, n] for s in each]
                for s in each:
                    inv[s][p] = pl.reciprocal(a[s][p, p], approx=True)
                    inv[s][n] = pl.reciprocal(delta[s], approx=True) * a[s][p, p]
                for j in range(n, 4):
                    for s in each:
                        low[s][j, p] = a[s][p, j] * inv[s][p]
                for j in range(n + 1, 4):
                    for s in each:
                        a[s][n, j] = a[s][n, j] - low[s][n, p] * a[s][p, j]
                for j in range(n + 1, 4):
                    for s in each:
                        low[s][j, n] = a[s][n, j] * inv[s][n]
                for i in range(n + 1, 4):
                    for j in range(i, 4):
                        for s in each:
                            a[s][i, j] = (a[s][i, j] - low[s][i, p] * a[s][p, j]) - low[s][i, n] * a[s][n, j]
            for q in range(4):
                at = start + q
                for s in each:
                    for k in range(q):
                        for g in tall:
                            u[s][q][g] = u[s][q][g] - u[s][k][g] * low[s][q, k]
                        y[s][q] = y[s][q] - y[s][k] * low[s][q, k]
                    inverses[s] = inv[s][q] if at == 0 else jnp.where(sub >= at, inv[s][q], inverses[s])
                    for g in tall:
                        m = u[s][q][g] * inv[s][q]
                        if g == top:
                            m = jnp.where(sub > at, m, 0.0)
                        packs[s][g] = packs[s][g] - m * y[s][q]
                while placed * STEP < (first + q + 1) * len(pieces):
                    pieces[placed]()
                    placed += 1
            if start + 4 == 8:
                for s, x in enumerate(packs):
                    x[top] = x[top] * (inverses[s] * lax.rsqrt(inverses[s]))

    for t in range(teams):
        for i in range(team):
            slab_ref[t, i * STEP:(i + 1) * STEP] = ref[t * team + i, 0:STEP]
        past_ref[t] = jnp.zeros(past_ref.shape[1:], past_ref.dtype)

    def block(kb, carry):
        base = pl.multiple_of(kb * STEP, STEP)
        after = pl.multiple_of(jnp.minimum(base + STEP, width - STEP), STEP)
        done = (col_all >= base - STEP) & (col_all < base) & (row_all >= base + STEP)
        pieces = []
        for s in range(systems):
            held = {}

            def prepare(s=s, held=held):
                i = s % team
                p1, p2, p3 = split3(past_ref[s // team, i * STEP:(i + 1) * STEP])
                zero = jnp.zeros_like(p1)
                m1, m2, m3 = (jnp.where(col_in >= base + STEP, p, zero) for p in (p1, p2, p3))
                held["left"] = jnp.concatenate([m1, m1, m2, m2, m1, m3], axis=0)
                held["right"] = jnp.concatenate([p1, p2, p1, p2, p3, p1], axis=0)

            def trail(at, s=s, held=held):
                rows = slice(at, at + 128)
                update = dot(held["left"][:, rows], held["right"], TN)
                ref[s, rows] = jnp.where(done[rows], 0.0, ref[s, rows]) - update

            pieces.append(prepare)
            pieces.extend(functools.partial(trail, at) for at in range(0, width, 128))
        packs = []
        for t in range(teams):
            pack = []
            for g in range(groups):
                x = jnp.where(place - 8 * g == sub, 1.0, 0.0)
                for i in range(team):
                    piece = slab_ref[t, i * STEP + 8 * g:i * STEP + 8 * g + 8, 0:128]
                    if i > 0:
                        piece = pltpu.roll(piece, i * STEP, 1)
                    x = jnp.where(member == i, piece, x)
                pack.append(x)
            packs.append(pack)
        sides = []
        for t in range(teams):
            ident = jnp.where(col_team == row_team % STEP, 1.0, 0.0)
            sides.append(deep(padded(split3(jnp.where(col_team < STEP, ident, slab_ref[t])))))
        pivots(packs, pieces)
        for t in range(teams):
            inner = jnp.concatenate(packs[t], axis=0)
            inner = jnp.where(lower, jnp.concatenate([inner] * team, axis=0), 0.0)
            slab = dot(wide(split3(inner)), sides[t], NN)
            ahead = []
            for i in range(team):
                piece = slab[i * STEP:(i + 1) * STEP, 0:128]
                if i != 1:
                    piece = pltpu.roll(piece, (i - 1) * STEP % 128, 1)
                ahead.append(piece)
            ahead = jnp.where(same, jnp.concatenate(ahead, axis=0), 0.0)
            if height < 128:
                ahead = jnp.concatenate([ahead, jnp.zeros((128 - height, 128), jnp.float32)], axis=0)
            ahead = wide(split3(ahead.T[:height]))
            update = dot(ahead, deep(padded(split3(pltpu.roll(slab, width - STEP, 1)))), NN)
            coming = [pltpu.roll(ref[t * team + i, pl.ds(after, STEP), :], width - after, 1) for i in range(team)]
            slab_ref[t] = jnp.where(col_team >= width - STEP, 0.0, jnp.concatenate(coming, axis=0)) - update
            slab = pltpu.roll(slab, base, 1)
            past_ref[t] = slab
            for i in range(team):
                own_rows = slab[i * STEP:(i + 1) * STEP]
                ref[t * team + i, pl.ds(base, STEP), :] = jnp.where(col_in >= base + STEP, 0.0, own_rows)
        return carry

    lax.fori_loop(0, width // STEP, block, 0)


def factor_scratch(systems, width):
    team = max(n for n in range(1, 128 // STEP + 1) if systems % n == 0)
    return [pltpu.VMEM((systems // team, team * STEP, width), jnp.float32)] * 2


def scaled(matrix):
    factor_of = 1.0 / jnp.max(jnp.max(matrix, axis=1, keepdims=True), axis=0, keepdims=True)
    return matrix * factor_of, jnp.sqrt(factor_of)


def pick_kernel(slot_ref, tiles_ref, *refs):
    out_refs, sems = refs[:-1], refs[-1]
    copies = []
    for e, out_ref in enumerate(out_refs):
        source = tiles_ref.at[jnp.maximum(slot_ref[e], 0), 0:2]
        copies.append(pltpu.make_async_copy(source, out_ref, sems.at[e]))
    for copy in copies:
        copy.start()
    for copy in copies:
        copy.wait()


def own_kernel(counts_ref, tiles_ref, w_ref, g_ref, *scratch):
    systems, kslots, width, _ = tiles_ref.shape
    for s in range(systems):
        near = tiles_ref[s, 0:2].reshape(2 * width, width)
        g_ref[s] = dot(near, near, TN)
    for s in range(systems):
        for k in range(2, kslots):
            @pl.when(k < counts_ref[s])
            def _():
                tile = tiles_ref[s, k]
                g_ref[s] += dot(tile, tile, TN)
    roots = []
    for s in range(systems):
        g_ref[s], root = scaled(g_ref[s])
        roots.append(root)
    factor(g_ref, *scratch)
    for s in range(systems):
        for i, part in enumerate(split3(g_ref[s] * roots[s])):
            w_ref[s, i] = part


def collect(slot_ref, shifts, got_refs, near_ref, sems):
    spare = near_ref.shape[0] - len(shifts)
    copies = []
    for i, (e, got_ref) in enumerate(zip(shifts, got_refs)):
        slot = jnp.where(slot_ref[e - 1] >= 0, slot_ref[e - 1], spare + i)
        copies.append(pltpu.make_async_copy(got_ref, near_ref.at[slot], sems.at[i]))
    for copy in copies:
        copy.start()
    return copies


def schur(near, z):
    near_t = near.T
    v = split3(dot(near_t, z[0], NT) + (dot(near_t, z[1], NT) + dot(near_t, z[2], NT)))
    return v, dot(near_t, near, NN) - dot6(v, v, NT)


def link_kernel(shifts, slot_ref, w_ref, tiles_any, *refs):
    got_refs, refs = refs[:len(shifts)], refs[len(shifts):]
    z_ref, v_ref, t_ref, own_ref, near_ref, own_sem, sems = refs
    systems, _, width, _ = w_ref.shape
    own_copy = pltpu.make_async_copy(tiles_any.at[:, 0:2], own_ref, own_sem)
    own_copy.start()
    for s in range(systems):
        near_ref[s] = jnp.zeros(near_ref.shape[1:], near_ref.dtype)
    copies = collect(slot_ref, shifts, got_refs, near_ref, sems)
    own_copy.wait()
    for s in range(systems):
        own = jnp.concatenate([own_ref[s, 1], own_ref[s, 0]], axis=0)
        z = split3(dot(w_ref[s, 0], own, NT) + (dot(w_ref[s, 1], own, NT) + dot(w_ref[s, 2], own, NT)))
        for i in range(3):
            z_ref[s, i] = z[i]
    for copy in copies:
        copy.wait()
    for s in range(systems):
        v, t_ref[s] = schur(near_ref[s].reshape(2 * width, width), [z_ref[s, i] for i in range(3)])
        v_ref[s, 0] = v[0]
        v_ref[s, 1] = v[1]


def pair_kernel(lanes, shifts, late, place_ref, slot_ref, x_ref, w_any, z_any, v_any, t_any, *refs):
    got_refs, up_refs, refs = refs[:len(shifts)], refs[len(shifts):len(shifts) + lanes], refs[len(shifts) + lanes:]
    low_ref, near_ref, w_ref, z_ref, zj_ref, v_ref, t_ref, r_ref, first_ref, near_sems, sems, *scratch = refs
    _, _, width, _ = z_ref.shape
    systems = first_ref.shape[0]
    count = x_ref.shape[0] // lanes
    near_copies = collect(slot_ref, shifts, got_refs, near_ref, near_sems)
    late_slots = [slot_ref[e - 1] for e in late]
    copies = [
        pltpu.make_async_copy(z_any.at[jnp.maximum(slot, 0)], z_ref.at[i], sems.at[i]) for i, slot in enumerate(late_slots)
    ] + [
        pltpu.make_async_copy(t_any, t_ref.at[0:systems], sems.at[2]),
        pltpu.make_async_copy(v_any, v_ref.at[0:systems], sems.at[3]),
        pltpu.make_async_copy(z_any.at[:, 0:2, :, width:], zj_ref, sems.at[4]),
    ]
    w_copy = pltpu.make_async_copy(w_any.at[:, 0:2], w_ref, sems.at[5])
    for copy in copies + [w_copy]:
        copy.start()
    low_ref[...] = jnp.zeros(low_ref.shape, low_ref.dtype)
    for copy in near_copies + copies:
        copy.wait()
    for i, slot in enumerate(late_slots):
        at = jnp.where(slot >= 0, slot, systems + i)
        near = near_ref[jnp.maximum(slot, 0)].reshape(2 * width, width)
        v, t_ref[at] = schur(near, [z_ref[i, p] for p in range(3)])
        v_ref[at, 0] = v[0]
        v_ref[at, 1] = v[1]
    roots = []
    for s in range(systems):
        x = x_ref[:, s * width:(s + 1) * width]
        first_ref[s] = dot(x, zj_ref[s, 0], NT) + dot(x, zj_ref[s, 1], NT)
        r_ref[s] = dot(x, near_ref[s, 1], NN)
    for s in range(systems):
        r_ref[s] = r_ref[s] - apply(first_ref[s], (v_ref[s, 0], v_ref[s, 1]), NT)
        t_ref[s], root = scaled(t_ref[s])
        roots.append(root)
    factor(t_ref.at[0:systems], *scratch)
    w_copy.wait()
    parts = [split3(t_ref[s] * roots[s])[:2] for s in range(systems)]
    half = [apply(r_ref[s], parts[s], NT) for s in range(systems)]
    last = [apply(half[s], parts[s], NN) for s in range(systems)]
    mid = [first_ref[s] - apply(last[s], (v_ref[s, 0], v_ref[s, 1]), NN) for s in range(systems)]
    for s in range(systems):
        up = apply(mid[s], (w_ref[s, 0], w_ref[s, 1]), NN)
        for e in range(lanes):
            up_refs[e][s] = up[e * count:(e + 1) * count]
            owner = lax.rem(place_ref[systems] + e, lanes)
            low_ref[place_ref[s] * lanes + owner] = last[s][e * count:(e + 1) * count].astype(low_ref.dtype)


def place_kernel(lanes, place_ref, low_ref, *refs):
    up_refs, out_ref = refs[:lanes], refs[lanes]
    systems, _, width = up_refs[0].shape
    for e in range(lanes):
        owner = lax.rem(place_ref[systems * lanes] + lanes - e, lanes)
        for s in range(systems):
            at = owner * systems + s
            total = up_refs[e][s] + low_ref[place_ref[at] * lanes + owner].astype(jnp.float32)
            out_ref[:, pl.ds(pl.multiple_of(at * width, width), width)] = total.astype(out_ref.dtype)


def on_device(tiles, pattern, counts, inputs):
    shards = lax.axis_size("panel")
    lanes = lax.axis_size("rhs")
    systems, kslots, width, _ = tiles.shape
    nrhs_dev = inputs.shape[0]
    own_width = systems * width
    my_panel = lax.axis_index("panel")
    my_lane = lax.axis_index("rhs")
    per_panel = systems * lanes
    own_cnt = lax.dynamic_slice_in_dim(counts, my_panel * per_panel + my_lane * systems, systems, 0)
    panel_mates = lax.dynamic_slice(pattern, (my_panel * per_panel, 1), (per_panel, 1))[:, 0] // per_panel
    mate_panel = lax.dynamic_slice_in_dim(panel_mates, my_lane * systems, systems, 0)
    hops = jnp.arange(1, shards, dtype=jnp.int32)

    def slots(panels):
        hit = mate_panel[None, :] == panels[:, None]
        return jnp.max(jnp.where(hit, jnp.arange(systems, dtype=jnp.int32)[None, :], -1), axis=1)

    lane_word = my_lane[None].astype(jnp.int32)

    def shift(value, axis, by):
        size = lax.axis_size(axis)
        return lax.ppermute(value, axis, [(i, (i + by) % size) for i in range(size)])

    vmem = pl.BlockSpec(memory_space=pltpu.VMEM)
    smem = pl.BlockSpec(memory_space=pltpu.SMEM)
    anywhere = pl.BlockSpec(memory_space=pl.ANY)
    params = pltpu.CompilerParams(vmem_limit_bytes=48 * 1024 * 1024)
    pairs = shards - 1
    every = tuple(range(1, shards))
    late = (1, shards - 1)
    early = tuple(e for e in every if e not in late)
    pieces = pl.pallas_call(
        pick_kernel,
        out_shape=[jax.ShapeDtypeStruct((2, width, width), jnp.bfloat16)] * pairs,
        in_specs=[smem, anywhere],
        out_specs=[anywhere] * pairs,
        scratch_shapes=[pltpu.SemaphoreType.DMA((pairs,))],
    )(slots((my_panel + hops) % shards), tiles)
    received = {e: shift(pieces[e - 1], "panel", e) for e in early}

    w = pl.pallas_call(
        own_kernel,
        out_shape=jax.ShapeDtypeStruct((systems, 3, width, width), jnp.bfloat16),
        in_specs=[smem, vmem],
        out_specs=vmem,
        scratch_shapes=[pltpu.VMEM((systems, width, width), jnp.float32)] + factor_scratch(systems, width),
        compiler_params=params,
        cost_estimate=pl.CostEstimate(flops=30 * 10**9, bytes_accessed=8 * 10**6, transcendentals=0),
    )(own_cnt, tiles)

    come = [received[e] for e in early]
    held, inputs, w, come = lax.optimization_barrier(([pieces[e - 1] for e in late], inputs, w, come))
    received.update(zip(early, come))
    received.update({e: shift(piece, "panel", e) for e, piece in zip(late, held)})
    parts = [lax.dynamic_slice_in_dim(inputs, my_lane * own_width, own_width, 1)]
    for e in range(1, lanes):
        block = lax.dynamic_slice_in_dim(inputs, (my_lane + lanes - e) % lanes * own_width, own_width, 1)
        parts.append(shift(block, "rhs", -e))
    x = jnp.concatenate(parts, axis=0)

    from_slot = slots((my_panel - hops) % shards)
    z, v, t = pl.pallas_call(
        functools.partial(link_kernel, early),
        out_shape=(
            jax.ShapeDtypeStruct((systems, 3, width, 2 * width), jnp.bfloat16),
            jax.ShapeDtypeStruct((systems, 2, width, width), jnp.bfloat16),
            jax.ShapeDtypeStruct((systems, width, width), jnp.float32),
        ),
        in_specs=[smem, vmem, anywhere] + [anywhere] * len(early),
        out_specs=(vmem, vmem, vmem),
        scratch_shapes=[
            pltpu.VMEM((systems, 2, width, width), jnp.bfloat16),
            pltpu.VMEM((systems + len(early), 2, width, width), jnp.bfloat16),
            pltpu.SemaphoreType.DMA,
            pltpu.SemaphoreType.DMA((len(early),)),
        ],
        compiler_params=params,
        cost_estimate=pl.CostEstimate(flops=12 * 10**9, bytes_accessed=8 * 10**6, transcendentals=0),
    )(from_slot, w, tiles, *[received[e] for e in early])

    nrhs = lanes * nrhs_dev
    piece = jax.ShapeDtypeStruct((systems, nrhs_dev, width), jnp.float32)
    *up, low = pl.pallas_call(
        functools.partial(pair_kernel, lanes, every, late),
        out_shape=[piece] * lanes + [jax.ShapeDtypeStruct((shards * lanes, nrhs_dev, width), jnp.bfloat16)],
        in_specs=[smem, smem, vmem] + [anywhere] * (4 + pairs),
        out_specs=[vmem] * (lanes + 1),
        scratch_shapes=[
            pltpu.VMEM((systems + pairs, 2, width, width), jnp.bfloat16),
            pltpu.VMEM((systems, 2, width, width), jnp.bfloat16),
            pltpu.VMEM((len(late), 3, width, 2 * width), jnp.bfloat16),
            pltpu.VMEM((systems, 2, width, width), jnp.bfloat16),
            pltpu.VMEM((systems + len(late), 2, width, width), jnp.bfloat16),
            pltpu.VMEM((systems + len(late), width, width), jnp.float32),
            pltpu.VMEM((systems, nrhs, width), jnp.float32),
            pltpu.VMEM((systems, nrhs, width), jnp.float32),
            pltpu.SemaphoreType.DMA((pairs,)),
            pltpu.SemaphoreType.DMA((6,)),
        ] + factor_scratch(systems, width),
        compiler_params=params,
    )(
        jnp.concatenate([mate_panel, lane_word]), from_slot, x, w, z, v, t,
        *[received[e] for e in every],
    )
    low = lax.all_to_all(low, ("panel", "rhs"), split_axis=0, concat_axis=0, tiled=True)
    up = [up[0]] + [shift(up[e], "rhs", e) for e in range(1, lanes)]
    return pl.pallas_call(
        functools.partial(place_kernel, lanes),
        out_shape=jax.ShapeDtypeStruct((nrhs_dev, per_panel * width), jnp.bfloat16),
        in_specs=[smem] + [vmem] * (lanes + 1),
        out_specs=vmem,
    )(jnp.concatenate([panel_mates, lane_word]), low, *up)


def solution(mesh):
    return jax.shard_map(
        on_device,
        mesh=mesh,
        in_specs=(P(("panel", "rhs"), None, None, None), P(), P(), P("rhs", "panel")),
        out_specs=P("rhs", "panel"),
        check_vma=False,
    )
```

```python
import functools
import jax
import jax.numpy as jnp
from jax import lax
from jax.experimental import pallas as pl
from jax.experimental.pallas import tpu as pltpu
from jax.sharding import PartitionSpec as P

STEP = 32
NT = (((1,), (1,)), ((), ()))
NN = (((1,), (0,)), ((), ()))
TN = (((0,), (0,)), ((), ()))


def dot(a, b, dims):
    return lax.dot_general(a, b, dims, preferred_element_type=jnp.float32)


def split3(a):
    one = a.astype(jnp.bfloat16)
    rest = a - one.astype(jnp.float32)
    two = rest.astype(jnp.bfloat16)
    three = (rest - two.astype(jnp.float32)).astype(jnp.bfloat16)
    return one, two, three


def dot6(a, b, dims):
    a1, a2, a3 = a
    b1, b2, b3 = b
    small = dot(a1, b3, dims) + dot(a3, b1, dims) + dot(a2, b2, dims)
    return dot(a1, b1, dims) + ((dot(a1, b2, dims) + dot(a2, b1, dims)) + small)


def wide(parts):
    one, two, three = parts
    return jnp.concatenate([one, one, two, two, one, three], axis=1)


def deep(parts):
    one, two, three = parts
    return jnp.concatenate([one, two, one, two, three, one], axis=0)


def thirds(array):
    count = array.shape[0] // 3
    return array[:count] + (array[count:2 * count] + array[2 * count:])


def apply(rows, parts, dims):
    count = rows.shape[0]
    stack = jnp.concatenate(split3(rows), axis=0)
    high = dot(stack, parts[0], dims)
    low = dot(stack[:2 * count], parts[1], dims)
    return high[:count] + ((high[count:2 * count] + low[:count]) + (high[2 * count:] + low[count:]))


def factor(ref, slab_ref, past_ref):
    systems, width, _ = ref.shape
    teams, height, _ = slab_ref.shape
    team = height // STEP
    groups = STEP // 8
    lane = lax.broadcasted_iota(jnp.int32, (8, 128), 1)
    sub = lax.broadcasted_iota(jnp.int32, (8, 128), 0)
    member = lane // STEP
    place = lane % STEP
    col_in = lax.broadcasted_iota(jnp.int32, (STEP, width), 1)
    row_all = lax.broadcasted_iota(jnp.int32, (width, width), 0)
    col_all = lax.broadcasted_iota(jnp.int32, (width, width), 1)
    row_team = lax.broadcasted_iota(jnp.int32, (height, width), 0)
    col_team = lax.broadcasted_iota(jnp.int32, (height, width), 1)
    row_diag = lax.broadcasted_iota(jnp.int32, (height, 128), 0)
    col_diag = lax.broadcasted_iota(jnp.int32, (height, 128), 1)
    same = row_diag // STEP == col_diag // STEP
    lower = same & (col_diag <= row_diag)

    def spread(row):
        return jnp.broadcast_to(row, (8, 128))

    def padded(parts):
        if height == 128:
            return parts
        filler = jnp.zeros((128 - height, width), jnp.bfloat16)
        return [jnp.concatenate([part, filler], axis=0) for part in parts]

    def pivots(packs, pieces):
        placed = 0
        for first in range(0, STEP, 4):
            top, start = first // 8, first % 8
            tall = range(top, groups)
            own = (place >= first) & (place < first + 4)
            one = jnp.where(place - 8 * top == sub, 1.0, 0.0)
            each = range(len(packs))
            if start == 0:
                inverses = [None for _ in each]
            u = [
                [{g: jnp.take_along_axis(x[g], lane - place + (first + q), axis=1) for g in tall} for q in range(4)]
                for x in packs
            ]
            a = [{(i, j): spread(u[s][j][top][start + i:start + i + 1, :]) for j in range(4) for i in range(j + 1)} for s in each]
            for x in packs:
                for g in tall:
                    x[g] = jnp.where(own, one if g == top else 0.0, x[g])
            y = [[spread(x[top][start + q:start + q + 1, :]) for q in range(4)] for x in packs]
            low = [{} for _ in each]
            inv = [[None] * 4 for _ in each]
            for p in (0, 2):
                n = p + 1
                delta = [a[s][p, p] * a[s][n, n] - a[s][p, n] * a[s][p, n] for s in each]
                for s in each:
                    inv[s][p] = pl.reciprocal(a[s][p, p], approx=True)
                    inv[s][n] = pl.reciprocal(delta[s], approx=True) * a[s][p, p]
                for j in range(n, 4):
                    for s in each:
                        low[s][j, p] = a[s][p, j] * inv[s][p]
                for j in range(n + 1, 4):
                    for s in each:
                        a[s][n, j] = a[s][n, j] - low[s][n, p] * a[s][p, j]
                for j in range(n + 1, 4):
                    for s in each:
                        low[s][j, n] = a[s][n, j] * inv[s][n]
                for i in range(n + 1, 4):
                    for j in range(i, 4):
                        for s in each:
                            a[s][i, j] = (a[s][i, j] - low[s][i, p] * a[s][p, j]) - low[s][i, n] * a[s][n, j]
            for q in range(4):
                at = start + q
                for s in each:
                    for k in range(q):
                        for g in tall:
                            u[s][q][g] = u[s][q][g] - u[s][k][g] * low[s][q, k]
                        y[s][q] = y[s][q] - y[s][k] * low[s][q, k]
                    inverses[s] = inv[s][q] if at == 0 else jnp.where(sub >= at, inv[s][q], inverses[s])
                    for g in tall:
                        m = u[s][q][g] * inv[s][q]
                        if g == top:
                            m = jnp.where(sub > at, m, 0.0)
                        packs[s][g] = packs[s][g] - m * y[s][q]
                while placed * STEP < (first + q + 1) * len(pieces):
                    pieces[placed]()
                    placed += 1
            if start + 4 == 8:
                for s, x in enumerate(packs):
                    x[top] = x[top] * (inverses[s] * lax.rsqrt(inverses[s]))

    for t in range(teams):
        for i in range(team):
            slab_ref[t, i * STEP:(i + 1) * STEP] = ref[t * team + i, 0:STEP]
        past_ref[t] = jnp.zeros(past_ref.shape[1:], past_ref.dtype)

    def block(kb, carry):
        base = pl.multiple_of(kb * STEP, STEP)
        after = pl.multiple_of(jnp.minimum(base + STEP, width - STEP), STEP)
        done = (col_all >= base - STEP) & (col_all < base) & (row_all >= base + STEP)
        pieces = []
        for s in range(systems):
            held = {}

            def prepare(s=s, held=held):
                i = s % team
                p1, p2, p3 = split3(past_ref[s // team, i * STEP:(i + 1) * STEP])
                zero = jnp.zeros_like(p1)
                m1, m2, m3 = (jnp.where(col_in >= base + STEP, p, zero) for p in (p1, p2, p3))
                held["left"] = jnp.concatenate([m1, m1, m2, m2, m1, m3], axis=0)
                held["right"] = jnp.concatenate([p1, p2, p1, p2, p3, p1], axis=0)

            def trail(at, s=s, held=held):
                rows = slice(at, at + 128)
                update = dot(held["left"][:, rows], held["right"], TN)
                ref[s, rows] = jnp.where(done[rows], 0.0, ref[s, rows]) - update

            pieces.append(prepare)
            pieces.extend(functools.partial(trail, at) for at in range(0, width, 128))
        packs = []
        for t in range(teams):
            pack = []
            for g in range(groups):
                x = jnp.where(place - 8 * g == sub, 1.0, 0.0)
                for i in range(team):
                    piece = slab_ref[t, i * STEP + 8 * g:i * STEP + 8 * g + 8, 0:128]
                    if i > 0:
                        piece = pltpu.roll(piece, i * STEP, 1)
                    x = jnp.where(member == i, piece, x)
                pack.append(x)
            packs.append(pack)
        sides = []
        for t in range(teams):
            ident = jnp.where(col_team == row_team % STEP, 1.0, 0.0)
            sides.append(deep(padded(split3(jnp.where(col_team < STEP, ident, slab_ref[t])))))
        pivots(packs, pieces)
        for t in range(teams):
            inner = jnp.concatenate(packs[t], axis=0)
            inner = jnp.where(lower, jnp.concatenate([inner] * team, axis=0), 0.0)
            slab = dot(wide(split3(inner)), sides[t], NN)
            ahead = []
            for i in range(team):
                piece = slab[i * STEP:(i + 1) * STEP, 0:128]
                if i != 1:
                    piece = pltpu.roll(piece, (i - 1) * STEP % 128, 1)
                ahead.append(piece)
            ahead = jnp.where(same, jnp.concatenate(ahead, axis=0), 0.0)
            if height < 128:
                ahead = jnp.concatenate([ahead, jnp.zeros((128 - height, 128), jnp.float32)], axis=0)
            ahead = wide(split3(ahead.T[:height]))
            update = dot(ahead, deep(padded(split3(pltpu.roll(slab, width - STEP, 1)))), NN)
            coming = [pltpu.roll(ref[t * team + i, pl.ds(after, STEP), :], width - after, 1) for i in range(team)]
            slab_ref[t] = jnp.where(col_team >= width - STEP, 0.0, jnp.concatenate(coming, axis=0)) - update
            slab = pltpu.roll(slab, base, 1)
            past_ref[t] = slab
            for i in range(team):
                own_rows = slab[i * STEP:(i + 1) * STEP]
                ref[t * team + i, pl.ds(base, STEP), :] = jnp.where(col_in >= base + STEP, 0.0, own_rows)
        return carry

    lax.fori_loop(0, width // STEP, block, 0)


def factor_scratch(systems, width):
    team = max(n for n in range(1, 128 // STEP + 1) if systems % n == 0)
    return [pltpu.VMEM((systems // team, team * STEP, width), jnp.float32)] * 2


def scaled(matrix):
    factor_of = 1.0 / jnp.max(jnp.max(matrix, axis=1, keepdims=True), axis=0, keepdims=True)
    return matrix * factor_of, jnp.sqrt(factor_of)


def pick_kernel(slot_ref, tiles_ref, *refs):
    out_refs, sems = refs[:-1], refs[-1]
    copies = []
    for e, out_ref in enumerate(out_refs):
        source = tiles_ref.at[jnp.maximum(slot_ref[e], 0), 0:2]
        copies.append(pltpu.make_async_copy(source, out_ref, sems.at[e]))
    for copy in copies:
        copy.start()
    for copy in copies:
        copy.wait()


def own_kernel(counts_ref, tiles_ref, w_ref, z_ref, g_ref, *scratch):
    systems, kslots, width, _ = tiles_ref.shape
    for s in range(systems):
        near = tiles_ref[s, 0:2].reshape(2 * width, width)
        g_ref[s] = dot(near, near, TN)
    for s in range(systems):
        for k in range(2, kslots):
            @pl.when(k < counts_ref[s])
            def _():
                tile = tiles_ref[s, k]
                g_ref[s] += dot(tile, tile, TN)
    roots = []
    for s in range(systems):
        g_ref[s], root = scaled(g_ref[s])
        roots.append(root)
    factor(g_ref, *scratch)
    for s in range(systems):
        w = split3(g_ref[s] * roots[s])
        w_ref[s, 0] = w[0]
        w_ref[s, 1] = w[1]
        own = jnp.concatenate([tiles_ref[s, 1], tiles_ref[s, 0]], axis=0)
        z = split3(dot(w[0], own, NT) + (dot(w[1], own, NT) + dot(w[2], own, NT)))
        for i in range(3):
            z_ref[s, i] = z[i]


def collect(slot_ref, shifts, got_refs, near_ref, sems):
    spare = near_ref.shape[0] - len(shifts)
    copies = []
    for i, (e, got_ref) in enumerate(zip(shifts, got_refs)):
        slot = jnp.where(slot_ref[e - 1] >= 0, slot_ref[e - 1], spare + i)
        copies.append(pltpu.make_async_copy(got_ref, near_ref.at[slot], sems.at[i]))
    for copy in copies:
        copy.start()
    return copies


def schur(near, z):
    near_t = near.T
    v = split3(dot(near_t, z[0], NT) + (dot(near_t, z[1], NT) + dot(near_t, z[2], NT)))
    return v, dot(near_t, near, NN) - dot6(v, v, NT)


def link_kernel(shifts, slot_ref, z_any, *refs):
    got_refs, refs = refs[:len(shifts)], refs[len(shifts):]
    v_ref, t_ref, z_ref, near_ref, z_sems, sems = refs
    systems, _, width, _ = z_ref.shape
    for s in range(systems):
        near_ref[s] = jnp.zeros(near_ref.shape[1:], near_ref.dtype)
    copies = collect(slot_ref, shifts, got_refs, near_ref, sems)
    z_copies = [pltpu.make_async_copy(z_any.at[s], z_ref.at[s], z_sems.at[s]) for s in range(systems)]
    for copy in z_copies:
        copy.start()
    for copy in copies:
        copy.wait()
    for s in range(systems):
        z_copies[s].wait()
        v, t_ref[s] = schur(near_ref[s].reshape(2 * width, width), [z_ref[s, i] for i in range(3)])
        v_ref[s, 0] = v[0]
        v_ref[s, 1] = v[1]


def pair_kernel(lanes, shifts, late, place_ref, slot_ref, x_ref, w_any, z_any, v_any, t_any, *refs):
    got_refs, up_refs, refs = refs[:len(shifts)], refs[len(shifts):len(shifts) + lanes], refs[len(shifts) + lanes:]
    low_ref, near_ref, w_ref, z_ref, zj_ref, v_ref, t_ref, r_ref, first_ref, near_sems, sems, *scratch = refs
    _, _, width, _ = z_ref.shape
    systems = first_ref.shape[0]
    count = x_ref.shape[0] // lanes
    near_copies = collect(slot_ref, shifts, got_refs, near_ref, near_sems)
    late_slots = [slot_ref[e - 1] for e in late]
    copies = [
        pltpu.make_async_copy(z_any.at[jnp.maximum(slot, 0)], z_ref.at[i], sems.at[i]) for i, slot in enumerate(late_slots)
    ] + [
        pltpu.make_async_copy(t_any, t_ref.at[0:systems], sems.at[2]),
        pltpu.make_async_copy(v_any, v_ref.at[0:systems], sems.at[3]),
        pltpu.make_async_copy(z_any.at[:, 0:2, :, width:], zj_ref, sems.at[4]),
    ]
    w_copy = pltpu.make_async_copy(w_any, w_ref, sems.at[5])
    for copy in copies + [w_copy]:
        copy.start()
    low_ref[...] = jnp.zeros(low_ref.shape, low_ref.dtype)
    for copy in near_copies + copies[:-1]:
        copy.wait()
    for i, slot in enumerate(late_slots):
        at = jnp.where(slot >= 0, slot, systems + i)
        near = near_ref[jnp.maximum(slot, 0)].reshape(2 * width, width)
        v, t_ref[at] = schur(near, [z_ref[i, p] for p in range(3)])
        v_ref[at, 0] = v[0]
        v_ref[at, 1] = v[1]
    copies[-1].wait()
    roots = []
    for s in range(systems):
        x = x_ref[:, s * width:(s + 1) * width]
        first_ref[s] = dot(x, zj_ref[s, 0], NT) + dot(x, zj_ref[s, 1], NT)
        r_ref[s] = dot(x, near_ref[s, 1], NN)
    for s in range(systems):
        r_ref[s] = r_ref[s] - apply(first_ref[s], (v_ref[s, 0], v_ref[s, 1]), NT)
        t_ref[s], root = scaled(t_ref[s])
        roots.append(root)
    factor(t_ref.at[0:systems], *scratch)
    w_copy.wait()
    parts = [split3(t_ref[s] * roots[s])[:2] for s in range(systems)]
    half = [apply(r_ref[s], parts[s], NT) for s in range(systems)]
    last = [apply(half[s], parts[s], NN) for s in range(systems)]
    mid = [first_ref[s] - apply(last[s], (v_ref[s, 0], v_ref[s, 1]), NN) for s in range(systems)]
    for s in range(systems):
        up = apply(mid[s], (w_ref[s, 0], w_ref[s, 1]), NN)
        for e in range(lanes):
            up_refs[e][s] = up[e * count:(e + 1) * count]
            owner = lax.rem(place_ref[systems] + e, lanes)
            low_ref[place_ref[s] * lanes + owner] = last[s][e * count:(e + 1) * count].astype(low_ref.dtype)


def place_kernel(lanes, place_ref, low_ref, *refs):
    up_refs, out_ref = refs[:lanes], refs[lanes]
    systems, _, width = up_refs[0].shape
    for e in range(lanes):
        owner = lax.rem(place_ref[systems * lanes] + lanes - e, lanes)
        for s in range(systems):
            at = owner * systems + s
            total = up_refs[e][s] + low_ref[place_ref[at] * lanes + owner].astype(jnp.float32)
            out_ref[:, pl.ds(pl.multiple_of(at * width, width), width)] = total.astype(out_ref.dtype)


def on_device(tiles, pattern, counts, inputs):
    shards = lax.axis_size("panel")
    lanes = lax.axis_size("rhs")
    systems, kslots, width, _ = tiles.shape
    nrhs_dev = inputs.shape[0]
    own_width = systems * width
    my_panel = lax.axis_index("panel")
    my_lane = lax.axis_index("rhs")
    per_panel = systems * lanes
    own_cnt = lax.dynamic_slice_in_dim(counts, my_panel * per_panel + my_lane * systems, systems, 0)
    panel_mates = lax.dynamic_slice(pattern, (my_panel * per_panel, 1), (per_panel, 1))[:, 0] // per_panel
    mate_panel = lax.dynamic_slice_in_dim(panel_mates, my_lane * systems, systems, 0)
    hops = jnp.arange(1, shards, dtype=jnp.int32)

    def slots(panels):
        hit = mate_panel[None, :] == panels[:, None]
        return jnp.max(jnp.where(hit, jnp.arange(systems, dtype=jnp.int32)[None, :], -1), axis=1)

    lane_word = my_lane[None].astype(jnp.int32)

    def shift(value, axis, by):
        size = lax.axis_size(axis)
        return lax.ppermute(value, axis, [(i, (i + by) % size) for i in range(size)])

    vmem = pl.BlockSpec(memory_space=pltpu.VMEM)
    smem = pl.BlockSpec(memory_space=pltpu.SMEM)
    anywhere = pl.BlockSpec(memory_space=pl.ANY)
    params = pltpu.CompilerParams(vmem_limit_bytes=48 * 1024 * 1024)
    pairs = shards - 1
    every = tuple(range(1, shards))
    late = (1, shards - 1)
    early = tuple(e for e in every if e not in late)
    pieces = pl.pallas_call(
        pick_kernel,
        out_shape=[jax.ShapeDtypeStruct((2, width, width), jnp.bfloat16)] * pairs,
        in_specs=[smem, anywhere],
        out_specs=[vmem] * pairs,
        scratch_shapes=[pltpu.SemaphoreType.DMA((pairs,))],
        compiler_params=params,
    )(slots((my_panel + hops) % shards), tiles)
    received = {e: shift(pieces[e - 1], "panel", e) for e in early}

    w, z = pl.pallas_call(
        own_kernel,
        out_shape=(
            jax.ShapeDtypeStruct((systems, 2, width, width), jnp.bfloat16),
            jax.ShapeDtypeStruct((systems, 3, width, 2 * width), jnp.bfloat16),
        ),
        in_specs=[smem, vmem],
        out_specs=(vmem, vmem),
        scratch_shapes=[pltpu.VMEM((systems, width, width), jnp.float32)] + factor_scratch(systems, width),
        compiler_params=params,
        cost_estimate=pl.CostEstimate(flops=30 * 10**9, bytes_accessed=8 * 10**6, transcendentals=0),
    )(own_cnt, tiles)

    inputs, w = lax.optimization_barrier((inputs, w))
    x = lax.all_to_all(inputs, "rhs", split_axis=1, concat_axis=0, tiled=True)
    x = lax.dynamic_slice_in_dim(jnp.concatenate([x, x], axis=0), my_lane * nrhs_dev, lanes * nrhs_dev, 0)

    come = [received[e] for e in early]
    held, z, come = lax.optimization_barrier(([pieces[e - 1] for e in late], z, come))
    received.update(zip(early, come))
    received.update({e: shift(piece, "panel", e) for e, piece in zip(late, held)})
    from_slot = slots((my_panel - hops) % shards)
    v, t = pl.pallas_call(
        functools.partial(link_kernel, early),
        out_shape=(
            jax.ShapeDtypeStruct((systems, 2, width, width), jnp.bfloat16),
            jax.ShapeDtypeStruct((systems, width, width), jnp.float32),
        ),
        in_specs=[smem] + [anywhere] * (1 + len(early)),
        out_specs=(vmem, vmem),
        scratch_shapes=[
            pltpu.VMEM((systems, 3, width, 2 * width), jnp.bfloat16),
            pltpu.VMEM((systems + len(early), 2, width, width), jnp.bfloat16),
            pltpu.SemaphoreType.DMA((systems,)),
            pltpu.SemaphoreType.DMA((len(early),)),
        ],
        compiler_params=params,
        cost_estimate=pl.CostEstimate(flops=12 * 10**9, bytes_accessed=8 * 10**6, transcendentals=0),
    )(from_slot, z, *[received[e] for e in early])

    nrhs = lanes * nrhs_dev
    piece = jax.ShapeDtypeStruct((systems, nrhs_dev, width), jnp.float32)
    *up, low = pl.pallas_call(
        functools.partial(pair_kernel, lanes, every, late),
        out_shape=[piece] * lanes + [jax.ShapeDtypeStruct((shards * lanes, nrhs_dev, width), jnp.bfloat16)],
        in_specs=[smem, smem, vmem] + [anywhere] * (4 + pairs),
        out_specs=[vmem] * (lanes + 1),
        scratch_shapes=[
            pltpu.VMEM((systems + pairs, 2, width, width), jnp.bfloat16),
            pltpu.VMEM((systems, 2, width, width), jnp.bfloat16),
            pltpu.VMEM((len(late), 3, width, 2 * width), jnp.bfloat16),
            pltpu.VMEM((systems, 2, width, width), jnp.bfloat16),
            pltpu.VMEM((systems + len(late), 2, width, width), jnp.bfloat16),
            pltpu.VMEM((systems + len(late), width, width), jnp.float32),
            pltpu.VMEM((systems, nrhs, width), jnp.float32),
            pltpu.VMEM((systems, nrhs, width), jnp.float32),
            pltpu.SemaphoreType.DMA((pairs,)),
            pltpu.SemaphoreType.DMA((6,)),
        ] + factor_scratch(systems, width),
        compiler_params=params,
    )(
        jnp.concatenate([mate_panel, lane_word]), from_slot, x, w, z, v, t,
        *[received[e] for e in every],
    )
    low = lax.all_to_all(low, ("panel", "rhs"), split_axis=0, concat_axis=0, tiled=True)
    up = [up[0]] + [shift(up[e], "rhs", e) for e in range(1, lanes)]
    return pl.pallas_call(
        functools.partial(place_kernel, lanes),
        out_shape=jax.ShapeDtypeStruct((nrhs_dev, per_panel * width), jnp.bfloat16),
        in_specs=[smem] + [vmem] * (lanes + 1),
        out_specs=vmem,
    )(jnp.concatenate([panel_mates, lane_word]), low, *up)


def solution(mesh):
    return jax.shard_map(
        on_device,
        mesh=mesh,
        in_specs=(P(("panel", "rhs"), None, None, None), P(), P(), P("rhs", "panel")),
        out_specs=P("rhs", "panel"),
        check_vma=False,
    )
```

```python
import functools
import jax
import jax.numpy as jnp
from jax import lax
from jax.experimental import pallas as pl
from jax.experimental.pallas import tpu as pltpu
from jax.sharding import PartitionSpec as P

STEP = 32
NT = (((1,), (1,)), ((), ()))
NN = (((1,), (0,)), ((), ()))
TN = (((0,), (0,)), ((), ()))


def dot(a, b, dims):
    return lax.dot_general(a, b, dims, preferred_element_type=jnp.float32)


def split3(a):
    one = a.astype(jnp.bfloat16)
    rest = a - one.astype(jnp.float32)
    two = rest.astype(jnp.bfloat16)
    three = (rest - two.astype(jnp.float32)).astype(jnp.bfloat16)
    return one, two, three


def dot6(a, b, dims):
    a1, a2, a3 = a
    b1, b2, b3 = b
    small = dot(a1, b3, dims) + dot(a3, b1, dims) + dot(a2, b2, dims)
    return dot(a1, b1, dims) + ((dot(a1, b2, dims) + dot(a2, b1, dims)) + small)


def wide(parts):
    one, two, three = parts
    return jnp.concatenate([one, one, two, two, one, three], axis=1)


def deep(parts):
    one, two, three = parts
    return jnp.concatenate([one, two, one, two, three, one], axis=0)


def thirds(array):
    count = array.shape[0] // 3
    return array[:count] + (array[count:2 * count] + array[2 * count:])


def apply(rows, parts, dims):
    count = rows.shape[0]
    stack = jnp.concatenate(split3(rows), axis=0)
    high = dot(stack, parts[0], dims)
    low = dot(stack[:2 * count], parts[1], dims)
    return high[:count] + ((high[count:2 * count] + low[:count]) + (high[2 * count:] + low[count:]))


def factor(ref, slab_ref, past_ref):
    systems, width, _ = ref.shape
    teams, height, _ = slab_ref.shape
    team = height // STEP
    groups = STEP // 8
    lane = lax.broadcasted_iota(jnp.int32, (8, 128), 1)
    sub = lax.broadcasted_iota(jnp.int32, (8, 128), 0)
    member = lane // STEP
    place = lane % STEP
    col_in = lax.broadcasted_iota(jnp.int32, (STEP, width), 1)
    row_all = lax.broadcasted_iota(jnp.int32, (width, width), 0)
    col_all = lax.broadcasted_iota(jnp.int32, (width, width), 1)
    row_team = lax.broadcasted_iota(jnp.int32, (height, width), 0)
    col_team = lax.broadcasted_iota(jnp.int32, (height, width), 1)
    row_diag = lax.broadcasted_iota(jnp.int32, (height, 128), 0)
    col_diag = lax.broadcasted_iota(jnp.int32, (height, 128), 1)
    same = row_diag // STEP == col_diag // STEP
    lower = same & (col_diag <= row_diag)

    def spread(row):
        return jnp.broadcast_to(row, (8, 128))

    def padded(parts):
        if height == 128:
            return parts
        filler = jnp.zeros((128 - height, width), jnp.bfloat16)
        return [jnp.concatenate([part, filler], axis=0) for part in parts]

    def pivots(packs, pieces):
        placed = 0
        for first in range(0, STEP, 4):
            top, start = first // 8, first % 8
            tall = range(top, groups)
            own = (place >= first) & (place < first + 4)
            one = jnp.where(place - 8 * top == sub, 1.0, 0.0)
            each = range(len(packs))
            if start == 0:
                inverses = [None for _ in each]
            u = [
                [{g: jnp.take_along_axis(x[g], lane - place + (first + q), axis=1) for g in tall} for q in range(4)]
                for x in packs
            ]
            a = [{(i, j): spread(u[s][j][top][start + i:start + i + 1, :]) for j in range(4) for i in range(j + 1)} for s in each]
            for x in packs:
                for g in tall:
                    x[g] = jnp.where(own, one if g == top else 0.0, x[g])
            y = [[spread(x[top][start + q:start + q + 1, :]) for q in range(4)] for x in packs]
            low = [{} for _ in each]
            inv = [[None] * 4 for _ in each]
            for p in (0, 2):
                n = p + 1
                delta = [a[s][p, p] * a[s][n, n] - a[s][p, n] * a[s][p, n] for s in each]
                for s in each:
                    inv[s][p] = pl.reciprocal(a[s][p, p], approx=True)
                    inv[s][n] = pl.reciprocal(delta[s], approx=True) * a[s][p, p]
                for j in range(n, 4):
                    for s in each:
                        low[s][j, p] = a[s][p, j] * inv[s][p]
                for j in range(n + 1, 4):
                    for s in each:
                        a[s][n, j] = a[s][n, j] - low[s][n, p] * a[s][p, j]
                for j in range(n + 1, 4):
                    for s in each:
                        low[s][j, n] = a[s][n, j] * inv[s][n]
                for i in range(n + 1, 4):
                    for j in range(i, 4):
                        for s in each:
                            a[s][i, j] = (a[s][i, j] - low[s][i, p] * a[s][p, j]) - low[s][i, n] * a[s][n, j]
            for q in range(4):
                at = start + q
                for s in each:
                    for k in range(q):
                        for g in tall:
                            u[s][q][g] = u[s][q][g] - u[s][k][g] * low[s][q, k]
                        y[s][q] = y[s][q] - y[s][k] * low[s][q, k]
                    inverses[s] = inv[s][q] if at == 0 else jnp.where(sub >= at, inv[s][q], inverses[s])
                    for g in tall:
                        m = u[s][q][g] * inv[s][q]
                        if g == top:
                            m = jnp.where(sub > at, m, 0.0)
                        packs[s][g] = packs[s][g] - m * y[s][q]
                while placed * STEP < (first + q + 1) * len(pieces):
                    pieces[placed]()
                    placed += 1
            if start + 4 == 8:
                for s, x in enumerate(packs):
                    x[top] = x[top] * (inverses[s] * lax.rsqrt(inverses[s]))

    for t in range(teams):
        for i in range(team):
            slab_ref[t, i * STEP:(i + 1) * STEP] = ref[t * team + i, 0:STEP]
        past_ref[t] = jnp.zeros(past_ref.shape[1:], past_ref.dtype)

    def block(kb, carry):
        base = pl.multiple_of(kb * STEP, STEP)
        after = pl.multiple_of(jnp.minimum(base + STEP, width - STEP), STEP)
        done = (col_all >= base - STEP) & (col_all < base) & (row_all >= base + STEP)
        pieces = []
        for s in range(systems):
            held = {}

            def prepare(s=s, held=held):
                i = s % team
                p1, p2, p3 = split3(past_ref[s // team, i * STEP:(i + 1) * STEP])
                zero = jnp.zeros_like(p1)
                m1, m2, m3 = (jnp.where(col_in >= base + STEP, p, zero) for p in (p1, p2, p3))
                held["left"] = jnp.concatenate([m1, m1, m2, m2, m1, m3], axis=0)
                held["right"] = jnp.concatenate([p1, p2, p1, p2, p3, p1], axis=0)

            def trail(at, s=s, held=held):
                rows = slice(at, at + 128)
                update = dot(held["left"][:, rows], held["right"], TN)
                ref[s, rows] = jnp.where(done[rows], 0.0, ref[s, rows]) - update

            pieces.append(prepare)
            pieces.extend(functools.partial(trail, at) for at in range(0, width, 128))
        packs = []
        for t in range(teams):
            pack = []
            for g in range(groups):
                x = jnp.where(place - 8 * g == sub, 1.0, 0.0)
                for i in range(team):
                    piece = slab_ref[t, i * STEP + 8 * g:i * STEP + 8 * g + 8, 0:128]
                    if i > 0:
                        piece = pltpu.roll(piece, i * STEP, 1)
                    x = jnp.where(member == i, piece, x)
                pack.append(x)
            packs.append(pack)
        sides = []
        for t in range(teams):
            ident = jnp.where(col_team == row_team % STEP, 1.0, 0.0)
            sides.append(deep(padded(split3(jnp.where(col_team < STEP, ident, slab_ref[t])))))
        pivots(packs, pieces)
        for t in range(teams):
            inner = jnp.concatenate(packs[t], axis=0)
            inner = jnp.where(lower, jnp.concatenate([inner] * team, axis=0), 0.0)
            slab = dot(wide(split3(inner)), sides[t], NN)
            ahead = []
            for i in range(team):
                piece = slab[i * STEP:(i + 1) * STEP, 0:128]
                if i != 1:
                    piece = pltpu.roll(piece, (i - 1) * STEP % 128, 1)
                ahead.append(piece)
            ahead = jnp.where(same, jnp.concatenate(ahead, axis=0), 0.0)
            if height < 128:
                ahead = jnp.concatenate([ahead, jnp.zeros((128 - height, 128), jnp.float32)], axis=0)
            ahead = wide(split3(ahead.T[:height]))
            update = dot(ahead, deep(padded(split3(pltpu.roll(slab, width - STEP, 1)))), NN)
            coming = [pltpu.roll(ref[t * team + i, pl.ds(after, STEP), :], width - after, 1) for i in range(team)]
            slab_ref[t] = jnp.where(col_team >= width - STEP, 0.0, jnp.concatenate(coming, axis=0)) - update
            slab = pltpu.roll(slab, base, 1)
            past_ref[t] = slab
            for i in range(team):
                own_rows = slab[i * STEP:(i + 1) * STEP]
                ref[t * team + i, pl.ds(base, STEP), :] = jnp.where(col_in >= base + STEP, 0.0, own_rows)
        return carry

    lax.fori_loop(0, width // STEP, block, 0)


def factor_scratch(systems, width):
    team = max(n for n in range(1, 128 // STEP + 1) if systems % n == 0)
    return [pltpu.VMEM((systems // team, team * STEP, width), jnp.float32)] * 2


def scaled(matrix):
    factor_of = 1.0 / jnp.max(jnp.max(matrix, axis=1, keepdims=True), axis=0, keepdims=True)
    return matrix * factor_of, jnp.sqrt(factor_of)


def pick_kernel(slot_ref, tiles_ref, *refs):
    out_refs, sems = refs[:-1], refs[-1]
    copies = []
    for e, out_ref in enumerate(out_refs):
        source = tiles_ref.at[jnp.maximum(slot_ref[e], 0), 0:2]
        copies.append(pltpu.make_async_copy(source, out_ref, sems.at[e]))
    for copy in copies:
        copy.start()
    for copy in copies:
        copy.wait()


def own_kernel(counts_ref, tiles_ref, x_ref, w_ref, z_ref, first_ref, rhs_ref, g_ref, *scratch):
    systems, kslots, width, _ = tiles_ref.shape
    for s in range(systems):
        near = tiles_ref[s, 0:2].reshape(2 * width, width)
        g_ref[s] = dot(near, near, TN)
    for s in range(systems):
        for k in range(2, kslots):
            @pl.when(k < counts_ref[s])
            def _():
                tile = tiles_ref[s, k]
                g_ref[s] += dot(tile, tile, TN)
    roots = []
    for s in range(systems):
        g_ref[s], root = scaled(g_ref[s])
        roots.append(root)
    factor(g_ref, *scratch)
    for s in range(systems):
        w = split3(g_ref[s] * roots[s])
        w_ref[s, 0] = w[0]
        w_ref[s, 1] = w[1]
        own = jnp.concatenate([tiles_ref[s, 1], tiles_ref[s, 0]], axis=0)
        z = split3(dot(w[0], own, NT) + (dot(w[1], own, NT) + dot(w[2], own, NT)))
        for i in range(3):
            z_ref[s, i] = z[i]
        x = x_ref[:, s * width:(s + 1) * width]
        first = dot(x, z[0][:, width:], NT) + (dot(x, z[1][:, width:], NT) + dot(x, z[2][:, width:], NT))
        first_ref[s] = first
        x = x.astype(jnp.float32)
        rhs_ref[s] = jnp.concatenate([jnp.zeros_like(x), x], axis=1) - apply(first, z, NN)


def collect(slot_ref, shifts, got_refs, near_ref, sems):
    spare = near_ref.shape[0] - len(shifts)
    copies = []
    for i, (e, got_ref) in enumerate(zip(shifts, got_refs)):
        slot = jnp.where(slot_ref[e - 1] >= 0, slot_ref[e - 1], spare + i)
        copies.append(pltpu.make_async_copy(got_ref, near_ref.at[slot], sems.at[i]))
    for copy in copies:
        copy.start()
    return copies


def schur(near, z):
    near_t = near.T
    v = split3(dot(near_t, z[0], NT) + (dot(near_t, z[1], NT) + dot(near_t, z[2], NT)))
    return v, dot(near_t, near, NN) - dot6(v, v, NT)


def link_kernel(shifts, slot_ref, z_any, *refs):
    got_refs, refs = refs[:len(shifts)], refs[len(shifts):]
    v_ref, t_ref, z_ref, near_ref, z_sems, sems = refs
    systems, _, width, _ = z_ref.shape
    for s in range(systems):
        near_ref[s] = jnp.zeros(near_ref.shape[1:], near_ref.dtype)
    copies = collect(slot_ref, shifts, got_refs, near_ref, sems)
    z_copies = [pltpu.make_async_copy(z_any.at[s], z_ref.at[s], z_sems.at[s]) for s in range(systems)]
    for copy in z_copies:
        copy.start()
    for copy in copies:
        copy.wait()
    for s in range(systems):
        z_copies[s].wait()
        v, t_ref[s] = schur(near_ref[s].reshape(2 * width, width), [z_ref[s, i] for i in range(3)])
        v_ref[s, 0] = v[0]
        v_ref[s, 1] = v[1]


def pair_kernel(lanes, shifts, late, place_ref, slot_ref, first_ref, rhs_ref, w_any, z_any, v_any, t_any, *refs):
    got_refs, up_refs, refs = refs[:len(shifts)], refs[len(shifts):len(shifts) + lanes], refs[len(shifts) + lanes:]
    low_ref, near_ref, w_ref, z_ref, v_ref, t_ref, r_ref, near_sems, sems, *scratch = refs
    systems, nrhs, width = first_ref.shape
    count = nrhs // lanes
    near_copies = collect(slot_ref, shifts, got_refs, near_ref, near_sems)
    late_slots = [slot_ref[e - 1] for e in late]
    copies = [
        pltpu.make_async_copy(z_any.at[jnp.maximum(slot, 0)], z_ref.at[i], sems.at[i]) for i, slot in enumerate(late_slots)
    ] + [
        pltpu.make_async_copy(t_any, t_ref.at[0:systems], sems.at[2]),
        pltpu.make_async_copy(v_any, v_ref.at[0:systems], sems.at[3]),
    ]
    w_copy = pltpu.make_async_copy(w_any, w_ref, sems.at[4])
    for copy in copies + [w_copy]:
        copy.start()
    low_ref[...] = jnp.zeros(low_ref.shape, low_ref.dtype)
    for copy in near_copies + copies:
        copy.wait()
    for i, slot in enumerate(late_slots):
        at = jnp.where(slot >= 0, slot, systems + i)
        near = near_ref[jnp.maximum(slot, 0)].reshape(2 * width, width)
        v, t_ref[at] = schur(near, [z_ref[i, p] for p in range(3)])
        v_ref[at, 0] = v[0]
        v_ref[at, 1] = v[1]
    roots = []
    for s in range(systems):
        near = near_ref[s].reshape(2 * width, width)
        r_ref[s] = thirds(dot(jnp.concatenate(split3(rhs_ref[s]), axis=0), near, NN))
        t_ref[s], root = scaled(t_ref[s])
        roots.append(root)
    factor(t_ref.at[0:systems], *scratch)
    w_copy.wait()
    parts = [split3(t_ref[s] * roots[s])[:2] for s in range(systems)]
    half = [apply(r_ref[s], parts[s], NT) for s in range(systems)]
    last = [apply(half[s], parts[s], NN) for s in range(systems)]
    mid = [first_ref[s] - apply(last[s], (v_ref[s, 0], v_ref[s, 1]), NN) for s in range(systems)]
    for s in range(systems):
        up = apply(mid[s], (w_ref[s, 0], w_ref[s, 1]), NN)
        for e in range(lanes):
            up_refs[e][s] = up[e * count:(e + 1) * count]
            owner = lax.rem(place_ref[systems] + e, lanes)
            low_ref[place_ref[s] * lanes + owner] = last[s][e * count:(e + 1) * count].astype(low_ref.dtype)


def place_kernel(lanes, place_ref, low_ref, *refs):
    up_refs, out_ref = refs[:lanes], refs[lanes]
    systems, _, width = up_refs[0].shape
    for e in range(lanes):
        owner = lax.rem(place_ref[systems * lanes] + lanes - e, lanes)
        for s in range(systems):
            at = owner * systems + s
            total = up_refs[e][s] + low_ref[place_ref[at] * lanes + owner].astype(jnp.float32)
            out_ref[:, pl.ds(pl.multiple_of(at * width, width), width)] = total.astype(out_ref.dtype)


def on_device(tiles, pattern, counts, inputs):
    shards = lax.axis_size("panel")
    lanes = lax.axis_size("rhs")
    systems, kslots, width, _ = tiles.shape
    nrhs_dev = inputs.shape[0]
    own_width = systems * width
    my_panel = lax.axis_index("panel")
    my_lane = lax.axis_index("rhs")
    per_panel = systems * lanes
    own_cnt = lax.dynamic_slice_in_dim(counts, my_panel * per_panel + my_lane * systems, systems, 0)
    panel_mates = lax.dynamic_slice(pattern, (my_panel * per_panel, 1), (per_panel, 1))[:, 0] // per_panel
    mate_panel = lax.dynamic_slice_in_dim(panel_mates, my_lane * systems, systems, 0)
    hops = jnp.arange(1, shards, dtype=jnp.int32)

    def slots(panels):
        hit = mate_panel[None, :] == panels[:, None]
        return jnp.max(jnp.where(hit, jnp.arange(systems, dtype=jnp.int32)[None, :], -1), axis=1)

    lane_word = my_lane[None].astype(jnp.int32)

    def shift(value, axis, by):
        size = lax.axis_size(axis)
        return lax.ppermute(value, axis, [(i, (i + by) % size) for i in range(size)])

    vmem = pl.BlockSpec(memory_space=pltpu.VMEM)
    smem = pl.BlockSpec(memory_space=pltpu.SMEM)
    anywhere = pl.BlockSpec(memory_space=pl.ANY)
    params = pltpu.CompilerParams(vmem_limit_bytes=48 * 1024 * 1024)
    pairs = shards - 1
    every = tuple(range(1, shards))
    late = (1, shards - 1)
    early = tuple(sorted((e for e in every if e not in late), key=lambda e: abs(2 * e - shards)))
    most = pltpu.CompilerParams(vmem_limit_bytes=60 * 1024 * 1024)
    pieces = pl.pallas_call(
        pick_kernel,
        out_shape=[jax.ShapeDtypeStruct((2, width, width), jnp.bfloat16)] * pairs,
        in_specs=[smem, anywhere],
        out_specs=[vmem] * pairs,
        scratch_shapes=[pltpu.SemaphoreType.DMA((pairs,))],
        compiler_params=most,
    )(slots((my_panel + hops) % shards), tiles)
    received = {e: shift(pieces[e - 1], "panel", e) for e in early}

    inputs, pieces = lax.optimization_barrier((inputs, pieces))
    x = lax.all_to_all(inputs, "rhs", split_axis=1, concat_axis=0, tiled=True)
    x = lax.dynamic_slice_in_dim(jnp.concatenate([x, x], axis=0), my_lane * nrhs_dev, lanes * nrhs_dev, 0)
    nrhs = lanes * nrhs_dev

    w, z, first, rhs = pl.pallas_call(
        own_kernel,
        out_shape=(
            jax.ShapeDtypeStruct((systems, 2, width, width), jnp.bfloat16),
            jax.ShapeDtypeStruct((systems, 3, width, 2 * width), jnp.bfloat16),
            jax.ShapeDtypeStruct((systems, nrhs, width), jnp.float32),
            jax.ShapeDtypeStruct((systems, nrhs, 2 * width), jnp.float32),
        ),
        in_specs=[smem, vmem, vmem],
        out_specs=(vmem,) * 4,
        scratch_shapes=[pltpu.VMEM((systems, width, width), jnp.float32)] + factor_scratch(systems, width),
        compiler_params=most,
        cost_estimate=pl.CostEstimate(flops=30 * 10**9, bytes_accessed=8 * 10**6, transcendentals=0),
    )(own_cnt, tiles, x)

    come = [received[e] for e in early]
    held, z, come = lax.optimization_barrier(([pieces[e - 1] for e in late], z, come))
    received.update(zip(early, come))
    received.update({e: shift(piece, "panel", e) for e, piece in zip(late, held)})
    from_slot = slots((my_panel - hops) % shards)
    v, t = pl.pallas_call(
        functools.partial(link_kernel, early),
        out_shape=(
            jax.ShapeDtypeStruct((systems, 2, width, width), jnp.bfloat16),
            jax.ShapeDtypeStruct((systems, width, width), jnp.float32),
        ),
        in_specs=[smem] + [anywhere] * (1 + len(early)),
        out_specs=(vmem, vmem),
        scratch_shapes=[
            pltpu.VMEM((systems, 3, width, 2 * width), jnp.bfloat16),
            pltpu.VMEM((systems + len(early), 2, width, width), jnp.bfloat16),
            pltpu.SemaphoreType.DMA((systems,)),
            pltpu.SemaphoreType.DMA((len(early),)),
        ],
        compiler_params=most,
        cost_estimate=pl.CostEstimate(flops=12 * 10**9, bytes_accessed=8 * 10**6, transcendentals=0),
    )(from_slot, z, *[received[e] for e in early])

    piece = jax.ShapeDtypeStruct((systems, nrhs_dev, width), jnp.float32)
    *up, low = pl.pallas_call(
        functools.partial(pair_kernel, lanes, every, late),
        out_shape=[piece] * lanes + [jax.ShapeDtypeStruct((shards * lanes, nrhs_dev, width), jnp.bfloat16)],
        in_specs=[smem, smem, vmem, vmem] + [anywhere] * (4 + pairs),
        out_specs=[vmem] * (lanes + 1),
        scratch_shapes=[
            pltpu.VMEM((systems + pairs, 2, width, width), jnp.bfloat16),
            pltpu.VMEM((systems, 2, width, width), jnp.bfloat16),
            pltpu.VMEM((len(late), 3, width, 2 * width), jnp.bfloat16),
            pltpu.VMEM((systems + len(late), 2, width, width), jnp.bfloat16),
            pltpu.VMEM((systems + len(late), width, width), jnp.float32),
            pltpu.VMEM((systems, nrhs, width), jnp.float32),
            pltpu.SemaphoreType.DMA((pairs,)),
            pltpu.SemaphoreType.DMA((5,)),
        ] + factor_scratch(systems, width),
        compiler_params=params,
    )(
        jnp.concatenate([mate_panel, lane_word]), from_slot, first, rhs, w, z, v, t,
        *[received[e] for e in every],
    )
    low = lax.all_to_all(low, ("panel", "rhs"), split_axis=0, concat_axis=0, tiled=True)
    up = [up[0]] + [shift(up[e], "rhs", e) for e in range(1, lanes)]
    return pl.pallas_call(
        functools.partial(place_kernel, lanes),
        out_shape=jax.ShapeDtypeStruct((nrhs_dev, per_panel * width), jnp.bfloat16),
        in_specs=[smem] + [vmem] * (lanes + 1),
        out_specs=vmem,
    )(jnp.concatenate([panel_mates, lane_word]), low, *up)


def solution(mesh):
    return jax.shard_map(
        on_device,
        mesh=mesh,
        in_specs=(P(("panel", "rhs"), None, None, None), P(), P(), P("rhs", "panel")),
        out_specs=P("rhs", "panel"),
        check_vma=False,
    )
```

```python
import functools
import jax
import jax.numpy as jnp
from jax import lax
from jax.experimental import pallas as pl
from jax.experimental.pallas import tpu as pltpu
from jax.sharding import PartitionSpec as P

STEP = 32
NT = (((1,), (1,)), ((), ()))
NN = (((1,), (0,)), ((), ()))
TN = (((0,), (0,)), ((), ()))


def dot(a, b, dims):
    return lax.dot_general(a, b, dims, preferred_element_type=jnp.float32)


def split3(a):
    one = a.astype(jnp.bfloat16)
    rest = a - one.astype(jnp.float32)
    two = rest.astype(jnp.bfloat16)
    three = (rest - two.astype(jnp.float32)).astype(jnp.bfloat16)
    return one, two, three


def dot6(a, b, dims):
    a1, a2, a3 = a
    b1, b2, b3 = b
    small = dot(a1, b3, dims) + dot(a3, b1, dims) + dot(a2, b2, dims)
    return dot(a1, b1, dims) + ((dot(a1, b2, dims) + dot(a2, b1, dims)) + small)


def dot3(a, b, dims):
    return dot(a[0], b[0], dims) + (dot(a[0], b[1], dims) + dot(a[1], b[0], dims))


def wide(parts):
    one, two, three = parts
    return jnp.concatenate([one, one, two, two, one, three], axis=1)


def deep(parts):
    one, two, three = parts
    return jnp.concatenate([one, two, one, two, three, one], axis=0)


def thirds(array):
    count = array.shape[0] // 3
    return array[:count] + (array[count:2 * count] + array[2 * count:])


def apply(rows, parts, dims):
    count = rows.shape[0]
    stack = jnp.concatenate(split3(rows), axis=0)
    high = dot(stack, parts[0], dims)
    low = dot(stack[:2 * count], parts[1], dims)
    return high[:count] + ((high[count:2 * count] + low[:count]) + (high[2 * count:] + low[count:]))


def factor(ref, slab_ref, past_ref):
    systems, width, _ = ref.shape
    teams, height, _ = slab_ref.shape
    team = height // STEP
    groups = STEP // 8
    lane = lax.broadcasted_iota(jnp.int32, (8, 128), 1)
    sub = lax.broadcasted_iota(jnp.int32, (8, 128), 0)
    member = lane // STEP
    place = lane % STEP
    col_in = lax.broadcasted_iota(jnp.int32, (STEP, width), 1)
    row_all = lax.broadcasted_iota(jnp.int32, (width, width), 0)
    col_all = lax.broadcasted_iota(jnp.int32, (width, width), 1)
    row_team = lax.broadcasted_iota(jnp.int32, (height, width), 0)
    col_team = lax.broadcasted_iota(jnp.int32, (height, width), 1)
    row_diag = lax.broadcasted_iota(jnp.int32, (height, 128), 0)
    col_diag = lax.broadcasted_iota(jnp.int32, (height, 128), 1)
    same = row_diag // STEP == col_diag // STEP
    lower = same & (col_diag <= row_diag)

    def spread(row):
        return jnp.broadcast_to(row, (8, 128))

    def padded(parts):
        if height == 128:
            return parts
        filler = jnp.zeros((128 - height, width), jnp.bfloat16)
        return [jnp.concatenate([part, filler], axis=0) for part in parts]

    def pivots(packs, pieces):
        placed = 0
        for first in range(0, STEP, 4):
            top, start = first // 8, first % 8
            tall = range(top, groups)
            own = (place >= first) & (place < first + 4)
            one = jnp.where(place - 8 * top == sub, 1.0, 0.0)
            each = range(len(packs))
            if start == 0:
                inverses = [None for _ in each]
            u = [
                [{g: jnp.take_along_axis(x[g], lane - place + (first + q), axis=1) for g in tall} for q in range(4)]
                for x in packs
            ]
            a = [{(i, j): spread(u[s][j][top][start + i:start + i + 1, :]) for j in range(4) for i in range(j + 1)} for s in each]
            for x in packs:
                for g in tall:
                    x[g] = jnp.where(own, one if g == top else 0.0, x[g])
            y = [[spread(x[top][start + q:start + q + 1, :]) for q in range(4)] for x in packs]
            low = [{} for _ in each]
            inv = [[None] * 4 for _ in each]
            for p in (0, 2):
                n = p + 1
                delta = [a[s][p, p] * a[s][n, n] - a[s][p, n] * a[s][p, n] for s in each]
                for s in each:
                    inv[s][p] = pl.reciprocal(a[s][p, p], approx=True)
                    inv[s][n] = pl.reciprocal(delta[s], approx=True) * a[s][p, p]
                for j in range(n, 4):
                    for s in each:
                        low[s][j, p] = a[s][p, j] * inv[s][p]
                for j in range(n + 1, 4):
                    for s in each:
                        a[s][n, j] = a[s][n, j] - low[s][n, p] * a[s][p, j]
                for j in range(n + 1, 4):
                    for s in each:
                        low[s][j, n] = a[s][n, j] * inv[s][n]
                for i in range(n + 1, 4):
                    for j in range(i, 4):
                        for s in each:
                            a[s][i, j] = (a[s][i, j] - low[s][i, p] * a[s][p, j]) - low[s][i, n] * a[s][n, j]
            for q in range(4):
                at = start + q
                for s in each:
                    for k in range(q):
                        for g in tall:
                            u[s][q][g] = u[s][q][g] - u[s][k][g] * low[s][q, k]
                        y[s][q] = y[s][q] - y[s][k] * low[s][q, k]
                    inverses[s] = inv[s][q] if at == 0 else jnp.where(sub >= at, inv[s][q], inverses[s])
                    for g in tall:
                        m = u[s][q][g] * inv[s][q]
                        if g == top:
                            m = jnp.where(sub > at, m, 0.0)
                        packs[s][g] = packs[s][g] - m * y[s][q]
                while placed * STEP < (first + q + 1) * len(pieces):
                    pieces[placed]()
                    placed += 1
            if start + 4 == 8:
                for s, x in enumerate(packs):
                    x[top] = x[top] * (inverses[s] * lax.rsqrt(inverses[s]))

    for t in range(teams):
        for i in range(team):
            slab_ref[t, i * STEP:(i + 1) * STEP] = ref[t * team + i, 0:STEP]
        past_ref[t] = jnp.zeros(past_ref.shape[1:], past_ref.dtype)

    def block(kb, carry):
        base = pl.multiple_of(kb * STEP, STEP)
        after = pl.multiple_of(jnp.minimum(base + STEP, width - STEP), STEP)
        done = (col_all >= base - STEP) & (col_all < base) & (row_all >= base + STEP)
        pieces = []
        for s in range(systems):
            held = {}

            def prepare(s=s, held=held):
                i = s % team
                p1, p2, p3 = split3(past_ref[s // team, i * STEP:(i + 1) * STEP])
                zero = jnp.zeros_like(p1)
                m1, m2, m3 = (jnp.where(col_in >= base + STEP, p, zero) for p in (p1, p2, p3))
                held["left"] = jnp.concatenate([m1, m1, m2, m2, m1, m3], axis=0)
                held["right"] = jnp.concatenate([p1, p2, p1, p2, p3, p1], axis=0)

            def trail(at, s=s, held=held):
                rows = slice(at, at + 128)
                update = dot(held["left"][:, rows], held["right"], TN)
                ref[s, rows] = jnp.where(done[rows], 0.0, ref[s, rows]) - update

            pieces.append(prepare)
            pieces.extend(functools.partial(trail, at) for at in range(0, width, 128))
        packs = []
        for t in range(teams):
            pack = []
            for g in range(groups):
                x = jnp.where(place - 8 * g == sub, 1.0, 0.0)
                for i in range(team):
                    piece = slab_ref[t, i * STEP + 8 * g:i * STEP + 8 * g + 8, 0:128]
                    if i > 0:
                        piece = pltpu.roll(piece, i * STEP, 1)
                    x = jnp.where(member == i, piece, x)
                pack.append(x)
            packs.append(pack)
        sides = []
        for t in range(teams):
            ident = jnp.where(col_team == row_team % STEP, 1.0, 0.0)
            sides.append(deep(padded(split3(jnp.where(col_team < STEP, ident, slab_ref[t])))))
        pivots(packs, pieces)
        for t in range(teams):
            inner = jnp.concatenate(packs[t], axis=0)
            inner = jnp.where(lower, jnp.concatenate([inner] * team, axis=0), 0.0)
            slab = dot(wide(split3(inner)), sides[t], NN)
            ahead = []
            for i in range(team):
                piece = slab[i * STEP:(i + 1) * STEP, 0:128]
                if i != 1:
                    piece = pltpu.roll(piece, (i - 1) * STEP % 128, 1)
                ahead.append(piece)
            ahead = jnp.where(same, jnp.concatenate(ahead, axis=0), 0.0)
            if height < 128:
                ahead = jnp.concatenate([ahead, jnp.zeros((128 - height, 128), jnp.float32)], axis=0)
            ahead = wide(split3(ahead.T[:height]))
            update = dot(ahead, deep(padded(split3(pltpu.roll(slab, width - STEP, 1)))), NN)
            coming = [pltpu.roll(ref[t * team + i, pl.ds(after, STEP), :], width - after, 1) for i in range(team)]
            slab_ref[t] = jnp.where(col_team >= width - STEP, 0.0, jnp.concatenate(coming, axis=0)) - update
            slab = pltpu.roll(slab, base, 1)
            past_ref[t] = slab
            for i in range(team):
                own_rows = slab[i * STEP:(i + 1) * STEP]
                ref[t * team + i, pl.ds(base, STEP), :] = jnp.where(col_in >= base + STEP, 0.0, own_rows)
        return carry

    lax.fori_loop(0, width // STEP, block, 0)


def factor_scratch(systems, width):
    team = max(n for n in range(1, 128 // STEP + 1) if systems % n == 0)
    return [pltpu.VMEM((systems // team, team * STEP, width), jnp.float32)] * 2


def scaled(matrix):
    factor_of = 1.0 / jnp.max(jnp.max(matrix, axis=1, keepdims=True), axis=0, keepdims=True)
    return matrix * factor_of, jnp.sqrt(factor_of)


def own_kernel(counts_ref, tiles_ref, w_ref, z_ref, g_ref, *scratch):
    systems, kslots, width, _ = tiles_ref.shape
    for s in range(systems):
        near = tiles_ref[s, 0:2].reshape(2 * width, width)
        g_ref[s] = dot(near, near, TN)
        for k in range(2, kslots):
            @pl.when(k < counts_ref[s])
            def _():
                tile = tiles_ref[s, k]
                g_ref[s] += dot(tile, tile, TN)
    roots = []
    for s in range(systems):
        g_ref[s], root = scaled(g_ref[s])
        roots.append(root)
    factor(g_ref, *scratch)
    for s in range(systems):
        w1, w2, w3 = split3(g_ref[s] * roots[s])
        w_ref[s, 0] = w1
        w_ref[s, 1] = w2
        near = jnp.concatenate([tiles_ref[s, 1], tiles_ref[s, 0]], axis=0)
        z = dot(w1, near, NT) + (dot(w2, near, NT) + dot(w3, near, NT))
        z1, z2, z3 = split3(z)
        z_ref[s, 0] = z1
        z_ref[s, 1] = z2
        z_ref[s, 2] = z3


def ready_kernel(x_ref, w_any, z_any, base_ref, rhs_ref, m_ref, w_ref, z_ref, sems):
    systems, _, width, _ = z_ref.shape
    w_copy = pltpu.make_async_copy(w_any, w_ref, sems.at[systems])
    w_copy.start()
    copies = [pltpu.make_async_copy(z_any.at[s], z_ref.at[s], sems.at[s]) for s in range(systems)]
    for copy in copies:
        copy.start()
    w_copy.wait()
    for s in range(systems):
        copies[s].wait()
        z = [z_ref[s, i] for i in range(3)]
        w = [w_ref[s, i] for i in range(2)]
        x = x_ref[:, s * width:(s + 1) * width]
        first = dot(x, z[0][:, width:], NT) + (dot(x, z[1][:, width:], NT) + dot(x, z[2][:, width:], NT))
        base_ref[s] = apply(first, w, NN)
        x = x.astype(jnp.float32)
        rhs = jnp.concatenate([jnp.zeros_like(x), x], axis=1) - apply(first, z, NN)
        rhs_ref[s] = jnp.concatenate(split3(rhs), axis=0)
        m = split3(dot3(z, w, TN))
        m_ref[s, 0] = m[0]
        m_ref[s, 1] = m[1]


def pair_kernel(lanes, place_ref, rhs_ref, z_any, got_ref, low_ref, y_ref, near_ref, z_ref, t_ref, r_ref, sems, *scratch):
    systems, _, width, _ = z_ref.shape
    count = y_ref.shape[1] // lanes
    copies = []
    for s in range(systems):
        pairs = ((got_ref.at[place_ref[s]], near_ref.at[s]), (z_any.at[s], z_ref.at[s]))
        copies.append([pltpu.make_async_copy(a, b, sems.at[s, i]) for i, (a, b) in enumerate(pairs)])
        for copy in copies[s]:
            copy.start()
    low_ref[...] = jnp.zeros(low_ref.shape, low_ref.dtype)
    roots = []
    for s in range(systems):
        for copy in copies[s]:
            copy.wait()
        near = near_ref[s].reshape(2 * width, width)
        near_t = near.T
        v = split3(thirds(dot(z_ref[s].reshape(3 * width, 2 * width), near, NN)))
        vt = [one.T for one in v]
        once = dot(jnp.concatenate(vt, axis=0), v[0], NN)
        twice = dot(jnp.concatenate(vt[:2], axis=0), v[1], NN)
        small = once[2 * width:] + twice[width:] + dot(vt[0], v[2], NN)
        square = once[:width] + ((once[width:2 * width] + twice[:width]) + small)
        t_ref[s], root = scaled(dot(near_t, near, NN) - square)
        roots.append(root)
        r_ref[s] = thirds(dot(rhs_ref[s], near, NN))
    factor(t_ref, *scratch)
    parts = [split3(t_ref[s] * roots[s])[:2] for s in range(systems)]
    half = [apply(r_ref[s], parts[s], NT) for s in range(systems)]
    for s in range(systems):
        y = apply(half[s], parts[s], NN)
        y_ref[s] = y
        for e in range(lanes):
            owner = lax.rem(place_ref[systems] + e, lanes)
            low_ref[place_ref[s] * lanes + owner] = y[e * count:(e + 1) * count].astype(low_ref.dtype)


def own_part_kernel(lanes, place_ref, y_ref, base_ref, m_any, got_ref, *refs):
    up_refs, (near_ref, m_ref, sems) = refs[:lanes], refs[lanes:]
    systems, nrhs, width = y_ref.shape
    count = nrhs // lanes
    copies = []
    for s in range(systems):
        pairs = ((got_ref.at[place_ref[s]], near_ref.at[s]), (m_any.at[s], m_ref.at[s]))
        copies.append([pltpu.make_async_copy(a, b, sems.at[s, i]) for i, (a, b) in enumerate(pairs)])
        for copy in copies[s]:
            copy.start()
    for s in range(systems):
        for copy in copies[s]:
            copy.wait()
        back = thirds(dot(jnp.concatenate(split3(y_ref[s]), axis=0), near_ref[s].reshape(2 * width, width), NT))
        up = base_ref[s] - apply(back, (m_ref[s, 0], m_ref[s, 1]), NN)
        for e in range(lanes):
            up_refs[e][s] = up[e * count:(e + 1) * count]


def place_kernel(lanes, place_ref, low_ref, *refs):
    up_refs, out_ref = refs[:lanes], refs[lanes]
    systems, _, width = up_refs[0].shape
    for e in range(lanes):
        owner = lax.rem(place_ref[systems * lanes] + lanes - e, lanes)
        for s in range(systems):
            at = owner * systems + s
            total = up_refs[e][s] + low_ref[place_ref[at] * lanes + owner].astype(jnp.float32)
            out_ref[:, pl.ds(pl.multiple_of(at * width, width), width)] = total.astype(out_ref.dtype)


def on_device(tiles, pattern, counts, inputs):
    shards = lax.axis_size("panel")
    lanes = lax.axis_size("rhs")
    systems, kslots, width, _ = tiles.shape
    nrhs_dev = inputs.shape[0]
    own_width = systems * width
    my_panel = lax.axis_index("panel")
    my_lane = lax.axis_index("rhs")
    per_panel = systems * lanes
    own_cnt = lax.dynamic_slice_in_dim(counts, my_panel * per_panel + my_lane * systems, systems, 0)
    panel_mates = lax.dynamic_slice(pattern, (my_panel * per_panel, 1), (per_panel, 1))[:, 0] // per_panel
    mate_panel = lax.dynamic_slice_in_dim(panel_mates, my_lane * systems, systems, 0)
    hit = mate_panel[None, :] == jnp.arange(shards, dtype=jnp.int32)[:, None]
    slot_of = jnp.sum(hit * jnp.arange(systems, dtype=jnp.int32)[None, :], axis=1)
    lane_word = my_lane[None].astype(jnp.int32)

    def shift(value, by):
        return lax.ppermute(value, "rhs", [(i, (i + by) % lanes) for i in range(lanes)])

    received = lax.all_to_all(tiles[:, :2][slot_of], "panel", split_axis=0, concat_axis=0, tiled=True)

    vmem = pl.BlockSpec(memory_space=pltpu.VMEM)
    smem = pl.BlockSpec(memory_space=pltpu.SMEM)
    anywhere = pl.BlockSpec(memory_space=pl.ANY)
    params = pltpu.CompilerParams(vmem_limit_bytes=56 * 1024 * 1024)
    w, z = pl.pallas_call(
        own_kernel,
        out_shape=(
            jax.ShapeDtypeStruct((systems, 2, width, width), jnp.bfloat16),
            jax.ShapeDtypeStruct((systems, 3, width, 2 * width), jnp.bfloat16),
        ),
        in_specs=[smem, vmem],
        out_specs=(vmem, vmem),
        scratch_shapes=[pltpu.VMEM((systems, width, width), jnp.float32)] + factor_scratch(systems, width),
        compiler_params=params,
        cost_estimate=pl.CostEstimate(flops=40 * 10**9, bytes_accessed=8 * 10**6, transcendentals=0),
    )(own_cnt, tiles)

    inputs, w = lax.optimization_barrier((inputs, w))
    parts = [lax.dynamic_slice_in_dim(inputs, my_lane * own_width, own_width, 1)]
    for e in range(1, lanes):
        part = lax.dynamic_slice_in_dim(inputs, (my_lane + lanes - e) % lanes * own_width, own_width, 1)
        parts.append(shift(part, -e))
    x = jnp.concatenate(parts, axis=0)

    nrhs = lanes * nrhs_dev
    rows = jax.ShapeDtypeStruct((systems, nrhs, width), jnp.float32)
    base, rhs, m = pl.pallas_call(
        ready_kernel,
        out_shape=(
            rows,
            jax.ShapeDtypeStruct((systems, 3 * nrhs, 2 * width), jnp.bfloat16),
            jax.ShapeDtypeStruct((systems, 2, 2 * width, width), jnp.bfloat16),
        ),
        in_specs=[vmem, anywhere, anywhere],
        out_specs=(vmem,) * 3,
        scratch_shapes=[
            pltpu.VMEM((systems, 2, width, width), jnp.bfloat16),
            pltpu.VMEM((systems, 3, width, 2 * width), jnp.bfloat16),
            pltpu.SemaphoreType.DMA((systems + 1,)),
        ],
        compiler_params=params,
        cost_estimate=pl.CostEstimate(flops=5 * 10**9, bytes_accessed=8 * 10**6, transcendentals=0),
    )(x, w, z)

    where = jnp.concatenate([mate_panel, lane_word])
    piece = jax.ShapeDtypeStruct((systems, nrhs_dev, width), jnp.float32)
    less = pltpu.CompilerParams(vmem_limit_bytes=40 * 1024 * 1024)
    low, y = pl.pallas_call(
        functools.partial(pair_kernel, lanes),
        out_shape=(jax.ShapeDtypeStruct((shards * lanes, nrhs_dev, width), jnp.bfloat16), rows),
        in_specs=[smem, vmem, anywhere, anywhere],
        out_specs=(vmem, vmem),
        scratch_shapes=[
            pltpu.VMEM((systems, 2, width, width), jnp.bfloat16),
            pltpu.VMEM((systems, 3, width, 2 * width), jnp.bfloat16),
            pltpu.VMEM((systems, width, width), jnp.float32),
            pltpu.VMEM((systems, nrhs, width), jnp.float32),
            pltpu.SemaphoreType.DMA((systems, 2)),
        ] + factor_scratch(systems, width),
        compiler_params=less,
    )(where, rhs, z, received)
    up = pl.pallas_call(
        functools.partial(own_part_kernel, lanes),
        out_shape=[piece] * lanes,
        in_specs=[smem, vmem, vmem, anywhere, anywhere],
        out_specs=[vmem] * lanes,
        scratch_shapes=[
            pltpu.VMEM((systems, 2, width, width), jnp.bfloat16),
            pltpu.VMEM((systems, 2, 2 * width, width), jnp.bfloat16),
            pltpu.SemaphoreType.DMA((systems, 2)),
        ],
        compiler_params=less,
        cost_estimate=pl.CostEstimate(flops=10**9, bytes_accessed=6 * 10**6, transcendentals=0),
    )(where, y, base, m, received)
    low = lax.all_to_all(low, ("panel", "rhs"), split_axis=0, concat_axis=0, tiled=True)
    up = [up[0]] + [shift(up[e], e) for e in range(1, lanes)]
    return pl.pallas_call(
        functools.partial(place_kernel, lanes),
        out_shape=jax.ShapeDtypeStruct((nrhs_dev, per_panel * width), jnp.bfloat16),
        in_specs=[smem] + [vmem] * (lanes + 1),
        out_specs=vmem,
    )(jnp.concatenate([panel_mates, lane_word]), low, *up)


def solution(mesh):
    return jax.shard_map(
        on_device,
        mesh=mesh,
        in_specs=(P(("panel", "rhs"), None, None, None), P(), P(), P("rhs", "panel")),
        out_specs=P("rhs", "panel"),
        check_vma=False,
    )
```

```python
import functools
import jax
import jax.numpy as jnp
from jax import lax
from jax.experimental import pallas as pl
from jax.experimental.pallas import tpu as pltpu
from jax.sharding import PartitionSpec as P

STEP = 32
NT = (((1,), (1,)), ((), ()))
NN = (((1,), (0,)), ((), ()))
TN = (((0,), (0,)), ((), ()))


def dot(a, b, dims):
    return lax.dot_general(a, b, dims, preferred_element_type=jnp.float32)


def split3(a):
    one = a.astype(jnp.bfloat16)
    rest = a - one.astype(jnp.float32)
    two = rest.astype(jnp.bfloat16)
    three = (rest - two.astype(jnp.float32)).astype(jnp.bfloat16)
    return one, two, three


def dot6(a, b, dims):
    a1, a2, a3 = a
    b1, b2, b3 = b
    small = dot(a1, b3, dims) + dot(a3, b1, dims) + dot(a2, b2, dims)
    return dot(a1, b1, dims) + ((dot(a1, b2, dims) + dot(a2, b1, dims)) + small)


def wide(parts):
    one, two, three = parts
    return jnp.concatenate([one, one, two, two, one, three], axis=1)


def deep(parts):
    one, two, three = parts
    return jnp.concatenate([one, two, one, two, three, one], axis=0)


def thirds(array):
    count = array.shape[0] // 3
    return array[:count] + (array[count:2 * count] + array[2 * count:])


def apply(rows, parts, dims):
    count = rows.shape[0]
    stack = jnp.concatenate(split3(rows), axis=0)
    high = dot(stack, parts[0], dims)
    low = dot(stack[:2 * count], parts[1], dims)
    return high[:count] + ((high[count:2 * count] + low[:count]) + (high[2 * count:] + low[count:]))


def factor(ref, slab_ref, past_ref):
    systems, width, _ = ref.shape
    teams, height, _ = slab_ref.shape
    team = height // STEP
    groups = STEP // 8
    lane = lax.broadcasted_iota(jnp.int32, (8, 128), 1)
    sub = lax.broadcasted_iota(jnp.int32, (8, 128), 0)
    member = lane // STEP
    place = lane % STEP
    col_in = lax.broadcasted_iota(jnp.int32, (STEP, width), 1)
    row_all = lax.broadcasted_iota(jnp.int32, (width, width), 0)
    col_all = lax.broadcasted_iota(jnp.int32, (width, width), 1)
    row_team = lax.broadcasted_iota(jnp.int32, (height, width), 0)
    col_team = lax.broadcasted_iota(jnp.int32, (height, width), 1)
    row_diag = lax.broadcasted_iota(jnp.int32, (height, 128), 0)
    col_diag = lax.broadcasted_iota(jnp.int32, (height, 128), 1)
    same = row_diag // STEP == col_diag // STEP
    lower = same & (col_diag <= row_diag)

    def spread(row):
        return jnp.broadcast_to(row, (8, 128))

    def padded(parts):
        if height == 128:
            return parts
        filler = jnp.zeros((128 - height, width), jnp.bfloat16)
        return [jnp.concatenate([part, filler], axis=0) for part in parts]

    def pivots(packs, pieces):
        placed = 0
        for first in range(0, STEP, 4):
            top, start = first // 8, first % 8
            tall = range(top, groups)
            own = (place >= first) & (place < first + 4)
            one = jnp.where(place - 8 * top == sub, 1.0, 0.0)
            each = range(len(packs))
            if start == 0:
                inverses = [None for _ in each]
            u = [
                [{g: jnp.take_along_axis(x[g], lane - place + (first + q), axis=1) for g in tall} for q in range(4)]
                for x in packs
            ]
            a = [{(i, j): spread(u[s][j][top][start + i:start + i + 1, :]) for j in range(4) for i in range(j + 1)} for s in each]
            for x in packs:
                for g in tall:
                    x[g] = jnp.where(own, one if g == top else 0.0, x[g])
            y = [[spread(x[top][start + q:start + q + 1, :]) for q in range(4)] for x in packs]
            low = [{} for _ in each]
            inv = [[None] * 4 for _ in each]
            for p in (0, 2):
                n = p + 1
                delta = [a[s][p, p] * a[s][n, n] - a[s][p, n] * a[s][p, n] for s in each]
                for s in each:
                    inv[s][p] = pl.reciprocal(a[s][p, p], approx=True)
                    inv[s][n] = pl.reciprocal(delta[s], approx=True) * a[s][p, p]
                for j in range(n, 4):
                    for s in each:
                        low[s][j, p] = a[s][p, j] * inv[s][p]
                for j in range(n + 1, 4):
                    for s in each:
                        a[s][n, j] = a[s][n, j] - low[s][n, p] * a[s][p, j]
                for j in range(n + 1, 4):
                    for s in each:
                        low[s][j, n] = a[s][n, j] * inv[s][n]
                for i in range(n + 1, 4):
                    for j in range(i, 4):
                        for s in each:
                            a[s][i, j] = (a[s][i, j] - low[s][i, p] * a[s][p, j]) - low[s][i, n] * a[s][n, j]
            for q in range(4):
                at = start + q
                for s in each:
                    for k in range(q):
                        for g in tall:
                            u[s][q][g] = u[s][q][g] - u[s][k][g] * low[s][q, k]
                        y[s][q] = y[s][q] - y[s][k] * low[s][q, k]
                    inverses[s] = inv[s][q] if at == 0 else jnp.where(sub >= at, inv[s][q], inverses[s])
                    for g in tall:
                        m = u[s][q][g] * inv[s][q]
                        if g == top:
                            m = jnp.where(sub > at, m, 0.0)
                        packs[s][g] = packs[s][g] - m * y[s][q]
                while placed * STEP < (first + q + 1) * len(pieces):
                    pieces[placed]()
                    placed += 1
            if start + 4 == 8:
                for s, x in enumerate(packs):
                    x[top] = x[top] * (inverses[s] * lax.rsqrt(inverses[s]))

    for t in range(teams):
        for i in range(team):
            slab_ref[t, i * STEP:(i + 1) * STEP] = ref[t * team + i, 0:STEP]
        past_ref[t] = jnp.zeros(past_ref.shape[1:], past_ref.dtype)

    def block(kb, carry):
        base = pl.multiple_of(kb * STEP, STEP)
        after = pl.multiple_of(jnp.minimum(base + STEP, width - STEP), STEP)
        done = (col_all >= base - STEP) & (col_all < base) & (row_all >= base + STEP)
        pieces = []
        for s in range(systems):
            held = {}

            def prepare(s=s, held=held):
                i = s % team
                p1, p2, p3 = split3(past_ref[s // team, i * STEP:(i + 1) * STEP])
                zero = jnp.zeros_like(p1)
                m1, m2, m3 = (jnp.where(col_in >= base + STEP, p, zero) for p in (p1, p2, p3))
                held["left"] = jnp.concatenate([m1, m1, m2, m2, m1, m3], axis=0)
                held["right"] = jnp.concatenate([p1, p2, p1, p2, p3, p1], axis=0)

            def trail(at, s=s, held=held):
                rows = slice(at, at + 128)
                update = dot(held["left"][:, rows], held["right"], TN)
                ref[s, rows] = jnp.where(done[rows], 0.0, ref[s, rows]) - update

            pieces.append(prepare)
            pieces.extend(functools.partial(trail, at) for at in range(0, width, 128))
        packs = []
        for t in range(teams):
            pack = []
            for g in range(groups):
                x = jnp.where(place - 8 * g == sub, 1.0, 0.0)
                for i in range(team):
                    piece = slab_ref[t, i * STEP + 8 * g:i * STEP + 8 * g + 8, 0:128]
                    if i > 0:
                        piece = pltpu.roll(piece, i * STEP, 1)
                    x = jnp.where(member == i, piece, x)
                pack.append(x)
            packs.append(pack)
        sides = []
        for t in range(teams):
            ident = jnp.where(col_team == row_team % STEP, 1.0, 0.0)
            sides.append(deep(padded(split3(jnp.where(col_team < STEP, ident, slab_ref[t])))))
        pivots(packs, pieces)
        for t in range(teams):
            inner = jnp.concatenate(packs[t], axis=0)
            inner = jnp.where(lower, jnp.concatenate([inner] * team, axis=0), 0.0)
            slab = dot(wide(split3(inner)), sides[t], NN)
            ahead = []
            for i in range(team):
                piece = slab[i * STEP:(i + 1) * STEP, 0:128]
                if i != 1:
                    piece = pltpu.roll(piece, (i - 1) * STEP % 128, 1)
                ahead.append(piece)
            ahead = jnp.where(same, jnp.concatenate(ahead, axis=0), 0.0)
            if height < 128:
                ahead = jnp.concatenate([ahead, jnp.zeros((128 - height, 128), jnp.float32)], axis=0)
            ahead = wide(split3(ahead.T[:height]))
            update = dot(ahead, deep(padded(split3(pltpu.roll(slab, width - STEP, 1)))), NN)
            coming = [pltpu.roll(ref[t * team + i, pl.ds(after, STEP), :], width - after, 1) for i in range(team)]
            slab_ref[t] = jnp.where(col_team >= width - STEP, 0.0, jnp.concatenate(coming, axis=0)) - update
            slab = pltpu.roll(slab, base, 1)
            past_ref[t] = slab
            for i in range(team):
                own_rows = slab[i * STEP:(i + 1) * STEP]
                ref[t * team + i, pl.ds(base, STEP), :] = jnp.where(col_in >= base + STEP, 0.0, own_rows)
        return carry

    lax.fori_loop(0, width // STEP, block, 0)


def factor_scratch(systems, width):
    team = max(n for n in range(1, 128 // STEP + 1) if systems % n == 0)
    return [pltpu.VMEM((systems // team, team * STEP, width), jnp.float32)] * 2


def scaled(matrix):
    factor_of = 1.0 / jnp.max(jnp.max(matrix, axis=1, keepdims=True), axis=0, keepdims=True)
    return matrix * factor_of, jnp.sqrt(factor_of)


def own_kernel(counts_ref, tiles_ref, w_ref, z_ref, g_ref, *scratch):
    systems, kslots, width, _ = tiles_ref.shape
    for s in range(systems):
        near = tiles_ref[s, 0:2].reshape(2 * width, width)
        g_ref[s] = dot(near, near, TN)
        for k in range(2, kslots):
            @pl.when(k < counts_ref[s])
            def _():
                tile = tiles_ref[s, k]
                g_ref[s] += dot(tile, tile, TN)
    roots = []
    for s in range(systems):
        g_ref[s], root = scaled(g_ref[s])
        roots.append(root)
    factor(g_ref, *scratch)
    for s in range(systems):
        w1, w2, w3 = split3(g_ref[s] * roots[s])
        w_ref[s, 0] = w1
        w_ref[s, 1] = w2
        near = jnp.concatenate([tiles_ref[s, 1], tiles_ref[s, 0]], axis=0)
        z = dot(jnp.concatenate([w1, w2, w3], axis=1), jnp.concatenate([near] * 3, axis=1), NT)
        for i, part in enumerate(split3(z)):
            z_ref[s, :, i * 2 * width:(i + 1) * 2 * width] = part


def ready_kernel(x_ref, z_any, first_ref, rhs_ref, z_ref, sems):
    systems, _, width = first_ref.shape
    copies = [pltpu.make_async_copy(z_any.at[s], z_ref.at[s], sems.at[s]) for s in range(systems)]
    for copy in copies:
        copy.start()
    for s in range(systems):
        copies[s].wait()
        z = [z_ref[s, :, i * 2 * width:(i + 1) * 2 * width] for i in range(3)]
        x = x_ref[:, s * width:(s + 1) * width]
        first = dot(x, z[0][:, width:], NT) + (dot(x, z[1][:, width:], NT) + dot(x, z[2][:, width:], NT))
        first_ref[s] = first
        x = x.astype(jnp.float32)
        rhs = jnp.concatenate([jnp.zeros_like(x), x], axis=1) - apply(first, z, NN)
        rhs_ref[s] = jnp.concatenate(split3(rhs), axis=0)


def pair_kernel(lanes, place_ref, first_ref, rhs_ref, w_any, z_any, got_ref, *refs):
    up_refs, refs = refs[:lanes], refs[lanes:]
    low_ref, near_ref, w_ref, z_ref, t_ref, v_ref, r_ref, sems, *scratch = refs
    systems, nrhs, width = first_ref.shape
    count = nrhs // lanes
    copies = []
    for s in range(systems):
        pairs = ((got_ref.at[place_ref[s]], near_ref.at[s]), (z_any.at[s], z_ref.at[s]))
        copies.append([pltpu.make_async_copy(a, b, sems.at[s, i]) for i, (a, b) in enumerate(pairs)])
        for copy in copies[s]:
            copy.start()
    w_copy = pltpu.make_async_copy(w_any, w_ref, sems.at[systems, 0])
    w_copy.start()
    low_ref[...] = jnp.zeros(low_ref.shape, low_ref.dtype)
    roots = []
    for s in range(systems):
        for copy in copies[s]:
            copy.wait()
        near = near_ref[s].reshape(2 * width, width)
        v = dot(z_ref[s], jnp.concatenate([near] * 3, axis=0), NN)
        v1, v2, v3 = split3(v)
        n1, n2, n3 = split3(-v.T)
        v_ref[s, 0] = n1
        v_ref[s, 1] = n2
        t_ref[s], root = scaled(dot(
            jnp.concatenate([near.T, n1, n1, n2, n2, n1, n3], axis=1),
            jnp.concatenate([near, v1, v2, v1, v2, v3, v1], axis=0),
            NN,
        ))
        roots.append(root)
        r_ref[s] = thirds(dot(rhs_ref[s], near, NN))
    factor(t_ref, *scratch)
    w_copy.wait()
    parts = [split3(t_ref[s] * roots[s])[:2] for s in range(systems)]
    half = [apply(r_ref[s], parts[s], NT) for s in range(systems)]
    last = [apply(half[s], parts[s], NN) for s in range(systems)]
    mid = [first_ref[s] + apply(last[s], (v_ref[s, 0], v_ref[s, 1]), NN) for s in range(systems)]
    for s in range(systems):
        up = apply(mid[s], (w_ref[s, 0], w_ref[s, 1]), NN)
        for e in range(lanes):
            up_refs[e][s] = up[e * count:(e + 1) * count]
            owner = lax.rem(place_ref[systems] + e, lanes)
            low_ref[place_ref[s] * lanes + owner] = last[s][e * count:(e + 1) * count].astype(low_ref.dtype)


def place_kernel(lanes, place_ref, low_ref, *refs):
    up_refs, out_ref = refs[:lanes], refs[lanes]
    systems, _, width = up_refs[0].shape
    for e in range(lanes):
        owner = lax.rem(place_ref[systems * lanes] + lanes - e, lanes)
        for s in range(systems):
            at = owner * systems + s
            total = up_refs[e][s] + low_ref[place_ref[at] * lanes + owner].astype(jnp.float32)
            out_ref[:, pl.ds(pl.multiple_of(at * width, width), width)] = total.astype(out_ref.dtype)


def on_device(tiles, pattern, counts, inputs):
    shards = lax.axis_size("panel")
    lanes = lax.axis_size("rhs")
    systems, kslots, width, _ = tiles.shape
    nrhs_dev = inputs.shape[0]
    own_width = systems * width
    my_panel = lax.axis_index("panel")
    my_lane = lax.axis_index("rhs")
    per_panel = systems * lanes
    own_cnt = lax.dynamic_slice_in_dim(counts, my_panel * per_panel + my_lane * systems, systems, 0)
    panel_mates = lax.dynamic_slice(pattern, (my_panel * per_panel, 1), (per_panel, 1))[:, 0] // per_panel
    mate_panel = lax.dynamic_slice_in_dim(panel_mates, my_lane * systems, systems, 0)
    hit = mate_panel[None, :] == jnp.arange(shards, dtype=jnp.int32)[:, None]
    slot_of = jnp.sum(hit * jnp.arange(systems, dtype=jnp.int32)[None, :], axis=1)
    lane_word = my_lane[None].astype(jnp.int32)

    def shift(value, by):
        return lax.ppermute(value, "rhs", [(i, (i + by) % lanes) for i in range(lanes)])

    received = lax.all_to_all(tiles[:, :2][slot_of], "panel", split_axis=0, concat_axis=0, tiled=True)

    vmem = pl.BlockSpec(memory_space=pltpu.VMEM)
    smem = pl.BlockSpec(memory_space=pltpu.SMEM)
    anywhere = pl.BlockSpec(memory_space=pl.ANY)
    params = pltpu.CompilerParams(vmem_limit_bytes=56 * 1024 * 1024)
    w, z = pl.pallas_call(
        own_kernel,
        out_shape=(
            jax.ShapeDtypeStruct((systems, 2, width, width), jnp.bfloat16),
            jax.ShapeDtypeStruct((systems, width, 6 * width), jnp.bfloat16),
        ),
        in_specs=[smem, vmem],
        out_specs=(vmem, vmem),
        scratch_shapes=[pltpu.VMEM((systems, width, width), jnp.float32)] + factor_scratch(systems, width),
        compiler_params=params,
        cost_estimate=pl.CostEstimate(flops=40 * 10**9, bytes_accessed=8 * 10**6, transcendentals=0),
    )(own_cnt, tiles)

    inputs, w = lax.optimization_barrier((inputs, w))
    parts = [lax.dynamic_slice_in_dim(inputs, my_lane * own_width, own_width, 1)]
    for e in range(1, lanes):
        part = lax.dynamic_slice_in_dim(inputs, (my_lane + lanes - e) % lanes * own_width, own_width, 1)
        parts.append(shift(part, -e))
    x = jnp.concatenate(parts, axis=0)

    nrhs = lanes * nrhs_dev
    rows = jax.ShapeDtypeStruct((systems, nrhs, width), jnp.float32)
    first, rhs = pl.pallas_call(
        ready_kernel,
        out_shape=(rows, jax.ShapeDtypeStruct((systems, 3 * nrhs, 2 * width), jnp.bfloat16)),
        in_specs=[vmem, anywhere],
        out_specs=(vmem, vmem),
        scratch_shapes=[
            pltpu.VMEM((systems, width, 6 * width), jnp.bfloat16),
            pltpu.SemaphoreType.DMA((systems,)),
        ],
        compiler_params=params,
        cost_estimate=pl.CostEstimate(flops=5 * 10**9, bytes_accessed=8 * 10**6, transcendentals=0),
    )(x, z)

    piece = jax.ShapeDtypeStruct((systems, nrhs_dev, width), jnp.float32)
    *up, low = pl.pallas_call(
        functools.partial(pair_kernel, lanes),
        out_shape=[piece] * lanes + [jax.ShapeDtypeStruct((shards * lanes, nrhs_dev, width), jnp.bfloat16)],
        in_specs=[smem, vmem, vmem, anywhere, anywhere, anywhere],
        out_specs=[vmem] * (lanes + 1),
        scratch_shapes=[
            pltpu.VMEM((systems, 2, width, width), jnp.bfloat16),
            pltpu.VMEM((systems, 2, width, width), jnp.bfloat16),
            pltpu.VMEM((systems, width, 6 * width), jnp.bfloat16),
            pltpu.VMEM((systems, width, width), jnp.float32),
            pltpu.VMEM((systems, 2, width, width), jnp.bfloat16),
            pltpu.VMEM((systems, nrhs, width), jnp.float32),
            pltpu.SemaphoreType.DMA((systems + 1, 2)),
        ] + factor_scratch(systems, width),
        compiler_params=params,
    )(jnp.concatenate([mate_panel, lane_word]), first, rhs, w, z, received)
    low = lax.all_to_all(low, ("panel", "rhs"), split_axis=0, concat_axis=0, tiled=True)
    up = [up[0]] + [shift(up[e], e) for e in range(1, lanes)]
    return pl.pallas_call(
        functools.partial(place_kernel, lanes),
        out_shape=jax.ShapeDtypeStruct((nrhs_dev, per_panel * width), jnp.bfloat16),
        in_specs=[smem] + [vmem] * (lanes + 1),
        out_specs=vmem,
    )(jnp.concatenate([panel_mates, lane_word]), low, *up)


def solution(mesh):
    return jax.shard_map(
        on_device,
        mesh=mesh,
        in_specs=(P(("panel", "rhs"), None, None, None), P(), P(), P("rhs", "panel")),
        out_specs=P("rhs", "panel"),
        check_vma=False,
    )
```

```python
import functools
import jax
import jax.numpy as jnp
from jax import lax
from jax.experimental import pallas as pl
from jax.experimental.pallas import tpu as pltpu
from jax.sharding import PartitionSpec as P

STEP = 64
NT = (((1,), (1,)), ((), ()))
NN = (((1,), (0,)), ((), ()))
TN = (((0,), (0,)), ((), ()))


def dot(a, b, dims):
    return lax.dot_general(a, b, dims, preferred_element_type=jnp.float32)


def split3(a):
    one = a.astype(jnp.bfloat16)
    rest = a - one.astype(jnp.float32)
    two = rest.astype(jnp.bfloat16)
    three = (rest - two.astype(jnp.float32)).astype(jnp.bfloat16)
    return one, two, three


def dot6(a, b, dims):
    a1, a2, a3 = a
    b1, b2, b3 = b
    small = dot(a1, b3, dims) + dot(a3, b1, dims) + dot(a2, b2, dims)
    return dot(a1, b1, dims) + ((dot(a1, b2, dims) + dot(a2, b1, dims)) + small)


def wide(parts):
    one, two, three = parts
    return jnp.concatenate([one, one, two, two, one, three], axis=1)


def deep(parts):
    one, two, three = parts
    return jnp.concatenate([one, two, one, two, three, one], axis=0)


def thirds(array):
    count = array.shape[0] // 3
    return array[:count] + (array[count:2 * count] + array[2 * count:])


def apply(rows, parts, dims):
    count = rows.shape[0]
    stack = jnp.concatenate(split3(rows), axis=0)
    high = dot(stack, parts[0], dims)
    low = dot(stack[:2 * count], parts[1], dims)
    return high[:count] + ((high[count:2 * count] + low[:count]) + (high[2 * count:] + low[count:]))


def factor(ref, slab_ref, past_ref):
    systems, width, _ = ref.shape
    teams, height, _ = slab_ref.shape
    team = height // STEP
    groups = STEP // 8
    lane = lax.broadcasted_iota(jnp.int32, (8, 128), 1)
    sub = lax.broadcasted_iota(jnp.int32, (8, 128), 0)
    member = lane // STEP
    place = lane % STEP
    col_in = lax.broadcasted_iota(jnp.int32, (STEP, width), 1)
    row_all = lax.broadcasted_iota(jnp.int32, (width, width), 0)
    col_all = lax.broadcasted_iota(jnp.int32, (width, width), 1)
    row_team = lax.broadcasted_iota(jnp.int32, (height, width), 0)
    col_team = lax.broadcasted_iota(jnp.int32, (height, width), 1)
    row_diag = lax.broadcasted_iota(jnp.int32, (height, 128), 0)
    col_diag = lax.broadcasted_iota(jnp.int32, (height, 128), 1)
    same = row_diag // STEP == col_diag // STEP
    lower = same & (col_diag <= row_diag)

    def spread(row):
        return jnp.broadcast_to(row, (8, 128))

    def padded(parts):
        if height == 128:
            return parts
        filler = jnp.zeros((128 - height, width), jnp.bfloat16)
        return [jnp.concatenate([part, filler], axis=0) for part in parts]

    def pivots(packs, pieces):
        placed = 0
        for first in range(0, STEP, 4):
            top, start = first // 8, first % 8
            tall = range(top, groups)
            own = (place >= first) & (place < first + 4)
            one = jnp.where(place - 8 * top == sub, 1.0, 0.0)
            each = range(len(packs))
            if start == 0:
                inverses = [None for _ in each]
            u = [
                [{g: jnp.take_along_axis(x[g], lane - place + (first + q), axis=1) for g in tall} for q in range(4)]
                for x in packs
            ]
            a = [{(i, j): spread(u[s][j][top][start + i:start + i + 1, :]) for j in range(4) for i in range(j + 1)} for s in each]
            for x in packs:
                for g in tall:
                    x[g] = jnp.where(own, one if g == top else 0.0, x[g])
            y = [[spread(x[top][start + q:start + q + 1, :]) for q in range(4)] for x in packs]
            low = [{} for _ in each]
            inv = [[None] * 4 for _ in each]
            for p in (0, 2):
                n = p + 1
                delta = [a[s][p, p] * a[s][n, n] - a[s][p, n] * a[s][p, n] for s in each]
                for s in each:
                    inv[s][p] = pl.reciprocal(a[s][p, p], approx=True)
                    inv[s][n] = pl.reciprocal(delta[s], approx=True) * a[s][p, p]
                for j in range(n, 4):
                    for s in each:
                        low[s][j, p] = a[s][p, j] * inv[s][p]
                for j in range(n + 1, 4):
                    for s in each:
                        a[s][n, j] = a[s][n, j] - low[s][n, p] * a[s][p, j]
                for j in range(n + 1, 4):
                    for s in each:
                        low[s][j, n] = a[s][n, j] * inv[s][n]
                for i in range(n + 1, 4):
                    for j in range(i, 4):
                        for s in each:
                            a[s][i, j] = (a[s][i, j] - low[s][i, p] * a[s][p, j]) - low[s][i, n] * a[s][n, j]
            for q in range(4):
                at = start + q
                for s in each:
                    for k in range(q):
                        for g in tall:
                            u[s][q][g] = u[s][q][g] - u[s][k][g] * low[s][q, k]
                        y[s][q] = y[s][q] - y[s][k] * low[s][q, k]
                    inverses[s] = inv[s][q] if at == 0 else jnp.where(sub >= at, inv[s][q], inverses[s])
                    for g in tall:
                        m = u[s][q][g] * inv[s][q]
                        if g == top:
                            m = jnp.where(sub > at, m, 0.0)
                        packs[s][g] = packs[s][g] - m * y[s][q]
                while placed * STEP < (first + q + 1) * len(pieces):
                    pieces[placed]()
                    placed += 1
            if start + 4 == 8:
                for s, x in enumerate(packs):
                    x[top] = x[top] * (inverses[s] * lax.rsqrt(inverses[s]))

    for t in range(teams):
        for i in range(team):
            slab_ref[t, i * STEP:(i + 1) * STEP] = ref[t * team + i, 0:STEP]
        past_ref[t] = jnp.zeros(past_ref.shape[1:], past_ref.dtype)

    def block(kb, carry):
        base = pl.multiple_of(kb * STEP, STEP)
        after = pl.multiple_of(jnp.minimum(base + STEP, width - STEP), STEP)
        done = (col_all >= base - STEP) & (col_all < base) & (row_all >= base + STEP)
        pieces = []
        for s in range(systems):
            held = {}

            def prepare(s=s, held=held):
                i = s % team
                p1, p2, p3 = split3(past_ref[s // team, i * STEP:(i + 1) * STEP])
                zero = jnp.zeros_like(p1)
                m1, m2, m3 = (jnp.where(col_in >= base + STEP, p, zero) for p in (p1, p2, p3))
                held["left"] = jnp.concatenate([m1, m1, m2, m2, m1, m3], axis=0)
                held["right"] = jnp.concatenate([p1, p2, p1, p2, p3, p1], axis=0)

            def trail(at, s=s, held=held):
                rows = slice(at, at + 128)
                update = dot(held["left"][:, rows], held["right"], TN)
                ref[s, rows] = jnp.where(done[rows], 0.0, ref[s, rows]) - update

            pieces.append(prepare)
            pieces.extend(functools.partial(trail, at) for at in range(0, width, 128))
        packs = []
        for t in range(teams):
            pack = []
            for g in range(groups):
                x = jnp.where(place - 8 * g == sub, 1.0, 0.0)
                for i in range(team):
                    piece = slab_ref[t, i * STEP + 8 * g:i * STEP + 8 * g + 8, 0:128]
                    if i > 0:
                        piece = pltpu.roll(piece, i * STEP, 1)
                    x = jnp.where(member == i, piece, x)
                pack.append(x)
            packs.append(pack)
        sides = []
        for t in range(teams):
            ident = jnp.where(col_team == row_team % STEP, 1.0, 0.0)
            sides.append(deep(padded(split3(jnp.where(col_team < STEP, ident, slab_ref[t])))))
        pivots(packs, pieces)
        for t in range(teams):
            inner = jnp.concatenate(packs[t], axis=0)
            inner = jnp.where(lower, jnp.concatenate([inner] * team, axis=0), 0.0)
            slab = dot(wide(split3(inner)), sides[t], NN)
            ahead = []
            for i in range(team):
                piece = slab[i * STEP:(i + 1) * STEP, 0:128]
                if i != 1:
                    piece = pltpu.roll(piece, (i - 1) * STEP % 128, 1)
                ahead.append(piece)
            ahead = jnp.where(same, jnp.concatenate(ahead, axis=0), 0.0)
            if height < 128:
                ahead = jnp.concatenate([ahead, jnp.zeros((128 - height, 128), jnp.float32)], axis=0)
            ahead = wide(split3(ahead.T[:height]))
            update = dot(ahead, deep(padded(split3(pltpu.roll(slab, width - STEP, 1)))), NN)
            coming = [pltpu.roll(ref[t * team + i, pl.ds(after, STEP), :], width - after, 1) for i in range(team)]
            slab_ref[t] = jnp.where(col_team >= width - STEP, 0.0, jnp.concatenate(coming, axis=0)) - update
            slab = pltpu.roll(slab, base, 1)
            past_ref[t] = slab
            for i in range(team):
                own_rows = slab[i * STEP:(i + 1) * STEP]
                ref[t * team + i, pl.ds(base, STEP), :] = jnp.where(col_in >= base + STEP, 0.0, own_rows)
        return carry

    lax.fori_loop(0, width // STEP, block, 0)


def factor_scratch(systems, width):
    team = max(n for n in range(1, 128 // STEP + 1) if systems % n == 0)
    return [pltpu.VMEM((systems // team, team * STEP, width), jnp.float32)] * 2


def scaled(matrix):
    factor_of = 1.0 / jnp.max(jnp.max(matrix, axis=1, keepdims=True), axis=0, keepdims=True)
    return matrix * factor_of, jnp.sqrt(factor_of)


def own_kernel(counts_ref, tiles_ref, w_ref, z_ref, g_ref, *scratch):
    systems, kslots, width, _ = tiles_ref.shape
    for s in range(systems):
        near = tiles_ref[s, 0:2].reshape(2 * width, width)
        g_ref[s] = dot(near, near, TN)
        for k in range(2, kslots):
            @pl.when(k < counts_ref[s])
            def _():
                tile = tiles_ref[s, k]
                g_ref[s] += dot(tile, tile, TN)
    roots = []
    for s in range(systems):
        g_ref[s], root = scaled(g_ref[s])
        roots.append(root)
    factor(g_ref, *scratch)
    for s in range(systems):
        w1, w2, w3 = split3(g_ref[s] * roots[s])
        w_ref[s, 0] = w1
        w_ref[s, 1] = w2
        near = jnp.concatenate([tiles_ref[s, 1], tiles_ref[s, 0]], axis=0)
        z = dot(jnp.concatenate([w1, w2, w3], axis=1), jnp.concatenate([near] * 3, axis=1), NT)
        for i, part in enumerate(split3(z)):
            z_ref[s, :, i * 2 * width:(i + 1) * 2 * width] = part


def ready_kernel(x_ref, z_any, first_ref, rhs_ref, z_ref, sems):
    systems, _, width = first_ref.shape
    copies = [pltpu.make_async_copy(z_any.at[s], z_ref.at[s], sems.at[s]) for s in range(systems)]
    for copy in copies:
        copy.start()
    for s in range(systems):
        copies[s].wait()
        z = [z_ref[s, :, i * 2 * width:(i + 1) * 2 * width] for i in range(3)]
        x = x_ref[:, s * width:(s + 1) * width]
        first = dot(x, z[0][:, width:], NT) + (dot(x, z[1][:, width:], NT) + dot(x, z[2][:, width:], NT))
        first_ref[s] = first
        x = x.astype(jnp.float32)
        rhs = jnp.concatenate([jnp.zeros_like(x), x], axis=1) - apply(first, z, NN)
        rhs_ref[s] = jnp.concatenate(split3(rhs), axis=0)


def pair_kernel(lanes, place_ref, first_ref, rhs_ref, w_any, z_any, got_ref, *refs):
    up_refs, refs = refs[:lanes], refs[lanes:]
    low_ref, near_ref, w_ref, z_ref, t_ref, v_ref, r_ref, sems, *scratch = refs
    systems, nrhs, width = first_ref.shape
    count = nrhs // lanes
    copies = []
    for s in range(systems):
        pairs = ((got_ref.at[place_ref[s]], near_ref.at[s]), (z_any.at[s], z_ref.at[s]))
        copies.append([pltpu.make_async_copy(a, b, sems.at[s, i]) for i, (a, b) in enumerate(pairs)])
        for copy in copies[s]:
            copy.start()
    w_copy = pltpu.make_async_copy(w_any, w_ref, sems.at[systems, 0])
    w_copy.start()
    low_ref[...] = jnp.zeros(low_ref.shape, low_ref.dtype)
    roots = []
    for s in range(systems):
        for copy in copies[s]:
            copy.wait()
        near = near_ref[s].reshape(2 * width, width)
        v = dot(z_ref[s], jnp.concatenate([near] * 3, axis=0), NN)
        v1, v2, v3 = split3(v)
        n1, n2, n3 = split3(-v.T)
        v_ref[s, 0] = n1
        v_ref[s, 1] = n2
        t_ref[s], root = scaled(dot(
            jnp.concatenate([near.T, n1, n1, n2, n2, n1, n3], axis=1),
            jnp.concatenate([near, v1, v2, v1, v2, v3, v1], axis=0),
            NN,
        ))
        roots.append(root)
        r_ref[s] = thirds(dot(rhs_ref[s], near, NN))
    factor(t_ref, *scratch)
    w_copy.wait()
    parts = [split3(t_ref[s] * roots[s])[:2] for s in range(systems)]
    half = [apply(r_ref[s], parts[s], NT) for s in range(systems)]
    last = [apply(half[s], parts[s], NN) for s in range(systems)]
    mid = [first_ref[s] + apply(last[s], (v_ref[s, 0], v_ref[s, 1]), NN) for s in range(systems)]
    for s in range(systems):
        up = apply(mid[s], (w_ref[s, 0], w_ref[s, 1]), NN)
        for e in range(lanes):
            up_refs[e][s] = up[e * count:(e + 1) * count]
            owner = lax.rem(place_ref[systems] + e, lanes)
            low_ref[place_ref[s] * lanes + owner] = last[s][e * count:(e + 1) * count].astype(low_ref.dtype)


def place_kernel(lanes, place_ref, low_ref, *refs):
    up_refs, out_ref = refs[:lanes], refs[lanes]
    systems, _, width = up_refs[0].shape
    for e in range(lanes):
        owner = lax.rem(place_ref[systems * lanes] + lanes - e, lanes)
        for s in range(systems):
            at = owner * systems + s
            total = up_refs[e][s] + low_ref[place_ref[at] * lanes + owner].astype(jnp.float32)
            out_ref[:, pl.ds(pl.multiple_of(at * width, width), width)] = total.astype(out_ref.dtype)


def on_device(tiles, pattern, counts, inputs):
    shards = lax.axis_size("panel")
    lanes = lax.axis_size("rhs")
    systems, kslots, width, _ = tiles.shape
    nrhs_dev = inputs.shape[0]
    own_width = systems * width
    my_panel = lax.axis_index("panel")
    my_lane = lax.axis_index("rhs")
    per_panel = systems * lanes
    own_cnt = lax.dynamic_slice_in_dim(counts, my_panel * per_panel + my_lane * systems, systems, 0)
    panel_mates = lax.dynamic_slice(pattern, (my_panel * per_panel, 1), (per_panel, 1))[:, 0] // per_panel
    mate_panel = lax.dynamic_slice_in_dim(panel_mates, my_lane * systems, systems, 0)
    hit = mate_panel[None, :] == jnp.arange(shards, dtype=jnp.int32)[:, None]
    slot_of = jnp.sum(hit * jnp.arange(systems, dtype=jnp.int32)[None, :], axis=1)
    lane_word = my_lane[None].astype(jnp.int32)

    def shift(value, by):
        return lax.ppermute(value, "rhs", [(i, (i + by) % lanes) for i in range(lanes)])

    received = lax.all_to_all(tiles[:, :2][slot_of], "panel", split_axis=0, concat_axis=0, tiled=True)

    vmem = pl.BlockSpec(memory_space=pltpu.VMEM)
    smem = pl.BlockSpec(memory_space=pltpu.SMEM)
    anywhere = pl.BlockSpec(memory_space=pl.ANY)
    params = pltpu.CompilerParams(vmem_limit_bytes=56 * 1024 * 1024)
    w, z = pl.pallas_call(
        own_kernel,
        out_shape=(
            jax.ShapeDtypeStruct((systems, 2, width, width), jnp.bfloat16),
            jax.ShapeDtypeStruct((systems, width, 6 * width), jnp.bfloat16),
        ),
        in_specs=[smem, vmem],
        out_specs=(vmem, vmem),
        scratch_shapes=[pltpu.VMEM((systems, width, width), jnp.float32)] + factor_scratch(systems, width),
        compiler_params=params,
        cost_estimate=pl.CostEstimate(flops=40 * 10**9, bytes_accessed=8 * 10**6, transcendentals=0),
    )(own_cnt, tiles)

    inputs, w = lax.optimization_barrier((inputs, w))
    parts = [lax.dynamic_slice_in_dim(inputs, my_lane * own_width, own_width, 1)]
    for e in range(1, lanes):
        part = lax.dynamic_slice_in_dim(inputs, (my_lane + lanes - e) % lanes * own_width, own_width, 1)
        parts.append(shift(part, -e))
    x = jnp.concatenate(parts, axis=0)

    nrhs = lanes * nrhs_dev
    rows = jax.ShapeDtypeStruct((systems, nrhs, width), jnp.float32)
    first, rhs = pl.pallas_call(
        ready_kernel,
        out_shape=(rows, jax.ShapeDtypeStruct((systems, 3 * nrhs, 2 * width), jnp.bfloat16)),
        in_specs=[vmem, anywhere],
        out_specs=(vmem, vmem),
        scratch_shapes=[
            pltpu.VMEM((systems, width, 6 * width), jnp.bfloat16),
            pltpu.SemaphoreType.DMA((systems,)),
        ],
        compiler_params=params,
        cost_estimate=pl.CostEstimate(flops=5 * 10**9, bytes_accessed=8 * 10**6, transcendentals=0),
    )(x, z)

    piece = jax.ShapeDtypeStruct((systems, nrhs_dev, width), jnp.float32)
    *up, low = pl.pallas_call(
        functools.partial(pair_kernel, lanes),
        out_shape=[piece] * lanes + [jax.ShapeDtypeStruct((shards * lanes, nrhs_dev, width), jnp.bfloat16)],
        in_specs=[smem, vmem, vmem, anywhere, anywhere, anywhere],
        out_specs=[vmem] * (lanes + 1),
        scratch_shapes=[
            pltpu.VMEM((systems, 2, width, width), jnp.bfloat16),
            pltpu.VMEM((systems, 2, width, width), jnp.bfloat16),
            pltpu.VMEM((systems, width, 6 * width), jnp.bfloat16),
            pltpu.VMEM((systems, width, width), jnp.float32),
            pltpu.VMEM((systems, 2, width, width), jnp.bfloat16),
            pltpu.VMEM((systems, nrhs, width), jnp.float32),
            pltpu.SemaphoreType.DMA((systems + 1, 2)),
        ] + factor_scratch(systems, width),
        compiler_params=params,
    )(jnp.concatenate([mate_panel, lane_word]), first, rhs, w, z, received)
    low = lax.all_to_all(low, ("panel", "rhs"), split_axis=0, concat_axis=0, tiled=True)
    up = [up[0]] + [shift(up[e], e) for e in range(1, lanes)]
    return pl.pallas_call(
        functools.partial(place_kernel, lanes),
        out_shape=jax.ShapeDtypeStruct((nrhs_dev, per_panel * width), jnp.bfloat16),
        in_specs=[smem] + [vmem] * (lanes + 1),
        out_specs=vmem,
    )(jnp.concatenate([panel_mates, lane_word]), low, *up)


def solution(mesh):
    return jax.shard_map(
        on_device,
        mesh=mesh,
        in_specs=(P(("panel", "rhs"), None, None, None), P(), P(), P("rhs", "panel")),
        out_specs=P("rhs", "panel"),
        check_vma=False,
    )
```

```python
import functools
import jax
import jax.numpy as jnp
from jax import lax
from jax.experimental import pallas as pl
from jax.experimental.pallas import tpu as pltpu
from jax.sharding import PartitionSpec as P

STEP = 32
ROUND = 8
NT = (((1,), (1,)), ((), ()))
NN = (((1,), (0,)), ((), ()))
TN = (((0,), (0,)), ((), ()))


def dot(a, b, dims):
    return lax.dot_general(a, b, dims, preferred_element_type=jnp.float32)


def split3(a):
    one = a.astype(jnp.bfloat16)
    rest = a - one.astype(jnp.float32)
    two = rest.astype(jnp.bfloat16)
    three = (rest - two.astype(jnp.float32)).astype(jnp.bfloat16)
    return one, two, three


def dot6(a, b, dims):
    a1, a2, a3 = a
    b1, b2, b3 = b
    small = dot(a1, b3, dims) + dot(a3, b1, dims) + dot(a2, b2, dims)
    return dot(a1, b1, dims) + ((dot(a1, b2, dims) + dot(a2, b1, dims)) + small)


def wide(parts):
    one, two, three = parts
    return jnp.concatenate([one, one, two, two, one, three], axis=1)


def deep(parts):
    one, two, three = parts
    return jnp.concatenate([one, two, one, two, three, one], axis=0)


def thirds(array):
    count = array.shape[0] // 3
    return array[:count] + (array[count:2 * count] + array[2 * count:])


def apply(rows, parts, dims):
    count = rows.shape[0]
    stack = jnp.concatenate(split3(rows), axis=0)
    high = dot(stack, parts[0], dims)
    low = dot(stack[:2 * count], parts[1], dims)
    return high[:count] + ((high[count:2 * count] + low[:count]) + (high[2 * count:] + low[count:]))


def factor(ref, slab_ref, past_ref):
    systems, width, _ = ref.shape
    teams, height, _ = slab_ref.shape
    team = height // STEP
    groups = STEP // 8
    lane = lax.broadcasted_iota(jnp.int32, (8, 128), 1)
    sub = lax.broadcasted_iota(jnp.int32, (8, 128), 0)
    member = lane // STEP
    place = lane % STEP
    col_in = lax.broadcasted_iota(jnp.int32, (STEP, width), 1)
    row_all = lax.broadcasted_iota(jnp.int32, (width, width), 0)
    col_all = lax.broadcasted_iota(jnp.int32, (width, width), 1)
    row_team = lax.broadcasted_iota(jnp.int32, (height, width), 0)
    col_team = lax.broadcasted_iota(jnp.int32, (height, width), 1)
    row_diag = lax.broadcasted_iota(jnp.int32, (height, 128), 0)
    col_diag = lax.broadcasted_iota(jnp.int32, (height, 128), 1)
    same = row_diag // STEP == col_diag // STEP
    lower = same & (col_diag <= row_diag)

    def spread(row):
        return jnp.broadcast_to(row, (8, 128))

    def padded(parts):
        if height == 128:
            return parts
        filler = jnp.zeros((128 - height, width), jnp.bfloat16)
        return [jnp.concatenate([part, filler], axis=0) for part in parts]

    def pivots(packs, pieces):
        placed = 0
        for first in range(0, STEP, ROUND):
            top, start = first // 8, first % 8
            tall = range(top, groups)
            own = (place >= first) & (place < first + ROUND)
            one = jnp.where(place - 8 * top == sub, 1.0, 0.0)
            each = range(len(packs))
            if start == 0:
                inverses = [None for _ in each]
            u = [
                [{g: jnp.take_along_axis(x[g], lane - place + (first + q), axis=1) for g in tall} for q in range(ROUND)]
                for x in packs
            ]
            a = [{(i, j): spread(u[s][j][top][start + i:start + i + 1, :]) for j in range(ROUND) for i in range(j + 1)} for s in each]
            for x in packs:
                for g in tall:
                    x[g] = jnp.where(own, one if g == top else 0.0, x[g])
            y = [[spread(x[top][start + q:start + q + 1, :]) for q in range(ROUND)] for x in packs]
            low = [{} for _ in each]
            inv = [[None] * ROUND for _ in each]
            for p in range(0, ROUND, 2):
                n = p + 1
                delta = [a[s][p, p] * a[s][n, n] - a[s][p, n] * a[s][p, n] for s in each]
                for s in each:
                    inv[s][p] = pl.reciprocal(a[s][p, p], approx=True)
                    inv[s][n] = pl.reciprocal(delta[s], approx=True) * a[s][p, p]
                for j in range(n, ROUND):
                    for s in each:
                        low[s][j, p] = a[s][p, j] * inv[s][p]
                for j in range(n + 1, ROUND):
                    for s in each:
                        a[s][n, j] = a[s][n, j] - low[s][n, p] * a[s][p, j]
                for j in range(n + 1, ROUND):
                    for s in each:
                        low[s][j, n] = a[s][n, j] * inv[s][n]
                for i in range(n + 1, ROUND):
                    for j in range(i, ROUND):
                        for s in each:
                            a[s][i, j] = (a[s][i, j] - low[s][i, p] * a[s][p, j]) - low[s][i, n] * a[s][n, j]
            for q in range(ROUND):
                at = start + q
                for s in each:
                    for k in range(q):
                        for g in tall:
                            u[s][q][g] = u[s][q][g] - u[s][k][g] * low[s][q, k]
                        y[s][q] = y[s][q] - y[s][k] * low[s][q, k]
                    inverses[s] = inv[s][q] if at == 0 else jnp.where(sub >= at, inv[s][q], inverses[s])
                    for g in tall:
                        m = u[s][q][g] * inv[s][q]
                        if g == top:
                            m = jnp.where(sub > at, m, 0.0)
                        packs[s][g] = packs[s][g] - m * y[s][q]
                while placed * STEP < (first + q + 1) * len(pieces):
                    pieces[placed]()
                    placed += 1
            if start + ROUND == 8:
                for s, x in enumerate(packs):
                    x[top] = x[top] * (inverses[s] * lax.rsqrt(inverses[s]))

    for t in range(teams):
        for i in range(team):
            slab_ref[t, i * STEP:(i + 1) * STEP] = ref[t * team + i, 0:STEP]
        past_ref[t] = jnp.zeros(past_ref.shape[1:], past_ref.dtype)

    def block(kb, carry):
        base = pl.multiple_of(kb * STEP, STEP)
        after = pl.multiple_of(jnp.minimum(base + STEP, width - STEP), STEP)
        done = (col_all >= base - STEP) & (col_all < base) & (row_all >= base + STEP)
        pieces = []
        for s in range(systems):
            held = {}

            def prepare(s=s, held=held):
                i = s % team
                p1, p2, p3 = split3(past_ref[s // team, i * STEP:(i + 1) * STEP])
                zero = jnp.zeros_like(p1)
                m1, m2, m3 = (jnp.where(col_in >= base + STEP, p, zero) for p in (p1, p2, p3))
                held["left"] = jnp.concatenate([m1, m1, m2, m2, m1, m3], axis=0)
                held["right"] = jnp.concatenate([p1, p2, p1, p2, p3, p1], axis=0)

            def trail(at, s=s, held=held):
                rows = slice(at, at + 128)
                update = dot(held["left"][:, rows], held["right"], TN)
                ref[s, rows] = jnp.where(done[rows], 0.0, ref[s, rows]) - update

            pieces.append(prepare)
            pieces.extend(functools.partial(trail, at) for at in range(0, width, 128))
        packs = []
        for t in range(teams):
            pack = []
            for g in range(groups):
                x = jnp.where(place - 8 * g == sub, 1.0, 0.0)
                for i in range(team):
                    piece = slab_ref[t, i * STEP + 8 * g:i * STEP + 8 * g + 8, 0:128]
                    if i > 0:
                        piece = pltpu.roll(piece, i * STEP, 1)
                    x = jnp.where(member == i, piece, x)
                pack.append(x)
            packs.append(pack)
        sides = []
        for t in range(teams):
            ident = jnp.where(col_team == row_team % STEP, 1.0, 0.0)
            sides.append(deep(padded(split3(jnp.where(col_team < STEP, ident, slab_ref[t])))))
        pivots(packs, pieces)
        for t in range(teams):
            inner = jnp.concatenate(packs[t], axis=0)
            inner = jnp.where(lower, jnp.concatenate([inner] * team, axis=0), 0.0)
            slab = dot(wide(split3(inner)), sides[t], NN)
            ahead = []
            for i in range(team):
                piece = slab[i * STEP:(i + 1) * STEP, 0:128]
                if i != 1:
                    piece = pltpu.roll(piece, (i - 1) * STEP % 128, 1)
                ahead.append(piece)
            ahead = jnp.where(same, jnp.concatenate(ahead, axis=0), 0.0)
            if height < 128:
                ahead = jnp.concatenate([ahead, jnp.zeros((128 - height, 128), jnp.float32)], axis=0)
            ahead = wide(split3(ahead.T[:height]))
            update = dot(ahead, deep(padded(split3(pltpu.roll(slab, width - STEP, 1)))), NN)
            coming = [pltpu.roll(ref[t * team + i, pl.ds(after, STEP), :], width - after, 1) for i in range(team)]
            slab_ref[t] = jnp.where(col_team >= width - STEP, 0.0, jnp.concatenate(coming, axis=0)) - update
            slab = pltpu.roll(slab, base, 1)
            past_ref[t] = slab
            for i in range(team):
                own_rows = slab[i * STEP:(i + 1) * STEP]
                ref[t * team + i, pl.ds(base, STEP), :] = jnp.where(col_in >= base + STEP, 0.0, own_rows)
        return carry

    lax.fori_loop(0, width // STEP, block, 0)


def factor_scratch(systems, width):
    team = max(n for n in range(1, 128 // STEP + 1) if systems % n == 0)
    return [pltpu.VMEM((systems // team, team * STEP, width), jnp.float32)] * 2


def scaled(matrix):
    factor_of = 1.0 / jnp.max(jnp.max(matrix, axis=1, keepdims=True), axis=0, keepdims=True)
    return matrix * factor_of, jnp.sqrt(factor_of)


def own_kernel(counts_ref, tiles_ref, w_ref, z_ref, g_ref, *scratch):
    systems, kslots, width, _ = tiles_ref.shape
    for s in range(systems):
        near = tiles_ref[s, 0:2].reshape(2 * width, width)
        g_ref[s] = dot(near, near, TN)
        for k in range(2, kslots):
            @pl.when(k < counts_ref[s])
            def _():
                tile = tiles_ref[s, k]
                g_ref[s] += dot(tile, tile, TN)
    roots = []
    for s in range(systems):
        g_ref[s], root = scaled(g_ref[s])
        roots.append(root)
    factor(g_ref, *scratch)
    for s in range(systems):
        w1, w2, w3 = split3(g_ref[s] * roots[s])
        w_ref[s, 0] = w1
        w_ref[s, 1] = w2
        near = jnp.concatenate([tiles_ref[s, 1], tiles_ref[s, 0]], axis=0)
        z = dot(jnp.concatenate([w1, w2, w3], axis=1), jnp.concatenate([near] * 3, axis=1), NT)
        for i, part in enumerate(split3(z)):
            z_ref[s, :, i * 2 * width:(i + 1) * 2 * width] = part


def ready_kernel(x_ref, z_any, first_ref, rhs_ref, z_ref, sems):
    systems, _, width = first_ref.shape
    copies = [pltpu.make_async_copy(z_any.at[s], z_ref.at[s], sems.at[s]) for s in range(systems)]
    for copy in copies:
        copy.start()
    for s in range(systems):
        copies[s].wait()
        z = [z_ref[s, :, i * 2 * width:(i + 1) * 2 * width] for i in range(3)]
        x = x_ref[:, s * width:(s + 1) * width]
        first = dot(x, z[0][:, width:], NT) + (dot(x, z[1][:, width:], NT) + dot(x, z[2][:, width:], NT))
        first_ref[s] = first
        x = x.astype(jnp.float32)
        rhs = jnp.concatenate([jnp.zeros_like(x), x], axis=1) - apply(first, z, NN)
        rhs_ref[s] = jnp.concatenate(split3(rhs), axis=0)


def pair_kernel(lanes, place_ref, first_ref, rhs_ref, w_any, z_any, got_ref, *refs):
    up_refs, refs = refs[:lanes], refs[lanes:]
    low_ref, near_ref, w_ref, z_ref, t_ref, v_ref, r_ref, sems, *scratch = refs
    systems, nrhs, width = first_ref.shape
    count = nrhs // lanes
    copies = []
    for s in range(systems):
        pairs = ((got_ref.at[place_ref[s]], near_ref.at[s]), (z_any.at[s], z_ref.at[s]))
        copies.append([pltpu.make_async_copy(a, b, sems.at[s, i]) for i, (a, b) in enumerate(pairs)])
        for copy in copies[s]:
            copy.start()
    w_copy = pltpu.make_async_copy(w_any, w_ref, sems.at[systems, 0])
    w_copy.start()
    low_ref[...] = jnp.zeros(low_ref.shape, low_ref.dtype)
    roots = []
    for s in range(systems):
        for copy in copies[s]:
            copy.wait()
        near = near_ref[s].reshape(2 * width, width)
        v = dot(z_ref[s], jnp.concatenate([near] * 3, axis=0), NN)
        v1, v2, v3 = split3(v)
        n1, n2, n3 = split3(-v.T)
        v_ref[s, 0] = n1
        v_ref[s, 1] = n2
        t_ref[s], root = scaled(dot(
            jnp.concatenate([near.T, n1, n1, n2, n2, n1, n3], axis=1),
            jnp.concatenate([near, v1, v2, v1, v2, v3, v1], axis=0),
            NN,
        ))
        roots.append(root)
        r_ref[s] = thirds(dot(rhs_ref[s], near, NN))
    factor(t_ref, *scratch)
    w_copy.wait()
    parts = [split3(t_ref[s] * roots[s])[:2] for s in range(systems)]
    half = [apply(r_ref[s], parts[s], NT) for s in range(systems)]
    last = [apply(half[s], parts[s], NN) for s in range(systems)]
    mid = [first_ref[s] + apply(last[s], (v_ref[s, 0], v_ref[s, 1]), NN) for s in range(systems)]
    for s in range(systems):
        up = apply(mid[s], (w_ref[s, 0], w_ref[s, 1]), NN)
        for e in range(lanes):
            up_refs[e][s] = up[e * count:(e + 1) * count]
            owner = lax.rem(place_ref[systems] + e, lanes)
            low_ref[place_ref[s] * lanes + owner] = last[s][e * count:(e + 1) * count].astype(low_ref.dtype)


def place_kernel(lanes, place_ref, low_ref, *refs):
    up_refs, out_ref = refs[:lanes], refs[lanes]
    systems, _, width = up_refs[0].shape
    for e in range(lanes):
        owner = lax.rem(place_ref[systems * lanes] + lanes - e, lanes)
        for s in range(systems):
            at = owner * systems + s
            total = up_refs[e][s] + low_ref[place_ref[at] * lanes + owner].astype(jnp.float32)
            out_ref[:, pl.ds(pl.multiple_of(at * width, width), width)] = total.astype(out_ref.dtype)


def on_device(tiles, pattern, counts, inputs):
    shards = lax.axis_size("panel")
    lanes = lax.axis_size("rhs")
    systems, kslots, width, _ = tiles.shape
    nrhs_dev = inputs.shape[0]
    own_width = systems * width
    my_panel = lax.axis_index("panel")
    my_lane = lax.axis_index("rhs")
    per_panel = systems * lanes
    own_cnt = lax.dynamic_slice_in_dim(counts, my_panel * per_panel + my_lane * systems, systems, 0)
    panel_mates = lax.dynamic_slice(pattern, (my_panel * per_panel, 1), (per_panel, 1))[:, 0] // per_panel
    mate_panel = lax.dynamic_slice_in_dim(panel_mates, my_lane * systems, systems, 0)
    hit = mate_panel[None, :] == jnp.arange(shards, dtype=jnp.int32)[:, None]
    slot_of = jnp.sum(hit * jnp.arange(systems, dtype=jnp.int32)[None, :], axis=1)
    lane_word = my_lane[None].astype(jnp.int32)

    def shift(value, by):
        return lax.ppermute(value, "rhs", [(i, (i + by) % lanes) for i in range(lanes)])

    received = lax.all_to_all(tiles[:, :2][slot_of], "panel", split_axis=0, concat_axis=0, tiled=True)

    vmem = pl.BlockSpec(memory_space=pltpu.VMEM)
    smem = pl.BlockSpec(memory_space=pltpu.SMEM)
    anywhere = pl.BlockSpec(memory_space=pl.ANY)
    params = pltpu.CompilerParams(vmem_limit_bytes=56 * 1024 * 1024)
    w, z = pl.pallas_call(
        own_kernel,
        out_shape=(
            jax.ShapeDtypeStruct((systems, 2, width, width), jnp.bfloat16),
            jax.ShapeDtypeStruct((systems, width, 6 * width), jnp.bfloat16),
        ),
        in_specs=[smem, vmem],
        out_specs=(vmem, vmem),
        scratch_shapes=[pltpu.VMEM((systems, width, width), jnp.float32)] + factor_scratch(systems, width),
        compiler_params=params,
        cost_estimate=pl.CostEstimate(flops=40 * 10**9, bytes_accessed=8 * 10**6, transcendentals=0),
    )(own_cnt, tiles)

    inputs, w = lax.optimization_barrier((inputs, w))
    parts = [lax.dynamic_slice_in_dim(inputs, my_lane * own_width, own_width, 1)]
    for e in range(1, lanes):
        part = lax.dynamic_slice_in_dim(inputs, (my_lane + lanes - e) % lanes * own_width, own_width, 1)
        parts.append(shift(part, -e))
    x = jnp.concatenate(parts, axis=0)

    nrhs = lanes * nrhs_dev
    rows = jax.ShapeDtypeStruct((systems, nrhs, width), jnp.float32)
    first, rhs = pl.pallas_call(
        ready_kernel,
        out_shape=(rows, jax.ShapeDtypeStruct((systems, 3 * nrhs, 2 * width), jnp.bfloat16)),
        in_specs=[vmem, anywhere],
        out_specs=(vmem, vmem),
        scratch_shapes=[
            pltpu.VMEM((systems, width, 6 * width), jnp.bfloat16),
            pltpu.SemaphoreType.DMA((systems,)),
        ],
        compiler_params=params,
        cost_estimate=pl.CostEstimate(flops=5 * 10**9, bytes_accessed=8 * 10**6, transcendentals=0),
    )(x, z)

    piece = jax.ShapeDtypeStruct((systems, nrhs_dev, width), jnp.float32)
    *up, low = pl.pallas_call(
        functools.partial(pair_kernel, lanes),
        out_shape=[piece] * lanes + [jax.ShapeDtypeStruct((shards * lanes, nrhs_dev, width), jnp.bfloat16)],
        in_specs=[smem, vmem, vmem, anywhere, anywhere, anywhere],
        out_specs=[vmem] * (lanes + 1),
        scratch_shapes=[
            pltpu.VMEM((systems, 2, width, width), jnp.bfloat16),
            pltpu.VMEM((systems, 2, width, width), jnp.bfloat16),
            pltpu.VMEM((systems, width, 6 * width), jnp.bfloat16),
            pltpu.VMEM((systems, width, width), jnp.float32),
            pltpu.VMEM((systems, 2, width, width), jnp.bfloat16),
            pltpu.VMEM((systems, nrhs, width), jnp.float32),
            pltpu.SemaphoreType.DMA((systems + 1, 2)),
        ] + factor_scratch(systems, width),
        compiler_params=params,
    )(jnp.concatenate([mate_panel, lane_word]), first, rhs, w, z, received)
    low = lax.all_to_all(low, ("panel", "rhs"), split_axis=0, concat_axis=0, tiled=True)
    up = [up[0]] + [shift(up[e], e) for e in range(1, lanes)]
    return pl.pallas_call(
        functools.partial(place_kernel, lanes),
        out_shape=jax.ShapeDtypeStruct((nrhs_dev, per_panel * width), jnp.bfloat16),
        in_specs=[smem] + [vmem] * (lanes + 1),
        out_specs=vmem,
    )(jnp.concatenate([panel_mates, lane_word]), low, *up)


def solution(mesh):
    return jax.shard_map(
        on_device,
        mesh=mesh,
        in_specs=(P(("panel", "rhs"), None, None, None), P(), P(), P("rhs", "panel")),
        out_specs=P("rhs", "panel"),
        check_vma=False,
    )
```

```python
import functools
import jax
import jax.numpy as jnp
from jax import lax
from jax.experimental import pallas as pl
from jax.experimental.pallas import tpu as pltpu
from jax.sharding import PartitionSpec as P

STEP = 32
ROUND = 8
NT = (((1,), (1,)), ((), ()))
NN = (((1,), (0,)), ((), ()))
TN = (((0,), (0,)), ((), ()))


def dot(a, b, dims):
    return lax.dot_general(a, b, dims, preferred_element_type=jnp.float32)


def split3(a):
    one = a.astype(jnp.bfloat16)
    rest = a - one.astype(jnp.float32)
    two = rest.astype(jnp.bfloat16)
    three = (rest - two.astype(jnp.float32)).astype(jnp.bfloat16)
    return one, two, three


def dot6(a, b, dims):
    a1, a2, a3 = a
    b1, b2, b3 = b
    small = dot(a1, b3, dims) + dot(a3, b1, dims) + dot(a2, b2, dims)
    return dot(a1, b1, dims) + ((dot(a1, b2, dims) + dot(a2, b1, dims)) + small)


def wide(parts):
    one, two, three = parts
    return jnp.concatenate([one, one, two, two, one, three], axis=1)


def deep(parts):
    one, two, three = parts
    return jnp.concatenate([one, two, one, two, three, one], axis=0)


def thirds(array):
    count = array.shape[0] // 3
    return array[:count] + (array[count:2 * count] + array[2 * count:])


def apply(rows, parts, dims):
    count = rows.shape[0]
    stack = jnp.concatenate(split3(rows), axis=0)
    high = dot(stack, parts[0], dims)
    low = dot(stack[:2 * count], parts[1], dims)
    return high[:count] + ((high[count:2 * count] + low[:count]) + (high[2 * count:] + low[count:]))


def factor(ref, slab_ref, past_ref):
    systems, width, _ = ref.shape
    teams, height, _ = slab_ref.shape
    team = height // STEP
    groups = STEP // 8
    lane = lax.broadcasted_iota(jnp.int32, (8, 128), 1)
    sub = lax.broadcasted_iota(jnp.int32, (8, 128), 0)
    member = lane // STEP
    place = lane % STEP
    col_in = lax.broadcasted_iota(jnp.int32, (STEP, width), 1)
    row_all = lax.broadcasted_iota(jnp.int32, (width, width), 0)
    col_all = lax.broadcasted_iota(jnp.int32, (width, width), 1)
    row_team = lax.broadcasted_iota(jnp.int32, (height, width), 0)
    col_team = lax.broadcasted_iota(jnp.int32, (height, width), 1)
    row_diag = lax.broadcasted_iota(jnp.int32, (height, 128), 0)
    col_diag = lax.broadcasted_iota(jnp.int32, (height, 128), 1)
    same = row_diag // STEP == col_diag // STEP
    lower = same & (col_diag <= row_diag)

    def spread(row):
        return jnp.broadcast_to(row, (8, 128))

    def padded(parts):
        if height == 128:
            return parts
        filler = jnp.zeros((128 - height, width), jnp.bfloat16)
        return [jnp.concatenate([part, filler], axis=0) for part in parts]

    def pivots(packs, pieces):
        placed = 0
        for first in range(0, STEP, ROUND):
            top, start = first // 8, first % 8
            tall = range(top, groups)
            own = (place >= first) & (place < first + ROUND)
            one = jnp.where(place - 8 * top == sub, 1.0, 0.0)
            each = range(len(packs))
            if start == 0:
                inverses = [None for _ in each]
            u = [
                [{g: jnp.take_along_axis(x[g], lane - place + (first + q), axis=1) for g in tall} for q in range(ROUND)]
                for x in packs
            ]
            a = [{(i, j): spread(u[s][j][top][start + i:start + i + 1, :]) for j in range(ROUND) for i in range(j + 1)} for s in each]
            for x in packs:
                for g in tall:
                    x[g] = jnp.where(own, one if g == top else 0.0, x[g])
            y = [[spread(x[top][start + q:start + q + 1, :]) for q in range(ROUND)] for x in packs]
            low = [{} for _ in each]
            inv = [[None] * ROUND for _ in each]
            for p in range(0, ROUND, 2):
                n = p + 1
                delta = [a[s][p, p] * a[s][n, n] - a[s][p, n] * a[s][p, n] for s in each]
                for s in each:
                    inv[s][p] = pl.reciprocal(a[s][p, p], approx=True)
                    inv[s][n] = pl.reciprocal(delta[s], approx=True) * a[s][p, p]
                for j in range(n, ROUND):
                    for s in each:
                        low[s][j, p] = a[s][p, j] * inv[s][p]
                for j in range(n + 1, ROUND):
                    for s in each:
                        a[s][n, j] = a[s][n, j] - low[s][n, p] * a[s][p, j]
                for j in range(n + 1, ROUND):
                    for s in each:
                        low[s][j, n] = a[s][n, j] * inv[s][n]
                for i in range(n + 1, ROUND):
                    for j in range(i, ROUND):
                        for s in each:
                            a[s][i, j] = (a[s][i, j] - low[s][i, p] * a[s][p, j]) - low[s][i, n] * a[s][n, j]
            for q in range(ROUND):
                at = start + q
                for s in each:
                    for k in range(q):
                        for g in tall:
                            u[s][q][g] = u[s][q][g] - u[s][k][g] * low[s][q, k]
                        y[s][q] = y[s][q] - y[s][k] * low[s][q, k]
                    inverses[s] = inv[s][q] if at == 0 else jnp.where(sub >= at, inv[s][q], inverses[s])
                    for g in tall:
                        m = u[s][q][g] * inv[s][q]
                        if g == top:
                            m = jnp.where(sub > at, m, 0.0)
                        packs[s][g] = packs[s][g] - m * y[s][q]
                while placed * STEP < (first + q + 1) * len(pieces):
                    pieces[placed]()
                    placed += 1
            if start + ROUND == 8:
                for s, x in enumerate(packs):
                    x[top] = x[top] * (inverses[s] * lax.rsqrt(inverses[s]))

    for t in range(teams):
        for i in range(team):
            slab_ref[t, i * STEP:(i + 1) * STEP] = ref[t * team + i, 0:STEP]
        past_ref[t] = jnp.zeros(past_ref.shape[1:], past_ref.dtype)

    def block(kb, carry):
        base = pl.multiple_of(kb * STEP, STEP)
        after = pl.multiple_of(jnp.minimum(base + STEP, width - STEP), STEP)
        done = (col_all >= base - STEP) & (col_all < base) & (row_all >= base + STEP)
        pieces = []
        for s in range(systems):
            held = {}

            def prepare(s=s, held=held):
                i = s % team
                p1, p2, p3 = split3(past_ref[s // team, i * STEP:(i + 1) * STEP])
                zero = jnp.zeros_like(p1)
                m1, m2, m3 = (jnp.where(col_in >= base + STEP, p, zero) for p in (p1, p2, p3))
                held["left"] = jnp.concatenate([m1, m1, m2, m2, m1, m3], axis=0)
                held["right"] = jnp.concatenate([p1, p2, p1, p2, p3, p1], axis=0)

            def trail(at, s=s, held=held):
                rows = slice(at, at + 128)
                update = dot(held["left"][:, rows], held["right"], TN)
                ref[s, rows] = jnp.where(done[rows], 0.0, ref[s, rows]) - update

            pieces.append(prepare)
            pieces.extend(functools.partial(trail, at) for at in range(0, width, 128))
        packs = []
        for t in range(teams):
            pack = []
            for g in range(groups):
                x = jnp.where(place - 8 * g == sub, 1.0, 0.0)
                for i in range(team):
                    piece = slab_ref[t, i * STEP + 8 * g:i * STEP + 8 * g + 8, 0:128]
                    if i > 0:
                        piece = pltpu.roll(piece, i * STEP, 1)
                    x = jnp.where(member == i, piece, x)
                pack.append(x)
            packs.append(pack)
        sides = []
        for t in range(teams):
            ident = jnp.where(col_team == row_team % STEP, 1.0, 0.0)
            sides.append(deep(padded(split3(jnp.where(col_team < STEP, ident, slab_ref[t])))))
        pivots(packs, pieces)
        for t in range(teams):
            inner = jnp.concatenate(packs[t], axis=0)
            inner = jnp.where(lower, jnp.concatenate([inner] * team, axis=0), 0.0)
            slab = dot(wide(split3(inner)), sides[t], NN)
            ahead = []
            for i in range(team):
                piece = slab[i * STEP:(i + 1) * STEP, 0:128]
                if i != 1:
                    piece = pltpu.roll(piece, (i - 1) * STEP % 128, 1)
                ahead.append(piece)
            ahead = jnp.where(same, jnp.concatenate(ahead, axis=0), 0.0)
            if height < 128:
                ahead = jnp.concatenate([ahead, jnp.zeros((128 - height, 128), jnp.float32)], axis=0)
            ahead = wide(split3(ahead.T[:height]))
            update = dot(ahead, deep(padded(split3(pltpu.roll(slab, width - STEP, 1)))), NN)
            coming = [pltpu.roll(ref[t * team + i, pl.ds(after, STEP), :], width - after, 1) for i in range(team)]
            slab_ref[t] = jnp.where(col_team >= width - STEP, 0.0, jnp.concatenate(coming, axis=0)) - update
            slab = pltpu.roll(slab, base, 1)
            past_ref[t] = slab
            for i in range(team):
                own_rows = slab[i * STEP:(i + 1) * STEP]
                ref[t * team + i, pl.ds(base, STEP), :] = jnp.where(col_in >= base + STEP, 0.0, own_rows)
        return carry

    lax.fori_loop(0, width // STEP, block, 0)


def factor_scratch(systems, width):
    team = max(n for n in range(1, 128 // STEP + 1) if systems % n == 0)
    return [pltpu.VMEM((systems // team, team * STEP, width), jnp.float32)] * 2


def scaled(matrix):
    factor_of = 1.0 / jnp.max(jnp.max(matrix, axis=1, keepdims=True), axis=0, keepdims=True)
    return matrix * factor_of, jnp.sqrt(factor_of)


def pick_kernel(slot_ref, tiles_ref, *refs):
    out_refs, sems = refs[:-1], refs[-1]
    copies = []
    for e, out_ref in enumerate(out_refs):
        source = tiles_ref.at[jnp.maximum(slot_ref[e], 0), 0:2]
        copies.append(pltpu.make_async_copy(source, out_ref, sems.at[e]))
    for copy in copies:
        copy.start()
    for copy in copies:
        copy.wait()


def own_kernel(counts_ref, tiles_ref, w_ref, z_ref, g_ref, *scratch):
    systems, kslots, width, _ = tiles_ref.shape
    for s in range(systems):
        near = tiles_ref[s, 0:2].reshape(2 * width, width)
        g_ref[s] = dot(near, near, TN)
    for s in range(systems):
        for k in range(2, kslots):
            @pl.when(k < counts_ref[s])
            def _():
                tile = tiles_ref[s, k]
                g_ref[s] += dot(tile, tile, TN)
    roots = []
    for s in range(systems):
        g_ref[s], root = scaled(g_ref[s])
        roots.append(root)
    factor(g_ref, *scratch)
    for s in range(systems):
        w = split3(g_ref[s] * roots[s])
        w_ref[s, 0] = w[0]
        w_ref[s, 1] = w[1]
        own = jnp.concatenate([tiles_ref[s, 1], tiles_ref[s, 0]], axis=0)
        z = split3(dot(w[0], own, NT) + (dot(w[1], own, NT) + dot(w[2], own, NT)))
        for i in range(3):
            z_ref[s, i] = z[i]


def collect(slot_ref, shifts, got_refs, near_ref, sems):
    spare = near_ref.shape[0] - len(shifts)
    copies = []
    for i, (e, got_ref) in enumerate(zip(shifts, got_refs)):
        slot = jnp.where(slot_ref[e - 1] >= 0, slot_ref[e - 1], spare + i)
        copies.append(pltpu.make_async_copy(got_ref, near_ref.at[slot], sems.at[i]))
    for copy in copies:
        copy.start()
    return copies


def schur(near, z):
    near_t = near.T
    v = split3(dot(near_t, z[0], NT) + (dot(near_t, z[1], NT) + dot(near_t, z[2], NT)))
    return v, dot(near_t, near, NN) - dot6(v, v, NT)


def link_kernel(shifts, slot_ref, z_any, *refs):
    got_refs, refs = refs[:len(shifts)], refs[len(shifts):]
    v_ref, t_ref, z_ref, near_ref, z_sems, sems = refs
    systems, _, width, _ = z_ref.shape
    for s in range(systems):
        near_ref[s] = jnp.zeros(near_ref.shape[1:], near_ref.dtype)
    copies = collect(slot_ref, shifts, got_refs, near_ref, sems)
    z_copies = [pltpu.make_async_copy(z_any.at[s], z_ref.at[s], z_sems.at[s]) for s in range(systems)]
    for copy in z_copies:
        copy.start()
    for copy in copies:
        copy.wait()
    for s in range(systems):
        z_copies[s].wait()
        v, t_ref[s] = schur(near_ref[s].reshape(2 * width, width), [z_ref[s, i] for i in range(3)])
        v_ref[s, 0] = v[0]
        v_ref[s, 1] = v[1]


def pair_kernel(lanes, shifts, late, place_ref, slot_ref, x_ref, w_any, z_any, v_any, t_any, *refs):
    got_refs, up_refs, refs = refs[:len(shifts)], refs[len(shifts):len(shifts) + lanes], refs[len(shifts) + lanes:]
    low_ref, near_ref, w_ref, z_ref, zj_ref, v_ref, t_ref, r_ref, first_ref, near_sems, sems, *scratch = refs
    _, _, width, _ = z_ref.shape
    systems = first_ref.shape[0]
    count = x_ref.shape[0] // lanes
    near_copies = collect(slot_ref, shifts, got_refs, near_ref, near_sems)
    late_slots = [slot_ref[e - 1] for e in late]
    copies = [
        pltpu.make_async_copy(z_any.at[jnp.maximum(slot, 0)], z_ref.at[i], sems.at[i]) for i, slot in enumerate(late_slots)
    ] + [
        pltpu.make_async_copy(t_any, t_ref.at[0:systems], sems.at[2]),
        pltpu.make_async_copy(v_any, v_ref.at[0:systems], sems.at[3]),
        pltpu.make_async_copy(z_any.at[:, 0:2, :, width:], zj_ref, sems.at[4]),
    ]
    w_copy = pltpu.make_async_copy(w_any, w_ref, sems.at[5])
    for copy in copies + [w_copy]:
        copy.start()
    low_ref[...] = jnp.zeros(low_ref.shape, low_ref.dtype)
    for copy in near_copies + copies[:-1]:
        copy.wait()
    for i, slot in enumerate(late_slots):
        at = jnp.where(slot >= 0, slot, systems + i)
        near = near_ref[jnp.maximum(slot, 0)].reshape(2 * width, width)
        v, t_ref[at] = schur(near, [z_ref[i, p] for p in range(3)])
        v_ref[at, 0] = v[0]
        v_ref[at, 1] = v[1]
    copies[-1].wait()
    roots = []
    for s in range(systems):
        x = x_ref[:, s * width:(s + 1) * width]
        first_ref[s] = dot(x, zj_ref[s, 0], NT) + dot(x, zj_ref[s, 1], NT)
        r_ref[s] = dot(x, near_ref[s, 1], NN)
    for s in range(systems):
        r_ref[s] = r_ref[s] - apply(first_ref[s], (v_ref[s, 0], v_ref[s, 1]), NT)
        t_ref[s], root = scaled(t_ref[s])
        roots.append(root)
    factor(t_ref.at[0:systems], *scratch)
    w_copy.wait()
    parts = [split3(t_ref[s] * roots[s])[:2] for s in range(systems)]
    half = [apply(r_ref[s], parts[s], NT) for s in range(systems)]
    last = [apply(half[s], parts[s], NN) for s in range(systems)]
    mid = [first_ref[s] - apply(last[s], (v_ref[s, 0], v_ref[s, 1]), NN) for s in range(systems)]
    for s in range(systems):
        up = apply(mid[s], (w_ref[s, 0], w_ref[s, 1]), NN)
        for e in range(lanes):
            up_refs[e][s] = up[e * count:(e + 1) * count]
            owner = lax.rem(place_ref[systems] + e, lanes)
            low_ref[place_ref[s] * lanes + owner] = last[s][e * count:(e + 1) * count].astype(low_ref.dtype)


def place_kernel(lanes, place_ref, low_ref, *refs):
    up_refs, out_ref = refs[:lanes], refs[lanes]
    systems, _, width = up_refs[0].shape
    for e in range(lanes):
        owner = lax.rem(place_ref[systems * lanes] + lanes - e, lanes)
        for s in range(systems):
            at = owner * systems + s
            total = up_refs[e][s] + low_ref[place_ref[at] * lanes + owner].astype(jnp.float32)
            out_ref[:, pl.ds(pl.multiple_of(at * width, width), width)] = total.astype(out_ref.dtype)


def on_device(tiles, pattern, counts, inputs):
    shards = lax.axis_size("panel")
    lanes = lax.axis_size("rhs")
    systems, kslots, width, _ = tiles.shape
    nrhs_dev = inputs.shape[0]
    own_width = systems * width
    my_panel = lax.axis_index("panel")
    my_lane = lax.axis_index("rhs")
    per_panel = systems * lanes
    own_cnt = lax.dynamic_slice_in_dim(counts, my_panel * per_panel + my_lane * systems, systems, 0)
    panel_mates = lax.dynamic_slice(pattern, (my_panel * per_panel, 1), (per_panel, 1))[:, 0] // per_panel
    mate_panel = lax.dynamic_slice_in_dim(panel_mates, my_lane * systems, systems, 0)
    hops = jnp.arange(1, shards, dtype=jnp.int32)

    def slots(panels):
        hit = mate_panel[None, :] == panels[:, None]
        return jnp.max(jnp.where(hit, jnp.arange(systems, dtype=jnp.int32)[None, :], -1), axis=1)

    lane_word = my_lane[None].astype(jnp.int32)

    def shift(value, axis, by):
        size = lax.axis_size(axis)
        return lax.ppermute(value, axis, [(i, (i + by) % size) for i in range(size)])

    vmem = pl.BlockSpec(memory_space=pltpu.VMEM)
    smem = pl.BlockSpec(memory_space=pltpu.SMEM)
    anywhere = pl.BlockSpec(memory_space=pl.ANY)
    params = pltpu.CompilerParams(vmem_limit_bytes=48 * 1024 * 1024)
    pairs = shards - 1
    every = tuple(range(1, shards))
    late = (1, shards - 1)
    early = tuple(sorted((e for e in every if e not in late), key=lambda e: abs(2 * e - shards)))
    most = pltpu.CompilerParams(vmem_limit_bytes=60 * 1024 * 1024)
    pieces = pl.pallas_call(
        pick_kernel,
        out_shape=[jax.ShapeDtypeStruct((2, width, width), jnp.bfloat16)] * pairs,
        in_specs=[smem, anywhere],
        out_specs=[vmem] * pairs,
        scratch_shapes=[pltpu.SemaphoreType.DMA((pairs,))],
        compiler_params=most,
    )(slots((my_panel + hops) % shards), tiles)
    received = {e: shift(pieces[e - 1], "panel", e) for e in early}

    w, z = pl.pallas_call(
        own_kernel,
        out_shape=(
            jax.ShapeDtypeStruct((systems, 2, width, width), jnp.bfloat16),
            jax.ShapeDtypeStruct((systems, 3, width, 2 * width), jnp.bfloat16),
        ),
        in_specs=[smem, vmem],
        out_specs=(vmem, vmem),
        scratch_shapes=[pltpu.VMEM((systems, width, width), jnp.float32)] + factor_scratch(systems, width),
        compiler_params=params,
        cost_estimate=pl.CostEstimate(flops=30 * 10**9, bytes_accessed=8 * 10**6, transcendentals=0),
    )(own_cnt, tiles)

    inputs, w = lax.optimization_barrier((inputs, w))
    x = lax.all_to_all(inputs, "rhs", split_axis=1, concat_axis=0, tiled=True)
    x = lax.dynamic_slice_in_dim(jnp.concatenate([x, x], axis=0), my_lane * nrhs_dev, lanes * nrhs_dev, 0)

    come = [received[e] for e in early]
    held, z, come = lax.optimization_barrier(([pieces[e - 1] for e in late], z, come))
    received.update(zip(early, come))
    received.update({e: shift(piece, "panel", e) for e, piece in zip(late, held)})
    from_slot = slots((my_panel - hops) % shards)
    v, t = pl.pallas_call(
        functools.partial(link_kernel, early),
        out_shape=(
            jax.ShapeDtypeStruct((systems, 2, width, width), jnp.bfloat16),
            jax.ShapeDtypeStruct((systems, width, width), jnp.float32),
        ),
        in_specs=[smem] + [anywhere] * (1 + len(early)),
        out_specs=(vmem, vmem),
        scratch_shapes=[
            pltpu.VMEM((systems, 3, width, 2 * width), jnp.bfloat16),
            pltpu.VMEM((systems + len(early), 2, width, width), jnp.bfloat16),
            pltpu.SemaphoreType.DMA((systems,)),
            pltpu.SemaphoreType.DMA((len(early),)),
        ],
        compiler_params=params,
        cost_estimate=pl.CostEstimate(flops=12 * 10**9, bytes_accessed=8 * 10**6, transcendentals=0),
    )(from_slot, z, *[received[e] for e in early])

    nrhs = lanes * nrhs_dev
    piece = jax.ShapeDtypeStruct((systems, nrhs_dev, width), jnp.float32)
    *up, low = pl.pallas_call(
        functools.partial(pair_kernel, lanes, every, late),
        out_shape=[piece] * lanes + [jax.ShapeDtypeStruct((shards * lanes, nrhs_dev, width), jnp.bfloat16)],
        in_specs=[smem, smem, vmem] + [anywhere] * (4 + pairs),
        out_specs=[vmem] * (lanes + 1),
        scratch_shapes=[
            pltpu.VMEM((systems + pairs, 2, width, width), jnp.bfloat16),
            pltpu.VMEM((systems, 2, width, width), jnp.bfloat16),
            pltpu.VMEM((len(late), 3, width, 2 * width), jnp.bfloat16),
            pltpu.VMEM((systems, 2, width, width), jnp.bfloat16),
            pltpu.VMEM((systems + len(late), 2, width, width), jnp.bfloat16),
            pltpu.VMEM((systems + len(late), width, width), jnp.float32),
            pltpu.VMEM((systems, nrhs, width), jnp.float32),
            pltpu.VMEM((systems, nrhs, width), jnp.float32),
            pltpu.SemaphoreType.DMA((pairs,)),
            pltpu.SemaphoreType.DMA((6,)),
        ] + factor_scratch(systems, width),
        compiler_params=params,
    )(
        jnp.concatenate([mate_panel, lane_word]), from_slot, x, w, z, v, t,
        *[received[e] for e in every],
    )
    low = lax.all_to_all(low, ("panel", "rhs"), split_axis=0, concat_axis=0, tiled=True)
    up = [up[0]] + [shift(up[e], "rhs", e) for e in range(1, lanes)]
    return pl.pallas_call(
        functools.partial(place_kernel, lanes),
        out_shape=jax.ShapeDtypeStruct((nrhs_dev, per_panel * width), jnp.bfloat16),
        in_specs=[smem] + [vmem] * (lanes + 1),
        out_specs=vmem,
    )(jnp.concatenate([panel_mates, lane_word]), low, *up)


def solution(mesh):
    return jax.shard_map(
        on_device,
        mesh=mesh,
        in_specs=(P(("panel", "rhs"), None, None, None), P(), P(), P("rhs", "panel")),
        out_specs=P("rhs", "panel"),
        check_vma=False,
    )
```

```python
import functools
import jax
import jax.numpy as jnp
from jax import lax
from jax.experimental import pallas as pl
from jax.experimental.pallas import tpu as pltpu
from jax.sharding import PartitionSpec as P

STEP = 32
ROUND = 8
NT = (((1,), (1,)), ((), ()))
NN = (((1,), (0,)), ((), ()))
TN = (((0,), (0,)), ((), ()))


def dot(a, b, dims):
    return lax.dot_general(a, b, dims, preferred_element_type=jnp.float32)


def split3(a):
    one = a.astype(jnp.bfloat16)
    rest = a - one.astype(jnp.float32)
    two = rest.astype(jnp.bfloat16)
    three = (rest - two.astype(jnp.float32)).astype(jnp.bfloat16)
    return one, two, three


def dot6(a, b, dims):
    a1, a2, a3 = a
    b1, b2, b3 = b
    small = dot(a1, b3, dims) + dot(a3, b1, dims) + dot(a2, b2, dims)
    return dot(a1, b1, dims) + ((dot(a1, b2, dims) + dot(a2, b1, dims)) + small)


def wide(parts):
    one, two, three = parts
    return jnp.concatenate([one, one, two, two, one, three], axis=1)


def deep(parts):
    one, two, three = parts
    return jnp.concatenate([one, two, one, two, three, one], axis=0)


def thirds(array):
    count = array.shape[0] // 3
    return array[:count] + (array[count:2 * count] + array[2 * count:])


def apply(rows, parts, dims):
    count = rows.shape[0]
    stack = jnp.concatenate(split3(rows), axis=0)
    high = dot(stack, parts[0], dims)
    low = dot(stack[:2 * count], parts[1], dims)
    return high[:count] + ((high[count:2 * count] + low[:count]) + (high[2 * count:] + low[count:]))


def factor(ref, slab_ref, past_ref):
    systems, width, _ = ref.shape
    teams, height, _ = slab_ref.shape
    team = height // STEP
    groups = STEP // 8
    lane = lax.broadcasted_iota(jnp.int32, (8, 128), 1)
    sub = lax.broadcasted_iota(jnp.int32, (8, 128), 0)
    member = lane // STEP
    place = lane % STEP
    col_in = lax.broadcasted_iota(jnp.int32, (STEP, width), 1)
    row_all = lax.broadcasted_iota(jnp.int32, (width, width), 0)
    col_all = lax.broadcasted_iota(jnp.int32, (width, width), 1)
    row_team = lax.broadcasted_iota(jnp.int32, (height, width), 0)
    col_team = lax.broadcasted_iota(jnp.int32, (height, width), 1)
    row_diag = lax.broadcasted_iota(jnp.int32, (height, 128), 0)
    col_diag = lax.broadcasted_iota(jnp.int32, (height, 128), 1)
    same = row_diag // STEP == col_diag // STEP
    lower = same & (col_diag <= row_diag)

    def spread(row):
        return jnp.broadcast_to(row, (8, 128))

    def padded(parts):
        if height == 128:
            return parts
        filler = jnp.zeros((128 - height, width), jnp.bfloat16)
        return [jnp.concatenate([part, filler], axis=0) for part in parts]

    def pivots(packs, pieces):
        placed = 0
        for first in range(0, STEP, ROUND):
            top, start = first // 8, first % 8
            tall = range(top, groups)
            own = (place >= first) & (place < first + ROUND)
            one = jnp.where(place - 8 * top == sub, 1.0, 0.0)
            each = range(len(packs))
            if start == 0:
                inverses = [None for _ in each]
            u = [
                [{g: jnp.take_along_axis(x[g], lane - place + (first + q), axis=1) for g in tall} for q in range(ROUND)]
                for x in packs
            ]
            a = [{(i, j): spread(u[s][j][top][start + i:start + i + 1, :]) for j in range(ROUND) for i in range(j + 1)} for s in each]
            for x in packs:
                for g in tall:
                    x[g] = jnp.where(own, one if g == top else 0.0, x[g])
            y = [[spread(x[top][start + q:start + q + 1, :]) for q in range(ROUND)] for x in packs]
            low = [{} for _ in each]
            inv = [[None] * ROUND for _ in each]
            for p in range(0, ROUND, 2):
                n = p + 1
                delta = [a[s][p, p] * a[s][n, n] - a[s][p, n] * a[s][p, n] for s in each]
                for s in each:
                    inv[s][p] = pl.reciprocal(a[s][p, p], approx=True)
                    inv[s][n] = pl.reciprocal(delta[s], approx=True) * a[s][p, p]
                for j in range(n, ROUND):
                    for s in each:
                        low[s][j, p] = a[s][p, j] * inv[s][p]
                for j in range(n + 1, ROUND):
                    for s in each:
                        a[s][n, j] = a[s][n, j] - low[s][n, p] * a[s][p, j]
                for j in range(n + 1, ROUND):
                    for s in each:
                        low[s][j, n] = a[s][n, j] * inv[s][n]
                for i in range(n + 1, ROUND):
                    for j in range(i, ROUND):
                        for s in each:
                            a[s][i, j] = (a[s][i, j] - low[s][i, p] * a[s][p, j]) - low[s][i, n] * a[s][n, j]
            for q in range(ROUND):
                at = start + q
                for s in each:
                    for k in range(q):
                        for g in tall:
                            u[s][q][g] = u[s][q][g] - u[s][k][g] * low[s][q, k]
                        y[s][q] = y[s][q] - y[s][k] * low[s][q, k]
                    inverses[s] = inv[s][q] if at == 0 else jnp.where(sub >= at, inv[s][q], inverses[s])
                    for g in tall:
                        m = u[s][q][g] * inv[s][q]
                        if g == top:
                            m = jnp.where(sub > at, m, 0.0)
                        packs[s][g] = packs[s][g] - m * y[s][q]
                while placed * STEP < (first + q + 1) * len(pieces):
                    pieces[placed]()
                    placed += 1
            if start + ROUND == 8:
                for s, x in enumerate(packs):
                    x[top] = x[top] * (inverses[s] * lax.rsqrt(inverses[s]))

    for t in range(teams):
        for i in range(team):
            slab_ref[t, i * STEP:(i + 1) * STEP] = ref[t * team + i, 0:STEP]
        past_ref[t] = jnp.zeros(past_ref.shape[1:], past_ref.dtype)

    def block(kb, carry):
        base = pl.multiple_of(kb * STEP, STEP)
        after = pl.multiple_of(jnp.minimum(base + STEP, width - STEP), STEP)
        done = (col_all >= base - STEP) & (col_all < base) & (row_all >= base + STEP)
        pieces = []
        for s in range(systems):
            held = {}

            def prepare(s=s, held=held):
                i = s % team
                p1, p2, p3 = split3(past_ref[s // team, i * STEP:(i + 1) * STEP])
                zero = jnp.zeros_like(p1)
                m1, m2, m3 = (jnp.where(col_in >= base + STEP, p, zero) for p in (p1, p2, p3))
                held["left"] = jnp.concatenate([m1, m1, m2, m2, m1, m3], axis=0)
                held["right"] = jnp.concatenate([p1, p2, p1, p2, p3, p1], axis=0)

            def trail(at, s=s, held=held):
                rows = slice(at, at + 128)
                update = dot(held["left"][:, rows], held["right"], TN)
                ref[s, rows] = jnp.where(done[rows], 0.0, ref[s, rows]) - update

            pieces.append(prepare)
            pieces.extend(functools.partial(trail, at) for at in range(0, width, 128))
        packs = []
        for t in range(teams):
            pack = []
            for g in range(groups):
                x = jnp.where(place - 8 * g == sub, 1.0, 0.0)
                for i in range(team):
                    piece = slab_ref[t, i * STEP + 8 * g:i * STEP + 8 * g + 8, 0:128]
                    if i > 0:
                        piece = pltpu.roll(piece, i * STEP, 1)
                    x = jnp.where(member == i, piece, x)
                pack.append(x)
            packs.append(pack)
        sides = []
        for t in range(teams):
            ident = jnp.where(col_team == row_team % STEP, 1.0, 0.0)
            sides.append(deep(padded(split3(jnp.where(col_team < STEP, ident, slab_ref[t])))))
        pivots(packs, pieces)
        for t in range(teams):
            inner = jnp.concatenate(packs[t], axis=0)
            inner = jnp.where(lower, jnp.concatenate([inner] * team, axis=0), 0.0)
            slab = dot(wide(split3(inner)), sides[t], NN)
            ahead = []
            for i in range(team):
                piece = slab[i * STEP:(i + 1) * STEP, 0:128]
                if i != 1:
                    piece = pltpu.roll(piece, (i - 1) * STEP % 128, 1)
                ahead.append(piece)
            ahead = jnp.where(same, jnp.concatenate(ahead, axis=0), 0.0)
            if height < 128:
                ahead = jnp.concatenate([ahead, jnp.zeros((128 - height, 128), jnp.float32)], axis=0)
            ahead = wide(split3(ahead.T[:height]))
            update = dot(ahead, deep(padded(split3(pltpu.roll(slab, width - STEP, 1)))), NN)
            coming = [pltpu.roll(ref[t * team + i, pl.ds(after, STEP), :], width - after, 1) for i in range(team)]
            slab_ref[t] = jnp.where(col_team >= width - STEP, 0.0, jnp.concatenate(coming, axis=0)) - update
            slab = pltpu.roll(slab, base, 1)
            past_ref[t] = slab
            for i in range(team):
                own_rows = slab[i * STEP:(i + 1) * STEP]
                ref[t * team + i, pl.ds(base, STEP), :] = jnp.where(col_in >= base + STEP, 0.0, own_rows)
        return carry

    lax.fori_loop(0, width // STEP, block, 0)


def factor_scratch(systems, width):
    team = max(n for n in range(1, 128 // STEP + 1) if systems % n == 0)
    return [pltpu.VMEM((systems // team, team * STEP, width), jnp.float32)] * 2


def scaled(matrix):
    factor_of = 1.0 / jnp.max(jnp.max(matrix, axis=1, keepdims=True), axis=0, keepdims=True)
    return matrix * factor_of, jnp.sqrt(factor_of)


def pick_kernel(slot_ref, tiles_ref, *refs):
    out_refs, sems = refs[:-1], refs[-1]
    copies = []
    for e, out_ref in enumerate(out_refs):
        source = tiles_ref.at[jnp.maximum(slot_ref[e], 0), 0:2]
        copies.append(pltpu.make_async_copy(source, out_ref, sems.at[e]))
    for copy in copies:
        copy.start()
    for copy in copies:
        copy.wait()


def own_kernel(counts_ref, tiles_ref, w_ref, z_ref, g_ref, *scratch):
    systems, kslots, width, _ = tiles_ref.shape
    for s in range(systems):
        near = tiles_ref[s, 0:2].reshape(2 * width, width)
        g_ref[s] = dot(near, near, TN)
    for s in range(systems):
        for k in range(2, kslots):
            @pl.when(k < counts_ref[s])
            def _():
                tile = tiles_ref[s, k]
                g_ref[s] += dot(tile, tile, TN)
    roots = []
    for s in range(systems):
        g_ref[s], root = scaled(g_ref[s])
        roots.append(root)
    factor(g_ref, *scratch)
    for s in range(systems):
        w = split3(g_ref[s] * roots[s])
        w_ref[s, 0] = w[0]
        w_ref[s, 1] = w[1]
        own = jnp.concatenate([tiles_ref[s, 1], tiles_ref[s, 0]], axis=0)
        z = split3(dot(w[0], own, NT) + (dot(w[1], own, NT) + dot(w[2], own, NT)))
        for i in range(3):
            z_ref[s, i] = z[i]


def collect(slot_ref, shifts, got_refs, near_ref, sems):
    spare = near_ref.shape[0] - len(shifts)
    copies = []
    for i, (e, got_ref) in enumerate(zip(shifts, got_refs)):
        slot = jnp.where(slot_ref[e - 1] >= 0, slot_ref[e - 1], spare + i)
        copies.append(pltpu.make_async_copy(got_ref, near_ref.at[slot], sems.at[i]))
    for copy in copies:
        copy.start()
    return copies


def schur(near, z):
    near_t = near.T
    v = split3(dot(near_t, z[0], NT) + (dot(near_t, z[1], NT) + dot(near_t, z[2], NT)))
    return v, dot(near_t, near, NN) - dot6(v, v, NT)


def link_kernel(shifts, slot_ref, z_any, *refs):
    got_refs, refs = refs[:len(shifts)], refs[len(shifts):]
    v_ref, t_ref, z_ref, near_ref, z_sems, sems = refs
    systems, _, width, _ = z_ref.shape
    for s in range(systems):
        near_ref[s] = jnp.zeros(near_ref.shape[1:], near_ref.dtype)
    copies = collect(slot_ref, shifts, got_refs, near_ref, sems)
    z_copies = [pltpu.make_async_copy(z_any.at[s], z_ref.at[s], z_sems.at[s]) for s in range(systems)]
    for copy in z_copies:
        copy.start()
    for copy in copies:
        copy.wait()
    for s in range(systems):
        z_copies[s].wait()
        v, t_ref[s] = schur(near_ref[s].reshape(2 * width, width), [z_ref[s, i] for i in range(3)])
        v_ref[s, 0] = v[0]
        v_ref[s, 1] = v[1]


def pair_kernel(lanes, shifts, late, place_ref, slot_ref, x_ref, w_any, z_any, v_any, t_any, *refs):
    got_refs, up_refs, refs = refs[:len(shifts)], refs[len(shifts):len(shifts) + lanes], refs[len(shifts) + lanes:]
    low_ref, near_ref, w_ref, z_ref, zj_ref, v_ref, t_ref, r_ref, first_ref, near_sems, sems, *scratch = refs
    _, _, width, _ = z_ref.shape
    systems = first_ref.shape[0]
    count = x_ref.shape[0] // lanes
    near_copies = collect(slot_ref, shifts, got_refs, near_ref, near_sems)
    late_slots = [slot_ref[e - 1] for e in late]
    copies = [
        pltpu.make_async_copy(z_any.at[jnp.maximum(slot, 0)], z_ref.at[i], sems.at[i]) for i, slot in enumerate(late_slots)
    ] + [
        pltpu.make_async_copy(t_any, t_ref.at[0:systems], sems.at[2]),
        pltpu.make_async_copy(v_any, v_ref.at[0:systems], sems.at[3]),
        pltpu.make_async_copy(z_any.at[:, 0:2, :, width:], zj_ref, sems.at[4]),
    ]
    w_copy = pltpu.make_async_copy(w_any, w_ref, sems.at[5])
    for copy in copies + [w_copy]:
        copy.start()
    low_ref[...] = jnp.zeros(low_ref.shape, low_ref.dtype)
    for copy in near_copies + copies[:-1]:
        copy.wait()
    for i, slot in enumerate(late_slots):
        at = jnp.where(slot >= 0, slot, systems + i)
        near = near_ref[jnp.maximum(slot, 0)].reshape(2 * width, width)
        v, t_ref[at] = schur(near, [z_ref[i, p] for p in range(3)])
        v_ref[at, 0] = v[0]
        v_ref[at, 1] = v[1]
    copies[-1].wait()
    roots = []
    for s in range(systems):
        x = x_ref[:, s * width:(s + 1) * width]
        first_ref[s] = dot(x, zj_ref[s, 0], NT) + dot(x, zj_ref[s, 1], NT)
        r_ref[s] = dot(x, near_ref[s, 1], NN)
    for s in range(systems):
        r_ref[s] = r_ref[s] - apply(first_ref[s], (v_ref[s, 0], v_ref[s, 1]), NT)
        t_ref[s], root = scaled(t_ref[s])
        roots.append(root)
    factor(t_ref.at[0:systems], *scratch)
    w_copy.wait()
    parts = [split3(t_ref[s] * roots[s])[:2] for s in range(systems)]
    half = [apply(r_ref[s], parts[s], NT) for s in range(systems)]
    last = [apply(half[s], parts[s], NN) for s in range(systems)]
    mid = [first_ref[s] - apply(last[s], (v_ref[s, 0], v_ref[s, 1]), NN) for s in range(systems)]
    for s in range(systems):
        up = apply(mid[s], (w_ref[s, 0], w_ref[s, 1]), NN)
        for e in range(lanes):
            up_refs[e][s] = up[e * count:(e + 1) * count]
            owner = lax.rem(place_ref[systems] + e, lanes)
            low_ref[place_ref[s] * lanes + owner] = last[s][e * count:(e + 1) * count].astype(low_ref.dtype)


def place_kernel(lanes, place_ref, low_ref, *refs):
    up_refs, out_ref = refs[:lanes], refs[lanes]
    systems, _, width = up_refs[0].shape
    for e in range(lanes):
        owner = lax.rem(place_ref[systems * lanes] + lanes - e, lanes)
        for s in range(systems):
            at = owner * systems + s
            total = up_refs[e][s] + low_ref[place_ref[at] * lanes + owner].astype(jnp.float32)
            out_ref[:, pl.ds(pl.multiple_of(at * width, width), width)] = total.astype(out_ref.dtype)


def on_device(tiles, pattern, counts, inputs):
    shards = lax.axis_size("panel")
    lanes = lax.axis_size("rhs")
    systems, kslots, width, _ = tiles.shape
    nrhs_dev = inputs.shape[0]
    own_width = systems * width
    my_panel = lax.axis_index("panel")
    my_lane = lax.axis_index("rhs")
    per_panel = systems * lanes
    own_cnt = lax.dynamic_slice_in_dim(counts, my_panel * per_panel + my_lane * systems, systems, 0)
    panel_mates = lax.dynamic_slice(pattern, (my_panel * per_panel, 1), (per_panel, 1))[:, 0] // per_panel
    mate_panel = lax.dynamic_slice_in_dim(panel_mates, my_lane * systems, systems, 0)
    hops = jnp.arange(1, shards, dtype=jnp.int32)

    def slots(panels):
        hit = mate_panel[None, :] == panels[:, None]
        return jnp.max(jnp.where(hit, jnp.arange(systems, dtype=jnp.int32)[None, :], -1), axis=1)

    lane_word = my_lane[None].astype(jnp.int32)

    def shift(value, axis, by):
        size = lax.axis_size(axis)
        return lax.ppermute(value, axis, [(i, (i + by) % size) for i in range(size)])

    vmem = pl.BlockSpec(memory_space=pltpu.VMEM)
    smem = pl.BlockSpec(memory_space=pltpu.SMEM)
    anywhere = pl.BlockSpec(memory_space=pl.ANY)
    params = pltpu.CompilerParams(vmem_limit_bytes=48 * 1024 * 1024)
    pairs = shards - 1
    every = tuple(range(1, shards))
    late = (1, shards - 1)
    early = tuple(e for e in every if e not in late)
    most = pltpu.CompilerParams(vmem_limit_bytes=60 * 1024 * 1024)
    pieces = pl.pallas_call(
        pick_kernel,
        out_shape=[jax.ShapeDtypeStruct((2, width, width), jnp.bfloat16)] * pairs,
        in_specs=[smem, anywhere],
        out_specs=[vmem] * pairs,
        scratch_shapes=[pltpu.SemaphoreType.DMA((pairs,))],
        compiler_params=most,
    )(slots((my_panel + hops) % shards), tiles)
    received = {e: shift(pieces[e - 1], "panel", e) for e in early}

    w, z = pl.pallas_call(
        own_kernel,
        out_shape=(
            jax.ShapeDtypeStruct((systems, 2, width, width), jnp.bfloat16),
            jax.ShapeDtypeStruct((systems, 3, width, 2 * width), jnp.bfloat16),
        ),
        in_specs=[smem, vmem],
        out_specs=(vmem, vmem),
        scratch_shapes=[pltpu.VMEM((systems, width, width), jnp.float32)] + factor_scratch(systems, width),
        compiler_params=params,
        cost_estimate=pl.CostEstimate(flops=30 * 10**9, bytes_accessed=8 * 10**6, transcendentals=0),
    )(own_cnt, tiles)

    come = [received[e] for e in early[:2]]
    held, z, come, inputs = lax.optimization_barrier(([pieces[e - 1] for e in late], z, come, inputs))
    received.update(zip(early, come))
    received.update({e: shift(piece, "panel", e) for e, piece in zip(late, held)})
    x = lax.all_to_all(inputs, "rhs", split_axis=1, concat_axis=0, tiled=True)
    x = lax.dynamic_slice_in_dim(jnp.concatenate([x, x], axis=0), my_lane * nrhs_dev, lanes * nrhs_dev, 0)

    from_slot = slots((my_panel - hops) % shards)
    v, t = pl.pallas_call(
        functools.partial(link_kernel, early),
        out_shape=(
            jax.ShapeDtypeStruct((systems, 2, width, width), jnp.bfloat16),
            jax.ShapeDtypeStruct((systems, width, width), jnp.float32),
        ),
        in_specs=[smem] + [anywhere] * (1 + len(early)),
        out_specs=(vmem, vmem),
        scratch_shapes=[
            pltpu.VMEM((systems, 3, width, 2 * width), jnp.bfloat16),
            pltpu.VMEM((systems + len(early), 2, width, width), jnp.bfloat16),
            pltpu.SemaphoreType.DMA((systems,)),
            pltpu.SemaphoreType.DMA((len(early),)),
        ],
        compiler_params=params,
        cost_estimate=pl.CostEstimate(flops=12 * 10**9, bytes_accessed=8 * 10**6, transcendentals=0),
    )(from_slot, z, *[received[e] for e in early])

    nrhs = lanes * nrhs_dev
    piece = jax.ShapeDtypeStruct((systems, nrhs_dev, width), jnp.float32)
    *up, low = pl.pallas_call(
        functools.partial(pair_kernel, lanes, every, late),
        out_shape=[piece] * lanes + [jax.ShapeDtypeStruct((shards * lanes, nrhs_dev, width), jnp.bfloat16)],
        in_specs=[smem, smem, vmem] + [anywhere] * (4 + pairs),
        out_specs=[vmem] * (lanes + 1),
        scratch_shapes=[
            pltpu.VMEM((systems + pairs, 2, width, width), jnp.bfloat16),
            pltpu.VMEM((systems, 2, width, width), jnp.bfloat16),
            pltpu.VMEM((len(late), 3, width, 2 * width), jnp.bfloat16),
            pltpu.VMEM((systems, 2, width, width), jnp.bfloat16),
            pltpu.VMEM((systems + len(late), 2, width, width), jnp.bfloat16),
            pltpu.VMEM((systems + len(late), width, width), jnp.float32),
            pltpu.VMEM((systems, nrhs, width), jnp.float32),
            pltpu.VMEM((systems, nrhs, width), jnp.float32),
            pltpu.SemaphoreType.DMA((pairs,)),
            pltpu.SemaphoreType.DMA((6,)),
        ] + factor_scratch(systems, width),
        compiler_params=params,
    )(
        jnp.concatenate([mate_panel, lane_word]), from_slot, x, w, z, v, t,
        *[received[e] for e in every],
    )
    low = lax.all_to_all(low, ("panel", "rhs"), split_axis=0, concat_axis=0, tiled=True)
    up = [up[0]] + [shift(up[e], "rhs", e) for e in range(1, lanes)]
    return pl.pallas_call(
        functools.partial(place_kernel, lanes),
        out_shape=jax.ShapeDtypeStruct((nrhs_dev, per_panel * width), jnp.bfloat16),
        in_specs=[smem] + [vmem] * (lanes + 1),
        out_specs=vmem,
    )(jnp.concatenate([panel_mates, lane_word]), low, *up)


def solution(mesh):
    return jax.shard_map(
        on_device,
        mesh=mesh,
        in_specs=(P(("panel", "rhs"), None, None, None), P(), P(), P("rhs", "panel")),
        out_specs=P("rhs", "panel"),
        check_vma=False,
    )
```

```python
import functools
import jax
import jax.numpy as jnp
from jax import lax
from jax.experimental import pallas as pl
from jax.experimental.pallas import tpu as pltpu
from jax.sharding import PartitionSpec as P

STEP = 32
ROUND = 8
NT = (((1,), (1,)), ((), ()))
NN = (((1,), (0,)), ((), ()))
TN = (((0,), (0,)), ((), ()))


def dot(a, b, dims):
    return lax.dot_general(a, b, dims, preferred_element_type=jnp.float32)


def split3(a):
    one = a.astype(jnp.bfloat16)
    rest = a - one.astype(jnp.float32)
    two = rest.astype(jnp.bfloat16)
    three = (rest - two.astype(jnp.float32)).astype(jnp.bfloat16)
    return one, two, three


def dot6(a, b, dims):
    a1, a2, a3 = a
    b1, b2, b3 = b
    small = dot(a1, b3, dims) + dot(a3, b1, dims) + dot(a2, b2, dims)
    return dot(a1, b1, dims) + ((dot(a1, b2, dims) + dot(a2, b1, dims)) + small)


def wide(parts):
    one, two, three = parts
    return jnp.concatenate([one, one, two, two, one, three], axis=1)


def deep(parts):
    one, two, three = parts
    return jnp.concatenate([one, two, one, two, three, one], axis=0)


def thirds(array):
    count = array.shape[0] // 3
    return array[:count] + (array[count:2 * count] + array[2 * count:])


def apply(rows, parts, dims):
    count = rows.shape[0]
    stack = jnp.concatenate(split3(rows), axis=0)
    high = dot(stack, parts[0], dims)
    low = dot(stack[:2 * count], parts[1], dims)
    return high[:count] + ((high[count:2 * count] + low[:count]) + (high[2 * count:] + low[count:]))


def factor(ref, slab_ref, past_ref):
    systems, width, _ = ref.shape
    teams, height, _ = slab_ref.shape
    team = height // STEP
    groups = STEP // 8
    lane = lax.broadcasted_iota(jnp.int32, (8, 128), 1)
    sub = lax.broadcasted_iota(jnp.int32, (8, 128), 0)
    member = lane // STEP
    place = lane % STEP
    col_in = lax.broadcasted_iota(jnp.int32, (STEP, width), 1)
    row_all = lax.broadcasted_iota(jnp.int32, (width, width), 0)
    col_all = lax.broadcasted_iota(jnp.int32, (width, width), 1)
    row_team = lax.broadcasted_iota(jnp.int32, (height, width), 0)
    col_team = lax.broadcasted_iota(jnp.int32, (height, width), 1)
    row_diag = lax.broadcasted_iota(jnp.int32, (height, 128), 0)
    col_diag = lax.broadcasted_iota(jnp.int32, (height, 128), 1)
    same = row_diag // STEP == col_diag // STEP
    lower = same & (col_diag <= row_diag)

    def spread(row):
        return jnp.broadcast_to(row, (8, 128))

    def padded(parts):
        if height == 128:
            return parts
        filler = jnp.zeros((128 - height, width), jnp.bfloat16)
        return [jnp.concatenate([part, filler], axis=0) for part in parts]

    def pivots(packs, pieces):
        placed = 0
        for first in range(0, STEP, ROUND):
            top, start = first // 8, first % 8
            tall = range(top, groups)
            own = (place >= first) & (place < first + ROUND)
            one = jnp.where(place - 8 * top == sub, 1.0, 0.0)
            each = range(len(packs))
            if start == 0:
                inverses = [None for _ in each]
            u = [
                [{g: jnp.take_along_axis(x[g], lane - place + (first + q), axis=1) for g in tall} for q in range(ROUND)]
                for x in packs
            ]
            a = [{(i, j): spread(u[s][j][top][start + i:start + i + 1, :]) for j in range(ROUND) for i in range(j + 1)} for s in each]
            for x in packs:
                for g in tall:
                    x[g] = jnp.where(own, one if g == top else 0.0, x[g])
            y = [[spread(x[top][start + q:start + q + 1, :]) for q in range(ROUND)] for x in packs]
            low = [{} for _ in each]
            inv = [[None] * ROUND for _ in each]
            for p in range(0, ROUND, 2):
                n = p + 1
                delta = [a[s][p, p] * a[s][n, n] - a[s][p, n] * a[s][p, n] for s in each]
                for s in each:
                    inv[s][p] = pl.reciprocal(a[s][p, p], approx=True)
                    inv[s][n] = pl.reciprocal(delta[s], approx=True) * a[s][p, p]
                for j in range(n, ROUND):
                    for s in each:
                        low[s][j, p] = a[s][p, j] * inv[s][p]
                for j in range(n + 1, ROUND):
                    for s in each:
                        a[s][n, j] = a[s][n, j] - low[s][n, p] * a[s][p, j]
                for j in range(n + 1, ROUND):
                    for s in each:
                        low[s][j, n] = a[s][n, j] * inv[s][n]
                for i in range(n + 1, ROUND):
                    for j in range(i, ROUND):
                        for s in each:
                            a[s][i, j] = (a[s][i, j] - low[s][i, p] * a[s][p, j]) - low[s][i, n] * a[s][n, j]
            for q in range(ROUND):
                at = start + q
                for s in each:
                    for k in range(q):
                        for g in tall:
                            u[s][q][g] = u[s][q][g] - u[s][k][g] * low[s][q, k]
                        y[s][q] = y[s][q] - y[s][k] * low[s][q, k]
                    inverses[s] = inv[s][q] if at == 0 else jnp.where(sub >= at, inv[s][q], inverses[s])
                    for g in tall:
                        m = u[s][q][g] * inv[s][q]
                        if g == top:
                            m = jnp.where(sub > at, m, 0.0)
                        packs[s][g] = packs[s][g] - m * y[s][q]
                while placed * STEP < (first + q + 1) * len(pieces):
                    pieces[placed]()
                    placed += 1
            if start + ROUND == 8:
                for s, x in enumerate(packs):
                    x[top] = x[top] * (inverses[s] * lax.rsqrt(inverses[s]))

    for t in range(teams):
        for i in range(team):
            slab_ref[t, i * STEP:(i + 1) * STEP] = ref[t * team + i, 0:STEP]
        past_ref[t] = jnp.zeros(past_ref.shape[1:], past_ref.dtype)

    def block(kb, carry):
        base = pl.multiple_of(kb * STEP, STEP)
        after = pl.multiple_of(jnp.minimum(base + STEP, width - STEP), STEP)
        done = (col_all >= base - STEP) & (col_all < base) & (row_all >= base + STEP)
        pieces = []
        for s in range(systems):
            held = {}

            def prepare(s=s, held=held):
                i = s % team
                p1, p2, p3 = split3(past_ref[s // team, i * STEP:(i + 1) * STEP])
                zero = jnp.zeros_like(p1)
                m1, m2, m3 = (jnp.where(col_in >= base + STEP, p, zero) for p in (p1, p2, p3))
                held["left"] = jnp.concatenate([m1, m1, m2, m2, m1, m3], axis=0)
                held["right"] = jnp.concatenate([p1, p2, p1, p2, p3, p1], axis=0)

            def trail(at, s=s, held=held):
                rows = slice(at, at + 128)
                update = dot(held["left"][:, rows], held["right"], TN)
                ref[s, rows] = jnp.where(done[rows], 0.0, ref[s, rows]) - update

            pieces.append(prepare)
            pieces.extend(functools.partial(trail, at) for at in range(0, width, 128))
        packs = []
        for t in range(teams):
            pack = []
            for g in range(groups):
                x = jnp.where(place - 8 * g == sub, 1.0, 0.0)
                for i in range(team):
                    piece = slab_ref[t, i * STEP + 8 * g:i * STEP + 8 * g + 8, 0:128]
                    if i > 0:
                        piece = pltpu.roll(piece, i * STEP, 1)
                    x = jnp.where(member == i, piece, x)
                pack.append(x)
            packs.append(pack)
        sides = []
        for t in range(teams):
            ident = jnp.where(col_team == row_team % STEP, 1.0, 0.0)
            sides.append(deep(padded(split3(jnp.where(col_team < STEP, ident, slab_ref[t])))))
        pivots(packs, pieces)
        for t in range(teams):
            inner = jnp.concatenate(packs[t], axis=0)
            inner = jnp.where(lower, jnp.concatenate([inner] * team, axis=0), 0.0)
            slab = dot(wide(split3(inner)), sides[t], NN)
            ahead = []
            for i in range(team):
                piece = slab[i * STEP:(i + 1) * STEP, 0:128]
                if i != 1:
                    piece = pltpu.roll(piece, (i - 1) * STEP % 128, 1)
                ahead.append(piece)
            ahead = jnp.where(same, jnp.concatenate(ahead, axis=0), 0.0)
            if height < 128:
                ahead = jnp.concatenate([ahead, jnp.zeros((128 - height, 128), jnp.float32)], axis=0)
            ahead = wide(split3(ahead.T[:height]))
            update = dot(ahead, deep(padded(split3(pltpu.roll(slab, width - STEP, 1)))), NN)
            coming = [pltpu.roll(ref[t * team + i, pl.ds(after, STEP), :], width - after, 1) for i in range(team)]
            slab_ref[t] = jnp.where(col_team >= width - STEP, 0.0, jnp.concatenate(coming, axis=0)) - update
            slab = pltpu.roll(slab, base, 1)
            past_ref[t] = slab
            for i in range(team):
                own_rows = slab[i * STEP:(i + 1) * STEP]
                ref[t * team + i, pl.ds(base, STEP), :] = jnp.where(col_in >= base + STEP, 0.0, own_rows)
        return carry

    lax.fori_loop(0, width // STEP, block, 0)


def factor_scratch(systems, width):
    team = max(n for n in range(1, 128 // STEP + 1) if systems % n == 0)
    return [pltpu.VMEM((systems // team, team * STEP, width), jnp.float32)] * 2


def scaled(matrix):
    factor_of = 1.0 / jnp.max(jnp.max(matrix, axis=1, keepdims=True), axis=0, keepdims=True)
    return matrix * factor_of, jnp.sqrt(factor_of)


def pick_kernel(slot_ref, tiles_ref, *refs):
    out_refs, sems = refs[:-1], refs[-1]
    copies = []
    for e, out_ref in enumerate(out_refs):
        source = tiles_ref.at[jnp.maximum(slot_ref[e], 0), 0:2]
        copies.append(pltpu.make_async_copy(source, out_ref, sems.at[e]))
    for copy in copies:
        copy.start()
    for copy in copies:
        copy.wait()


def own_kernel(counts_ref, tiles_ref, w_ref, z_ref, g_ref, *scratch):
    systems, kslots, width, _ = tiles_ref.shape
    for s in range(systems):
        near = tiles_ref[s, 0:2].reshape(2 * width, width)
        g_ref[s] = dot(near, near, TN)
    for s in range(systems):
        for k in range(2, kslots):
            @pl.when(k < counts_ref[s])
            def _():
                tile = tiles_ref[s, k]
                g_ref[s] += dot(tile, tile, TN)
    roots = []
    for s in range(systems):
        g_ref[s], root = scaled(g_ref[s])
        roots.append(root)
    factor(g_ref, *scratch)
    for s in range(systems):
        w = split3(g_ref[s] * roots[s])
        w_ref[s, 0] = w[0]
        w_ref[s, 1] = w[1]
        own = jnp.concatenate([tiles_ref[s, 1], tiles_ref[s, 0]], axis=0)
        z = split3(dot(w[0], own, NT) + (dot(w[1], own, NT) + dot(w[2], own, NT)))
        for i in range(3):
            z_ref[s, i] = z[i]


def collect(slot_ref, shifts, got_refs, near_ref, sems):
    spare = near_ref.shape[0] - len(shifts)
    copies = []
    for i, (e, got_ref) in enumerate(zip(shifts, got_refs)):
        slot = jnp.where(slot_ref[e - 1] >= 0, slot_ref[e - 1], spare + i)
        copies.append(pltpu.make_async_copy(got_ref, near_ref.at[slot], sems.at[i]))
    for copy in copies:
        copy.start()
    return copies


def schur(near, z):
    near_t = near.T
    v = split3(dot(near_t, z[0], NT) + (dot(near_t, z[1], NT) + dot(near_t, z[2], NT)))
    return v, dot(near_t, near, NN) - dot6(v, v, NT)


def link_kernel(shifts, slot_ref, z_any, *refs):
    got_refs, refs = refs[:len(shifts)], refs[len(shifts):]
    v_ref, t_ref, z_ref, near_ref, z_sems, sems = refs
    systems, _, width, _ = z_ref.shape
    for s in range(systems):
        near_ref[s] = jnp.zeros(near_ref.shape[1:], near_ref.dtype)
    copies = collect(slot_ref, shifts, got_refs, near_ref, sems)
    z_copies = [pltpu.make_async_copy(z_any.at[s], z_ref.at[s], z_sems.at[s]) for s in range(systems)]
    for copy in z_copies:
        copy.start()
    for copy in copies:
        copy.wait()
    for s in range(systems):
        z_copies[s].wait()
        v, t_ref[s] = schur(near_ref[s].reshape(2 * width, width), [z_ref[s, i] for i in range(3)])
        v_ref[s, 0] = v[0]
        v_ref[s, 1] = v[1]


def pair_kernel(lanes, shifts, late, place_ref, slot_ref, x_ref, w_any, z_any, v_any, t_any, *refs):
    got_refs, up_refs, refs = refs[:len(shifts)], refs[len(shifts):len(shifts) + lanes], refs[len(shifts) + lanes:]
    low_ref, near_ref, w_ref, z_ref, zj_ref, v_ref, t_ref, r_ref, first_ref, near_sems, sems, *scratch = refs
    _, _, width, _ = z_ref.shape
    systems = first_ref.shape[0]
    count = x_ref.shape[0] // lanes
    near_copies = collect(slot_ref, shifts, got_refs, near_ref, near_sems)
    late_slots = [slot_ref[e - 1] for e in late]
    copies = [
        pltpu.make_async_copy(z_any.at[jnp.maximum(slot, 0)], z_ref.at[i], sems.at[i]) for i, slot in enumerate(late_slots)
    ] + [
        pltpu.make_async_copy(t_any, t_ref.at[0:systems], sems.at[2]),
        pltpu.make_async_copy(v_any, v_ref.at[0:systems], sems.at[3]),
        pltpu.make_async_copy(z_any.at[:, 0:2, :, width:], zj_ref, sems.at[4]),
    ]
    w_copy = pltpu.make_async_copy(w_any, w_ref, sems.at[5])
    for copy in copies + [w_copy]:
        copy.start()
    low_ref[...] = jnp.zeros(low_ref.shape, low_ref.dtype)
    for copy in near_copies + copies[:-1]:
        copy.wait()
    for i, slot in enumerate(late_slots):
        at = jnp.where(slot >= 0, slot, systems + i)
        near = near_ref[jnp.maximum(slot, 0)].reshape(2 * width, width)
        v, t_ref[at] = schur(near, [z_ref[i, p] for p in range(3)])
        v_ref[at, 0] = v[0]
        v_ref[at, 1] = v[1]
    copies[-1].wait()
    roots = []
    for s in range(systems):
        x = x_ref[:, s * width:(s + 1) * width]
        first_ref[s] = dot(x, zj_ref[s, 0], NT) + dot(x, zj_ref[s, 1], NT)
        r_ref[s] = dot(x, near_ref[s, 1], NN)
    for s in range(systems):
        r_ref[s] = r_ref[s] - apply(first_ref[s], (v_ref[s, 0], v_ref[s, 1]), NT)
        t_ref[s], root = scaled(t_ref[s])
        roots.append(root)
    factor(t_ref.at[0:systems], *scratch)
    w_copy.wait()
    parts = [split3(t_ref[s] * roots[s])[:2] for s in range(systems)]
    half = [apply(r_ref[s], parts[s], NT) for s in range(systems)]
    last = [apply(half[s], parts[s], NN) for s in range(systems)]
    mid = [first_ref[s] - apply(last[s], (v_ref[s, 0], v_ref[s, 1]), NN) for s in range(systems)]
    for s in range(systems):
        up = apply(mid[s], (w_ref[s, 0], w_ref[s, 1]), NN)
        for e in range(lanes):
            up_refs[e][s] = up[e * count:(e + 1) * count]
            owner = lax.rem(place_ref[systems] + e, lanes)
            low_ref[place_ref[s] * lanes + owner] = last[s][e * count:(e + 1) * count].astype(low_ref.dtype)


def place_kernel(lanes, place_ref, low_ref, *refs):
    up_refs, out_ref = refs[:lanes], refs[lanes]
    systems, _, width = up_refs[0].shape
    for e in range(lanes):
        owner = lax.rem(place_ref[systems * lanes] + lanes - e, lanes)
        for s in range(systems):
            at = owner * systems + s
            total = up_refs[e][s] + low_ref[place_ref[at] * lanes + owner].astype(jnp.float32)
            out_ref[:, pl.ds(pl.multiple_of(at * width, width), width)] = total.astype(out_ref.dtype)


def on_device(tiles, pattern, counts, inputs):
    shards = lax.axis_size("panel")
    lanes = lax.axis_size("rhs")
    systems, kslots, width, _ = tiles.shape
    nrhs_dev = inputs.shape[0]
    own_width = systems * width
    my_panel = lax.axis_index("panel")
    my_lane = lax.axis_index("rhs")
    per_panel = systems * lanes
    own_cnt = lax.dynamic_slice_in_dim(counts, my_panel * per_panel + my_lane * systems, systems, 0)
    panel_mates = lax.dynamic_slice(pattern, (my_panel * per_panel, 1), (per_panel, 1))[:, 0] // per_panel
    mate_panel = lax.dynamic_slice_in_dim(panel_mates, my_lane * systems, systems, 0)
    hops = jnp.arange(1, shards, dtype=jnp.int32)

    def slots(panels):
        hit = mate_panel[None, :] == panels[:, None]
        return jnp.max(jnp.where(hit, jnp.arange(systems, dtype=jnp.int32)[None, :], -1), axis=1)

    lane_word = my_lane[None].astype(jnp.int32)

    def shift(value, axis, by):
        size = lax.axis_size(axis)
        return lax.ppermute(value, axis, [(i, (i + by) % size) for i in range(size)])

    vmem = pl.BlockSpec(memory_space=pltpu.VMEM)
    smem = pl.BlockSpec(memory_space=pltpu.SMEM)
    anywhere = pl.BlockSpec(memory_space=pl.ANY)
    params = pltpu.CompilerParams(vmem_limit_bytes=48 * 1024 * 1024)
    pairs = shards - 1
    every = tuple(range(1, shards))
    late = (1, shards - 1)
    early = tuple(e for e in every if e not in late)
    most = pltpu.CompilerParams(vmem_limit_bytes=60 * 1024 * 1024)
    pieces = pl.pallas_call(
        pick_kernel,
        out_shape=[jax.ShapeDtypeStruct((2, width, width), jnp.bfloat16)] * pairs,
        in_specs=[smem, anywhere],
        out_specs=[vmem] * pairs,
        scratch_shapes=[pltpu.SemaphoreType.DMA((pairs,))],
        compiler_params=most,
    )(slots((my_panel + hops) % shards), tiles)
    received = {e: shift(pieces[e - 1], "panel", e) for e in early}

    w, z = pl.pallas_call(
        own_kernel,
        out_shape=(
            jax.ShapeDtypeStruct((systems, 2, width, width), jnp.bfloat16),
            jax.ShapeDtypeStruct((systems, 3, width, 2 * width), jnp.bfloat16),
        ),
        in_specs=[smem, vmem],
        out_specs=(vmem, vmem),
        scratch_shapes=[pltpu.VMEM((systems, width, width), jnp.float32)] + factor_scratch(systems, width),
        compiler_params=params,
        cost_estimate=pl.CostEstimate(flops=30 * 10**9, bytes_accessed=8 * 10**6, transcendentals=0),
    )(own_cnt, tiles)

    inputs, w = lax.optimization_barrier((inputs, w))
    x = lax.all_to_all(inputs, "rhs", split_axis=1, concat_axis=0, tiled=True)
    x = lax.dynamic_slice_in_dim(jnp.concatenate([x, x], axis=0), my_lane * nrhs_dev, lanes * nrhs_dev, 0)

    come = [received[e] for e in early]
    held, z, come = lax.optimization_barrier(([pieces[e - 1] for e in late], z, come))
    received.update(zip(early, come))
    received.update({e: shift(piece, "panel", e) for e, piece in zip(late, held)})
    from_slot = slots((my_panel - hops) % shards)
    v, t = pl.pallas_call(
        functools.partial(link_kernel, early),
        out_shape=(
            jax.ShapeDtypeStruct((systems, 2, width, width), jnp.bfloat16),
            jax.ShapeDtypeStruct((systems, width, width), jnp.float32),
        ),
        in_specs=[smem] + [anywhere] * (1 + len(early)),
        out_specs=(vmem, vmem),
        scratch_shapes=[
            pltpu.VMEM((systems, 3, width, 2 * width), jnp.bfloat16),
            pltpu.VMEM((systems + len(early), 2, width, width), jnp.bfloat16),
            pltpu.SemaphoreType.DMA((systems,)),
            pltpu.SemaphoreType.DMA((len(early),)),
        ],
        compiler_params=params,
        cost_estimate=pl.CostEstimate(flops=12 * 10**9, bytes_accessed=8 * 10**6, transcendentals=0),
    )(from_slot, z, *[received[e] for e in early])

    nrhs = lanes * nrhs_dev
    piece = jax.ShapeDtypeStruct((systems, nrhs_dev, width), jnp.float32)
    *up, low = pl.pallas_call(
        functools.partial(pair_kernel, lanes, every, late),
        out_shape=[piece] * lanes + [jax.ShapeDtypeStruct((shards * lanes, nrhs_dev, width), jnp.bfloat16)],
        in_specs=[smem, smem, vmem] + [anywhere] * (4 + pairs),
        out_specs=[vmem] * (lanes + 1),
        scratch_shapes=[
            pltpu.VMEM((systems + pairs, 2, width, width), jnp.bfloat16),
            pltpu.VMEM((systems, 2, width, width), jnp.bfloat16),
            pltpu.VMEM((len(late), 3, width, 2 * width), jnp.bfloat16),
            pltpu.VMEM((systems, 2, width, width), jnp.bfloat16),
            pltpu.VMEM((systems + len(late), 2, width, width), jnp.bfloat16),
            pltpu.VMEM((systems + len(late), width, width), jnp.float32),
            pltpu.VMEM((systems, nrhs, width), jnp.float32),
            pltpu.VMEM((systems, nrhs, width), jnp.float32),
            pltpu.SemaphoreType.DMA((pairs,)),
            pltpu.SemaphoreType.DMA((6,)),
        ] + factor_scratch(systems, width),
        compiler_params=params,
    )(
        jnp.concatenate([mate_panel, lane_word]), from_slot, x, w, z, v, t,
        *[received[e] for e in every],
    )
    low = lax.all_to_all(low, ("panel", "rhs"), split_axis=0, concat_axis=0, tiled=True)
    up = [up[0]] + [shift(up[e], "rhs", e) for e in range(1, lanes)]
    return pl.pallas_call(
        functools.partial(place_kernel, lanes),
        out_shape=jax.ShapeDtypeStruct((nrhs_dev, per_panel * width), jnp.bfloat16),
        in_specs=[smem] + [vmem] * (lanes + 1),
        out_specs=vmem,
    )(jnp.concatenate([panel_mates, lane_word]), low, *up)


def solution(mesh):
    return jax.shard_map(
        on_device,
        mesh=mesh,
        in_specs=(P(("panel", "rhs"), None, None, None), P(), P(), P("rhs", "panel")),
        out_specs=P("rhs", "panel"),
        check_vma=False,
    )
```

```python
import functools
import jax
import jax.numpy as jnp
from jax import lax
from jax.experimental import pallas as pl
from jax.experimental.pallas import tpu as pltpu
from jax.sharding import PartitionSpec as P

STEP = 32
ROUND = 8
NT = (((1,), (1,)), ((), ()))
NN = (((1,), (0,)), ((), ()))
TN = (((0,), (0,)), ((), ()))


def dot(a, b, dims):
    return lax.dot_general(a, b, dims, preferred_element_type=jnp.float32)


def split3(a):
    one = a.astype(jnp.bfloat16)
    rest = a - one.astype(jnp.float32)
    two = rest.astype(jnp.bfloat16)
    three = (rest - two.astype(jnp.float32)).astype(jnp.bfloat16)
    return one, two, three


def dot6(a, b, dims):
    a1, a2, a3 = a
    b1, b2, b3 = b
    small = dot(a1, b3, dims) + dot(a3, b1, dims) + dot(a2, b2, dims)
    return dot(a1, b1, dims) + ((dot(a1, b2, dims) + dot(a2, b1, dims)) + small)


def wide(parts):
    one, two, three = parts
    return jnp.concatenate([one, one, two, two, one, three], axis=1)


def deep(parts):
    one, two, three = parts
    return jnp.concatenate([one, two, one, two, three, one], axis=0)


def thirds(array):
    count = array.shape[0] // 3
    return array[:count] + (array[count:2 * count] + array[2 * count:])


def apply(rows, parts, dims):
    count = rows.shape[0]
    stack = jnp.concatenate(split3(rows), axis=0)
    high = dot(stack, parts[0], dims)
    low = dot(stack[:2 * count], parts[1], dims)
    return high[:count] + ((high[count:2 * count] + low[:count]) + (high[2 * count:] + low[count:]))


def factor(ref, slab_ref, past_ref):
    systems, width, _ = ref.shape
    teams, height, _ = slab_ref.shape
    team = height // STEP
    groups = STEP // 8
    lane = lax.broadcasted_iota(jnp.int32, (8, 128), 1)
    sub = lax.broadcasted_iota(jnp.int32, (8, 128), 0)
    member = lane // STEP
    place = lane % STEP
    col_in = lax.broadcasted_iota(jnp.int32, (STEP, width), 1)
    row_all = lax.broadcasted_iota(jnp.int32, (width, width), 0)
    col_all = lax.broadcasted_iota(jnp.int32, (width, width), 1)
    row_team = lax.broadcasted_iota(jnp.int32, (height, width), 0)
    col_team = lax.broadcasted_iota(jnp.int32, (height, width), 1)
    row_diag = lax.broadcasted_iota(jnp.int32, (height, 128), 0)
    col_diag = lax.broadcasted_iota(jnp.int32, (height, 128), 1)
    same = row_diag // STEP == col_diag // STEP
    lower = same & (col_diag <= row_diag)

    def spread(row):
        return jnp.broadcast_to(row, (8, 128))

    def padded(parts):
        if height == 128:
            return parts
        filler = jnp.zeros((128 - height, width), jnp.bfloat16)
        return [jnp.concatenate([part, filler], axis=0) for part in parts]

    def pivots(packs, pieces):
        placed = 0
        for first in range(0, STEP, ROUND):
            top, start = first // 8, first % 8
            tall = range(top, groups)
            own = (place >= first) & (place < first + ROUND)
            one = jnp.where(place - 8 * top == sub, 1.0, 0.0)
            each = range(len(packs))
            if start == 0:
                inverses = [None for _ in each]
            u = [
                [{g: jnp.take_along_axis(x[g], lane - place + (first + q), axis=1) for g in tall} for q in range(ROUND)]
                for x in packs
            ]
            a = [{(i, j): spread(u[s][j][top][start + i:start + i + 1, :]) for j in range(ROUND) for i in range(j + 1)} for s in each]
            for x in packs:
                for g in tall:
                    x[g] = jnp.where(own, one if g == top else 0.0, x[g])
            y = [[spread(x[top][start + q:start + q + 1, :]) for q in range(ROUND)] for x in packs]
            low = [{} for _ in each]
            inv = [[None] * ROUND for _ in each]
            for p in range(0, ROUND, 2):
                n = p + 1
                delta = [a[s][p, p] * a[s][n, n] - a[s][p, n] * a[s][p, n] for s in each]
                for s in each:
                    inv[s][p] = pl.reciprocal(a[s][p, p], approx=True)
                    inv[s][n] = pl.reciprocal(delta[s], approx=True) * a[s][p, p]
                for j in range(n, ROUND):
                    for s in each:
                        low[s][j, p] = a[s][p, j] * inv[s][p]
                for j in range(n + 1, ROUND):
                    for s in each:
                        a[s][n, j] = a[s][n, j] - low[s][n, p] * a[s][p, j]
                for j in range(n + 1, ROUND):
                    for s in each:
                        low[s][j, n] = a[s][n, j] * inv[s][n]
                for i in range(n + 1, ROUND):
                    for j in range(i, ROUND):
                        for s in each:
                            a[s][i, j] = (a[s][i, j] - low[s][i, p] * a[s][p, j]) - low[s][i, n] * a[s][n, j]
            for q in range(ROUND):
                at = start + q
                for s in each:
                    for k in range(q):
                        for g in tall:
                            u[s][q][g] = u[s][q][g] - u[s][k][g] * low[s][q, k]
                        y[s][q] = y[s][q] - y[s][k] * low[s][q, k]
                    inverses[s] = inv[s][q] if at == 0 else jnp.where(sub >= at, inv[s][q], inverses[s])
                    for g in tall:
                        m = u[s][q][g] * inv[s][q]
                        if g == top:
                            m = jnp.where(sub > at, m, 0.0)
                        packs[s][g] = packs[s][g] - m * y[s][q]
                while placed * STEP < (first + q + 1) * len(pieces):
                    pieces[placed]()
                    placed += 1
            if start + ROUND == 8:
                for s, x in enumerate(packs):
                    x[top] = x[top] * (inverses[s] * lax.rsqrt(inverses[s]))

    for t in range(teams):
        for i in range(team):
            slab_ref[t, i * STEP:(i + 1) * STEP] = ref[t * team + i, 0:STEP]
        past_ref[t] = jnp.zeros(past_ref.shape[1:], past_ref.dtype)

    def block(kb, carry):
        base = pl.multiple_of(kb * STEP, STEP)
        after = pl.multiple_of(jnp.minimum(base + STEP, width - STEP), STEP)
        done = (col_all >= base - STEP) & (col_all < base) & (row_all >= base + STEP)
        pieces = []
        for s in range(systems):
            held = {}

            def prepare(s=s, held=held):
                i = s % team
                p1, p2, p3 = split3(past_ref[s // team, i * STEP:(i + 1) * STEP])
                zero = jnp.zeros_like(p1)
                m1, m2, m3 = (jnp.where(col_in >= base + STEP, p, zero) for p in (p1, p2, p3))
                held["left"] = jnp.concatenate([m1, m1, m2, m2, m1, m3], axis=0)
                held["right"] = jnp.concatenate([p1, p2, p1, p2, p3, p1], axis=0)

            def trail(at, s=s, held=held):
                rows = slice(at, at + 128)
                update = dot(held["left"][:, rows], held["right"], TN)
                ref[s, rows] = jnp.where(done[rows], 0.0, ref[s, rows]) - update

            pieces.append(prepare)
            pieces.extend(functools.partial(trail, at) for at in range(0, width, 128))
        packs = []
        for t in range(teams):
            pack = []
            for g in range(groups):
                x = jnp.where(place - 8 * g == sub, 1.0, 0.0)
                for i in range(team):
                    piece = slab_ref[t, i * STEP + 8 * g:i * STEP + 8 * g + 8, 0:128]
                    if i > 0:
                        piece = pltpu.roll(piece, i * STEP, 1)
                    x = jnp.where(member == i, piece, x)
                pack.append(x)
            packs.append(pack)
        sides = []
        for t in range(teams):
            ident = jnp.where(col_team == row_team % STEP, 1.0, 0.0)
            sides.append(deep(padded(split3(jnp.where(col_team < STEP, ident, slab_ref[t])))))
        pivots(packs, pieces)
        for t in range(teams):
            inner = jnp.concatenate(packs[t], axis=0)
            inner = jnp.where(lower, jnp.concatenate([inner] * team, axis=0), 0.0)
            slab = dot(wide(split3(inner)), sides[t], NN)
            ahead = []
            for i in range(team):
                piece = slab[i * STEP:(i + 1) * STEP, 0:128]
                if i != 1:
                    piece = pltpu.roll(piece, (i - 1) * STEP % 128, 1)
                ahead.append(piece)
            ahead = jnp.where(same, jnp.concatenate(ahead, axis=0), 0.0)
            if height < 128:
                ahead = jnp.concatenate([ahead, jnp.zeros((128 - height, 128), jnp.float32)], axis=0)
            ahead = wide(split3(ahead.T[:height]))
            update = dot(ahead, deep(padded(split3(pltpu.roll(slab, width - STEP, 1)))), NN)
            coming = [pltpu.roll(ref[t * team + i, pl.ds(after, STEP), :], width - after, 1) for i in range(team)]
            slab_ref[t] = jnp.where(col_team >= width - STEP, 0.0, jnp.concatenate(coming, axis=0)) - update
            slab = pltpu.roll(slab, base, 1)
            past_ref[t] = slab
            for i in range(team):
                own_rows = slab[i * STEP:(i + 1) * STEP]
                ref[t * team + i, pl.ds(base, STEP), :] = jnp.where(col_in >= base + STEP, 0.0, own_rows)
        return carry

    lax.fori_loop(0, width // STEP, block, 0)


def factor_scratch(systems, width):
    team = max(n for n in range(1, 128 // STEP + 1) if systems % n == 0)
    return [pltpu.VMEM((systems // team, team * STEP, width), jnp.float32)] * 2


def scaled(matrix):
    factor_of = 1.0 / jnp.max(jnp.max(matrix, axis=1, keepdims=True), axis=0, keepdims=True)
    return matrix * factor_of, jnp.sqrt(factor_of)


def pick_kernel(slot_ref, tiles_ref, *refs):
    out_refs, sems = refs[:-1], refs[-1]
    copies = []
    for e, out_ref in enumerate(out_refs):
        source = tiles_ref.at[jnp.maximum(slot_ref[e], 0), 0:2]
        copies.append(pltpu.make_async_copy(source, out_ref, sems.at[e]))
    for copy in copies:
        copy.start()
    for copy in copies:
        copy.wait()


def own_kernel(counts_ref, tiles_ref, w_ref, z_ref, g_ref, *scratch):
    systems, kslots, width, _ = tiles_ref.shape
    for s in range(systems):
        near = tiles_ref[s, 0:2].reshape(2 * width, width)
        g_ref[s] = dot(near, near, TN)
    for s in range(systems):
        for k in range(2, kslots):
            @pl.when(k < counts_ref[s])
            def _():
                tile = tiles_ref[s, k]
                g_ref[s] += dot(tile, tile, TN)
    roots = []
    for s in range(systems):
        g_ref[s], root = scaled(g_ref[s])
        roots.append(root)
    factor(g_ref, *scratch)
    for s in range(systems):
        w = split3(g_ref[s] * roots[s])
        w_ref[s, 0] = w[0]
        w_ref[s, 1] = w[1]
        own = jnp.concatenate([tiles_ref[s, 1], tiles_ref[s, 0]], axis=0)
        z = split3(dot(w[0], own, NT) + (dot(w[1], own, NT) + dot(w[2], own, NT)))
        for i in range(3):
            z_ref[s, i] = z[i]


def collect(slot_ref, shifts, got_refs, near_ref, sems):
    spare = near_ref.shape[0] - len(shifts)
    copies = []
    for i, (e, got_ref) in enumerate(zip(shifts, got_refs)):
        slot = jnp.where(slot_ref[e - 1] >= 0, slot_ref[e - 1], spare + i)
        copies.append(pltpu.make_async_copy(got_ref, near_ref.at[slot], sems.at[i]))
    for copy in copies:
        copy.start()
    return copies


def schur(near, z):
    near_t = near.T
    v = split3(dot(near_t, z[0], NT) + (dot(near_t, z[1], NT) + dot(near_t, z[2], NT)))
    return v, dot(near_t, near, NN) - dot6(v, v, NT)


def link_kernel(shifts, slot_ref, x_ref, z_any, *refs):
    got_refs, refs = refs[:len(shifts)], refs[len(shifts):]
    v_ref, t_ref, first_ref, z_ref, near_ref, z_sems, sems = refs
    systems, _, width, _ = z_ref.shape
    for s in range(systems):
        near_ref[s] = jnp.zeros(near_ref.shape[1:], near_ref.dtype)
    copies = collect(slot_ref, shifts, got_refs, near_ref, sems)
    z_copies = [pltpu.make_async_copy(z_any.at[s], z_ref.at[s], z_sems.at[s]) for s in range(systems)]
    for copy in z_copies:
        copy.start()
    for copy in copies:
        copy.wait()
    for s in range(systems):
        z_copies[s].wait()
        x = x_ref[:, s * width:(s + 1) * width]
        first_ref[s] = dot(x, z_ref[s, 0, :, width:], NT) + dot(x, z_ref[s, 1, :, width:], NT)
        v, t_ref[s] = schur(near_ref[s].reshape(2 * width, width), [z_ref[s, i] for i in range(3)])
        v_ref[s, 0] = v[0]
        v_ref[s, 1] = v[1]


def pair_kernel(lanes, shifts, late, place_ref, slot_ref, x_ref, first_ref, w_any, z_any, v_any, t_any, *refs):
    got_refs, up_refs, refs = refs[:len(shifts)], refs[len(shifts):len(shifts) + lanes], refs[len(shifts) + lanes:]
    low_ref, near_ref, w_ref, z_ref, v_ref, t_ref, r_ref, near_sems, sems, *scratch = refs
    _, _, width, _ = z_ref.shape
    systems = first_ref.shape[0]
    count = x_ref.shape[0] // lanes
    near_copies = collect(slot_ref, shifts, got_refs, near_ref, near_sems)
    late_slots = [slot_ref[e - 1] for e in late]
    copies = [
        pltpu.make_async_copy(z_any.at[jnp.maximum(slot, 0)], z_ref.at[i], sems.at[i]) for i, slot in enumerate(late_slots)
    ] + [
        pltpu.make_async_copy(t_any, t_ref.at[0:systems], sems.at[2]),
        pltpu.make_async_copy(v_any, v_ref.at[0:systems], sems.at[3]),
    ]
    w_copy = pltpu.make_async_copy(w_any, w_ref, sems.at[4])
    for copy in copies + [w_copy]:
        copy.start()
    low_ref[...] = jnp.zeros(low_ref.shape, low_ref.dtype)
    for copy in near_copies + copies[:-2]:
        copy.wait()
    formed = []
    for i, slot in enumerate(late_slots):
        near = near_ref[jnp.maximum(slot, 0)].reshape(2 * width, width)
        formed.append(schur(near, [z_ref[i, p] for p in range(3)]))
    for s in range(systems):
        r_ref[s] = dot(x_ref[:, s * width:(s + 1) * width], near_ref[s, 1], NN)
    for copy in copies[-2:]:
        copy.wait()
    for i, slot in enumerate(late_slots):
        at = jnp.where(slot >= 0, slot, systems + i)
        v, t_ref[at] = formed[i]
        v_ref[at, 0] = v[0]
        v_ref[at, 1] = v[1]
    roots = []
    for s in range(systems):
        r_ref[s] = r_ref[s] - apply(first_ref[s], (v_ref[s, 0], v_ref[s, 1]), NT)
        t_ref[s], root = scaled(t_ref[s])
        roots.append(root)
    factor(t_ref.at[0:systems], *scratch)
    w_copy.wait()
    parts = [split3(t_ref[s] * roots[s])[:2] for s in range(systems)]
    half = [apply(r_ref[s], parts[s], NT) for s in range(systems)]
    last = [apply(half[s], parts[s], NN) for s in range(systems)]
    mid = [first_ref[s] - apply(last[s], (v_ref[s, 0], v_ref[s, 1]), NN) for s in range(systems)]
    for s in range(systems):
        up = apply(mid[s], (w_ref[s, 0], w_ref[s, 1]), NN)
        for e in range(lanes):
            up_refs[e][s] = up[e * count:(e + 1) * count]
            owner = lax.rem(place_ref[systems] + e, lanes)
            low_ref[place_ref[s] * lanes + owner] = last[s][e * count:(e + 1) * count].astype(low_ref.dtype)


def place_kernel(lanes, place_ref, low_ref, *refs):
    up_refs, out_ref = refs[:lanes], refs[lanes]
    systems, _, width = up_refs[0].shape
    for e in range(lanes):
        owner = lax.rem(place_ref[systems * lanes] + lanes - e, lanes)
        for s in range(systems):
            at = owner * systems + s
            total = up_refs[e][s] + low_ref[place_ref[at] * lanes + owner].astype(jnp.float32)
            out_ref[:, pl.ds(pl.multiple_of(at * width, width), width)] = total.astype(out_ref.dtype)


def on_device(tiles, pattern, counts, inputs):
    shards = lax.axis_size("panel")
    lanes = lax.axis_size("rhs")
    systems, kslots, width, _ = tiles.shape
    nrhs_dev = inputs.shape[0]
    own_width = systems * width
    my_panel = lax.axis_index("panel")
    my_lane = lax.axis_index("rhs")
    per_panel = systems * lanes
    own_cnt = lax.dynamic_slice_in_dim(counts, my_panel * per_panel + my_lane * systems, systems, 0)
    panel_mates = lax.dynamic_slice(pattern, (my_panel * per_panel, 1), (per_panel, 1))[:, 0] // per_panel
    mate_panel = lax.dynamic_slice_in_dim(panel_mates, my_lane * systems, systems, 0)
    hops = jnp.arange(1, shards, dtype=jnp.int32)

    def slots(panels):
        hit = mate_panel[None, :] == panels[:, None]
        return jnp.max(jnp.where(hit, jnp.arange(systems, dtype=jnp.int32)[None, :], -1), axis=1)

    lane_word = my_lane[None].astype(jnp.int32)

    def shift(value, axis, by):
        size = lax.axis_size(axis)
        return lax.ppermute(value, axis, [(i, (i + by) % size) for i in range(size)])

    vmem = pl.BlockSpec(memory_space=pltpu.VMEM)
    smem = pl.BlockSpec(memory_space=pltpu.SMEM)
    anywhere = pl.BlockSpec(memory_space=pl.ANY)
    params = pltpu.CompilerParams(vmem_limit_bytes=48 * 1024 * 1024)
    pairs = shards - 1
    every = tuple(range(1, shards))
    late = (1, shards - 1)
    early = tuple(e for e in every if e not in late)
    most = pltpu.CompilerParams(vmem_limit_bytes=60 * 1024 * 1024)
    pieces = pl.pallas_call(
        pick_kernel,
        out_shape=[jax.ShapeDtypeStruct((2, width, width), jnp.bfloat16)] * pairs,
        in_specs=[smem, anywhere],
        out_specs=[vmem] * pairs,
        scratch_shapes=[pltpu.SemaphoreType.DMA((pairs,))],
        compiler_params=most,
    )(slots((my_panel + hops) % shards), tiles)
    received = {e: shift(pieces[e - 1], "panel", e) for e in early}

    w, z = pl.pallas_call(
        own_kernel,
        out_shape=(
            jax.ShapeDtypeStruct((systems, 2, width, width), jnp.bfloat16),
            jax.ShapeDtypeStruct((systems, 3, width, 2 * width), jnp.bfloat16),
        ),
        in_specs=[smem, vmem],
        out_specs=(vmem, vmem),
        scratch_shapes=[pltpu.VMEM((systems, width, width), jnp.float32)] + factor_scratch(systems, width),
        compiler_params=params,
        cost_estimate=pl.CostEstimate(flops=30 * 10**9, bytes_accessed=8 * 10**6, transcendentals=0),
    )(own_cnt, tiles)

    inputs, w = lax.optimization_barrier((inputs, w))
    x = lax.all_to_all(inputs, "rhs", split_axis=1, concat_axis=0, tiled=True)
    x = lax.dynamic_slice_in_dim(jnp.concatenate([x, x], axis=0), my_lane * nrhs_dev, lanes * nrhs_dev, 0)

    come = [received[e] for e in early]
    held, z, come = lax.optimization_barrier(([pieces[e - 1] for e in late], z, come))
    received.update(zip(early, come))
    received.update({e: shift(piece, "panel", e) for e, piece in zip(late, held)})
    from_slot = slots((my_panel - hops) % shards)
    v, t, first = pl.pallas_call(
        functools.partial(link_kernel, early),
        out_shape=(
            jax.ShapeDtypeStruct((systems, 2, width, width), jnp.bfloat16),
            jax.ShapeDtypeStruct((systems, width, width), jnp.float32),
            jax.ShapeDtypeStruct((systems, lanes * nrhs_dev, width), jnp.float32),
        ),
        in_specs=[smem, vmem] + [anywhere] * (1 + len(early)),
        out_specs=(vmem, vmem, vmem),
        scratch_shapes=[
            pltpu.VMEM((systems, 3, width, 2 * width), jnp.bfloat16),
            pltpu.VMEM((systems + len(early), 2, width, width), jnp.bfloat16),
            pltpu.SemaphoreType.DMA((systems,)),
            pltpu.SemaphoreType.DMA((len(early),)),
        ],
        compiler_params=params,
        cost_estimate=pl.CostEstimate(flops=12 * 10**9, bytes_accessed=8 * 10**6, transcendentals=0),
    )(from_slot, x, z, *[received[e] for e in early])

    nrhs = lanes * nrhs_dev
    piece = jax.ShapeDtypeStruct((systems, nrhs_dev, width), jnp.float32)
    *up, low = pl.pallas_call(
        functools.partial(pair_kernel, lanes, every, late),
        out_shape=[piece] * lanes + [jax.ShapeDtypeStruct((shards * lanes, nrhs_dev, width), jnp.bfloat16)],
        in_specs=[smem, smem, vmem, vmem] + [anywhere] * (4 + pairs),
        out_specs=[vmem] * (lanes + 1),
        scratch_shapes=[
            pltpu.VMEM((systems + pairs, 2, width, width), jnp.bfloat16),
            pltpu.VMEM((systems, 2, width, width), jnp.bfloat16),
            pltpu.VMEM((len(late), 3, width, 2 * width), jnp.bfloat16),
            pltpu.VMEM((systems + len(late), 2, width, width), jnp.bfloat16),
            pltpu.VMEM((systems + len(late), width, width), jnp.float32),
            pltpu.VMEM((systems, nrhs, width), jnp.float32),
            pltpu.SemaphoreType.DMA((pairs,)),
            pltpu.SemaphoreType.DMA((5,)),
        ] + factor_scratch(systems, width),
        compiler_params=params,
    )(
        jnp.concatenate([mate_panel, lane_word]), from_slot, x, first, w, z, v, t,
        *[received[e] for e in every],
    )
    low = lax.all_to_all(low, ("panel", "rhs"), split_axis=0, concat_axis=0, tiled=True)
    up = [up[0]] + [shift(up[e], "rhs", e) for e in range(1, lanes)]
    return pl.pallas_call(
        functools.partial(place_kernel, lanes),
        out_shape=jax.ShapeDtypeStruct((nrhs_dev, per_panel * width), jnp.bfloat16),
        in_specs=[smem] + [vmem] * (lanes + 1),
        out_specs=vmem,
    )(jnp.concatenate([panel_mates, lane_word]), low, *up)


def solution(mesh):
    return jax.shard_map(
        on_device,
        mesh=mesh,
        in_specs=(P(("panel", "rhs"), None, None, None), P(), P(), P("rhs", "panel")),
        out_specs=P("rhs", "panel"),
        check_vma=False,
    )
```

```python
import functools
import jax
import jax.numpy as jnp
from jax import lax
from jax.experimental import pallas as pl
from jax.experimental.pallas import tpu as pltpu
from jax.sharding import PartitionSpec as P

STEP = 64
ROUND = 8
NT = (((1,), (1,)), ((), ()))
NN = (((1,), (0,)), ((), ()))
TN = (((0,), (0,)), ((), ()))


def dot(a, b, dims):
    return lax.dot_general(a, b, dims, preferred_element_type=jnp.float32)


def split3(a):
    one = a.astype(jnp.bfloat16)
    rest = a - one.astype(jnp.float32)
    two = rest.astype(jnp.bfloat16)
    three = (rest - two.astype(jnp.float32)).astype(jnp.bfloat16)
    return one, two, three


def dot6(a, b, dims):
    a1, a2, a3 = a
    b1, b2, b3 = b
    small = dot(a1, b3, dims) + dot(a3, b1, dims) + dot(a2, b2, dims)
    return dot(a1, b1, dims) + ((dot(a1, b2, dims) + dot(a2, b1, dims)) + small)


def wide(parts):
    one, two, three = parts
    return jnp.concatenate([one, one, two, two, one, three], axis=1)


def deep(parts):
    one, two, three = parts
    return jnp.concatenate([one, two, one, two, three, one], axis=0)


def thirds(array):
    count = array.shape[0] // 3
    return array[:count] + (array[count:2 * count] + array[2 * count:])


def apply(rows, parts, dims):
    count = rows.shape[0]
    stack = jnp.concatenate(split3(rows), axis=0)
    high = dot(stack, parts[0], dims)
    low = dot(stack[:2 * count], parts[1], dims)
    return high[:count] + ((high[count:2 * count] + low[:count]) + (high[2 * count:] + low[count:]))


def factor(ref, slab_ref, past_ref):
    systems, width, _ = ref.shape
    teams, height, _ = slab_ref.shape
    team = height // STEP
    groups = STEP // 8
    lane = lax.broadcasted_iota(jnp.int32, (8, 128), 1)
    sub = lax.broadcasted_iota(jnp.int32, (8, 128), 0)
    member = lane // STEP
    place = lane % STEP
    col_in = lax.broadcasted_iota(jnp.int32, (STEP, width), 1)
    row_all = lax.broadcasted_iota(jnp.int32, (width, width), 0)
    col_all = lax.broadcasted_iota(jnp.int32, (width, width), 1)
    row_team = lax.broadcasted_iota(jnp.int32, (height, width), 0)
    col_team = lax.broadcasted_iota(jnp.int32, (height, width), 1)
    row_diag = lax.broadcasted_iota(jnp.int32, (height, 128), 0)
    col_diag = lax.broadcasted_iota(jnp.int32, (height, 128), 1)
    same = row_diag // STEP == col_diag // STEP
    lower = same & (col_diag <= row_diag)

    def spread(row):
        return jnp.broadcast_to(row, (8, 128))

    def padded(parts):
        if height == 128:
            return parts
        filler = jnp.zeros((128 - height, width), jnp.bfloat16)
        return [jnp.concatenate([part, filler], axis=0) for part in parts]

    def pivots(packs, pieces):
        placed = 0
        for first in range(0, STEP, ROUND):
            top, start = first // 8, first % 8
            tall = range(top, groups)
            own = (place >= first) & (place < first + ROUND)
            one = jnp.where(place - 8 * top == sub, 1.0, 0.0)
            each = range(len(packs))
            if start == 0:
                inverses = [None for _ in each]
            u = [
                [{g: jnp.take_along_axis(x[g], lane - place + (first + q), axis=1) for g in tall} for q in range(ROUND)]
                for x in packs
            ]
            a = [{(i, j): spread(u[s][j][top][start + i:start + i + 1, :]) for j in range(ROUND) for i in range(j + 1)} for s in each]
            for x in packs:
                for g in tall:
                    x[g] = jnp.where(own, one if g == top else 0.0, x[g])
            y = [[spread(x[top][start + q:start + q + 1, :]) for q in range(ROUND)] for x in packs]
            low = [{} for _ in each]
            inv = [[None] * ROUND for _ in each]
            for p in range(0, ROUND, 2):
                n = p + 1
                delta = [a[s][p, p] * a[s][n, n] - a[s][p, n] * a[s][p, n] for s in each]
                for s in each:
                    inv[s][p] = pl.reciprocal(a[s][p, p], approx=True)
                    inv[s][n] = pl.reciprocal(delta[s], approx=True) * a[s][p, p]
                for j in range(n, ROUND):
                    for s in each:
                        low[s][j, p] = a[s][p, j] * inv[s][p]
                for j in range(n + 1, ROUND):
                    for s in each:
                        a[s][n, j] = a[s][n, j] - low[s][n, p] * a[s][p, j]
                for j in range(n + 1, ROUND):
                    for s in each:
                        low[s][j, n] = a[s][n, j] * inv[s][n]
                for i in range(n + 1, ROUND):
                    for j in range(i, ROUND):
                        for s in each:
                            a[s][i, j] = (a[s][i, j] - low[s][i, p] * a[s][p, j]) - low[s][i, n] * a[s][n, j]
            for q in range(ROUND):
                at = start + q
                for s in each:
                    for k in range(q):
                        for g in tall:
                            u[s][q][g] = u[s][q][g] - u[s][k][g] * low[s][q, k]
                        y[s][q] = y[s][q] - y[s][k] * low[s][q, k]
                    inverses[s] = inv[s][q] if at == 0 else jnp.where(sub >= at, inv[s][q], inverses[s])
                    for g in tall:
                        m = u[s][q][g] * inv[s][q]
                        if g == top:
                            m = jnp.where(sub > at, m, 0.0)
                        packs[s][g] = packs[s][g] - m * y[s][q]
                while placed * STEP < (first + q + 1) * len(pieces):
                    pieces[placed]()
                    placed += 1
            if start + ROUND == 8:
                for s, x in enumerate(packs):
                    x[top] = x[top] * (inverses[s] * lax.rsqrt(inverses[s]))

    for t in range(teams):
        for i in range(team):
            slab_ref[t, i * STEP:(i + 1) * STEP] = ref[t * team + i, 0:STEP]
        past_ref[t] = jnp.zeros(past_ref.shape[1:], past_ref.dtype)

    def block(kb, carry):
        base = pl.multiple_of(kb * STEP, STEP)
        after = pl.multiple_of(jnp.minimum(base + STEP, width - STEP), STEP)
        done = (col_all >= base - STEP) & (col_all < base) & (row_all >= base + STEP)
        pieces = []
        for s in range(systems):
            held = {}

            def prepare(s=s, held=held):
                i = s % team
                p1, p2, p3 = split3(past_ref[s // team, i * STEP:(i + 1) * STEP])
                zero = jnp.zeros_like(p1)
                m1, m2, m3 = (jnp.where(col_in >= base + STEP, p, zero) for p in (p1, p2, p3))
                held["left"] = jnp.concatenate([m1, m1, m2, m2, m1, m3], axis=0)
                held["right"] = jnp.concatenate([p1, p2, p1, p2, p3, p1], axis=0)

            def trail(at, s=s, held=held):
                rows = slice(at, at + 128)
                update = dot(held["left"][:, rows], held["right"], TN)
                ref[s, rows] = jnp.where(done[rows], 0.0, ref[s, rows]) - update

            pieces.append(prepare)
            pieces.extend(functools.partial(trail, at) for at in range(0, width, 128))
        packs = []
        for t in range(teams):
            pack = []
            for g in range(groups):
                x = jnp.where(place - 8 * g == sub, 1.0, 0.0)
                for i in range(team):
                    piece = slab_ref[t, i * STEP + 8 * g:i * STEP + 8 * g + 8, 0:128]
                    if i > 0:
                        piece = pltpu.roll(piece, i * STEP, 1)
                    x = jnp.where(member == i, piece, x)
                pack.append(x)
            packs.append(pack)
        sides = []
        for t in range(teams):
            ident = jnp.where(col_team == row_team % STEP, 1.0, 0.0)
            sides.append(deep(padded(split3(jnp.where(col_team < STEP, ident, slab_ref[t])))))
        pivots(packs, pieces)
        for t in range(teams):
            inner = jnp.concatenate(packs[t], axis=0)
            inner = jnp.where(lower, jnp.concatenate([inner] * team, axis=0), 0.0)
            slab = dot(wide(split3(inner)), sides[t], NN)
            ahead = []
            for i in range(team):
                piece = slab[i * STEP:(i + 1) * STEP, 0:128]
                if i != 1:
                    piece = pltpu.roll(piece, (i - 1) * STEP % 128, 1)
                ahead.append(piece)
            ahead = jnp.where(same, jnp.concatenate(ahead, axis=0), 0.0)
            if height < 128:
                ahead = jnp.concatenate([ahead, jnp.zeros((128 - height, 128), jnp.float32)], axis=0)
            ahead = wide(split3(ahead.T[:height]))
            update = dot(ahead, deep(padded(split3(pltpu.roll(slab, width - STEP, 1)))), NN)
            coming = [pltpu.roll(ref[t * team + i, pl.ds(after, STEP), :], width - after, 1) for i in range(team)]
            slab_ref[t] = jnp.where(col_team >= width - STEP, 0.0, jnp.concatenate(coming, axis=0)) - update
            slab = pltpu.roll(slab, base, 1)
            past_ref[t] = slab
            for i in range(team):
                own_rows = slab[i * STEP:(i + 1) * STEP]
                ref[t * team + i, pl.ds(base, STEP), :] = jnp.where(col_in >= base + STEP, 0.0, own_rows)
        return carry

    lax.fori_loop(0, width // STEP, block, 0)


def factor_scratch(systems, width):
    team = max(n for n in range(1, 128 // STEP + 1) if systems % n == 0)
    return [pltpu.VMEM((systems // team, team * STEP, width), jnp.float32)] * 2


def scaled(matrix):
    factor_of = 1.0 / jnp.max(jnp.max(matrix, axis=1, keepdims=True), axis=0, keepdims=True)
    return matrix * factor_of, jnp.sqrt(factor_of)


def pick_kernel(slot_ref, tiles_ref, *refs):
    out_refs, sems = refs[:-1], refs[-1]
    copies = []
    for e, out_ref in enumerate(out_refs):
        source = tiles_ref.at[jnp.maximum(slot_ref[e], 0), 0:2]
        copies.append(pltpu.make_async_copy(source, out_ref, sems.at[e]))
    for copy in copies:
        copy.start()
    for copy in copies:
        copy.wait()


def own_kernel(counts_ref, tiles_ref, w_ref, z_ref, g_ref, *scratch):
    systems, kslots, width, _ = tiles_ref.shape
    for s in range(systems):
        near = tiles_ref[s, 0:2].reshape(2 * width, width)
        g_ref[s] = dot(near, near, TN)
    for s in range(systems):
        for k in range(2, kslots):
            @pl.when(k < counts_ref[s])
            def _():
                tile = tiles_ref[s, k]
                g_ref[s] += dot(tile, tile, TN)
    roots = []
    for s in range(systems):
        g_ref[s], root = scaled(g_ref[s])
        roots.append(root)
    factor(g_ref, *scratch)
    for s in range(systems):
        w = split3(g_ref[s] * roots[s])
        w_ref[s, 0] = w[0]
        w_ref[s, 1] = w[1]
        own = jnp.concatenate([tiles_ref[s, 1], tiles_ref[s, 0]], axis=0)
        z = split3(dot(w[0], own, NT) + (dot(w[1], own, NT) + dot(w[2], own, NT)))
        for i in range(3):
            z_ref[s, i] = z[i]


def collect(slot_ref, shifts, got_refs, near_ref, sems):
    spare = near_ref.shape[0] - len(shifts)
    copies = []
    for i, (e, got_ref) in enumerate(zip(shifts, got_refs)):
        slot = jnp.where(slot_ref[e - 1] >= 0, slot_ref[e - 1], spare + i)
        copies.append(pltpu.make_async_copy(got_ref, near_ref.at[slot], sems.at[i]))
    for copy in copies:
        copy.start()
    return copies


def schur(near, z):
    near_t = near.T
    v = split3(dot(near_t, z[0], NT) + (dot(near_t, z[1], NT) + dot(near_t, z[2], NT)))
    return v, dot(near_t, near, NN) - dot6(v, v, NT)


def link_kernel(shifts, slot_ref, x_ref, z_any, *refs):
    got_refs, refs = refs[:len(shifts)], refs[len(shifts):]
    v_ref, t_ref, first_ref, z_ref, near_ref, z_sems, sems = refs
    systems, _, width, _ = z_ref.shape
    for s in range(systems):
        near_ref[s] = jnp.zeros(near_ref.shape[1:], near_ref.dtype)
    copies = collect(slot_ref, shifts, got_refs, near_ref, sems)
    z_copies = [pltpu.make_async_copy(z_any.at[s], z_ref.at[s], z_sems.at[s]) for s in range(systems)]
    for copy in z_copies:
        copy.start()
    for copy in copies:
        copy.wait()
    for s in range(systems):
        z_copies[s].wait()
        x = x_ref[:, s * width:(s + 1) * width]
        first_ref[s] = dot(x, z_ref[s, 0, :, width:], NT) + dot(x, z_ref[s, 1, :, width:], NT)
        v, t_ref[s] = schur(near_ref[s].reshape(2 * width, width), [z_ref[s, i] for i in range(3)])
        v_ref[s, 0] = v[0]
        v_ref[s, 1] = v[1]


def pair_kernel(lanes, shifts, late, place_ref, slot_ref, x_ref, first_ref, w_any, z_any, v_any, t_any, *refs):
    got_refs, up_refs, refs = refs[:len(shifts)], refs[len(shifts):len(shifts) + lanes], refs[len(shifts) + lanes:]
    low_ref, near_ref, w_ref, z_ref, v_ref, t_ref, r_ref, near_sems, sems, *scratch = refs
    _, _, width, _ = z_ref.shape
    systems = first_ref.shape[0]
    count = x_ref.shape[0] // lanes
    near_copies = collect(slot_ref, shifts, got_refs, near_ref, near_sems)
    late_slots = [slot_ref[e - 1] for e in late]
    copies = [
        pltpu.make_async_copy(z_any.at[jnp.maximum(slot, 0)], z_ref.at[i], sems.at[i]) for i, slot in enumerate(late_slots)
    ] + [
        pltpu.make_async_copy(t_any, t_ref.at[0:systems], sems.at[2]),
        pltpu.make_async_copy(v_any, v_ref.at[0:systems], sems.at[3]),
    ]
    w_copy = pltpu.make_async_copy(w_any, w_ref, sems.at[4])
    for copy in copies + [w_copy]:
        copy.start()
    low_ref[...] = jnp.zeros(low_ref.shape, low_ref.dtype)
    for copy in near_copies + copies[:-2]:
        copy.wait()
    formed = []
    for i, slot in enumerate(late_slots):
        near = near_ref[jnp.maximum(slot, 0)].reshape(2 * width, width)
        formed.append(schur(near, [z_ref[i, p] for p in range(3)]))
    for s in range(systems):
        r_ref[s] = dot(x_ref[:, s * width:(s + 1) * width], near_ref[s, 1], NN)
    for copy in copies[-2:]:
        copy.wait()
    for i, slot in enumerate(late_slots):
        at = jnp.where(slot >= 0, slot, systems + i)
        v, t_ref[at] = formed[i]
        v_ref[at, 0] = v[0]
        v_ref[at, 1] = v[1]
    roots = []
    for s in range(systems):
        r_ref[s] = r_ref[s] - apply(first_ref[s], (v_ref[s, 0], v_ref[s, 1]), NT)
        t_ref[s], root = scaled(t_ref[s])
        roots.append(root)
    factor(t_ref.at[0:systems], *scratch)
    w_copy.wait()
    parts = [split3(t_ref[s] * roots[s])[:2] for s in range(systems)]
    half = [apply(r_ref[s], parts[s], NT) for s in range(systems)]
    last = [apply(half[s], parts[s], NN) for s in range(systems)]
    mid = [first_ref[s] - apply(last[s], (v_ref[s, 0], v_ref[s, 1]), NN) for s in range(systems)]
    for s in range(systems):
        up = apply(mid[s], (w_ref[s, 0], w_ref[s, 1]), NN)
        for e in range(lanes):
            up_refs[e][s] = up[e * count:(e + 1) * count]
            owner = lax.rem(place_ref[systems] + e, lanes)
            low_ref[place_ref[s] * lanes + owner] = last[s][e * count:(e + 1) * count].astype(low_ref.dtype)


def place_kernel(lanes, place_ref, low_ref, *refs):
    up_refs, out_ref = refs[:lanes], refs[lanes]
    systems, _, width = up_refs[0].shape
    for e in range(lanes):
        owner = lax.rem(place_ref[systems * lanes] + lanes - e, lanes)
        for s in range(systems):
            at = owner * systems + s
            total = up_refs[e][s] + low_ref[place_ref[at] * lanes + owner].astype(jnp.float32)
            out_ref[:, pl.ds(pl.multiple_of(at * width, width), width)] = total.astype(out_ref.dtype)


def on_device(tiles, pattern, counts, inputs):
    shards = lax.axis_size("panel")
    lanes = lax.axis_size("rhs")
    systems, kslots, width, _ = tiles.shape
    nrhs_dev = inputs.shape[0]
    own_width = systems * width
    my_panel = lax.axis_index("panel")
    my_lane = lax.axis_index("rhs")
    per_panel = systems * lanes
    own_cnt = lax.dynamic_slice_in_dim(counts, my_panel * per_panel + my_lane * systems, systems, 0)
    panel_mates = lax.dynamic_slice(pattern, (my_panel * per_panel, 1), (per_panel, 1))[:, 0] // per_panel
    mate_panel = lax.dynamic_slice_in_dim(panel_mates, my_lane * systems, systems, 0)
    hops = jnp.arange(1, shards, dtype=jnp.int32)

    def slots(panels):
        hit = mate_panel[None, :] == panels[:, None]
        return jnp.max(jnp.where(hit, jnp.arange(systems, dtype=jnp.int32)[None, :], -1), axis=1)

    lane_word = my_lane[None].astype(jnp.int32)

    def shift(value, axis, by):
        size = lax.axis_size(axis)
        return lax.ppermute(value, axis, [(i, (i + by) % size) for i in range(size)])

    vmem = pl.BlockSpec(memory_space=pltpu.VMEM)
    smem = pl.BlockSpec(memory_space=pltpu.SMEM)
    anywhere = pl.BlockSpec(memory_space=pl.ANY)
    params = pltpu.CompilerParams(vmem_limit_bytes=48 * 1024 * 1024)
    pairs = shards - 1
    every = tuple(range(1, shards))
    late = (1, shards - 1)
    early = tuple(e for e in every if e not in late)
    most = pltpu.CompilerParams(vmem_limit_bytes=60 * 1024 * 1024)
    pieces = pl.pallas_call(
        pick_kernel,
        out_shape=[jax.ShapeDtypeStruct((2, width, width), jnp.bfloat16)] * pairs,
        in_specs=[smem, anywhere],
        out_specs=[vmem] * pairs,
        scratch_shapes=[pltpu.SemaphoreType.DMA((pairs,))],
        compiler_params=most,
    )(slots((my_panel + hops) % shards), tiles)
    received = {e: shift(pieces[e - 1], "panel", e) for e in early}

    w, z = pl.pallas_call(
        own_kernel,
        out_shape=(
            jax.ShapeDtypeStruct((systems, 2, width, width), jnp.bfloat16),
            jax.ShapeDtypeStruct((systems, 3, width, 2 * width), jnp.bfloat16),
        ),
        in_specs=[smem, vmem],
        out_specs=(vmem, vmem),
        scratch_shapes=[pltpu.VMEM((systems, width, width), jnp.float32)] + factor_scratch(systems, width),
        compiler_params=params,
        cost_estimate=pl.CostEstimate(flops=30 * 10**9, bytes_accessed=8 * 10**6, transcendentals=0),
    )(own_cnt, tiles)

    inputs, w = lax.optimization_barrier((inputs, w))
    x = lax.all_to_all(inputs, "rhs", split_axis=1, concat_axis=0, tiled=True)
    x = lax.dynamic_slice_in_dim(jnp.concatenate([x, x], axis=0), my_lane * nrhs_dev, lanes * nrhs_dev, 0)

    come = [received[e] for e in early]
    held, z, come = lax.optimization_barrier(([pieces[e - 1] for e in late], z, come))
    received.update(zip(early, come))
    received.update({e: shift(piece, "panel", e) for e, piece in zip(late, held)})
    from_slot = slots((my_panel - hops) % shards)
    v, t, first = pl.pallas_call(
        functools.partial(link_kernel, early),
        out_shape=(
            jax.ShapeDtypeStruct((systems, 2, width, width), jnp.bfloat16),
            jax.ShapeDtypeStruct((systems, width, width), jnp.float32),
            jax.ShapeDtypeStruct((systems, lanes * nrhs_dev, width), jnp.float32),
        ),
        in_specs=[smem, vmem] + [anywhere] * (1 + len(early)),
        out_specs=(vmem, vmem, vmem),
        scratch_shapes=[
            pltpu.VMEM((systems, 3, width, 2 * width), jnp.bfloat16),
            pltpu.VMEM((systems + len(early), 2, width, width), jnp.bfloat16),
            pltpu.SemaphoreType.DMA((systems,)),
            pltpu.SemaphoreType.DMA((len(early),)),
        ],
        compiler_params=params,
        cost_estimate=pl.CostEstimate(flops=12 * 10**9, bytes_accessed=8 * 10**6, transcendentals=0),
    )(from_slot, x, z, *[received[e] for e in early])

    nrhs = lanes * nrhs_dev
    piece = jax.ShapeDtypeStruct((systems, nrhs_dev, width), jnp.float32)
    *up, low = pl.pallas_call(
        functools.partial(pair_kernel, lanes, every, late),
        out_shape=[piece] * lanes + [jax.ShapeDtypeStruct((shards * lanes, nrhs_dev, width), jnp.bfloat16)],
        in_specs=[smem, smem, vmem, vmem] + [anywhere] * (4 + pairs),
        out_specs=[vmem] * (lanes + 1),
        scratch_shapes=[
            pltpu.VMEM((systems + pairs, 2, width, width), jnp.bfloat16),
            pltpu.VMEM((systems, 2, width, width), jnp.bfloat16),
            pltpu.VMEM((len(late), 3, width, 2 * width), jnp.bfloat16),
            pltpu.VMEM((systems + len(late), 2, width, width), jnp.bfloat16),
            pltpu.VMEM((systems + len(late), width, width), jnp.float32),
            pltpu.VMEM((systems, nrhs, width), jnp.float32),
            pltpu.SemaphoreType.DMA((pairs,)),
            pltpu.SemaphoreType.DMA((5,)),
        ] + factor_scratch(systems, width),
        compiler_params=params,
    )(
        jnp.concatenate([mate_panel, lane_word]), from_slot, x, first, w, z, v, t,
        *[received[e] for e in every],
    )
    low = lax.all_to_all(low, ("panel", "rhs"), split_axis=0, concat_axis=0, tiled=True)
    up = [up[0]] + [shift(up[e], "rhs", e) for e in range(1, lanes)]
    return pl.pallas_call(
        functools.partial(place_kernel, lanes),
        out_shape=jax.ShapeDtypeStruct((nrhs_dev, per_panel * width), jnp.bfloat16),
        in_specs=[smem] + [vmem] * (lanes + 1),
        out_specs=vmem,
    )(jnp.concatenate([panel_mates, lane_word]), low, *up)


def solution(mesh):
    return jax.shard_map(
        on_device,
        mesh=mesh,
        in_specs=(P(("panel", "rhs"), None, None, None), P(), P(), P("rhs", "panel")),
        out_specs=P("rhs", "panel"),
        check_vma=False,
    )
```
